32 devices in a mesh: rows: 8 (over y, x, core), cols: 4 (over z).
Axes of the slice: x: 2, y: 2, z: 4, core: 2. Of those that a mesh axis runs over, the one named last changes fastest.
Arguments:
- coadd_flux: float32 [1024, 4096], P('rows', 'cols'), may hold values from -8 to 8
- inverse_variance: float32 [1024, 4096], P('rows', 'cols'), may hold values from 0.25 to 4
- source_mask: int32 [1024, 4096], P('rows', 'cols'), may hold values 0 or 1
Outputs:
- background: float32 [1024, 4096], P('rows', 'cols')
- rms_map: float32 [1024, 4096], P('rows', 'cols')
The draws below stay inside these ranges and needn't reach their ends.
All inputs are finite; a program needn't handle non-finite values. No bound on the sum of `source_mask` on one device may be relied on, other than what follows from the above.
Results may differ from the reference program's by a relative error of at most 0.0001.
Values sent between devices are 32-bit elements; how exact they have to be, the bound alone decides.
No kernel may reach another device: no remote copies, remote signals or barrier semaphores. Data moves between devices by JAX's collectives and lax.ppermute only.
A program may use at most 64 MiB of HBM per device.

```python
import math
import jax
import jax.numpy as jnp

ITERS = 2
RADIUS = 32
NR = 1024
NC = 4096


def with_ends(entries, key, smallest, largest):
    index_at = [jax.random.randint(jax.random.fold_in(key, axis), (), 0, length) for axis, length in enumerate(entries.shape)]
    widest = entries.shape.index(max(entries.shape))
    neighbour = index_at[:widest] + [(index_at[widest] + 1) % entries.shape[widest]] + index_at[widest + 1:]
    return entries.at[tuple(index_at)].set(smallest).at[tuple(neighbour)].set(largest)


def block_scale(stream_key, shape, cuts, low, high):
    def one(dim, blocks):
        heights = jax.random.uniform(jax.random.fold_in(jax.random.fold_in(stream_key, 6), dim), (blocks,), jnp.float32, low / len(cuts), high / len(cuts))
        return jnp.repeat(jnp.exp(heights), shape[dim] // blocks).reshape((-1,) + (1,) * (len(shape) - dim - 1))

    loudness = one(*cuts[0])
    for cut in cuts[1:]:
        loudness = loudness * one(*cut)
    return loudness


def gaussian(own_key, dims, scale, reach, cuts=(), kind=jnp.bfloat16):
    drawn = scale * jax.random.normal(own_key, dims, jnp.float32)
    if cuts:
        drawn = drawn * block_scale(own_key, dims, cuts, -0.22, 0.18)
    return jnp.clip(drawn, -reach, reach).astype(kind)


def setup_inputs(seed: int = 0) -> dict:
    key_list = jax.random.split(jax.random.key(seed), 4)
    return {
        "coadd_flux": gaussian(key_list[0], (NR, NC), 1.0, 8.0, ((0, 8), (1, 4)), jnp.float32),
        "inverse_variance": jnp.clip(jnp.exp(math.log(4.0) - 2.7725887 * jax.random.uniform(key_list[1], (NR, NC), jnp.float32) ** block_scale(key_list[1], (NR, NC), ((0, 8), (1, 4)), -0.2, 0.2)), 0.25, 4.0),
        "source_mask": with_ends((jax.random.randint(key_list[2], (NR, NC), 0, 4) < 1).astype(jnp.int32), jax.random.fold_in(key_list[2], 1), 0, 1),
    }


smooth_weight = 2.0
blur_sigma = 10.0

def apply_operator(field, weight):
    padded = jnp.pad(field, 1)
    beside = padded[2:, 1:-1] + padded[:-2, 1:-1] + padded[1:-1, 2:] + padded[1:-1, :-2]
    return weight * field + smooth_weight * (4.0 * field - beside)

def tap_values():
    offsets = jnp.arange(2 * RADIUS + 1).astype(jnp.float32) - RADIUS
    raw_taps = jnp.exp(-offsets * offsets / (2.0 * blur_sigma * blur_sigma))
    return raw_taps / jnp.sum(raw_taps)

def blur_leading(field):
    taps = tap_values()
    padded = jnp.pad(field, ((RADIUS, RADIUS), (0, 0)))
    length = field.shape[0]
    summed = jnp.zeros_like(field)
    for offset in range(2 * RADIUS + 1):
        summed = summed + taps[offset] * padded[offset:offset + length]
    return summed

def reference(coadd_flux, inverse_variance, source_mask):
    weight = inverse_variance * (1.0 - source_mask.astype(jnp.float32))
    background = jnp.zeros_like(coadd_flux)
    residual = weight * coadd_flux
    direction = residual
    norm_now = jnp.sum(residual * residual)
    for step in range(ITERS):
        image_term = apply_operator(direction, weight)
        alpha = norm_now / jnp.sum(direction * image_term)
        background = background + alpha * direction
        residual = residual - alpha * image_term
        if step + 1 < ITERS:
            norm_next = jnp.sum(residual * residual)
            direction = residual + norm_next / norm_now * direction
            norm_now = norm_next
    scatter = coadd_flux - background
    smoothed = scatter * scatter
    for repeat in range(2):
        smoothed = blur_leading(smoothed)
        smoothed = blur_leading(smoothed.T).T
    return (background, jnp.sqrt(smoothed + 1e-06))
```

```python
import functools

import jax
import jax.numpy as jnp
import ml_dtypes
import numpy as np
from jax import lax
from jax.experimental import pallas as pl
from jax.experimental.pallas import tpu as pltpu
from jax.sharding import PartitionSpec as P

RADIUS = 32
REACH = 2 * RADIUS
LANES = 128
WIDE = REACH + 8
NEAR = 8

smooth_weight = 2.0
blur_sigma = 10.0


def squared_taps(length, first, last):
    offsets = np.arange(2 * RADIUS + 1) - RADIUS
    taps = np.exp(-offsets * offsets / (2.0 * blur_sigma * blur_sigma))
    taps = taps / taps.sum()

    def band(count):
        table = np.zeros((count, count + 2 * RADIUS))
        for k in range(2 * RADIUS + 1):
            table[np.arange(count), np.arange(count) + k] = taps[k]
        return table

    inner = band(length + 2 * RADIUS)
    if first:
        inner[:RADIUS] = 0.0
    if last:
        inner[-RADIUS:] = 0.0
    return band(length) @ inner


def split(table):
    high = table.astype(np.float32).astype(ml_dtypes.bfloat16)
    low = (table - high.astype(np.float64)).astype(np.float32).astype(ml_dtypes.bfloat16)
    return high, low


def row_tables(length):
    tables = []
    for first, last in ((False, False), (True, False), (False, True), (True, True)):
        tables.append(np.concatenate(split(squared_taps(length, first, last)), axis=0))
    return np.stack(tables)


def col_tables():
    tables = []
    for first, last in ((False, False), (True, False), (False, True)):
        tables.append(np.concatenate(split(squared_taps(LANES, first, last).T), axis=1))
    return np.stack(tables)


def split_values(values):
    high = values.astype(jnp.bfloat16)
    return high, (values - high.astype(jnp.float32)).astype(jnp.bfloat16)


def at_edges():
    row, col = lax.axis_index("rows"), lax.axis_index("cols")
    return (
        row == 0,
        row == lax.axis_size("rows") - 1,
        col == 0,
        col == lax.axis_size("cols") - 1,
    )


def beside_columns(field):
    width = field.shape[1]
    return pltpu.roll(field, 1, 1) + pltpu.roll(field, width - 1, 1)


def moments_kernel(f_ref, w_ref, top_ref, bottom_ref, left_ref, right_ref, out_ref, v0_ref, v1_ref):
    rows, cols = f_ref.shape
    width = cols + 2 * LANES
    first_row, last_row, first_col, last_col = at_edges()

    def pair(start):
        if start < NEAR:
            return top_ref[0], top_ref[1]
        if start >= NEAR + rows:
            return bottom_ref[0], bottom_ref[1]
        at = pl.ds(start - NEAR, 8)
        return tuple(
            jnp.concatenate([left_ref[i, at, :], ref[at, :], right_ref[i, at, :]], axis=1)
            for i, ref in enumerate((f_ref, w_ref))
        )

    for start in range(0, rows + 2 * NEAR, 8):
        flux, weight = pair(start)
        v0_ref[pl.ds(start, 8), :] = flux * weight

    zeros = jnp.zeros((8, width), jnp.float32)
    v1_ref[pl.ds(0, 8), :] = zeros
    v1_ref[pl.ds(rows + 2 * NEAR - 8, 8), :] = zeros

    def image(ref, weight, start, count):
        here = ref[pl.ds(start, count), :]
        beside = ref[pl.ds(start - 1, count), :] + ref[pl.ds(start + 1, count), :] + beside_columns(here)
        return here, weight * here + smooth_weight * (4.0 * here - beside)

    for start in range(NEAR, NEAR + rows, 8):
        _, weight = pair(start)
        _, out = image(v0_ref, weight, start, 8)
        v1_ref[pl.ds(start, 8), :] = out

    @pl.when(jnp.logical_not(first_row))
    def _():
        _, out = image(v0_ref, top_ref[1, pl.ds(NEAR - 1, 1), :], NEAR - 1, 1)
        v1_ref[pl.ds(NEAR - 1, 1), :] = out

    @pl.when(jnp.logical_not(last_row))
    def _():
        _, out = image(v0_ref, bottom_ref[1, pl.ds(0, 1), :], NEAR + rows, 1)
        v1_ref[pl.ds(NEAR + rows, 1), :] = out

    @pl.when(first_col)
    def _():
        v1_ref[:, pl.ds(0, LANES)] = jnp.zeros((rows + 2 * NEAR, LANES), jnp.float32)

    @pl.when(last_col)
    def _():
        v1_ref[:, pl.ds(width - LANES, LANES)] = jnp.zeros((rows + 2 * NEAR, LANES), jnp.float32)

    sums = [jnp.zeros((8, cols), jnp.float32) for _ in range(4)]
    for start in range(NEAR, NEAR + rows, 8):
        _, weight = pair(start)
        v1, v2 = image(v1_ref, weight, start, 8)
        v0, v1, v2 = (x[:, LANES : LANES + cols] for x in (v0_ref[pl.ds(start, 8), :], v1, v2))
        sums = [total + term for total, term in zip(sums, (v0 * v0, v0 * v1, v1 * v1, v1 * v2))]
    for i, total in enumerate(sums):
        narrow = sum(total[:, k : k + LANES] for k in range(0, cols, LANES))
        out_ref[pl.ds(i, 1), :] = jnp.sum(narrow, axis=0, keepdims=True)
    out_ref[pl.ds(4, 4), :] = jnp.zeros((4, LANES), jnp.float32)


def coefficients(m0, m1, m2, m3):
    alpha0 = m0 / m1
    norm1 = jnp.maximum(m0 - 2.0 * alpha0 * m1 + alpha0 * alpha0 * m2, 0.0)
    grown = 1.0 + norm1 / m0
    image1 = grown * grown * m1 - 2.0 * grown * alpha0 * m2 + alpha0 * alpha0 * m3
    alpha1 = jnp.where(image1 > 0.0, norm1 / image1, 0.0)
    return alpha0 + alpha1 * grown, -alpha1 * alpha0


def finish_kernel(
    parts_ref, f_ref, w_ref, top_ref, bottom_ref, left_ref, right_ref, rowtaps_ref, coltaps_ref,
    background_ref, rms_ref, v0_ref, high_ref, low_ref,
):
    rows, cols = f_ref.shape
    width = cols + 2 * LANES
    first_row, last_row, first_col, last_col = at_edges()

    totals = jnp.sum(parts_ref[...], axis=0)
    c0, c1 = coefficients(*(jnp.sum(totals[i : i + 1, :], axis=1, keepdims=True) for i in range(4)))

    def pair(start, count):
        if start < WIDE:
            at = pl.ds(start, count)
            return top_ref[0, at, :], top_ref[1, at, :]
        if start >= WIDE + rows:
            at = pl.ds(start - WIDE - rows, count)
            return bottom_ref[0, at, :], bottom_ref[1, at, :]
        at = pl.ds(start - WIDE, count)
        return tuple(
            jnp.concatenate([left_ref[i, at, :], ref[at, :], right_ref[i, at, :]], axis=1)
            for i, ref in enumerate((f_ref, w_ref))
        )

    for start in range(0, rows + 2 * WIDE, 8):
        flux, weight = pair(start, 8)
        v0_ref[pl.ds(start, 8), :] = flux * weight

    step = 16
    for start in range(8, rows + 2 * WIDE - 8, step):
        flux, weight = pair(start, step)
        v0 = v0_ref[pl.ds(start, step), :]
        beside = v0_ref[pl.ds(start - 1, step), :] + v0_ref[pl.ds(start + 1, step), :] + beside_columns(v0)
        v1 = weight * v0 + smooth_weight * (4.0 * v0 - beside)
        background = c0 * v0 + c1 * v1
        if WIDE <= start < WIDE + rows:
            background_ref[pl.ds(start - WIDE, step), :] = background[:, LANES : LANES + cols]
        scatter = flux - background
        high, low = split_values(scatter * scatter)
        high_ref[pl.ds(start - 8, step), :] = high
        low_ref[pl.ds(start - 8, step), :] = low

    def clear(at_rows, at_cols):
        for ref in (high_ref, low_ref):
            ref[at_rows, at_cols] = jnp.zeros((at_rows.size, at_cols.size), jnp.bfloat16)

    everywhere_r, everywhere_c = pl.ds(0, rows + 2 * REACH), pl.ds(0, width)
    pl.when(first_row)(lambda: clear(pl.ds(0, REACH), everywhere_c))
    pl.when(last_row)(lambda: clear(pl.ds(REACH + rows, REACH), everywhere_c))
    pl.when(first_col)(lambda: clear(everywhere_r, pl.ds(0, LANES)))
    pl.when(last_col)(lambda: clear(everywhere_r, pl.ds(width - LANES, LANES)))

    dot = functools.partial(jnp.dot, preferred_element_type=jnp.float32)
    table = rowtaps_ref[first_row.astype(jnp.int32) + 2 * last_row.astype(jnp.int32)]
    high = dot(table, high_ref[...])
    passed = high[:rows] + (high[rows:] + dot(table[:rows], low_ref[...]))
    passed = pltpu.roll(passed, width - (LANES - REACH), 1)
    high, low = split_values(passed)
    blocks = cols // LANES
    for j in range(blocks):
        which = 0
        if j == 0:
            which = first_col.astype(jnp.int32)
        elif j == blocks - 1:
            which = 2 * last_col.astype(jnp.int32)
        table = coltaps_ref[which]
        at = slice(j * LANES, j * LANES + 2 * LANES)
        both = dot(high[:, at], table)
        smoothed = both[:, :LANES] + (both[:, LANES:] + dot(low[:, at], table[:, :LANES]))
        rms_ref[:, pl.ds(j * LANES, LANES)] = jnp.sqrt(smoothed + 1e-06)


def shift(block, axis, step):
    count = lax.axis_size(axis)
    pairs = [(i, i + step) for i in range(count) if 0 <= i + step < count]
    return lax.ppermute(block, axis, pairs)


def shards(coadd_flux, inverse_variance, source_mask):
    rows, cols = coadd_flux.shape
    width = cols + 2 * LANES
    devices = lax.axis_size("rows") * lax.axis_size("cols")
    weight = inverse_variance * (1.0 - source_mask.astype(jnp.float32))
    both = jnp.stack([coadd_flux, weight])
    left = shift(both[:, :, cols - LANES :], "cols", 1)
    right = shift(both[:, :, :LANES], "cols", -1)
    extended = jnp.concatenate([left, both, right], axis=2)
    near_top = shift(extended[:, rows - NEAR :], "rows", 1)
    near_bottom = shift(extended[:, :NEAR], "rows", -1)
    top = shift(extended[:, rows - WIDE :], "rows", 1)
    bottom = shift(extended[:, :WIDE], "rows", -1)

    vmem = pl.BlockSpec(memory_space=pltpu.VMEM)
    field = jax.ShapeDtypeStruct((rows, cols), jnp.float32)
    parts = pl.pallas_call(
        moments_kernel,
        out_shape=jax.ShapeDtypeStruct((8, LANES), jnp.float32),
        in_specs=[vmem] * 6,
        out_specs=vmem,
        scratch_shapes=[pltpu.VMEM((rows + 2 * NEAR, width), jnp.float32)] * 2,
        compiler_params=pltpu.CompilerParams(vmem_limit_bytes=16 << 20),
        name="moments",
    )(coadd_flux, weight, near_top, near_bottom, left, right)

    parts = jnp.broadcast_to(parts[None], (devices, 8, LANES))
    parts = lax.all_to_all(parts, ("rows", "cols"), 0, 0, tiled=True)

    return tuple(
        pl.pallas_call(
            finish_kernel,
            out_shape=(field, field),
            in_specs=[vmem] * 9,
            out_specs=(vmem, vmem),
            scratch_shapes=[
                pltpu.VMEM((rows + 2 * WIDE, width), jnp.float32),
                pltpu.VMEM((rows + 2 * REACH, width), jnp.bfloat16),
                pltpu.VMEM((rows + 2 * REACH, width), jnp.bfloat16),
            ],
            compiler_params=pltpu.CompilerParams(vmem_limit_bytes=32 << 20),
            name="finish",
        )(
            parts, coadd_flux, weight, top, bottom, left, right,
            jnp.asarray(row_tables(rows)), jnp.asarray(col_tables()),
        )
    )


def solution(mesh):
    return jax.shard_map(
        shards,
        mesh=mesh,
        in_specs=(P("rows", "cols"), P("rows", "cols"), P("rows", "cols")),
        out_specs=(P("rows", "cols"), P("rows", "cols")),
        check_vma=False,
    )
```

```python
import functools

import jax
import jax.numpy as jnp
import ml_dtypes
import numpy as np
from jax import lax
from jax.experimental import pallas as pl
from jax.experimental.pallas import tpu as pltpu
from jax.sharding import PartitionSpec as P

RADIUS = 32
REACH = 2 * RADIUS
LANES = 128
WIDE = REACH + 8
NEAR = 8

smooth_weight = 2.0
blur_sigma = 10.0


def squared_taps(length, first, last):
    offsets = np.arange(2 * RADIUS + 1) - RADIUS
    taps = np.exp(-offsets * offsets / (2.0 * blur_sigma * blur_sigma))
    taps = taps / taps.sum()

    def band(count):
        table = np.zeros((count, count + 2 * RADIUS))
        for k in range(2 * RADIUS + 1):
            table[np.arange(count), np.arange(count) + k] = taps[k]
        return table

    inner = band(length + 2 * RADIUS)
    if first:
        inner[:RADIUS] = 0.0
    if last:
        inner[-RADIUS:] = 0.0
    return band(length) @ inner


def split(table):
    high = table.astype(np.float32).astype(ml_dtypes.bfloat16)
    low = (table - high.astype(np.float64)).astype(np.float32).astype(ml_dtypes.bfloat16)
    return high, low


def row_tables(length):
    tables = []
    for first, last in ((False, False), (True, False), (False, True), (True, True)):
        tables.append(np.concatenate(split(squared_taps(length, first, last)), axis=0))
    return np.stack(tables)


def col_tables():
    tables = []
    for first, last in ((False, False), (True, False), (False, True)):
        tables.append(np.concatenate(split(squared_taps(LANES, first, last).T), axis=1))
    return np.stack(tables)


def split_values(values):
    high = values.astype(jnp.bfloat16)
    return high, (values - high.astype(jnp.float32)).astype(jnp.bfloat16)


def at_edges():
    row, col = lax.axis_index("rows"), lax.axis_index("cols")
    return (
        row == 0,
        row == lax.axis_size("rows") - 1,
        col == 0,
        col == lax.axis_size("cols") - 1,
    )


def beside_columns(field):
    width = field.shape[1]
    return pltpu.roll(field, 1, 1) + pltpu.roll(field, width - 1, 1)


def weights(inverse_variance, source_mask):
    return inverse_variance * (1.0 - source_mask.astype(jnp.float32))


def moments_kernel(f_ref, iv_ref, mask_ref, top_ref, bottom_ref, left_ref, right_ref, out_ref, v0_ref, v1_ref):
    rows, cols = f_ref.shape
    width = cols + 2 * LANES
    first_row, last_row, first_col, last_col = at_edges()
    centre = pl.ds(LANES, cols)

    def weight_of(start):
        at = pl.ds(start, 8)
        own = weights(iv_ref[at, :], mask_ref[at, :])
        return jnp.concatenate([left_ref[1, at, :], own, right_ref[1, at, :]], axis=1)

    for at, near_ref in ((pl.ds(0, NEAR), top_ref), (pl.ds(NEAR + rows, NEAR), bottom_ref)):
        v0_ref[at, :] = jnp.zeros((NEAR, width), jnp.float32)
        v1_ref[at, :] = jnp.zeros((NEAR, width), jnp.float32)
        v0_ref[at, centre] = near_ref[...]
    for start in range(0, rows, 8):
        at = pl.ds(start, 8)
        flux = jnp.concatenate([left_ref[0, at, :], f_ref[at, :], right_ref[0, at, :]], axis=1)
        v0_ref[pl.ds(NEAR + start, 8), :] = flux * weight_of(start)

    def image(ref, weight, start, count):
        here = ref[pl.ds(start, count), :]
        beside = ref[pl.ds(start - 1, count), :] + ref[pl.ds(start + 1, count), :] + beside_columns(here)
        return here, weight * here + smooth_weight * (4.0 * here - beside)

    for start in range(0, rows, 8):
        _, out = image(v0_ref, weight_of(start), NEAR + start, 8)
        v1_ref[pl.ds(NEAR + start, 8), :] = out

    def edge_row(near_ref, row, at):
        weight = jnp.concatenate([jnp.zeros((1, LANES), jnp.float32), near_ref[pl.ds(row, 1), :], jnp.zeros((1, LANES), jnp.float32)], axis=1)
        _, out = image(v0_ref, weight, at, 1)
        v1_ref[pl.ds(at, 1), :] = out

    pl.when(jnp.logical_not(first_row))(lambda: edge_row(top_ref, 5, NEAR - 1))
    pl.when(jnp.logical_not(last_row))(lambda: edge_row(bottom_ref, 2, NEAR + rows))

    def clear(start):
        v1_ref[:, pl.ds(start, LANES)] = jnp.zeros((rows + 2 * NEAR, LANES), jnp.float32)

    pl.when(first_col)(lambda: clear(0))
    pl.when(last_col)(lambda: clear(width - LANES))

    sums = [jnp.zeros((8, cols), jnp.float32) for _ in range(4)]
    for start in range(0, rows, 8):
        v1, v2 = image(v1_ref, weight_of(start), NEAR + start, 8)
        v0 = v0_ref[pl.ds(NEAR + start, 8), centre]
        v1, v2 = v1[:, LANES : LANES + cols], v2[:, LANES : LANES + cols]
        sums = [total + term for total, term in zip(sums, (v0 * v0, v0 * v1, v1 * v1, v1 * v2))]
    for i, total in enumerate(sums):
        narrow = sum(total[:, k : k + LANES] for k in range(0, cols, LANES))
        out_ref[pl.ds(i, 1), :] = jnp.sum(narrow, axis=0, keepdims=True)
    on_left = lax.broadcasted_iota(jnp.int32, (1, LANES), 1) < LANES // 2
    corners = ((v1_ref, NEAR), (v1_ref, NEAR + rows - 1), (v0_ref, NEAR), (v0_ref, NEAR + rows - 1))
    for i, (ref, row) in enumerate(corners):
        at = pl.ds(row, 1)
        out_ref[pl.ds(4 + i, 1), :] = jnp.where(on_left, ref[at, pl.ds(LANES, LANES)], ref[at, pl.ds(cols, LANES)])


def corner_terms(parts):
    ncols, nrows = parts.shape[:2]
    flat = parts.reshape(ncols * nrows, 8, LANES)
    v1_top, v1_bottom, v0_top, v0_bottom = (flat[:, i, :] for i in range(4, 8))
    index = lax.broadcasted_iota(jnp.int32, (ncols * nrows, LANES), 0)
    lane = lax.broadcasted_iota(jnp.int32, (ncols * nrows, LANES), 1)
    col, row = index // nrows, index % nrows
    total = jnp.zeros((ncols * nrows, LANES), jnp.float32)
    for mine, theirs, step_row in ((v1_top, v0_bottom, -1), (v1_bottom, v0_top, 1)):
        for step_col in (-1, 1):
            shifted = pltpu.roll(theirs, (-(step_col * nrows + step_row)) % (ncols * nrows), 0)
            shifted = pltpu.roll(shifted, 1 if step_col < 0 else LANES - 1, 1)
            there = (row + step_row >= 0) & (row + step_row < nrows) & (col + step_col >= 0) & (col + step_col < ncols)
            there = there & (lane == (0 if step_col < 0 else LANES - 1))
            total = total + jnp.where(there, mine * shifted, 0.0)
    return 8.0 * jnp.sum(jnp.sum(total, axis=0, keepdims=True), axis=1, keepdims=True)


def coefficients(m0, m1, m2, m3):
    alpha0 = m0 / m1
    norm1 = jnp.maximum(m0 - 2.0 * alpha0 * m1 + alpha0 * alpha0 * m2, 0.0)
    grown = 1.0 + norm1 / m0
    image1 = grown * grown * m1 - 2.0 * grown * alpha0 * m2 + alpha0 * alpha0 * m3
    alpha1 = jnp.where(image1 > 0.0, norm1 / image1, 0.0)
    return alpha0 + alpha1 * grown, -alpha1 * alpha0


def finish_kernel(
    parts_ref, f_ref, iv_ref, mask_ref, top_ref, bottom_ref, left_ref, right_ref, rowtaps_ref, coltaps_ref,
    background_ref, rms_ref, v0_ref, high_ref, low_ref,
):
    rows, cols = f_ref.shape
    width = cols + 2 * LANES
    first_row, last_row, first_col, last_col = at_edges()

    parts = parts_ref[...]
    totals = jnp.sum(parts.reshape(-1, 8, LANES), axis=0)
    moments = [jnp.sum(totals[i : i + 1, :], axis=1, keepdims=True) for i in range(4)]
    moments[3] = moments[3] + corner_terms(parts)
    c0, c1 = coefficients(*moments)

    def pair(start, count):
        for ref, begin in ((top_ref, WIDE - REACH), (bottom_ref, WIDE + rows)):
            if begin <= start < begin + REACH:
                return ref[pl.ds(start - begin, count), :], ref[pl.ds(REACH + start - begin, count), :]
        at = pl.ds(start - WIDE, count)
        flux = jnp.concatenate([left_ref[0, at, :], f_ref[at, :], right_ref[0, at, :]], axis=1)
        own = weights(iv_ref[at, :], mask_ref[at, :])
        return flux, jnp.concatenate([left_ref[1, at, :], own, right_ref[1, at, :]], axis=1)

    v0_ref[pl.ds(0, 8), :] = top_ref[pl.ds(2 * REACH, 8), :]
    v0_ref[pl.ds(rows + 2 * WIDE - 8, 8), :] = bottom_ref[pl.ds(2 * REACH, 8), :]
    for start in range(8, rows + 2 * WIDE - 8, 8):
        flux, weight = pair(start, 8)
        v0_ref[pl.ds(start, 8), :] = flux * weight

    step = 16
    for start in range(8, rows + 2 * WIDE - 8, step):
        flux, weight = pair(start, step)
        v0 = v0_ref[pl.ds(start, step), :]
        beside = v0_ref[pl.ds(start - 1, step), :] + v0_ref[pl.ds(start + 1, step), :] + beside_columns(v0)
        v1 = weight * v0 + smooth_weight * (4.0 * v0 - beside)
        background = c0 * v0 + c1 * v1
        if WIDE <= start < WIDE + rows:
            background_ref[pl.ds(start - WIDE, step), :] = background[:, LANES : LANES + cols]
        scatter = flux - background
        high, low = split_values(scatter * scatter)
        high_ref[pl.ds(start - 8, step), :] = high
        low_ref[pl.ds(start - 8, step), :] = low

    def clear(at_rows, at_cols):
        for ref in (high_ref, low_ref):
            ref[at_rows, at_cols] = jnp.zeros((at_rows.size, at_cols.size), jnp.bfloat16)

    everywhere_r, everywhere_c = pl.ds(0, rows + 2 * REACH), pl.ds(0, width)
    pl.when(first_row)(lambda: clear(pl.ds(0, REACH), everywhere_c))
    pl.when(last_row)(lambda: clear(pl.ds(REACH + rows, REACH), everywhere_c))
    pl.when(first_col)(lambda: clear(everywhere_r, pl.ds(0, LANES)))
    pl.when(last_col)(lambda: clear(everywhere_r, pl.ds(width - LANES, LANES)))

    dot = functools.partial(jnp.dot, preferred_element_type=jnp.float32)
    table = rowtaps_ref[first_row.astype(jnp.int32) + 2 * last_row.astype(jnp.int32)]
    high = dot(table, high_ref[...])
    passed = high[:rows] + (high[rows:] + dot(table[:rows], low_ref[...]))
    passed = pltpu.roll(passed, width - (LANES - REACH), 1)
    high, low = split_values(passed)
    blocks = cols // LANES
    for j in range(blocks):
        which = 0
        if j == 0:
            which = first_col.astype(jnp.int32)
        elif j == blocks - 1:
            which = 2 * last_col.astype(jnp.int32)
        table = coltaps_ref[which]
        at = slice(j * LANES, j * LANES + 2 * LANES)
        both = dot(high[:, at], table)
        smoothed = both[:, :LANES] + (both[:, LANES:] + dot(low[:, at], table[:, :LANES]))
        rms_ref[:, pl.ds(j * LANES, LANES)] = jnp.sqrt(smoothed + 1e-06)


def shift(block, axis, step):
    count = lax.axis_size(axis)
    pairs = [(i, i + step) for i in range(count) if 0 <= i + step < count]
    return lax.ppermute(block, axis, pairs)


def shards(coadd_flux, inverse_variance, source_mask):
    rows, cols = coadd_flux.shape
    width = cols + 2 * LANES
    nrows, ncols = lax.axis_size("rows"), lax.axis_size("cols")

    def edge(start, stop, dim):
        flux, variance, mask = (
            lax.slice_in_dim(x, start, stop, axis=dim) for x in (coadd_flux, inverse_variance, source_mask)
        )
        return flux, weights(variance, mask)

    left = shift(jnp.stack(edge(cols - LANES, cols, 1)), "cols", 1)
    right = shift(jnp.stack(edge(0, LANES, 1)), "cols", -1)
    flux, weight = edge(rows - NEAR, rows, 0)
    near_top = jnp.concatenate([flux[:5], weight[7:], (flux * weight)[6:]])
    flux, weight = edge(0, NEAR, 0)
    near_bottom = jnp.concatenate([(flux * weight)[:2], weight[:1], flux[3:]])
    near_top = shift(near_top, "rows", 1)
    near_bottom = shift(near_bottom, "rows", -1)

    def wide(start, beyond):
        flux, weight = (
            jnp.concatenate([left[i, start : start + WIDE], x, right[i, start : start + WIDE]], axis=1)
            for i, x in enumerate(edge(start, start + WIDE, 0))
        )
        at = slice(WIDE - REACH, WIDE) if beyond == 0 else slice(0, REACH)
        return jnp.concatenate([flux[at], weight[at], (flux * weight)[beyond : beyond + 8]])

    top = shift(wide(rows - WIDE, 0), "rows", 1)
    bottom = shift(wide(0, REACH), "rows", -1)

    vmem = pl.BlockSpec(memory_space=pltpu.VMEM)
    field = jax.ShapeDtypeStruct((rows, cols), jnp.float32)
    own = (coadd_flux, inverse_variance, source_mask)
    parts = pl.pallas_call(
        moments_kernel,
        out_shape=jax.ShapeDtypeStruct((8, LANES), jnp.float32),
        in_specs=[vmem] * 7,
        out_specs=vmem,
        scratch_shapes=[pltpu.VMEM((rows + 2 * NEAR, width), jnp.float32)] * 2,
        compiler_params=pltpu.CompilerParams(vmem_limit_bytes=16 << 20),
        name="moments",
    )(*own, near_top, near_bottom, left, right)

    for axis in ("rows", "cols"):
        parts = jnp.broadcast_to(parts[None], (lax.axis_size(axis),) + parts.shape)
        parts = lax.all_to_all(parts, axis, 0, 0, tiled=True)

    return tuple(
        pl.pallas_call(
            finish_kernel,
            out_shape=(field, field),
            in_specs=[vmem] * 10,
            out_specs=(vmem, vmem),
            scratch_shapes=[
                pltpu.VMEM((rows + 2 * WIDE, width), jnp.float32),
                pltpu.VMEM((rows + 2 * REACH, width), jnp.bfloat16),
                pltpu.VMEM((rows + 2 * REACH, width), jnp.bfloat16),
            ],
            compiler_params=pltpu.CompilerParams(vmem_limit_bytes=32 << 20),
            name="finish",
        )(
            parts, *own, top, bottom, left, right,
            jnp.asarray(row_tables(rows)), jnp.asarray(col_tables()),
        )
    )


def solution(mesh):
    return jax.shard_map(
        shards,
        mesh=mesh,
        in_specs=(P("rows", "cols"), P("rows", "cols"), P("rows", "cols")),
        out_specs=(P("rows", "cols"), P("rows", "cols")),
        check_vma=False,
    )
```

```python
import functools

import jax
import jax.numpy as jnp
import ml_dtypes
import numpy as np
from jax import lax
from jax.experimental import pallas as pl
from jax.experimental.pallas import tpu as pltpu
from jax.sharding import PartitionSpec as P

RADIUS = 32
REACH = 2 * RADIUS
LANES = 128
WIDE = REACH + 8
NEAR = 8

smooth_weight = 2.0
blur_sigma = 10.0


def squared_taps(length, first, last):
    offsets = np.arange(2 * RADIUS + 1) - RADIUS
    taps = np.exp(-offsets * offsets / (2.0 * blur_sigma * blur_sigma))
    taps = taps / taps.sum()

    def band(count):
        table = np.zeros((count, count + 2 * RADIUS))
        for k in range(2 * RADIUS + 1):
            table[np.arange(count), np.arange(count) + k] = taps[k]
        return table

    inner = band(length + 2 * RADIUS)
    if first:
        inner[:RADIUS] = 0.0
    if last:
        inner[-RADIUS:] = 0.0
    return band(length) @ inner


def split(table):
    high = table.astype(np.float32).astype(ml_dtypes.bfloat16)
    low = (table - high.astype(np.float64)).astype(np.float32).astype(ml_dtypes.bfloat16)
    return high, low


def row_tables(length):
    tables = []
    for first, last in ((False, False), (True, False), (False, True), (True, True)):
        tables.append(np.concatenate(split(squared_taps(length, first, last)), axis=0))
    return np.stack(tables)


def col_tables():
    tables = []
    for first, last in ((False, False), (True, False), (False, True)):
        tables.append(np.concatenate(split(squared_taps(LANES, first, last).T), axis=1))
    return np.stack(tables)


def split_values(values):
    high = values.astype(jnp.bfloat16)
    return high, (values - high.astype(jnp.float32)).astype(jnp.bfloat16)


def at_edges():
    row, col = lax.axis_index("rows"), lax.axis_index("cols")
    return (
        row == 0,
        row == lax.axis_size("rows") - 1,
        col == 0,
        col == lax.axis_size("cols") - 1,
    )


def beside_columns(field):
    width = field.shape[1]
    return pltpu.roll(field, 1, 1) + pltpu.roll(field, width - 1, 1)


def weights(inverse_variance, source_mask):
    return inverse_variance * (1.0 - source_mask.astype(jnp.float32))


def extended(f_ref, iv_ref, mask_ref, left_ref, right_ref, at):
    flux = jnp.concatenate([left_ref[0, at, :], f_ref[at, :], right_ref[0, at, :]], axis=1)
    weight = weights(iv_ref[at, :], mask_ref[at, :])
    return flux, jnp.concatenate([left_ref[1, at, :], weight, right_ref[1, at, :]], axis=1)


def wide_kernel(f_ref, iv_ref, mask_ref, left_ref, right_ref, down_ref, up_ref):
    rows = f_ref.shape[0]

    def pair(start, count):
        at = pl.ds(start, count)
        return extended(f_ref, iv_ref, mask_ref, left_ref, right_ref, at)

    for out_ref, begin, beyond in ((down_ref, rows - REACH, rows - WIDE), (up_ref, 0, REACH)):
        for start in range(0, REACH, 8):
            flux, weight = pair(begin + start, 8)
            out_ref[pl.ds(start, 8), :] = flux
            out_ref[pl.ds(REACH + start, 8), :] = weight
        flux, weight = pair(beyond, 8)
        out_ref[pl.ds(2 * REACH, 8), :] = flux * weight


def moments_kernel(f_ref, iv_ref, mask_ref, top_ref, left_ref, out_ref, v0_ref, v1_ref):
    rows, cols = f_ref.shape
    width = LANES + cols
    first_row, last_row, first_col, last_col = at_edges()
    base = 2 * NEAR
    lane = lax.broadcasted_iota(jnp.int32, (8, LANES), 1)
    row = lax.broadcasted_iota(jnp.int32, (8, width), 0)
    beside_image = lane >= jnp.where(first_col, LANES, LANES - 3)

    def weight_of(start):
        at = pl.ds(start, 8)
        return jnp.concatenate([left_ref[1, at, :], weights(iv_ref[at, :], mask_ref[at, :])], axis=1)

    def image(ref, weight, start):
        here = ref[pl.ds(start, 8), :]
        beside = ref[pl.ds(start - 1, 8), :] + ref[pl.ds(start + 1, 8), :] + beside_columns(here)
        return here, weight * here + smooth_weight * (4.0 * here - beside)

    def clean(field, keep):
        return jnp.concatenate([jnp.where(keep, field[:, :LANES], 0.0), field[:, LANES:]], axis=1)

    for ref in (v0_ref, v1_ref):
        for start in (0, NEAR, base + rows):
            ref[pl.ds(start, 8), :] = jnp.zeros((8, width), jnp.float32)
    top = top_ref[...]
    v0_ref[pl.ds(NEAR, 8), :] = clean(jnp.where(row >= 4, top, 0.0), lane >= LANES - 4)
    top_weight = pltpu.roll(top, 4, 0)
    for start in range(0, rows, 8):
        at = pl.ds(start, 8)
        flux = jnp.concatenate([left_ref[0, at, :], f_ref[at, :]], axis=1)
        v0_ref[pl.ds(base + start, 8), :] = clean(flux * weight_of(start), lane >= LANES - 4)

    _, out = image(v0_ref, top_weight, NEAR)
    out = jnp.where(row >= jnp.where(first_row, 8, 5), out, 0.0)
    v1_ref[pl.ds(NEAR, 8), :] = clean(out, beside_image)
    for start in range(0, rows, 8):
        _, out = image(v0_ref, weight_of(start), base + start)
        v1_ref[pl.ds(base + start, 8), :] = clean(out, beside_image)

    def terms(start, weight, keep=None):
        v1, v2 = image(v1_ref, weight, start)
        v0 = v0_ref[pl.ds(start, 8), :]
        if keep is not None:
            v0, v1 = jnp.where(keep, v0, 0.0), jnp.where(keep, v1, 0.0)
        return v0 * v0, v0 * v1, v1 * v1, v1 * v2

    sums = terms(NEAR, top_weight, row >= 6)
    for start in range(0, rows - 8, 8):
        sums = [total + term for total, term in zip(sums, terms(base + start, weight_of(start)))]
    keep = row < jnp.where(last_row, 8, 6)
    sums = [total + term for total, term in zip(sums, terms(base + rows - 8, weight_of(rows - 8), keep))]

    out_lane = lax.broadcasted_iota(jnp.int32, (1, LANES), 1)
    result = jnp.zeros((1, LANES), jnp.float32)
    for i, total in enumerate(sums):
        narrow = jnp.where(lane >= LANES - 2, total[:, :LANES], 0.0)
        for k in range(LANES, width - LANES, LANES):
            narrow = narrow + total[:, k : k + LANES]
        ends = jnp.where(lane < jnp.where(last_col, LANES, LANES - 2), total[:, width - LANES :], 0.0)
        total = jnp.sum(jnp.sum(narrow + ends, axis=0, keepdims=True), axis=1, keepdims=True)
        result = jnp.where(out_lane == i, total, result)
    out_ref[...] = result


def coefficients(m0, m1, m2, m3):
    alpha0 = m0 / m1
    norm1 = jnp.maximum(m0 - 2.0 * alpha0 * m1 + alpha0 * alpha0 * m2, 0.0)
    grown = 1.0 + norm1 / m0
    image1 = grown * grown * m1 - 2.0 * grown * alpha0 * m2 + alpha0 * alpha0 * m3
    alpha1 = jnp.where(image1 > 0.0, norm1 / image1, 0.0)
    return alpha0 + alpha1 * grown, -alpha1 * alpha0


def finish_kernel(
    parts_ref, f_ref, iv_ref, mask_ref, top_ref, bottom_ref, left_ref, right_ref, rowtaps_ref, coltaps_ref,
    background_ref, rms_ref, v0_ref, high_ref, low_ref,
):
    rows, cols = f_ref.shape
    width = cols + 2 * LANES
    first_row, last_row, first_col, last_col = at_edges()

    totals = jnp.sum(parts_ref[...].reshape(-1, LANES), axis=0, keepdims=True)
    lane = lax.broadcasted_iota(jnp.int32, (1, LANES), 1)
    moments = [jnp.sum(jnp.where(lane == i, totals, 0.0), axis=1, keepdims=True) for i in range(4)]
    c0, c1 = coefficients(*moments)

    def pair(start, count):
        for ref, begin in ((top_ref, WIDE - REACH), (bottom_ref, WIDE + rows)):
            if begin <= start < begin + REACH:
                return ref[pl.ds(start - begin, count), :], ref[pl.ds(REACH + start - begin, count), :]
        return extended(f_ref, iv_ref, mask_ref, left_ref, right_ref, pl.ds(start - WIDE, count))

    v0_ref[pl.ds(0, 8), :] = top_ref[pl.ds(2 * REACH, 8), :]
    v0_ref[pl.ds(rows + 2 * WIDE - 8, 8), :] = bottom_ref[pl.ds(2 * REACH, 8), :]
    for start in range(8, rows + 2 * WIDE - 8, 8):
        flux, weight = pair(start, 8)
        v0_ref[pl.ds(start, 8), :] = flux * weight

    step = 16
    for start in range(8, rows + 2 * WIDE - 8, step):
        flux, weight = pair(start, step)
        v0 = v0_ref[pl.ds(start, step), :]
        beside = v0_ref[pl.ds(start - 1, step), :] + v0_ref[pl.ds(start + 1, step), :] + beside_columns(v0)
        v1 = weight * v0 + smooth_weight * (4.0 * v0 - beside)
        background = c0 * v0 + c1 * v1
        if WIDE <= start < WIDE + rows:
            background_ref[pl.ds(start - WIDE, step), :] = background[:, LANES : LANES + cols]
        scatter = flux - background
        high, low = split_values(scatter * scatter)
        high_ref[pl.ds(start - 8, step), :] = high
        low_ref[pl.ds(start - 8, step), :] = low

    def clear(at_rows, at_cols):
        for ref in (high_ref, low_ref):
            ref[at_rows, at_cols] = jnp.zeros((at_rows.size, at_cols.size), jnp.bfloat16)

    everywhere_r, everywhere_c = pl.ds(0, rows + 2 * REACH), pl.ds(0, width)
    pl.when(first_row)(lambda: clear(pl.ds(0, REACH), everywhere_c))
    pl.when(last_row)(lambda: clear(pl.ds(REACH + rows, REACH), everywhere_c))
    pl.when(first_col)(lambda: clear(everywhere_r, pl.ds(0, LANES)))
    pl.when(last_col)(lambda: clear(everywhere_r, pl.ds(width - LANES, LANES)))

    dot = functools.partial(jnp.dot, preferred_element_type=jnp.float32)
    table = rowtaps_ref[first_row.astype(jnp.int32) + 2 * last_row.astype(jnp.int32)]
    high = dot(table, high_ref[...])
    passed = high[:rows] + (high[rows:] + dot(table[:rows], low_ref[...]))
    passed = pltpu.roll(passed, width - (LANES - REACH), 1)
    high, low = split_values(passed)
    blocks = cols // LANES
    for j in range(blocks):
        which = 0
        if j == 0:
            which = first_col.astype(jnp.int32)
        elif j == blocks - 1:
            which = 2 * last_col.astype(jnp.int32)
        table = coltaps_ref[which]
        at = slice(j * LANES, j * LANES + 2 * LANES)
        both = dot(high[:, at], table)
        smoothed = both[:, :LANES] + (both[:, LANES:] + dot(low[:, at], table[:, :LANES]))
        rms_ref[:, pl.ds(j * LANES, LANES)] = jnp.sqrt(smoothed + 1e-06)


def shift(block, axis, step):
    count = lax.axis_size(axis)
    pairs = [(i, i + step) for i in range(count) if 0 <= i + step < count]
    return lax.ppermute(block, axis, pairs)


def shards(coadd_flux, inverse_variance, source_mask):
    rows, cols = coadd_flux.shape
    width = cols + 2 * LANES
    devices = lax.axis_size("rows") * lax.axis_size("cols")

    def edge(start, stop, dim):
        flux, variance, mask = (
            lax.slice_in_dim(x, start, stop, axis=dim) for x in (coadd_flux, inverse_variance, source_mask)
        )
        return flux, weights(variance, mask)

    left = shift(jnp.stack(edge(cols - LANES, cols, 1)), "cols", 1)
    right = shift(jnp.stack(edge(0, LANES, 1)), "cols", -1)
    flux, weight = (
        jnp.concatenate([left[i, rows - NEAR :], x], axis=1) for i, x in enumerate(edge(rows - NEAR, rows, 0))
    )
    near = shift(jnp.concatenate([weight[4:], (flux * weight)[4:]]), "rows", 1)

    vmem = pl.BlockSpec(memory_space=pltpu.VMEM)
    field = jax.ShapeDtypeStruct((rows, cols), jnp.float32)
    own = (coadd_flux, inverse_variance, source_mask)
    (left_after, right_after), near = lax.optimization_barrier(((left, right), near))
    down, up = pl.pallas_call(
        wide_kernel,
        out_shape=(jax.ShapeDtypeStruct((2 * REACH + 8, width), jnp.float32),) * 2,
        in_specs=[vmem] * 5,
        out_specs=(vmem, vmem),
        compiler_params=pltpu.CompilerParams(vmem_limit_bytes=16 << 20),
        name="wide",
    )(*own, left_after, right_after)
    top = shift(down, "rows", 1)
    bottom = shift(up, "rows", -1)
    parts = pl.pallas_call(
        moments_kernel,
        out_shape=jax.ShapeDtypeStruct((1, LANES), jnp.float32),
        in_specs=[vmem] * 5,
        out_specs=vmem,
        scratch_shapes=[pltpu.VMEM((rows + 3 * NEAR, LANES + cols), jnp.float32)] * 2,
        compiler_params=pltpu.CompilerParams(vmem_limit_bytes=16 << 20),
        name="moments",
    )(*own, near, left)
    parts = jnp.broadcast_to(parts[None], (devices, 1, LANES))
    parts = lax.all_to_all(parts, ("rows", "cols"), 0, 0, tiled=True)

    return tuple(
        pl.pallas_call(
            finish_kernel,
            out_shape=(field, field),
            in_specs=[vmem] * 10,
            out_specs=(vmem, vmem),
            scratch_shapes=[
                pltpu.VMEM((rows + 2 * WIDE, width), jnp.float32),
                pltpu.VMEM((rows + 2 * REACH, width), jnp.bfloat16),
                pltpu.VMEM((rows + 2 * REACH, width), jnp.bfloat16),
            ],
            compiler_params=pltpu.CompilerParams(vmem_limit_bytes=32 << 20),
            name="finish",
        )(
            parts, *own, top, bottom, left, right,
            jnp.asarray(row_tables(rows)), jnp.asarray(col_tables()),
        )
    )


def solution(mesh):
    return jax.shard_map(
        shards,
        mesh=mesh,
        in_specs=(P("rows", "cols"), P("rows", "cols"), P("rows", "cols")),
        out_specs=(P("rows", "cols"), P("rows", "cols")),
        check_vma=False,
    )
```

```python
import functools

import jax
import jax.numpy as jnp
import ml_dtypes
import numpy as np
from jax import lax
from jax.experimental import pallas as pl
from jax.experimental.pallas import tpu as pltpu
from jax.sharding import PartitionSpec as P

RADIUS = 32
REACH = 2 * RADIUS
LANES = 128
WIDE = REACH + 8
NEAR = 8

smooth_weight = 2.0
blur_sigma = 10.0


def squared_taps(length, first, last):
    offsets = np.arange(2 * RADIUS + 1) - RADIUS
    taps = np.exp(-offsets * offsets / (2.0 * blur_sigma * blur_sigma))
    taps = taps / taps.sum()

    def band(count):
        table = np.zeros((count, count + 2 * RADIUS))
        for k in range(2 * RADIUS + 1):
            table[np.arange(count), np.arange(count) + k] = taps[k]
        return table

    inner = band(length + 2 * RADIUS)
    if first:
        inner[:RADIUS] = 0.0
    if last:
        inner[-RADIUS:] = 0.0
    return band(length) @ inner


def split(table):
    high = table.astype(np.float32).astype(ml_dtypes.bfloat16)
    low = (table - high.astype(np.float64)).astype(np.float32).astype(ml_dtypes.bfloat16)
    return high, low


def row_tables(length):
    tables = []
    for first, last in ((False, False), (True, False), (False, True), (True, True)):
        tables.append(np.concatenate(split(squared_taps(length, first, last)), axis=0))
    return np.stack(tables)


def col_tables():
    tables = []
    for first, last in ((False, False), (True, False), (False, True)):
        tables.append(np.concatenate(split(squared_taps(LANES, first, last).T), axis=1))
    return np.stack(tables)


def split_values(values):
    high = values.astype(jnp.bfloat16)
    return high, (values - high.astype(jnp.float32)).astype(jnp.bfloat16)


def at_edges():
    row, col = lax.axis_index("rows"), lax.axis_index("cols")
    return (
        row == 0,
        row == lax.axis_size("rows") - 1,
        col == 0,
        col == lax.axis_size("cols") - 1,
    )


def beside_columns(field):
    width = field.shape[1]
    return pltpu.roll(field, 1, 1) + pltpu.roll(field, width - 1, 1)


def weights(inverse_variance, source_mask):
    return inverse_variance * (1.0 - source_mask.astype(jnp.float32))


def extended(f_ref, w_ref, left_ref, right_ref, at):
    flux = jnp.concatenate([left_ref[0, at, :], f_ref[at, :], right_ref[0, at, :]], axis=1)
    weight = w_ref[at, :]
    return flux, jnp.concatenate([left_ref[1, at, :], weight, right_ref[1, at, :]], axis=1)


def wide_kernel(f_ref, w_ref, left_ref, right_ref, down_ref, up_ref):
    rows = f_ref.shape[0]

    def pair(start, count):
        at = pl.ds(start, count)
        return extended(f_ref, w_ref, left_ref, right_ref, at)

    for out_ref, begin, beyond in ((down_ref, rows - REACH, rows - WIDE), (up_ref, 0, REACH)):
        for start in range(0, REACH, 8):
            flux, weight = pair(begin + start, 8)
            out_ref[pl.ds(start, 8), :] = flux
            out_ref[pl.ds(REACH + start, 8), :] = weight
        flux, weight = pair(beyond, 8)
        out_ref[pl.ds(2 * REACH, 8), :] = flux * weight


def moments_kernel(f_ref, w_ref, top_ref, left_ref, out_ref, v0_ref, v1_ref):
    rows, cols = f_ref.shape
    width = LANES + cols
    first_row, last_row, first_col, last_col = at_edges()
    base = 2 * NEAR
    lane = lax.broadcasted_iota(jnp.int32, (8, LANES), 1)
    row = lax.broadcasted_iota(jnp.int32, (8, width), 0)
    beside_image = lane >= jnp.where(first_col, LANES, LANES - 3)

    def weight_of(start):
        at = pl.ds(start, 8)
        return jnp.concatenate([left_ref[1, at, :], w_ref[at, :]], axis=1)

    def image(ref, weight, start):
        here = ref[pl.ds(start, 8), :]
        beside = ref[pl.ds(start - 1, 8), :] + ref[pl.ds(start + 1, 8), :] + beside_columns(here)
        return here, weight * here + smooth_weight * (4.0 * here - beside)

    def clean(field, keep):
        return jnp.concatenate([jnp.where(keep, field[:, :LANES], 0.0), field[:, LANES:]], axis=1)

    for ref in (v0_ref, v1_ref):
        for start in (0, NEAR, base + rows):
            ref[pl.ds(start, 8), :] = jnp.zeros((8, width), jnp.float32)
    top = top_ref[...]
    v0_ref[pl.ds(NEAR, 8), :] = clean(jnp.where(row >= 4, top, 0.0), lane >= LANES - 4)
    top_weight = pltpu.roll(top, 4, 0)
    for start in range(0, rows, 8):
        at = pl.ds(start, 8)
        flux = jnp.concatenate([left_ref[0, at, :], f_ref[at, :]], axis=1)
        v0_ref[pl.ds(base + start, 8), :] = clean(flux * weight_of(start), lane >= LANES - 4)

    _, out = image(v0_ref, top_weight, NEAR)
    out = jnp.where(row >= jnp.where(first_row, 8, 5), out, 0.0)
    v1_ref[pl.ds(NEAR, 8), :] = clean(out, beside_image)
    for start in range(0, rows, 8):
        _, out = image(v0_ref, weight_of(start), base + start)
        v1_ref[pl.ds(base + start, 8), :] = clean(out, beside_image)

    def terms(start, weight, keep=None):
        v1, v2 = image(v1_ref, weight, start)
        v0 = v0_ref[pl.ds(start, 8), :]
        if keep is not None:
            v0, v1 = jnp.where(keep, v0, 0.0), jnp.where(keep, v1, 0.0)
        return v0 * v0, v0 * v1, v1 * v1, v1 * v2

    sums = terms(NEAR, top_weight, row >= 6)
    for start in range(0, rows - 8, 8):
        sums = [total + term for total, term in zip(sums, terms(base + start, weight_of(start)))]
    keep = row < jnp.where(last_row, 8, 6)
    sums = [total + term for total, term in zip(sums, terms(base + rows - 8, weight_of(rows - 8), keep))]

    out_lane = lax.broadcasted_iota(jnp.int32, (1, LANES), 1)
    result = jnp.zeros((1, LANES), jnp.float32)
    for i, total in enumerate(sums):
        narrow = jnp.where(lane >= LANES - 2, total[:, :LANES], 0.0)
        for k in range(LANES, width - LANES, LANES):
            narrow = narrow + total[:, k : k + LANES]
        ends = jnp.where(lane < jnp.where(last_col, LANES, LANES - 2), total[:, width - LANES :], 0.0)
        total = jnp.sum(jnp.sum(narrow + ends, axis=0, keepdims=True), axis=1, keepdims=True)
        result = jnp.where(out_lane == i, total, result)
    out_ref[...] = result


def coefficients(m0, m1, m2, m3):
    alpha0 = m0 / m1
    norm1 = jnp.maximum(m0 - 2.0 * alpha0 * m1 + alpha0 * alpha0 * m2, 0.0)
    grown = 1.0 + norm1 / m0
    image1 = grown * grown * m1 - 2.0 * grown * alpha0 * m2 + alpha0 * alpha0 * m3
    alpha1 = jnp.where(image1 > 0.0, norm1 / image1, 0.0)
    return alpha0 + alpha1 * grown, -alpha1 * alpha0


def finish_kernel(
    parts_ref, f_ref, w_ref, top_ref, bottom_ref, left_ref, right_ref, rowtaps_ref, coltaps_ref,
    background_ref, rms_ref, v0_ref, high_ref, low_ref,
):
    rows, cols = f_ref.shape
    width = cols + 2 * LANES
    first_row, last_row, first_col, last_col = at_edges()

    totals = jnp.sum(parts_ref[...].reshape(-1, LANES), axis=0, keepdims=True)
    lane = lax.broadcasted_iota(jnp.int32, (1, LANES), 1)
    moments = [jnp.sum(jnp.where(lane == i, totals, 0.0), axis=1, keepdims=True) for i in range(4)]
    c0, c1 = coefficients(*moments)

    def pair(start, count):
        for ref, begin in ((top_ref, WIDE - REACH), (bottom_ref, WIDE + rows)):
            if begin <= start < begin + REACH:
                return ref[pl.ds(start - begin, count), :], ref[pl.ds(REACH + start - begin, count), :]
        return extended(f_ref, w_ref, left_ref, right_ref, pl.ds(start - WIDE, count))

    v0_ref[pl.ds(0, 8), :] = top_ref[pl.ds(2 * REACH, 8), :]
    v0_ref[pl.ds(rows + 2 * WIDE - 8, 8), :] = bottom_ref[pl.ds(2 * REACH, 8), :]
    for start in range(8, rows + 2 * WIDE - 8, 8):
        flux, weight = pair(start, 8)
        v0_ref[pl.ds(start, 8), :] = flux * weight

    step = 16
    for start in range(8, rows + 2 * WIDE - 8, step):
        flux, weight = pair(start, step)
        v0 = v0_ref[pl.ds(start, step), :]
        beside = v0_ref[pl.ds(start - 1, step), :] + v0_ref[pl.ds(start + 1, step), :] + beside_columns(v0)
        v1 = weight * v0 + smooth_weight * (4.0 * v0 - beside)
        background = c0 * v0 + c1 * v1
        if WIDE <= start < WIDE + rows:
            background_ref[pl.ds(start - WIDE, step), :] = background[:, LANES : LANES + cols]
        scatter = flux - background
        high, low = split_values(scatter * scatter)
        high_ref[pl.ds(start - 8, step), :] = high
        low_ref[pl.ds(start - 8, step), :] = low

    def clear(at_rows, at_cols):
        for ref in (high_ref, low_ref):
            ref[at_rows, at_cols] = jnp.zeros((at_rows.size, at_cols.size), jnp.bfloat16)

    everywhere_r, everywhere_c = pl.ds(0, rows + 2 * REACH), pl.ds(0, width)
    pl.when(first_row)(lambda: clear(pl.ds(0, REACH), everywhere_c))
    pl.when(last_row)(lambda: clear(pl.ds(REACH + rows, REACH), everywhere_c))
    pl.when(first_col)(lambda: clear(everywhere_r, pl.ds(0, LANES)))
    pl.when(last_col)(lambda: clear(everywhere_r, pl.ds(width - LANES, LANES)))

    dot = functools.partial(jnp.dot, preferred_element_type=jnp.float32)
    table = rowtaps_ref[first_row.astype(jnp.int32) + 2 * last_row.astype(jnp.int32)]
    high = dot(table, high_ref[...])
    passed = high[:rows] + (high[rows:] + dot(table[:rows], low_ref[...]))
    passed = pltpu.roll(passed, width - (LANES - REACH), 1)
    high, low = split_values(passed)
    blocks = cols // LANES
    for j in range(blocks):
        which = 0
        if j == 0:
            which = first_col.astype(jnp.int32)
        elif j == blocks - 1:
            which = 2 * last_col.astype(jnp.int32)
        table = coltaps_ref[which]
        at = slice(j * LANES, j * LANES + 2 * LANES)
        both = dot(high[:, at], table)
        smoothed = both[:, :LANES] + (both[:, LANES:] + dot(low[:, at], table[:, :LANES]))
        rms_ref[:, pl.ds(j * LANES, LANES)] = jnp.sqrt(smoothed + 1e-06)


def shift(block, axis, step):
    count = lax.axis_size(axis)
    pairs = [(i, i + step) for i in range(count) if 0 <= i + step < count]
    return lax.ppermute(block, axis, pairs)


def shards(coadd_flux, inverse_variance, source_mask):
    rows, cols = coadd_flux.shape
    width = cols + 2 * LANES

    def edge(start, stop, dim):
        flux, variance, mask = (
            lax.slice_in_dim(x, start, stop, axis=dim) for x in (coadd_flux, inverse_variance, source_mask)
        )
        return flux, weights(variance, mask)

    left = shift(jnp.stack(edge(cols - LANES, cols, 1)), "cols", 1)
    right = shift(jnp.stack(edge(0, LANES, 1)), "cols", -1)
    flux, weight = (
        jnp.concatenate([left[i, rows - NEAR :], x], axis=1) for i, x in enumerate(edge(rows - NEAR, rows, 0))
    )
    near = shift(jnp.concatenate([weight[4:], (flux * weight)[4:]]), "rows", 1)

    vmem = pl.BlockSpec(memory_space=pltpu.VMEM)
    field = jax.ShapeDtypeStruct((rows, cols), jnp.float32)
    own = (coadd_flux, weights(inverse_variance, source_mask))
    parts = pl.pallas_call(
        moments_kernel,
        out_shape=jax.ShapeDtypeStruct((1, LANES), jnp.float32),
        in_specs=[vmem] * 4,
        out_specs=vmem,
        scratch_shapes=[pltpu.VMEM((rows + 3 * NEAR, LANES + cols), jnp.float32)] * 2,
        compiler_params=pltpu.CompilerParams(vmem_limit_bytes=16 << 20),
        name="moments",
    )(*own, near, left)
    left_after, right_after, parts = lax.optimization_barrier((left, right, parts))
    down, up = pl.pallas_call(
        wide_kernel,
        out_shape=(jax.ShapeDtypeStruct((2 * REACH + 8, width), jnp.float32),) * 2,
        in_specs=[vmem] * 4,
        out_specs=(vmem, vmem),
        compiler_params=pltpu.CompilerParams(vmem_limit_bytes=16 << 20),
        name="wide",
    )(*own, left_after, right_after)
    top = shift(down, "rows", 1)
    bottom = shift(up, "rows", -1)
    parts = lax.all_gather(parts, ("rows", "cols"))

    return tuple(
        pl.pallas_call(
            finish_kernel,
            out_shape=(field, field),
            in_specs=[vmem] * 9,
            out_specs=(vmem, vmem),
            scratch_shapes=[
                pltpu.VMEM((rows + 2 * WIDE, width), jnp.float32),
                pltpu.VMEM((rows + 2 * REACH, width), jnp.bfloat16),
                pltpu.VMEM((rows + 2 * REACH, width), jnp.bfloat16),
            ],
            compiler_params=pltpu.CompilerParams(vmem_limit_bytes=32 << 20),
            name="finish",
        )(
            parts, *own, top, bottom, left, right,
            jnp.asarray(row_tables(rows)), jnp.asarray(col_tables()),
        )
    )


def solution(mesh):
    return jax.shard_map(
        shards,
        mesh=mesh,
        in_specs=(P("rows", "cols"), P("rows", "cols"), P("rows", "cols")),
        out_specs=(P("rows", "cols"), P("rows", "cols")),
        check_vma=False,
    )
```

```python
import functools

import jax
import jax.numpy as jnp
import ml_dtypes
import numpy as np
from jax import lax
from jax.experimental import pallas as pl
from jax.experimental.pallas import tpu as pltpu
from jax.sharding import PartitionSpec as P

RADIUS = 32
REACH = 2 * RADIUS
LANES = 128
WIDE = REACH + 8
NEAR = 8

smooth_weight = 2.0
blur_sigma = 10.0


def squared_taps(length, first, last):
    offsets = np.arange(2 * RADIUS + 1) - RADIUS
    taps = np.exp(-offsets * offsets / (2.0 * blur_sigma * blur_sigma))
    taps = taps / taps.sum()

    def band(count):
        table = np.zeros((count, count + 2 * RADIUS))
        for k in range(2 * RADIUS + 1):
            table[np.arange(count), np.arange(count) + k] = taps[k]
        return table

    inner = band(length + 2 * RADIUS)
    if first:
        inner[:RADIUS] = 0.0
    if last:
        inner[-RADIUS:] = 0.0
    return band(length) @ inner


def split(table):
    high = table.astype(np.float32).astype(ml_dtypes.bfloat16)
    low = (table - high.astype(np.float64)).astype(np.float32).astype(ml_dtypes.bfloat16)
    return high, low


def row_tables(length):
    tables = []
    for first, last in ((False, False), (True, False), (False, True), (True, True)):
        tables.append(np.concatenate(split(squared_taps(length, first, last)), axis=0))
    return np.stack(tables)


def col_tables():
    tables = []
    for first, last in ((False, False), (True, False), (False, True)):
        tables.append(np.concatenate(split(squared_taps(LANES, first, last).T), axis=1))
    return np.stack(tables)


def split_values(values):
    high = values.astype(jnp.bfloat16)
    return high, (values - high.astype(jnp.float32)).astype(jnp.bfloat16)


def at_edges():
    row, col = lax.axis_index("rows"), lax.axis_index("cols")
    return (
        row == 0,
        row == lax.axis_size("rows") - 1,
        col == 0,
        col == lax.axis_size("cols") - 1,
    )


def beside_columns(field):
    width = field.shape[1]
    return pltpu.roll(field, 1, 1) + pltpu.roll(field, width - 1, 1)


def weights(inverse_variance, source_mask):
    return inverse_variance * (1.0 - source_mask.astype(jnp.float32))


def extended(f_ref, w_ref, left_ref, right_ref, at):
    flux = jnp.concatenate([left_ref[0, at, :], f_ref[at, :], right_ref[0, at, :]], axis=1)
    weight = w_ref[at, :]
    return flux, jnp.concatenate([left_ref[1, at, :], weight, right_ref[1, at, :]], axis=1)


def wide_kernel(f_ref, w_ref, left_ref, right_ref, near_ref, far_ref):
    rows = f_ref.shape[0]
    even = lax.axis_index("rows") % 2 == 0

    def write(out_ref, begin, beyond):
        for start in range(0, REACH, 8):
            flux, weight = extended(f_ref, w_ref, left_ref, right_ref, pl.ds(begin + start, 8))
            out_ref[pl.ds(start, 8), :] = flux
            out_ref[pl.ds(REACH + start, 8), :] = weight
        flux, weight = extended(f_ref, w_ref, left_ref, right_ref, pl.ds(beyond, 8))
        out_ref[pl.ds(2 * REACH, 8), :] = flux * weight

    @pl.when(even)
    def _():
        write(near_ref, rows - REACH, rows - WIDE)
        write(far_ref, 0, REACH)

    @pl.when(jnp.logical_not(even))
    def _():
        write(near_ref, 0, REACH)
        write(far_ref, rows - REACH, rows - WIDE)


def moments_kernel(f_ref, w_ref, top_ref, left_ref, out_ref, v0_ref, v1_ref):
    rows, cols = f_ref.shape
    width = LANES + cols
    first_row, last_row, first_col, last_col = at_edges()
    base = 2 * NEAR
    lane = lax.broadcasted_iota(jnp.int32, (8, LANES), 1)
    row = lax.broadcasted_iota(jnp.int32, (8, width), 0)
    beside_image = lane >= jnp.where(first_col, LANES, LANES - 3)

    def weight_of(start):
        at = pl.ds(start, 8)
        return jnp.concatenate([left_ref[1, at, :], w_ref[at, :]], axis=1)

    def image(ref, weight, start):
        here = ref[pl.ds(start, 8), :]
        beside = ref[pl.ds(start - 1, 8), :] + ref[pl.ds(start + 1, 8), :] + beside_columns(here)
        return here, weight * here + smooth_weight * (4.0 * here - beside)

    def clean(field, keep):
        return jnp.concatenate([jnp.where(keep, field[:, :LANES], 0.0), field[:, LANES:]], axis=1)

    for ref in (v0_ref, v1_ref):
        for start in (0, NEAR, base + rows):
            ref[pl.ds(start, 8), :] = jnp.zeros((8, width), jnp.float32)
    top = top_ref[...]
    v0_ref[pl.ds(NEAR, 8), :] = clean(jnp.where(row >= 4, top, 0.0), lane >= LANES - 4)
    top_weight = pltpu.roll(top, 4, 0)
    for start in range(0, rows, 8):
        at = pl.ds(start, 8)
        flux = jnp.concatenate([left_ref[0, at, :], f_ref[at, :]], axis=1)
        v0_ref[pl.ds(base + start, 8), :] = clean(flux * weight_of(start), lane >= LANES - 4)

    _, out = image(v0_ref, top_weight, NEAR)
    out = jnp.where(row >= jnp.where(first_row, 8, 5), out, 0.0)
    v1_ref[pl.ds(NEAR, 8), :] = clean(out, beside_image)
    for start in range(0, rows, 8):
        _, out = image(v0_ref, weight_of(start), base + start)
        v1_ref[pl.ds(base + start, 8), :] = clean(out, beside_image)

    def terms(start, weight, keep=None):
        v1, v2 = image(v1_ref, weight, start)
        v0 = v0_ref[pl.ds(start, 8), :]
        if keep is not None:
            v0, v1 = jnp.where(keep, v0, 0.0), jnp.where(keep, v1, 0.0)
        return v0 * v0, v0 * v1, v1 * v1, v1 * v2

    sums = terms(NEAR, top_weight, row >= 6)
    for start in range(0, rows - 8, 8):
        sums = [total + term for total, term in zip(sums, terms(base + start, weight_of(start)))]
    keep = row < jnp.where(last_row, 8, 6)
    sums = [total + term for total, term in zip(sums, terms(base + rows - 8, weight_of(rows - 8), keep))]

    out_lane = lax.broadcasted_iota(jnp.int32, (1, LANES), 1)
    result = jnp.zeros((1, LANES), jnp.float32)
    for i, total in enumerate(sums):
        narrow = jnp.where(lane >= LANES - 2, total[:, :LANES], 0.0)
        for k in range(LANES, width - LANES, LANES):
            narrow = narrow + total[:, k : k + LANES]
        ends = jnp.where(lane < jnp.where(last_col, LANES, LANES - 2), total[:, width - LANES :], 0.0)
        total = jnp.sum(jnp.sum(narrow + ends, axis=0, keepdims=True), axis=1, keepdims=True)
        result = jnp.where(out_lane == i, total, result)
    out_ref[...] = result


def coefficients(m0, m1, m2, m3):
    alpha0 = m0 / m1
    norm1 = jnp.maximum(m0 - 2.0 * alpha0 * m1 + alpha0 * alpha0 * m2, 0.0)
    grown = 1.0 + norm1 / m0
    image1 = grown * grown * m1 - 2.0 * grown * alpha0 * m2 + alpha0 * alpha0 * m3
    alpha1 = jnp.where(image1 > 0.0, norm1 / image1, 0.0)
    return alpha0 + alpha1 * grown, -alpha1 * alpha0


def finish_kernel(
    parts_ref, f_ref, w_ref, near_ref, far_ref, left_ref, right_ref, rowtaps_ref, coltaps_ref,
    background_ref, rms_ref, v0_ref, high_ref, low_ref,
):
    rows, cols = f_ref.shape
    width = cols + 2 * LANES
    first_row, last_row, first_col, last_col = at_edges()

    totals = jnp.sum(parts_ref[...].reshape(-1, LANES), axis=0, keepdims=True)
    lane = lax.broadcasted_iota(jnp.int32, (1, LANES), 1)
    moments = [jnp.sum(jnp.where(lane == i, totals, 0.0), axis=1, keepdims=True) for i in range(4)]
    c0, c1 = coefficients(*moments)

    even = lax.axis_index("rows") % 2 == 0

    def beyond(below, start, count):
        at = pl.ds(start, count)
        one, other = (near_ref, far_ref) if below else (far_ref, near_ref)
        return jnp.where(even, one[at, :], other[at, :])

    def pair(start, count):
        for below, begin in ((False, WIDE - REACH), (True, WIDE + rows)):
            if begin <= start < begin + REACH:
                return beyond(below, start - begin, count), beyond(below, REACH + start - begin, count)
        return extended(f_ref, w_ref, left_ref, right_ref, pl.ds(start - WIDE, count))

    v0_ref[pl.ds(0, 8), :] = beyond(False, 2 * REACH, 8)
    v0_ref[pl.ds(rows + 2 * WIDE - 8, 8), :] = beyond(True, 2 * REACH, 8)
    for start in range(8, rows + 2 * WIDE - 8, 8):
        flux, weight = pair(start, 8)
        v0_ref[pl.ds(start, 8), :] = flux * weight

    step = 16
    for start in range(8, rows + 2 * WIDE - 8, step):
        flux, weight = pair(start, step)
        v0 = v0_ref[pl.ds(start, step), :]
        beside = v0_ref[pl.ds(start - 1, step), :] + v0_ref[pl.ds(start + 1, step), :] + beside_columns(v0)
        v1 = weight * v0 + smooth_weight * (4.0 * v0 - beside)
        background = c0 * v0 + c1 * v1
        if WIDE <= start < WIDE + rows:
            background_ref[pl.ds(start - WIDE, step), :] = background[:, LANES : LANES + cols]
        scatter = flux - background
        high, low = split_values(scatter * scatter)
        high_ref[pl.ds(start - 8, step), :] = high
        low_ref[pl.ds(start - 8, step), :] = low

    def clear(at_rows, at_cols):
        for ref in (high_ref, low_ref):
            ref[at_rows, at_cols] = jnp.zeros((at_rows.size, at_cols.size), jnp.bfloat16)

    everywhere_r, everywhere_c = pl.ds(0, rows + 2 * REACH), pl.ds(0, width)
    pl.when(first_row)(lambda: clear(pl.ds(0, REACH), everywhere_c))
    pl.when(last_row)(lambda: clear(pl.ds(REACH + rows, REACH), everywhere_c))
    pl.when(first_col)(lambda: clear(everywhere_r, pl.ds(0, LANES)))
    pl.when(last_col)(lambda: clear(everywhere_r, pl.ds(width - LANES, LANES)))

    dot = functools.partial(jnp.dot, preferred_element_type=jnp.float32)
    table = rowtaps_ref[first_row.astype(jnp.int32) + 2 * last_row.astype(jnp.int32)]
    high = dot(table, high_ref[...])
    passed = high[:rows] + (high[rows:] + dot(table[:rows], low_ref[...]))
    passed = pltpu.roll(passed, width - (LANES - REACH), 1)
    high, low = split_values(passed)
    blocks = cols // LANES
    for j in range(blocks):
        which = 0
        if j == 0:
            which = first_col.astype(jnp.int32)
        elif j == blocks - 1:
            which = 2 * last_col.astype(jnp.int32)
        table = coltaps_ref[which]
        at = slice(j * LANES, j * LANES + 2 * LANES)
        both = dot(high[:, at], table)
        smoothed = both[:, :LANES] + (both[:, LANES:] + dot(low[:, at], table[:, :LANES]))
        rms_ref[:, pl.ds(j * LANES, LANES)] = jnp.sqrt(smoothed + 1e-06)


def shift(block, axis, step):
    count = lax.axis_size(axis)
    pairs = [(i, i + step) for i in range(count) if 0 <= i + step < count]
    return lax.ppermute(block, axis, pairs)


def swap(block, axis, first):
    count = lax.axis_size(axis)
    pairs = [(i, i + 1) for i in range(first, count - 1, 2)]
    return lax.ppermute(block, axis, pairs + [(j, i) for i, j in pairs])


def shards(coadd_flux, inverse_variance, source_mask):
    rows, cols = coadd_flux.shape
    width = cols + 2 * LANES

    def edge(start, stop, dim):
        flux, variance, mask = (
            lax.slice_in_dim(x, start, stop, axis=dim) for x in (coadd_flux, inverse_variance, source_mask)
        )
        return flux, weights(variance, mask)

    left = shift(jnp.stack(edge(cols - LANES, cols, 1)), "cols", 1)
    right = shift(jnp.stack(edge(0, LANES, 1)), "cols", -1)
    flux, weight = (
        jnp.concatenate([left[i, rows - NEAR :], x], axis=1) for i, x in enumerate(edge(rows - NEAR, rows, 0))
    )
    near = shift(jnp.concatenate([weight[4:], (flux * weight)[4:]]), "rows", 1)

    vmem = pl.BlockSpec(memory_space=pltpu.VMEM)
    field = jax.ShapeDtypeStruct((rows, cols), jnp.float32)
    own = (coadd_flux, weights(inverse_variance, source_mask))
    to_near, to_far = pl.pallas_call(
        wide_kernel,
        out_shape=(jax.ShapeDtypeStruct((2 * REACH + 8, width), jnp.float32),) * 2,
        in_specs=[vmem] * 4,
        out_specs=(vmem, vmem),
        compiler_params=pltpu.CompilerParams(vmem_limit_bytes=16 << 20),
        name="wide",
    )(*own, left, right)
    to_near, to_far, near = lax.optimization_barrier((to_near, to_far, near))
    from_near = swap(to_near, "rows", 0)
    from_far = swap(to_far, "rows", 1)
    parts = pl.pallas_call(
        moments_kernel,
        out_shape=jax.ShapeDtypeStruct((1, LANES), jnp.float32),
        in_specs=[vmem] * 4,
        out_specs=vmem,
        scratch_shapes=[pltpu.VMEM((rows + 3 * NEAR, LANES + cols), jnp.float32)] * 2,
        compiler_params=pltpu.CompilerParams(vmem_limit_bytes=16 << 20),
        name="moments",
    )(*own, near, left)
    devices = lax.axis_size("rows") * lax.axis_size("cols")
    parts = jnp.broadcast_to(parts[None], (devices, 1, LANES))
    parts = lax.all_to_all(parts, ("rows", "cols"), 0, 0, tiled=True)

    return tuple(
        pl.pallas_call(
            finish_kernel,
            out_shape=(field, field),
            in_specs=[vmem] * 9,
            out_specs=(vmem, vmem),
            scratch_shapes=[
                pltpu.VMEM((rows + 2 * WIDE, width), jnp.float32),
                pltpu.VMEM((rows + 2 * REACH, width), jnp.bfloat16),
                pltpu.VMEM((rows + 2 * REACH, width), jnp.bfloat16),
            ],
            compiler_params=pltpu.CompilerParams(vmem_limit_bytes=32 << 20),
            name="finish",
        )(
            parts, *own, from_near, from_far, left, right,
            jnp.asarray(row_tables(rows)), jnp.asarray(col_tables()),
        )
    )


def solution(mesh):
    return jax.shard_map(
        shards,
        mesh=mesh,
        in_specs=(P("rows", "cols"), P("rows", "cols"), P("rows", "cols")),
        out_specs=(P("rows", "cols"), P("rows", "cols")),
        check_vma=False,
    )
```

```python
import functools

import jax
import jax.numpy as jnp
import ml_dtypes
import numpy as np
from jax import lax
from jax.experimental import pallas as pl
from jax.experimental.pallas import tpu as pltpu
from jax.sharding import PartitionSpec as P

RADIUS = 32
REACH = 2 * RADIUS
LANES = 128
WIDE = REACH + 8
NEAR = 8
VECTORS = 8

smooth_weight = 2.0
blur_sigma = 10.0


def squared_taps(length, first, last):
    offsets = np.arange(2 * RADIUS + 1) - RADIUS
    taps = np.exp(-offsets * offsets / (2.0 * blur_sigma * blur_sigma))
    taps = taps / taps.sum()

    def band(count):
        table = np.zeros((count, count + 2 * RADIUS))
        for k in range(2 * RADIUS + 1):
            table[np.arange(count), np.arange(count) + k] = taps[k]
        return table

    inner = band(length + 2 * RADIUS)
    if first:
        inner[:RADIUS] = 0.0
    if last:
        inner[-RADIUS:] = 0.0
    return band(length) @ inner


def split(table):
    high = table.astype(np.float32).astype(ml_dtypes.bfloat16)
    low = (table - high.astype(np.float64)).astype(np.float32).astype(ml_dtypes.bfloat16)
    return high, low


def row_tables(length):
    tables = []
    for first, last in ((False, False), (True, False), (False, True), (True, True)):
        tables.append(np.concatenate(split(squared_taps(length, first, last)), axis=0))
    return np.stack(tables)


def col_tables():
    tables = []
    for first, last in ((False, False), (True, False), (False, True)):
        tables.append(np.concatenate(split(squared_taps(LANES, first, last).T), axis=1))
    return np.stack(tables)


def split_values(values):
    high = values.astype(jnp.bfloat16)
    return high, (values - high.astype(jnp.float32)).astype(jnp.bfloat16)


def at_edges():
    row, col = lax.axis_index("rows"), lax.axis_index("cols")
    return (
        row == 0,
        row == lax.axis_size("rows") - 1,
        col == 0,
        col == lax.axis_size("cols") - 1,
    )


def is_even():
    return lax.axis_index("rows") % 2 == 0


def beside_columns(field):
    width = field.shape[1]
    return pltpu.roll(field, 1, 1) + pltpu.roll(field, width - 1, 1)


def weights(inverse_variance, source_mask):
    return inverse_variance * (1.0 - source_mask.astype(jnp.float32))


def coefficients(m0, m1, m2, m3):
    alpha0 = m0 / m1
    norm1 = jnp.maximum(m0 - 2.0 * alpha0 * m1 + alpha0 * alpha0 * m2, 0.0)
    grown = 1.0 + norm1 / m0
    image1 = grown * grown * m1 - 2.0 * grown * alpha0 * m2 + alpha0 * alpha0 * m3
    alpha1 = jnp.where(image1 > 0.0, norm1 / image1, 0.0)
    return alpha0 + alpha1 * grown, -alpha1 * alpha0


def wide_kernel(f_ref, w_ref, near_ref, far_ref):
    rows = f_ref.shape[0]

    def write(out_ref, begin, beyond):
        out_ref[pl.ds(0, REACH), :] = f_ref[pl.ds(begin, REACH), :]
        out_ref[pl.ds(REACH, REACH), :] = w_ref[pl.ds(begin, REACH), :]
        out_ref[pl.ds(2 * REACH, 8), :] = f_ref[pl.ds(beyond, 8), :] * w_ref[pl.ds(beyond, 8), :]

    @pl.when(is_even())
    def _():
        write(near_ref, rows - REACH, rows - WIDE)
        write(far_ref, 0, REACH)

    @pl.when(jnp.logical_not(is_even()))
    def _():
        write(near_ref, 0, REACH)
        write(far_ref, rows - REACH, rows - WIDE)


def moments_kernel(f_ref, w_ref, far_ref, near_ref, out_ref, v0_ref, v1_ref, edge_ref):
    rows, cols = f_ref.shape
    width = cols + LANES
    first_row, last_row, _, _ = at_edges()
    even = is_even()
    own, pad = pl.ds(0, cols), pl.ds(cols, LANES)

    far_weight = far_ref[pl.ds(8, 8), :]
    far_v0 = far_ref[pl.ds(0, 8), :] * far_weight
    above, below = near_ref[pl.ds(2 * REACH - 8, 8), :], near_ref[pl.ds(REACH, 8), :]
    top = jnp.where(even, far_v0, near_ref[pl.ds(REACH - 8, 8), :] * above)
    bottom = jnp.where(even, near_ref[pl.ds(0, 8), :] * below, far_v0)
    top_weight = jnp.where(even, far_weight, above)[7:]
    bottom_weight = jnp.where(even, below, far_weight)[:1]

    for ref in (v0_ref, v1_ref):
        ref[:, pad] = jnp.zeros((rows + 2 * NEAR, LANES), jnp.float32)
    for start in (0, NEAR + rows):
        v1_ref[pl.ds(start, 8), own] = jnp.zeros((8, cols), jnp.float32)
    v0_ref[pl.ds(0, 8), own] = top
    v0_ref[pl.ds(NEAR + rows, 8), own] = bottom
    for start in range(0, rows, 8):
        at = pl.ds(start, 8)
        v0_ref[pl.ds(NEAR + start, 8), own] = f_ref[at, :] * w_ref[at, :]

    def image(ref, weight, start, count):
        here = ref[pl.ds(start, count), :]
        beside = ref[pl.ds(start - 1, count), own] + ref[pl.ds(start + 1, count), own] + beside_columns(here)[:, :cols]
        here = here[:, :cols]
        return here, weight * here + smooth_weight * (4.0 * here - beside)

    for start in range(0, rows, 8):
        _, out = image(v0_ref, w_ref[pl.ds(start, 8), :], NEAR + start, 8)
        v1_ref[pl.ds(NEAR + start, 8), own] = out

    def edge_row(weight, at):
        _, out = image(v0_ref, weight, at, 1)
        v1_ref[pl.ds(at, 1), own] = out

    pl.when(jnp.logical_not(first_row))(lambda: edge_row(top_weight, NEAR - 1))
    pl.when(jnp.logical_not(last_row))(lambda: edge_row(bottom_weight, NEAR + rows))

    lane = lax.broadcasted_iota(jnp.int32, (8, LANES), 1)
    sums = [jnp.zeros((8, cols), jnp.float32) for _ in range(4)]
    for start in range(0, rows, 8):
        weight = w_ref[pl.ds(start, 8), :]
        v0 = v0_ref[pl.ds(NEAR + start, 8), own]
        v1, v2 = image(v1_ref, weight, NEAR + start, 8)
        sums = [total + term for total, term in zip(sums, (v0 * v0, v0 * v1, v1 * v1, v1 * v2))]
        edges = jnp.zeros((8, LANES), jnp.float32)
        for k, field in enumerate((v0, v1, v2, weight)):
            edges = jnp.where(lane == k, pltpu.roll(field[:, cols - LANES :], k + 1, 1), edges)
            edges = jnp.where(lane == 4 + k, pltpu.roll(field[:, :LANES], 4 + k, 1), edges)
        edge_ref[pl.ds(start, 8), :] = edges

    result = jnp.zeros((1, LANES), jnp.float32)
    for i, total in enumerate(sums):
        narrow = sum(total[:, k : k + LANES] for k in range(0, cols, LANES))
        total = jnp.sum(jnp.sum(narrow, axis=0, keepdims=True), axis=1, keepdims=True)
        result = jnp.where(lane[:1] == i, total, result)
    out_ref[:, pl.ds(0, LANES)] = result
    vectors = edge_ref[...].T
    for k in range(VECTORS):
        out_ref[:, pl.ds((k + 1) * LANES, LANES)] = vectors[k : k + 1, :]


def coupled(parts_ref, nrows, ncols):
    count = nrows * ncols
    lam = smooth_weight

    def part(k):
        return parts_ref[:, :, pl.ds(k * LANES, LANES)].reshape(count, LANES)

    device = lax.broadcasted_iota(jnp.int32, (count, LANES), 0)
    lane = lax.broadcasted_iota(jnp.int32, (count, LANES), 1)
    joined = device % ncols < ncols - 1
    a0, a1, ua, wa = (jnp.where(joined, part(1 + k), 0.0) for k in range(4))
    b0, b1, ub, wb = (jnp.where(joined, pltpu.roll(part(5 + k), count - 1, 0), 0.0) for k in range(4))

    def next_row(field):
        inside = pltpu.roll(field, LANES - 1, 1)
        beyond = jnp.where(device < count - ncols, pltpu.roll(inside, count - ncols, 0), 0.0)
        return jnp.where(lane == LANES - 1, beyond, inside)

    def total(field):
        return jnp.sum(jnp.sum(field, axis=0, keepdims=True), axis=1, keepdims=True)

    scalars = jnp.sum(part(0), axis=0, keepdims=True)
    m0, m1, m2, m3 = (total(jnp.where(lane[:1] == i, scalars, 0.0)) for i in range(4))
    m1 = m1 - 2.0 * lam * total(a0 * b0)
    m2 = m2 + total(lam * lam * (a0 * a0 + b0 * b0) - 2.0 * lam * (a1 * b0 + b1 * a0))
    m3 = m3 + total(
        lam * lam * ((wa + 4.0 * lam) * b0 * b0 + (wb + 4.0 * lam) * a0 * a0)
        - 2.0 * lam * (b0 * ua + a0 * ub + (a1 - lam * b0) * (b1 - lam * a0))
        - 2.0 * lam * lam * lam * (a0 * next_row(a0) + b0 * next_row(b0))
    )
    return m0, m1, m2, m3


def neighbours(parts_ref, nrows, ncols):
    row, col = lax.axis_index("rows"), lax.axis_index("cols")
    lane = lax.broadcasted_iota(jnp.int32, (LANES, LANES), 1)
    vectors = []
    for vector, step_col in ((1, -1), (5, 1)):
        for step_row in (-1, 0, 1):
            r, c = row + step_row, col + step_col
            there = (r >= 0) & (r < nrows) & (c >= 0) & (c < ncols)
            index = jnp.where(there, r * ncols + c, 0)
            found = parts_ref[index, :, pl.ds(vector * LANES, LANES)]
            vectors.append(jnp.where(there, found, 0.0))
    vectors.append(jnp.zeros((LANES - len(vectors), LANES), jnp.float32))
    columns = jnp.concatenate(vectors, axis=0).T
    sides = []
    for begin, target in ((0, 0), (3, LANES - 1)):
        moved = [jnp.where(lane == target, pltpu.roll(columns, (target - begin - k) % LANES, 1), 0.0) for k in range(3)]
        sides.append(jnp.concatenate([moved[0][LANES - REACH :], moved[1], moved[2][:REACH]], axis=0))
    return sides


def halo(near_ref, far_ref, below, start, count, at_cols):
    at = pl.ds(start, count)
    one, other = (near_ref, far_ref) if below else (far_ref, near_ref)
    return jnp.where(is_even(), one[at, at_cols], other[at, at_cols])


def pair(f_ref, w_ref, near_ref, far_ref, start, count, at_cols):
    rows = f_ref.shape[0]
    for below, begin in ((False, WIDE - REACH), (True, WIDE + rows)):
        if begin <= start < begin + REACH:
            return tuple(halo(near_ref, far_ref, below, start - begin + k, count, at_cols) for k in (0, REACH))
    at = pl.ds(start - WIDE, count)
    return f_ref[at, at_cols], w_ref[at, at_cols]


def product(refs, v0_ref, at_cols, target):
    rows = refs[0].shape[0]
    v0_ref[pl.ds(0, 8), target] = halo(refs[2], refs[3], False, 2 * REACH, 8, at_cols)
    v0_ref[pl.ds(rows + 2 * WIDE - 8, 8), target] = halo(refs[2], refs[3], True, 2 * REACH, 8, at_cols)
    for start in range(8, rows + 2 * WIDE - 8, 8):
        flux, weight = pair(*refs, start, 8, at_cols)
        v0_ref[pl.ds(start, 8), target] = flux * weight


def clear_outside(refs, rows):
    first_row, last_row, _, _ = at_edges()

    def clear(start):
        for ref in refs:
            ref[pl.ds(start, REACH), :] = jnp.zeros((REACH, ref.shape[1]), jnp.bfloat16)

    pl.when(first_row)(lambda: clear(0))
    pl.when(last_row)(lambda: clear(REACH + rows))


def dot(left, right):
    return jnp.dot(left, right, preferred_element_type=jnp.float32)


def row_pass(rowtaps_ref, high, low, rows):
    first_row, last_row, _, _ = at_edges()
    table = rowtaps_ref[first_row.astype(jnp.int32) + 2 * last_row.astype(jnp.int32)]
    both = dot(table, high)
    return both[:rows] + (both[rows:] + dot(table[:rows], low))


def edges_kernel(
    nrows, ncols, parts_ref, f_ref, w_ref, near_ref, far_ref, rowtaps_ref,
    coefficients_ref, left_ref, right_ref, first_ref, last_ref, v0_ref, high_ref, low_ref,
):
    rows, cols = f_ref.shape
    refs = (f_ref, w_ref, near_ref, far_ref)
    c0, c1 = coefficients(*coupled(parts_ref, nrows, ncols))
    coefficients_ref[pl.ds(0, 8), :] = jnp.broadcast_to(c0, (8, LANES))
    coefficients_ref[pl.ds(8, 8), :] = jnp.broadcast_to(c1, (8, LANES))
    left_ref[...], right_ref[...] = neighbours(parts_ref, nrows, ncols)

    step = 16
    lane = lax.broadcasted_iota(jnp.int32, (step, 2 * LANES), 1)
    for side, begin in enumerate((0, cols - 2 * LANES)):
        target = pl.ds(side * 2 * LANES, 2 * LANES)
        product(refs, v0_ref, pl.ds(begin, 2 * LANES), target)
        at_cols = pl.ds(side * (cols - LANES), LANES)
        here_at = slice(side * LANES, side * LANES + LANES)
        wrapped = lane == side * (2 * LANES - 1)
        for start in range(8, rows + 2 * WIDE - 8, step):
            flux, weight = pair(*refs, start, step, at_cols)
            field = v0_ref[pl.ds(start, step), target]
            inner = pltpu.roll(field, 2 * LANES - 1 if side == 0 else 1, 1)
            outer = jnp.where(wrapped, 0.0, pltpu.roll(field, 1 if side == 0 else 2 * LANES - 1, 1))
            beside = v0_ref[pl.ds(start - 1, step), target] + v0_ref[pl.ds(start + 1, step), target] + inner + outer
            v0 = field[:, here_at]
            beside = beside[:, here_at] + (left_ref, right_ref)[side][pl.ds(start - 8, step), :]
            v1 = weight * v0 + smooth_weight * (4.0 * v0 - beside)
            scatter = flux - (c0 * v0 + c1 * v1)
            high, low = split_values(scatter * scatter)
            high_ref[pl.ds(start - 8, step), pl.ds(side * LANES, LANES)] = high
            low_ref[pl.ds(start - 8, step), pl.ds(side * LANES, LANES)] = low
    clear_outside((high_ref, low_ref), rows)
    passed = row_pass(rowtaps_ref, high_ref[...], low_ref[...], rows)
    first_ref[...] = passed[:, :LANES]
    last_ref[...] = passed[:, LANES:]


def main_kernel(
    coefficients_ref, left_ref, right_ref, f_ref, w_ref, near_ref, far_ref, rowtaps_ref,
    background_ref, passed_ref, v0_ref, high_ref, low_ref,
):
    rows, cols = f_ref.shape
    refs = (f_ref, w_ref, near_ref, far_ref)
    own = pl.ds(0, cols)
    c0, c1 = coefficients_ref[pl.ds(0, 1), pl.ds(0, 1)], coefficients_ref[pl.ds(8, 1), pl.ds(0, 1)]
    v0_ref[:, pl.ds(cols, LANES)] = jnp.zeros((rows + 2 * WIDE, LANES), jnp.float32)
    product(refs, v0_ref, own, own)
    step = 16
    for start in range(8, rows + 2 * WIDE - 8, step):
        flux, weight = pair(*refs, start, step, own)
        field = v0_ref[pl.ds(start, step), :]
        beside = v0_ref[pl.ds(start - 1, step), own] + v0_ref[pl.ds(start + 1, step), own] + beside_columns(field)[:, :cols]
        at = pl.ds(start - 8, step)
        beside = jnp.concatenate(
            [beside[:, :LANES] + left_ref[at, :], beside[:, LANES : cols - LANES], beside[:, cols - LANES :] + right_ref[at, :]],
            axis=1,
        )
        v0 = field[:, :cols]
        v1 = weight * v0 + smooth_weight * (4.0 * v0 - beside)
        background = c0 * v0 + c1 * v1
        if WIDE <= start < WIDE + rows:
            background_ref[pl.ds(start - WIDE, step), :] = background
        scatter = flux - background
        high_ref[at, :], low_ref[at, :] = split_values(scatter * scatter)
    clear_outside((high_ref, low_ref), rows)
    passed_ref[...] = row_pass(rowtaps_ref, high_ref[...], low_ref[...], rows)


def final_kernel(passed_ref, left_ref, right_ref, coltaps_ref, rms_ref):
    rows, cols = passed_ref.shape
    width = cols + 2 * LANES
    _, _, first_col, last_col = at_edges()
    passed = jnp.concatenate([left_ref[...], passed_ref[...], right_ref[...]], axis=1)
    passed = pltpu.roll(passed, width - (LANES - REACH), 1)
    high, low = split_values(passed)
    blocks = cols // LANES
    for j in range(blocks):
        which = 0
        if j == 0:
            which = first_col.astype(jnp.int32)
        elif j == blocks - 1:
            which = 2 * last_col.astype(jnp.int32)
        table = coltaps_ref[which]
        at = slice(j * LANES, j * LANES + 2 * LANES)
        both = dot(high[:, at], table)
        smoothed = both[:, :LANES] + (both[:, LANES:] + dot(low[:, at], table[:, :LANES]))
        rms_ref[:, pl.ds(j * LANES, LANES)] = jnp.sqrt(smoothed + 1e-06)


def shift(block, axis, step):
    count = lax.axis_size(axis)
    pairs = [(i, i + step) for i in range(count) if 0 <= i + step < count]
    return lax.ppermute(block, axis, pairs)


def swap(block, axis, first):
    count = lax.axis_size(axis)
    pairs = [(i, i + 1) for i in range(first, count - 1, 2)]
    return lax.ppermute(block, axis, pairs + [(j, i) for i, j in pairs])


def call(kernel, name, outs, scratch=(), limit=16):
    vmem = pl.BlockSpec(memory_space=pltpu.VMEM)

    def run(*args):
        return pl.pallas_call(
            kernel,
            out_shape=tuple(jax.ShapeDtypeStruct(shape, jnp.float32) for shape in outs),
            in_specs=[vmem] * len(args),
            out_specs=(vmem,) * len(outs),
            scratch_shapes=[pltpu.VMEM(shape, dtype) for shape, dtype in scratch],
            compiler_params=pltpu.CompilerParams(vmem_limit_bytes=limit << 20),
            name=name,
        )(*args)

    return run


def shards(coadd_flux, inverse_variance, source_mask):
    rows, cols = coadd_flux.shape
    nrows, ncols = lax.axis_size("rows"), lax.axis_size("cols")
    message = (VECTORS + 1) * LANES
    f32, bf16 = jnp.float32, jnp.bfloat16

    begin = jnp.where(is_even(), 0, rows - NEAR)
    flux, variance, mask = (
        lax.dynamic_slice(x, (begin, 0), (NEAR, cols)) for x in (coadd_flux, inverse_variance, source_mask)
    )
    narrow = swap(jnp.concatenate([flux, weights(variance, mask)]), "rows", 1)

    own = (coadd_flux, weights(inverse_variance, source_mask))
    wide = (2 * REACH + 8, cols)
    to_near, to_far = call(wide_kernel, "wide", (wide, wide))(*own)
    to_near, to_far, narrow = lax.optimization_barrier((to_near, to_far, narrow))
    near = swap(to_near, "rows", 0)
    far = swap(to_far, "rows", 1)

    field = ((rows + 2 * NEAR, cols + LANES), f32)
    (parts,) = call(moments_kernel, "moments", ((1, message),), (field, field, ((rows, LANES), f32)))(*own, narrow, near)
    parts = jnp.broadcast_to(parts[None], (nrows * ncols, 1, message))
    parts = lax.all_to_all(parts, ("rows", "cols"), 0, 0, tiled=True)

    row_taps, col_taps = jnp.asarray(row_tables(rows)), jnp.asarray(col_tables())
    column, reached, block = (rows + 2 * REACH, LANES), rows + 2 * REACH, (rows, LANES)
    numbers, left, right, first, last = call(
        functools.partial(edges_kernel, nrows, ncols),
        "edges",
        ((16, LANES), column, column, block, block),
        (((rows + 2 * WIDE, 4 * LANES), f32),) + (((reached, 2 * LANES), bf16),) * 2,
    )(parts, *own, near, far, row_taps)
    from_left = shift(last, "cols", 1)
    from_right = shift(first, "cols", -1)
    background, passed = call(
        main_kernel,
        "main",
        ((rows, cols), (rows, cols)),
        (((rows + 2 * WIDE, cols + LANES), f32),) + (((reached, cols), bf16),) * 2,
        32,
    )(numbers, left, right, *own, near, far, row_taps)
    (rms,) = call(final_kernel, "final", ((rows, cols),))(passed, from_left, from_right, col_taps)
    return background, rms


def solution(mesh):
    return jax.shard_map(
        shards,
        mesh=mesh,
        in_specs=(P("rows", "cols"), P("rows", "cols"), P("rows", "cols")),
        out_specs=(P("rows", "cols"), P("rows", "cols")),
        check_vma=False,
    )
```

```python
import functools

import jax
import jax.numpy as jnp
import ml_dtypes
import numpy as np
from jax import lax
from jax.experimental import pallas as pl
from jax.experimental.pallas import tpu as pltpu
from jax.sharding import PartitionSpec as P

RADIUS = 32
REACH = 2 * RADIUS
LANES = 128
WIDE = REACH + 8
NEAR = 8
VECTORS = 8

smooth_weight = 2.0
blur_sigma = 10.0


def squared_taps(length, first, last):
    offsets = np.arange(2 * RADIUS + 1) - RADIUS
    taps = np.exp(-offsets * offsets / (2.0 * blur_sigma * blur_sigma))
    taps = taps / taps.sum()

    def band(count):
        table = np.zeros((count, count + 2 * RADIUS))
        for k in range(2 * RADIUS + 1):
            table[np.arange(count), np.arange(count) + k] = taps[k]
        return table

    inner = band(length + 2 * RADIUS)
    if first:
        inner[:RADIUS] = 0.0
    if last:
        inner[-RADIUS:] = 0.0
    return band(length) @ inner


def split(table):
    high = table.astype(np.float32).astype(ml_dtypes.bfloat16)
    low = (table - high.astype(np.float64)).astype(np.float32).astype(ml_dtypes.bfloat16)
    return high, low


def row_tables(length):
    tables = []
    for first, last in ((False, False), (True, False), (False, True), (True, True)):
        tables.append(np.concatenate(split(squared_taps(length, first, last)), axis=0))
    return np.stack(tables)


def col_tables():
    tables = []
    for first, last in ((False, False), (True, False), (False, True)):
        tables.append(np.concatenate(split(squared_taps(LANES, first, last).T), axis=1))
    return np.stack(tables)


def split_values(values):
    high = values.astype(jnp.bfloat16)
    return high, (values - high.astype(jnp.float32)).astype(jnp.bfloat16)


def at_edges():
    row, col = lax.axis_index("rows"), lax.axis_index("cols")
    return (
        row == 0,
        row == lax.axis_size("rows") - 1,
        col == 0,
        col == lax.axis_size("cols") - 1,
    )


def is_even():
    return lax.axis_index("rows") % 2 == 0


def beside_columns(field):
    width = field.shape[1]
    return pltpu.roll(field, 1, 1) + pltpu.roll(field, width - 1, 1)


def weights(inverse_variance, source_mask):
    return inverse_variance * (1.0 - source_mask.astype(jnp.float32))


def coefficients(m0, m1, m2, m3):
    alpha0 = m0 / m1
    norm1 = jnp.maximum(m0 - 2.0 * alpha0 * m1 + alpha0 * alpha0 * m2, 0.0)
    grown = 1.0 + norm1 / m0
    image1 = grown * grown * m1 - 2.0 * grown * alpha0 * m2 + alpha0 * alpha0 * m3
    alpha1 = jnp.where(image1 > 0.0, norm1 / image1, 0.0)
    return alpha0 + alpha1 * grown, -alpha1 * alpha0


def prepare_kernel(f_ref, iv_ref, mask_ref, w_ref, near_ref, far_ref):
    rows = f_ref.shape[0]
    w_ref[...] = weights(iv_ref[...], mask_ref[...])

    def write(out_ref, begin):
        out_ref[pl.ds(0, REACH), :] = f_ref[pl.ds(begin, REACH), :]
        out_ref[pl.ds(REACH, REACH), :] = w_ref[pl.ds(begin, REACH), :]

    def near_product(begin):
        near_ref[pl.ds(2 * REACH, 8), :] = f_ref[pl.ds(begin, 8), :] * w_ref[pl.ds(begin, 8), :]

    @pl.when(is_even())
    def _():
        write(near_ref, rows - REACH)
        near_product(rows - WIDE)
        write(far_ref, 0)

    @pl.when(jnp.logical_not(is_even()))
    def _():
        write(near_ref, 0)
        near_product(REACH)
        write(far_ref, rows - REACH)


def moments_kernel(f_ref, w_ref, narrow_ref, near_ref, out_ref, v0_ref, v1_ref, edge_ref):
    rows, cols = f_ref.shape
    width = cols + LANES
    first_row, last_row, _, _ = at_edges()
    even = is_even()
    own, pad = pl.ds(0, cols), pl.ds(cols, LANES)

    above, below = near_ref[pl.ds(2 * REACH - 8, 8), :], near_ref[pl.ds(REACH, 8), :]
    nothing = jnp.zeros((6, cols), jnp.float32)
    nearest, second, far_weight = (narrow_ref[pl.ds(k, 1), :] for k in range(3))
    far_above = jnp.concatenate([nothing, second, nearest], axis=0)
    far_below = jnp.concatenate([nearest, second, nothing], axis=0)
    top = jnp.where(even, far_above, near_ref[pl.ds(REACH - 8, 8), :] * above)
    bottom = jnp.where(even, near_ref[pl.ds(0, 8), :] * below, far_below)
    top_weight = jnp.where(even, far_weight, above[7:])
    bottom_weight = jnp.where(even, below[:1], far_weight)

    for ref in (v0_ref, v1_ref):
        ref[:, pad] = jnp.zeros((rows + 2 * NEAR, LANES), jnp.float32)
    for start in (0, NEAR + rows):
        v1_ref[pl.ds(start, 8), own] = jnp.zeros((8, cols), jnp.float32)
    v0_ref[pl.ds(0, 8), own] = top
    v0_ref[pl.ds(NEAR + rows, 8), own] = bottom
    for start in range(0, rows, 8):
        at = pl.ds(start, 8)
        v0_ref[pl.ds(NEAR + start, 8), own] = f_ref[at, :] * w_ref[at, :]

    def image(ref, weight, start, count):
        here = ref[pl.ds(start, count), :]
        beside = ref[pl.ds(start - 1, count), own] + ref[pl.ds(start + 1, count), own] + beside_columns(here)[:, :cols]
        here = here[:, :cols]
        return here, weight * here + smooth_weight * (4.0 * here - beside)

    for start in range(0, rows, 8):
        _, out = image(v0_ref, w_ref[pl.ds(start, 8), :], NEAR + start, 8)
        v1_ref[pl.ds(NEAR + start, 8), own] = out

    def edge_row(weight, at):
        _, out = image(v0_ref, weight, at, 1)
        v1_ref[pl.ds(at, 1), own] = out

    pl.when(jnp.logical_not(first_row))(lambda: edge_row(top_weight, NEAR - 1))
    pl.when(jnp.logical_not(last_row))(lambda: edge_row(bottom_weight, NEAR + rows))

    lane = lax.broadcasted_iota(jnp.int32, (8, LANES), 1)
    sums = [jnp.zeros((8, cols), jnp.float32) for _ in range(4)]
    for start in range(0, rows, 8):
        weight = w_ref[pl.ds(start, 8), :]
        v0 = v0_ref[pl.ds(NEAR + start, 8), own]
        v1, v2 = image(v1_ref, weight, NEAR + start, 8)
        sums = [total + term for total, term in zip(sums, (v0 * v0, v0 * v1, v1 * v1, v1 * v2))]
        edges = jnp.zeros((8, LANES), jnp.float32)
        for k, field in enumerate((v0, v1, v2, weight)):
            edges = jnp.where(lane == k, pltpu.roll(field[:, cols - LANES :], k + 1, 1), edges)
            edges = jnp.where(lane == 4 + k, pltpu.roll(field[:, :LANES], 4 + k, 1), edges)
        edge_ref[pl.ds(start, 8), :] = edges

    result = jnp.zeros((1, LANES), jnp.float32)
    for i, total in enumerate(sums):
        narrow = sum(total[:, k : k + LANES] for k in range(0, cols, LANES))
        total = jnp.sum(jnp.sum(narrow, axis=0, keepdims=True), axis=1, keepdims=True)
        result = jnp.where(lane[:1] == i, total, result)
    vectors = edge_ref[...].T
    message = jnp.concatenate([result] + [vectors[k : k + 1, :] for k in range(VECTORS)], axis=1)
    for k in range(out_ref.shape[0]):
        out_ref[k] = message


def coupled(parts_ref, nrows, ncols):
    count = nrows * ncols
    lam = smooth_weight

    def part(k):
        return parts_ref[:, :, pl.ds(k * LANES, LANES)].reshape(count, LANES)

    device = lax.broadcasted_iota(jnp.int32, (count, LANES), 0)
    lane = lax.broadcasted_iota(jnp.int32, (count, LANES), 1)
    joined = device % ncols < ncols - 1
    a0, a1, ua, wa = (jnp.where(joined, part(1 + k), 0.0) for k in range(4))
    b0, b1, ub, wb = (jnp.where(joined, pltpu.roll(part(5 + k), count - 1, 0), 0.0) for k in range(4))

    def next_row(field):
        inside = pltpu.roll(field, LANES - 1, 1)
        beyond = jnp.where(device < count - ncols, pltpu.roll(inside, count - ncols, 0), 0.0)
        return jnp.where(lane == LANES - 1, beyond, inside)

    def total(field):
        return jnp.sum(jnp.sum(field, axis=0, keepdims=True), axis=1, keepdims=True)

    scalars = jnp.sum(part(0), axis=0, keepdims=True)
    m0, m1, m2, m3 = (total(jnp.where(lane[:1] == i, scalars, 0.0)) for i in range(4))
    m1 = m1 - 2.0 * lam * total(a0 * b0)
    m2 = m2 + total(lam * lam * (a0 * a0 + b0 * b0) - 2.0 * lam * (a1 * b0 + b1 * a0))
    m3 = m3 + total(
        lam * lam * ((wa + 4.0 * lam) * b0 * b0 + (wb + 4.0 * lam) * a0 * a0)
        - 2.0 * lam * (b0 * ua + a0 * ub + (a1 - lam * b0) * (b1 - lam * a0))
        - 2.0 * lam * lam * lam * (a0 * next_row(a0) + b0 * next_row(b0))
    )
    return m0, m1, m2, m3


def neighbours(parts_ref, nrows, ncols):
    row, col = lax.axis_index("rows"), lax.axis_index("cols")
    lane = lax.broadcasted_iota(jnp.int32, (LANES, LANES), 1)
    vectors = []
    for vector, step_col in ((1, -1), (5, 1)):
        for step_row in (-1, 0, 1):
            r, c = row + step_row, col + step_col
            there = (r >= 0) & (r < nrows) & (c >= 0) & (c < ncols)
            index = jnp.where(there, r * ncols + c, 0)
            found = parts_ref[index, :, pl.ds(vector * LANES, LANES)]
            vectors.append(jnp.where(there, found, 0.0))
    vectors.append(jnp.zeros((LANES - len(vectors), LANES), jnp.float32))
    columns = jnp.concatenate(vectors, axis=0).T
    sides = []
    for begin, target in ((0, 0), (3, LANES - 1)):
        moved = [jnp.where(lane == target, pltpu.roll(columns, (target - begin - k) % LANES, 1), 0.0) for k in range(3)]
        sides.append(jnp.concatenate([moved[0][LANES - REACH :], moved[1], moved[2][:REACH]], axis=0))
    return sides


def halo(near_ref, far_ref, below, start, count, at_cols):
    at = pl.ds(start, count)
    one, other = (near_ref, far_ref) if below else (far_ref, near_ref)
    return jnp.where(is_even(), one[at, at_cols], other[at, at_cols])


def last_row(near_ref, narrow_ref, below, at_cols):
    near = near_ref[pl.ds(2 * REACH + (0 if below else 7), 1), at_cols]
    far = narrow_ref[pl.ds(3, 1), at_cols]
    return jnp.where(is_even(), near, far) if below else jnp.where(is_even(), far, near)


def pair(f_ref, w_ref, near_ref, far_ref, narrow_ref, start, count, at_cols):
    rows = f_ref.shape[0]
    for below, begin in ((False, WIDE - REACH), (True, WIDE + rows)):
        if begin <= start < begin + REACH:
            return tuple(halo(near_ref, far_ref, below, start - begin + k, count, at_cols) for k in (0, REACH))
    at = pl.ds(start - WIDE, count)
    return f_ref[at, at_cols], w_ref[at, at_cols]


def product(refs, v0_ref, at_cols, target):
    rows = refs[0].shape[0]
    v0_ref[pl.ds(7, 1), target] = last_row(refs[2], refs[4], False, at_cols)
    v0_ref[pl.ds(rows + 2 * WIDE - 8, 1), target] = last_row(refs[2], refs[4], True, at_cols)
    for start in range(8, rows + 2 * WIDE - 8, 8):
        flux, weight = pair(*refs, start, 8, at_cols)
        v0_ref[pl.ds(start, 8), target] = flux * weight


def clear_outside(refs, rows):
    first_row, last_row, _, _ = at_edges()

    def clear(start):
        for ref in refs:
            ref[pl.ds(start, REACH), :] = jnp.zeros((REACH, ref.shape[1]), jnp.bfloat16)

    pl.when(first_row)(lambda: clear(0))
    pl.when(last_row)(lambda: clear(REACH + rows))


def dot(left, right):
    return jnp.dot(left, right, preferred_element_type=jnp.float32)


def row_pass(rowtaps_ref, high, low, rows):
    first_row, last_row, _, _ = at_edges()
    table = rowtaps_ref[first_row.astype(jnp.int32) + 2 * last_row.astype(jnp.int32)]
    both = dot(table, high)
    return both[:rows] + (both[rows:] + dot(table[:rows], low))


def edges_kernel(
    nrows, ncols, parts_ref, f_ref, w_ref, near_ref, far_ref, narrow_ref, rowtaps_ref,
    coefficients_ref, left_ref, right_ref, first_ref, last_ref, v0_ref, high_ref, low_ref,
):
    rows, cols = f_ref.shape
    refs = (f_ref, w_ref, near_ref, far_ref, narrow_ref)
    c0, c1 = coefficients(*coupled(parts_ref, nrows, ncols))
    coefficients_ref[pl.ds(0, 8), :] = jnp.broadcast_to(c0, (8, LANES))
    coefficients_ref[pl.ds(8, 8), :] = jnp.broadcast_to(c1, (8, LANES))
    left_ref[...], right_ref[...] = neighbours(parts_ref, nrows, ncols)

    step = 16
    lane = lax.broadcasted_iota(jnp.int32, (step, 2 * LANES), 1)
    for side, begin in enumerate((0, cols - 2 * LANES)):
        target = pl.ds(side * 2 * LANES, 2 * LANES)
        product(refs, v0_ref, pl.ds(begin, 2 * LANES), target)
        at_cols = pl.ds(side * (cols - LANES), LANES)
        here_at = slice(side * LANES, side * LANES + LANES)
        wrapped = lane == side * (2 * LANES - 1)
        for start in range(8, rows + 2 * WIDE - 8, step):
            flux, weight = pair(*refs, start, step, at_cols)
            field = v0_ref[pl.ds(start, step), target]
            inner = pltpu.roll(field, 2 * LANES - 1 if side == 0 else 1, 1)
            outer = jnp.where(wrapped, 0.0, pltpu.roll(field, 1 if side == 0 else 2 * LANES - 1, 1))
            beside = v0_ref[pl.ds(start - 1, step), target] + v0_ref[pl.ds(start + 1, step), target] + inner + outer
            v0 = field[:, here_at]
            beside = beside[:, here_at] + (left_ref, right_ref)[side][pl.ds(start - 8, step), :]
            v1 = weight * v0 + smooth_weight * (4.0 * v0 - beside)
            scatter = flux - (c0 * v0 + c1 * v1)
            high, low = split_values(scatter * scatter)
            high_ref[pl.ds(start - 8, step), pl.ds(side * LANES, LANES)] = high
            low_ref[pl.ds(start - 8, step), pl.ds(side * LANES, LANES)] = low
    clear_outside((high_ref, low_ref), rows)
    passed = row_pass(rowtaps_ref, high_ref[...], low_ref[...], rows)
    upper, lower = slice(0, rows // 2), slice(rows // 2, rows)
    first, last = passed[:, :LANES], passed[:, LANES:]
    on_left = lax.broadcasted_iota(jnp.int32, (rows // 2, LANES), 1) < REACH
    first_ref[...] = jnp.where(on_left, first[upper], pltpu.roll(first[lower], REACH, 1))
    last_ref[...] = jnp.where(on_left, pltpu.roll(last[upper], REACH, 1), last[lower])


def main_kernel(
    coefficients_ref, left_ref, right_ref, f_ref, w_ref, near_ref, far_ref, narrow_ref, rowtaps_ref, coltaps_ref,
    background_ref, rms_ref, sides_ref, v0_ref, high_ref, low_ref,
):
    rows, cols = f_ref.shape
    refs = (f_ref, w_ref, near_ref, far_ref, narrow_ref)
    own = pl.ds(0, cols)
    c0, c1 = coefficients_ref[pl.ds(0, 1), pl.ds(0, 1)], coefficients_ref[pl.ds(8, 1), pl.ds(0, 1)]
    v0_ref[:, pl.ds(cols, LANES)] = jnp.zeros((rows + 2 * WIDE, LANES), jnp.float32)
    product(refs, v0_ref, own, own)
    step = 16
    for start in range(8, rows + 2 * WIDE - 8, step):
        flux, weight = pair(*refs, start, step, own)
        field = v0_ref[pl.ds(start, step), :]
        beside = v0_ref[pl.ds(start - 1, step), own] + v0_ref[pl.ds(start + 1, step), own] + beside_columns(field)[:, :cols]
        at = pl.ds(start - 8, step)
        beside = jnp.concatenate(
            [beside[:, :LANES] + left_ref[at, :], beside[:, LANES : cols - LANES], beside[:, cols - LANES :] + right_ref[at, :]],
            axis=1,
        )
        v0 = field[:, :cols]
        v1 = weight * v0 + smooth_weight * (4.0 * v0 - beside)
        background = c0 * v0 + c1 * v1
        if WIDE <= start < WIDE + rows:
            background_ref[pl.ds(start - WIDE, step), :] = background
        scatter = flux - background
        high_ref[at, :], low_ref[at, :] = split_values(scatter * scatter)
    clear_outside((high_ref, low_ref), rows)
    passed = row_pass(rowtaps_ref, high_ref[...], low_ref[...], rows)
    sides_ref[:, pl.ds(0, 2 * LANES)] = passed[:, : 2 * LANES]
    sides_ref[:, pl.ds(2 * LANES, 2 * LANES)] = passed[:, cols - 2 * LANES :]
    high, low = split_values(pltpu.roll(passed, REACH, 1))
    for j in range(1, cols // LANES - 1):
        at = slice(j * LANES, j * LANES + 2 * LANES)
        rms_ref[:, pl.ds(j * LANES, LANES)] = column_pass(coltaps_ref[0], high[:, at], low[:, at])


def column_pass(table, high, low):
    both = dot(high, table)
    smoothed = both[:, :LANES] + (both[:, LANES:] + dot(low, table[:, :LANES]))
    return jnp.sqrt(smoothed + 1e-06)


def final_kernel(rms_in_ref, sides_ref, left_ref, right_ref, coltaps_ref, rms_ref, blocks_ref, sems):
    rows, cols = rms_ref.shape
    del rms_in_ref
    _, _, first_col, last_col = at_edges()
    left, right = left_ref[...], right_ref[...]
    left = jnp.concatenate([pltpu.roll(left, REACH, 1), left], axis=0)
    right = jnp.concatenate([right, pltpu.roll(right, REACH, 1)], axis=0)
    sides = sides_ref[...]
    windows = (
        pltpu.roll(jnp.concatenate([left, sides[:, : 2 * LANES]], axis=1), 3 * LANES - REACH, 1)[:, : 2 * LANES],
        pltpu.roll(jnp.concatenate([sides[:, 2 * LANES :], right], axis=1), 3 * LANES - REACH, 1)[:, : 2 * LANES],
    )
    copies = []
    for side, which in enumerate((first_col.astype(jnp.int32), 2 * last_col.astype(jnp.int32))):
        high, low = split_values(windows[side])
        blocks_ref[side] = column_pass(coltaps_ref[which], high, low)
        target = rms_ref.at[:, pl.ds(side * (cols - LANES), LANES)]
        copies.append(pltpu.make_async_copy(blocks_ref.at[side], target, sems.at[side]))
        copies[-1].start()
    for copy in copies:
        copy.wait()


def shift(block, axis, step):
    count = lax.axis_size(axis)
    pairs = [(i, i + step) for i in range(count) if 0 <= i + step < count]
    return lax.ppermute(block, axis, pairs)


def swap(block, axis, first):
    count = lax.axis_size(axis)
    pairs = [(i, i + 1) for i in range(first, count - 1, 2)]
    return lax.ppermute(block, axis, pairs + [(j, i) for i, j in pairs])


def call(kernel, name, outs, scratch=(), limit=16, in_place=False):
    vmem = pl.BlockSpec(memory_space=pltpu.VMEM)
    there = pl.BlockSpec(memory_space=pl.ANY)

    def run(*args):
        return pl.pallas_call(
            kernel,
            out_shape=tuple(jax.ShapeDtypeStruct(shape, jnp.float32) for shape in outs),
            in_specs=[there if in_place and i == 0 else vmem for i in range(len(args))],
            out_specs=(there if in_place else vmem,) * len(outs),
            scratch_shapes=list(scratch),
            input_output_aliases={0: 0} if in_place else {},
            compiler_params=pltpu.CompilerParams(vmem_limit_bytes=limit << 20),
            name=name,
        )(*args)

    return run


def shards(coadd_flux, inverse_variance, source_mask):
    rows, cols = coadd_flux.shape
    nrows, ncols = lax.axis_size("rows"), lax.axis_size("cols")
    message = (VECTORS + 1) * LANES

    def scratch(*shape, dtype=jnp.float32):
        return pltpu.VMEM(shape, dtype)

    taken = []
    for above, below in ((0, rows - 1), (1, rows - 2), (REACH, rows - 1 - REACH)):
        start = (jnp.where(is_even(), above, below), 0)
        flux, variance, mask = (
            lax.dynamic_slice(x, start, (1, cols)) for x in (coadd_flux, inverse_variance, source_mask)
        )
        taken.append((flux, weights(variance, mask)))
    products = [flux * weight for flux, weight in taken]
    narrow = swap(jnp.concatenate([products[0], products[1], taken[0][1], products[2]]), "rows", 1)

    weight, to_near, to_far = call(
        prepare_kernel, "prepare", ((rows, cols), (2 * REACH + 8, cols), (2 * REACH, cols))
    )(coadd_flux, inverse_variance, source_mask)
    own = (coadd_flux, weight)
    to_near, to_far, narrow = lax.optimization_barrier((to_near, to_far, narrow))
    near = swap(to_near, "rows", 0)
    far = swap(to_far, "rows", 1)

    field = scratch(rows + 2 * NEAR, cols + LANES)
    (parts,) = call(
        moments_kernel, "moments", ((nrows * ncols, 1, message),), (field, field, scratch(rows, LANES))
    )(*own, narrow, near)
    parts = lax.all_to_all(parts, ("rows", "cols"), 0, 0, tiled=True)

    row_taps, col_taps = jnp.asarray(row_tables(rows)), jnp.asarray(col_tables())
    halos = (near, far, narrow)
    reached, packed = rows + 2 * REACH, (rows // 2, LANES)
    numbers, left, right, first, last = call(
        functools.partial(edges_kernel, nrows, ncols),
        "edges",
        ((16, LANES), (reached, LANES), (reached, LANES), packed, packed),
        (scratch(rows + 2 * WIDE, 4 * LANES),) + (scratch(reached, 2 * LANES, dtype=jnp.bfloat16),) * 2,
    )(parts, *own, *halos, row_taps)
    from_left = shift(last, "cols", 1)
    from_right = shift(first, "cols", -1)
    background, rms, sides = call(
        main_kernel,
        "main",
        ((rows, cols), (rows, cols), (rows, 4 * LANES)),
        (scratch(rows + 2 * WIDE, cols + LANES),) + (scratch(reached, cols, dtype=jnp.bfloat16),) * 2,
        32,
    )(numbers, left, right, *own, *halos, row_taps, col_taps)
    (rms,) = call(
        final_kernel, "final", ((rows, cols),), (scratch(2, rows, LANES), pltpu.SemaphoreType.DMA((2,))), in_place=True
    )(rms, sides, from_left, from_right, col_taps)
    return background, rms


def solution(mesh):
    return jax.shard_map(
        shards,
        mesh=mesh,
        in_specs=(P("rows", "cols"), P("rows", "cols"), P("rows", "cols")),
        out_specs=(P("rows", "cols"), P("rows", "cols")),
        check_vma=False,
    )
```

```python
import functools

import jax
import jax.numpy as jnp
import ml_dtypes
import numpy as np
from jax import lax
from jax.experimental import pallas as pl
from jax.experimental.pallas import tpu as pltpu
from jax.sharding import PartitionSpec as P

RADIUS = 32
REACH = 2 * RADIUS
LANES = 128
WIDE = REACH + 8
NEAR = 8
VECTORS = 8

smooth_weight = 2.0
blur_sigma = 10.0


def squared_taps(length, first, last):
    offsets = np.arange(2 * RADIUS + 1) - RADIUS
    taps = np.exp(-offsets * offsets / (2.0 * blur_sigma * blur_sigma))
    taps = taps / taps.sum()

    def band(count):
        table = np.zeros((count, count + 2 * RADIUS))
        for k in range(2 * RADIUS + 1):
            table[np.arange(count), np.arange(count) + k] = taps[k]
        return table

    inner = band(length + 2 * RADIUS)
    if first:
        inner[:RADIUS] = 0.0
    if last:
        inner[-RADIUS:] = 0.0
    return band(length) @ inner


def split(table):
    high = table.astype(np.float32).astype(ml_dtypes.bfloat16)
    low = (table - high.astype(np.float64)).astype(np.float32).astype(ml_dtypes.bfloat16)
    return high, low


def row_tables(length):
    tables = []
    for first, last, odd in ((False, False, False), (True, False, False), (False, False, True), (False, True, True)):
        table = squared_taps(length, first, last)
        above, own, below = table[:, :REACH], table[:, REACH : REACH + length], table[:, REACH + length :]
        near, far = (above, below) if odd else (below, above)
        if first or last:
            far = np.zeros_like(far)
        tables.append(np.concatenate(split(np.concatenate([own, near, far], axis=1)), axis=0))
    return np.stack(tables)


def col_tables():
    tables = []
    for first, last in ((False, False), (True, False), (False, True)):
        tables.append(np.concatenate(split(squared_taps(LANES, first, last).T), axis=1))
    return np.stack(tables)


def split_values(values):
    high = values.astype(jnp.bfloat16)
    return high, (values - high.astype(jnp.float32)).astype(jnp.bfloat16)


def at_edges():
    row, col = lax.axis_index("rows"), lax.axis_index("cols")
    return (
        row == 0,
        row == lax.axis_size("rows") - 1,
        col == 0,
        col == lax.axis_size("cols") - 1,
    )


def is_even():
    return lax.axis_index("rows") % 2 == 0


def beside_columns(field):
    width = field.shape[1]
    return pltpu.roll(field, 1, 1) + pltpu.roll(field, width - 1, 1)


def weights(inverse_variance, source_mask):
    return inverse_variance * (1.0 - source_mask.astype(jnp.float32))


def coefficients(m0, m1, m2, m3):
    alpha0 = m0 / m1
    norm1 = jnp.maximum(m0 - 2.0 * alpha0 * m1 + alpha0 * alpha0 * m2, 0.0)
    grown = 1.0 + norm1 / m0
    image1 = grown * grown * m1 - 2.0 * grown * alpha0 * m2 + alpha0 * alpha0 * m3
    alpha1 = jnp.where(image1 > 0.0, norm1 / image1, 0.0)
    return alpha0 + alpha1 * grown, -alpha1 * alpha0


def wide_kernel(f_ref, w_ref, near_ref, far_ref):
    rows = f_ref.shape[0]

    def write(out_ref, begin):
        out_ref[pl.ds(0, REACH), :] = f_ref[pl.ds(begin, REACH), :]
        out_ref[pl.ds(REACH, REACH), :] = w_ref[pl.ds(begin, REACH), :]

    def near_product(begin):
        near_ref[pl.ds(2 * REACH, 8), :] = f_ref[pl.ds(begin, 8), :] * w_ref[pl.ds(begin, 8), :]

    @pl.when(is_even())
    def _():
        write(near_ref, rows - REACH)
        near_product(rows - WIDE)
        write(far_ref, 0)

    @pl.when(jnp.logical_not(is_even()))
    def _():
        write(near_ref, 0)
        near_product(REACH)
        write(far_ref, rows - REACH)


def moments_kernel(f_ref, w_ref, narrow_ref, near_ref, out_ref, v1_out_ref, v0_ref, v1_ref, edge_ref):
    rows, cols = f_ref.shape
    width = cols + LANES
    first_row, last_row, _, _ = at_edges()
    even = is_even()
    own, pad = pl.ds(0, cols), pl.ds(cols, LANES)

    above, below = near_ref[pl.ds(2 * REACH - 8, 8), :], near_ref[pl.ds(REACH, 8), :]
    nothing = jnp.zeros((6, cols), jnp.float32)
    nearest, second, far_weight = (narrow_ref[pl.ds(k, 1), :] for k in range(3))
    far_above = jnp.concatenate([nothing, second, nearest], axis=0)
    far_below = jnp.concatenate([nearest, second, nothing], axis=0)
    top = jnp.where(even, far_above, near_ref[pl.ds(REACH - 8, 8), :] * above)
    bottom = jnp.where(even, near_ref[pl.ds(0, 8), :] * below, far_below)
    top_weight = jnp.where(even, far_weight, above[7:])
    bottom_weight = jnp.where(even, below[:1], far_weight)

    for ref in (v0_ref, v1_ref):
        ref[:, pad] = jnp.zeros((rows + 2 * NEAR, LANES), jnp.float32)
    for start in (0, NEAR + rows):
        v1_ref[pl.ds(start, 8), own] = jnp.zeros((8, cols), jnp.float32)
    v0_ref[pl.ds(0, 8), own] = top
    v0_ref[pl.ds(NEAR + rows, 8), own] = bottom
    for start in range(0, rows, 8):
        at = pl.ds(start, 8)
        v0_ref[pl.ds(NEAR + start, 8), own] = f_ref[at, :] * w_ref[at, :]

    def image(ref, weight, start, count):
        here = ref[pl.ds(start, count), :]
        beside = ref[pl.ds(start - 1, count), own] + ref[pl.ds(start + 1, count), own] + beside_columns(here)[:, :cols]
        here = here[:, :cols]
        return here, weight * here + smooth_weight * (4.0 * here - beside)

    for start in range(0, rows, 8):
        _, out = image(v0_ref, w_ref[pl.ds(start, 8), :], NEAR + start, 8)
        v1_ref[pl.ds(NEAR + start, 8), own] = out
        v1_out_ref[pl.ds(start, 8), :] = out

    def edge_row(weight, at):
        _, out = image(v0_ref, weight, at, 1)
        v1_ref[pl.ds(at, 1), own] = out

    pl.when(jnp.logical_not(first_row))(lambda: edge_row(top_weight, NEAR - 1))
    pl.when(jnp.logical_not(last_row))(lambda: edge_row(bottom_weight, NEAR + rows))

    lane = lax.broadcasted_iota(jnp.int32, (8, LANES), 1)
    sums = [jnp.zeros((8, cols), jnp.float32) for _ in range(4)]
    for start in range(0, rows, 8):
        weight = w_ref[pl.ds(start, 8), :]
        v0 = v0_ref[pl.ds(NEAR + start, 8), own]
        v1, v2 = image(v1_ref, weight, NEAR + start, 8)
        sums = [total + term for total, term in zip(sums, (v0 * v0, v0 * v1, v1 * v1, v1 * v2))]
        edges = jnp.zeros((8, LANES), jnp.float32)
        for k, field in enumerate((v0, v1, v2, weight)):
            edges = jnp.where(lane == k, pltpu.roll(field[:, cols - LANES :], k + 1, 1), edges)
            edges = jnp.where(lane == 4 + k, pltpu.roll(field[:, :LANES], 4 + k, 1), edges)
        edge_ref[pl.ds(start, 8), :] = edges

    result = jnp.zeros((1, LANES), jnp.float32)
    for i, total in enumerate(sums):
        narrow = sum(total[:, k : k + LANES] for k in range(0, cols, LANES))
        total = jnp.sum(jnp.sum(narrow, axis=0, keepdims=True), axis=1, keepdims=True)
        result = jnp.where(lane[:1] == i, total, result)
    vectors = edge_ref[...].T
    message = [result] + [vectors[k : k + 1, :] for k in range(VECTORS)]
    copies = jnp.concatenate(message * 8, axis=0)
    for start in range(0, out_ref.shape[0], copies.shape[0]):
        out_ref[pl.ds(start, copies.shape[0]), :] = copies


def coupled(parts_ref, nrows, ncols):
    count = nrows * ncols
    lam = smooth_weight

    def part(k):
        return parts_ref[:, :, pl.ds(k * LANES, LANES)].reshape(count, LANES)

    device = lax.broadcasted_iota(jnp.int32, (count, LANES), 0)
    lane = lax.broadcasted_iota(jnp.int32, (count, LANES), 1)
    joined = device % ncols < ncols - 1
    a0, a1, ua, wa = (jnp.where(joined, part(1 + k), 0.0) for k in range(4))
    b0, b1, ub, wb = (jnp.where(joined, pltpu.roll(part(5 + k), count - 1, 0), 0.0) for k in range(4))

    def next_row(field):
        inside = pltpu.roll(field, LANES - 1, 1)
        beyond = jnp.where(device < count - ncols, pltpu.roll(inside, count - ncols, 0), 0.0)
        return jnp.where(lane == LANES - 1, beyond, inside)

    def total(field):
        return jnp.sum(jnp.sum(field, axis=0, keepdims=True), axis=1, keepdims=True)

    scalars = jnp.sum(part(0), axis=0, keepdims=True)
    m0, m1, m2, m3 = (total(jnp.where(lane[:1] == i, scalars, 0.0)) for i in range(4))
    m1 = m1 - 2.0 * lam * total(a0 * b0)
    m2 = m2 + total(lam * lam * (a0 * a0 + b0 * b0) - 2.0 * lam * (a1 * b0 + b1 * a0))
    m3 = m3 + total(
        lam * lam * ((wa + 4.0 * lam) * b0 * b0 + (wb + 4.0 * lam) * a0 * a0)
        - 2.0 * lam * (b0 * ua + a0 * ub + (a1 - lam * b0) * (b1 - lam * a0))
        - 2.0 * lam * lam * lam * (a0 * next_row(a0) + b0 * next_row(b0))
    )
    return m0, m1, m2, m3


def neighbours(parts_ref, nrows, ncols):
    row, col = lax.axis_index("rows"), lax.axis_index("cols")
    even = is_even()
    towards = jnp.where(even, 1, -1)
    lane = lax.broadcasted_iota(jnp.int32, (LANES, LANES), 1)
    vectors = []
    for vector, step_col in ((1, -1), (5, 1)):
        for step_row in (0, towards, -towards):
            r, c = row + step_row, col + step_col
            there = (r >= 0) & (r < nrows) & (c >= 0) & (c < ncols)
            index = jnp.where(there, r * ncols + c, 0)
            found = parts_ref[index, :, pl.ds(vector * LANES, LANES)]
            vectors.append(jnp.where(there, found, 0.0))
    vectors.append(jnp.zeros((LANES - len(vectors), LANES), jnp.float32))
    columns = jnp.concatenate(vectors, axis=0).T
    sides = []
    for begin, target in ((0, 0), (3, LANES - 1)):
        own, near, far = (
            jnp.where(lane == target, pltpu.roll(columns, (target - begin - k) % LANES, 1), 0.0) for k in range(3)
        )
        near = jnp.where(even, near[:REACH], near[LANES - REACH :])
        far = jnp.where(even, far[LANES - REACH :], far[:REACH])
        sides.append(jnp.concatenate([own, near, far], axis=0))
    return sides


def fields_kernel(f_ref, w_ref, narrow_ref, near_ref, far_ref, near_v1_ref, far_v1_ref, v0_ref):
    rows, cols = f_ref.shape
    own, pad = pl.ds(0, cols), pl.ds(cols, LANES)
    even = is_even()
    top = f_ref[pl.ds(0, 1), :] * w_ref[pl.ds(0, 1), :]
    bottom = f_ref[pl.ds(rows - 1, 1), :] * w_ref[pl.ds(rows - 1, 1), :]
    beyond_near = jnp.where(even, near_ref[pl.ds(2 * REACH, 1), :], near_ref[pl.ds(2 * REACH + 7, 1), :])
    beyond_far = narrow_ref[pl.ds(3, 1), :]
    v0_ref[:, pad] = jnp.zeros((REACH + 2 * NEAR, LANES), jnp.float32)
    guards = (
        (near_ref, near_v1_ref, jnp.where(even, bottom, beyond_near), jnp.where(even, beyond_near, top)),
        (far_ref, far_v1_ref, jnp.where(even, beyond_far, bottom), jnp.where(even, top, beyond_far)),
    )
    for halo_ref, v1_ref, above, below in guards:
        v0_ref[pl.ds(NEAR - 1, 1), own] = above
        v0_ref[pl.ds(NEAR + REACH, 1), own] = below
        for start in range(0, REACH, 8):
            v0_ref[pl.ds(NEAR + start, 8), own] = halo_ref[pl.ds(start, 8), :] * halo_ref[pl.ds(REACH + start, 8), :]
        for start in range(0, REACH, 8):
            at = NEAR + start
            here = v0_ref[pl.ds(at, 8), :]
            beside = v0_ref[pl.ds(at - 1, 8), own] + v0_ref[pl.ds(at + 1, 8), own] + beside_columns(here)[:, :cols]
            here = here[:, :cols]
            v1_ref[pl.ds(start, 8), :] = halo_ref[pl.ds(REACH + start, 8), :] * here + smooth_weight * (4.0 * here - beside)


def regions(f_ref, w_ref, v1_ref, near_ref, near_v1_ref, far_ref, far_v1_ref, step):
    for start in range(0, f_ref.shape[0], step):
        yield start, (f_ref, start), (w_ref, start), (v1_ref, start)
    for base, halo_ref, field_ref in ((f_ref.shape[0], near_ref, near_v1_ref), (f_ref.shape[0] + REACH, far_ref, far_v1_ref)):
        for start in range(0, REACH, step):
            yield base + start, (halo_ref, start), (halo_ref, REACH + start), (field_ref, start)


def dot(left, right):
    return jnp.dot(left, right, preferred_element_type=jnp.float32)


def row_pass(rowtaps_ref, high, low, rows):
    first_row, last_row, _, _ = at_edges()
    kind = jnp.where(is_even(), first_row.astype(jnp.int32), 2 + last_row.astype(jnp.int32))
    table = rowtaps_ref[kind]
    both = dot(table, high)
    return both[:rows] + (both[rows:] + dot(table[:rows], low))


def edges_kernel(
    nrows, ncols, parts_ref, f_ref, w_ref, v1_ref, near_ref, near_v1_ref, far_ref, far_v1_ref, rowtaps_ref,
    coefficients_ref, left_ref, right_ref, first_ref, last_ref, high_ref, low_ref,
):
    rows, cols = f_ref.shape
    c0, c1 = coefficients(*coupled(parts_ref, nrows, ncols))
    coefficients_ref[pl.ds(0, 8), :] = jnp.broadcast_to(c0, (8, LANES))
    coefficients_ref[pl.ds(8, 8), :] = jnp.broadcast_to(c1, (8, LANES))
    sides = neighbours(parts_ref, nrows, ncols)
    left_ref[...], right_ref[...] = sides

    step = 16
    fields = (f_ref, w_ref, v1_ref, near_ref, near_v1_ref, far_ref, far_v1_ref)
    for side, begin in enumerate((0, cols - LANES)):
        at_cols = pl.ds(begin, LANES)
        for start, *sources in regions(*fields, step):
            flux, weight, v1 = (ref[pl.ds(row, step), at_cols] for ref, row in sources)
            v1 = v1 - smooth_weight * sides[side][start : start + step]
            scatter = flux - (c0 * (flux * weight) + c1 * v1)
            high, low = split_values(scatter * scatter)
            high_ref[pl.ds(start, step), pl.ds(side * LANES, LANES)] = high
            low_ref[pl.ds(start, step), pl.ds(side * LANES, LANES)] = low
    passed = row_pass(rowtaps_ref, high_ref[...], low_ref[...], rows)
    upper, lower = slice(0, rows // 2), slice(rows // 2, rows)
    first, last = passed[:, :LANES], passed[:, LANES:]
    on_left = lax.broadcasted_iota(jnp.int32, (rows // 2, LANES), 1) < REACH
    first_ref[...] = jnp.where(on_left, first[upper], pltpu.roll(first[lower], REACH, 1))
    last_ref[...] = jnp.where(on_left, pltpu.roll(last[upper], REACH, 1), last[lower])


def main_kernel(
    coefficients_ref, left_ref, right_ref, f_ref, w_ref, v1_ref, near_ref, near_v1_ref, far_ref, far_v1_ref, rowtaps_ref, coltaps_ref,
    background_ref, rms_ref, sides_ref, high_ref, low_ref,
):
    rows, cols = f_ref.shape
    c0, c1 = coefficients_ref[pl.ds(0, 1), pl.ds(0, 1)], coefficients_ref[pl.ds(8, 1), pl.ds(0, 1)]
    step = 16
    fields = (f_ref, w_ref, v1_ref, near_ref, near_v1_ref, far_ref, far_v1_ref)
    for start, *sources in regions(*fields, step):
        flux, weight, v1 = (ref[pl.ds(row, step), :] for ref, row in sources)
        at = pl.ds(start, step)
        v1 = jnp.concatenate(
            [
                v1[:, :LANES] - smooth_weight * left_ref[at, :],
                v1[:, LANES : cols - LANES],
                v1[:, cols - LANES :] - smooth_weight * right_ref[at, :],
            ],
            axis=1,
        )
        background = c0 * (flux * weight) + c1 * v1
        if start < rows:
            background_ref[at, :] = background
        scatter = flux - background
        high_ref[at, :], low_ref[at, :] = split_values(scatter * scatter)
    passed = row_pass(rowtaps_ref, high_ref[...], low_ref[...], rows)
    sides_ref[:, pl.ds(0, 2 * LANES)] = passed[:, : 2 * LANES]
    sides_ref[:, pl.ds(2 * LANES, 2 * LANES)] = passed[:, cols - 2 * LANES :]
    high, low = split_values(pltpu.roll(passed, REACH, 1))
    for j in range(1, cols // LANES - 1):
        at = slice(j * LANES, j * LANES + 2 * LANES)
        rms_ref[:, pl.ds(j * LANES, LANES)] = column_pass(coltaps_ref[0], high[:, at], low[:, at])


def column_pass(table, high, low):
    both = dot(high, table)
    smoothed = both[:, :LANES] + (both[:, LANES:] + dot(low, table[:, :LANES]))
    return jnp.sqrt(smoothed + 1e-06)


def final_kernel(rms_in_ref, sides_ref, left_ref, right_ref, coltaps_ref, rms_ref, blocks_ref, sems):
    rows, cols = rms_ref.shape
    del rms_in_ref
    _, _, first_col, last_col = at_edges()
    left, right = left_ref[...], right_ref[...]
    left = jnp.concatenate([pltpu.roll(left, REACH, 1), left], axis=0)
    right = jnp.concatenate([right, pltpu.roll(right, REACH, 1)], axis=0)
    sides = sides_ref[...]
    windows = (
        pltpu.roll(jnp.concatenate([left, sides[:, : 2 * LANES]], axis=1), 3 * LANES - REACH, 1)[:, : 2 * LANES],
        pltpu.roll(jnp.concatenate([sides[:, 2 * LANES :], right], axis=1), 3 * LANES - REACH, 1)[:, : 2 * LANES],
    )
    copies = []
    for side, which in enumerate((first_col.astype(jnp.int32), 2 * last_col.astype(jnp.int32))):
        high, low = split_values(windows[side])
        blocks_ref[side] = column_pass(coltaps_ref[which], high, low)
        target = rms_ref.at[:, pl.ds(side * (cols - LANES), LANES)]
        copies.append(pltpu.make_async_copy(blocks_ref.at[side], target, sems.at[side]))
        copies[-1].start()
    for copy in copies:
        copy.wait()


def shift(block, axis, step):
    count = lax.axis_size(axis)
    pairs = [(i, i + step) for i in range(count) if 0 <= i + step < count]
    return lax.ppermute(block, axis, pairs)


def swap(block, axis, first):
    count = lax.axis_size(axis)
    pairs = [(i, i + 1) for i in range(first, count - 1, 2)]
    return lax.ppermute(block, axis, pairs + [(j, i) for i, j in pairs])


def call(kernel, name, outs, scratch=(), limit=16, in_place=False):
    vmem = pl.BlockSpec(memory_space=pltpu.VMEM)
    there = pl.BlockSpec(memory_space=pl.ANY)

    def run(*args):
        return pl.pallas_call(
            kernel,
            out_shape=tuple(jax.ShapeDtypeStruct(shape, jnp.float32) for shape in outs),
            in_specs=[there if in_place and i == 0 else vmem for i in range(len(args))],
            out_specs=(there if in_place else vmem,) * len(outs),
            scratch_shapes=list(scratch),
            input_output_aliases={0: 0} if in_place else {},
            compiler_params=pltpu.CompilerParams(vmem_limit_bytes=limit << 20),
            name=name,
        )(*args)

    return run


def shards(coadd_flux, inverse_variance, source_mask):
    rows, cols = coadd_flux.shape
    nrows, ncols = lax.axis_size("rows"), lax.axis_size("cols")
    message = (VECTORS + 1) * LANES

    def scratch(*shape, dtype=jnp.float32):
        return pltpu.VMEM(shape, dtype)

    taken = []
    for above, below in ((0, rows - 1), (1, rows - 2), (REACH, rows - 1 - REACH)):
        start = (jnp.where(is_even(), above, below), 0)
        flux, variance, mask = (
            lax.dynamic_slice(x, start, (1, cols)) for x in (coadd_flux, inverse_variance, source_mask)
        )
        taken.append((flux, weights(variance, mask)))
    products = [flux * weight for flux, weight in taken]
    narrow = swap(jnp.concatenate([products[0], products[1], taken[0][1], products[2]]), "rows", 1)

    own = (coadd_flux, weights(inverse_variance, source_mask))
    to_near, to_far = call(wide_kernel, "wide", ((2 * REACH + 8, cols), (2 * REACH, cols)))(*own)
    to_near, to_far, narrow = lax.optimization_barrier((to_near, to_far, narrow))
    near = swap(to_near, "rows", 0)
    far = swap(to_far, "rows", 1)

    field = scratch(rows + 2 * NEAR, cols + LANES)
    devices = nrows * ncols
    parts, own_v1 = call(
        moments_kernel,
        "moments",
        ((devices * (VECTORS + 1), LANES), (rows, cols)),
        (field, field, scratch(rows, LANES)),
    )(*own, narrow, near)
    parts = lax.all_to_all(parts.reshape(devices, 1, message), ("rows", "cols"), 0, 0, tiled=True)
    near_v1, far_v1 = call(
        fields_kernel, "fields", ((REACH, cols), (REACH, cols)), (scratch(REACH + 2 * NEAR, cols + LANES),)
    )(*own, narrow, near, far)

    row_taps, col_taps = jnp.asarray(row_tables(rows)), jnp.asarray(col_tables())
    fields = (*own, own_v1, near, near_v1, far, far_v1)
    reached, packed = rows + 2 * REACH, (rows // 2, LANES)
    numbers, left, right, first, last = call(
        functools.partial(edges_kernel, nrows, ncols),
        "edges",
        ((16, LANES), (reached, LANES), (reached, LANES), packed, packed),
        (scratch(reached, 2 * LANES, dtype=jnp.bfloat16),) * 2,
    )(parts, *fields, row_taps)
    from_left = shift(last, "cols", 1)
    from_right = shift(first, "cols", -1)
    background, rms, sides = call(
        main_kernel,
        "main",
        ((rows, cols), (rows, cols), (rows, 4 * LANES)),
        (scratch(reached, cols, dtype=jnp.bfloat16),) * 2,
        32,
    )(numbers, left, right, *fields, row_taps, col_taps)
    (rms,) = call(
        final_kernel, "final", ((rows, cols),), (scratch(2, rows, LANES), pltpu.SemaphoreType.DMA((2,))), in_place=True
    )(rms, sides, from_left, from_right, col_taps)
    return background, rms


def solution(mesh):
    return jax.shard_map(
        shards,
        mesh=mesh,
        in_specs=(P("rows", "cols"), P("rows", "cols"), P("rows", "cols")),
        out_specs=(P("rows", "cols"), P("rows", "cols")),
        check_vma=False,
    )
```

```python
import functools

import jax
import jax.numpy as jnp
import ml_dtypes
import numpy as np
from jax import lax
from jax.experimental import pallas as pl
from jax.experimental.pallas import tpu as pltpu
from jax.sharding import PartitionSpec as P

RADIUS = 32
REACH = 2 * RADIUS
LANES = 128
WIDE = REACH + 8
NEAR = 8
VECTORS = 8

smooth_weight = 2.0
blur_sigma = 10.0


def squared_taps(length, first, last):
    offsets = np.arange(2 * RADIUS + 1) - RADIUS
    taps = np.exp(-offsets * offsets / (2.0 * blur_sigma * blur_sigma))
    taps = taps / taps.sum()

    def band(count):
        table = np.zeros((count, count + 2 * RADIUS))
        for k in range(2 * RADIUS + 1):
            table[np.arange(count), np.arange(count) + k] = taps[k]
        return table

    inner = band(length + 2 * RADIUS)
    if first:
        inner[:RADIUS] = 0.0
    if last:
        inner[-RADIUS:] = 0.0
    return band(length) @ inner


def split(table):
    high = table.astype(np.float32).astype(ml_dtypes.bfloat16)
    low = (table - high.astype(np.float64)).astype(np.float32).astype(ml_dtypes.bfloat16)
    return high, low


def row_tables(length):
    tables = []
    for first, last, odd in ((False, False, False), (True, False, False), (False, False, True), (False, True, True)):
        table = squared_taps(length, first, last)
        above, own, below = table[:, :REACH], table[:, REACH : REACH + length], table[:, REACH + length :]
        near, far = (above, below) if odd else (below, above)
        if first or last:
            far = np.zeros_like(far)
        tables.append(np.concatenate(split(np.concatenate([own, near, far], axis=1)), axis=0))
    return np.stack(tables)


def col_tables():
    tables = []
    for first, last in ((False, False), (True, False), (False, True)):
        tables.append(np.concatenate(split(squared_taps(LANES, first, last).T), axis=1))
    return np.stack(tables)


def split_values(values):
    high = values.astype(jnp.bfloat16)
    return high, (values - high.astype(jnp.float32)).astype(jnp.bfloat16)


def at_edges():
    row, col = lax.axis_index("rows"), lax.axis_index("cols")
    return (
        row == 0,
        row == lax.axis_size("rows") - 1,
        col == 0,
        col == lax.axis_size("cols") - 1,
    )


def is_even():
    return lax.axis_index("rows") % 2 == 0


def beside_columns(field):
    width = field.shape[1]
    return pltpu.roll(field, 1, 1) + pltpu.roll(field, width - 1, 1)


def weights(inverse_variance, source_mask):
    return inverse_variance * (1.0 - source_mask.astype(jnp.float32))


def coefficients(m0, m1, m2, m3):
    alpha0 = m0 / m1
    norm1 = jnp.maximum(m0 - 2.0 * alpha0 * m1 + alpha0 * alpha0 * m2, 0.0)
    grown = 1.0 + norm1 / m0
    image1 = grown * grown * m1 - 2.0 * grown * alpha0 * m2 + alpha0 * alpha0 * m3
    alpha1 = jnp.where(image1 > 0.0, norm1 / image1, 0.0)
    return alpha0 + alpha1 * grown, -alpha1 * alpha0


def wide_kernel(f_ref, w_ref, near_ref, far_ref):
    rows = f_ref.shape[0]

    def write(out_ref, begin):
        out_ref[pl.ds(0, REACH), :] = f_ref[pl.ds(begin, REACH), :]
        out_ref[pl.ds(REACH, REACH), :] = w_ref[pl.ds(begin, REACH), :]

    def near_product(begin):
        near_ref[pl.ds(2 * REACH, 8), :] = f_ref[pl.ds(begin, 8), :] * w_ref[pl.ds(begin, 8), :]

    @pl.when(is_even())
    def _():
        write(near_ref, rows - REACH)
        near_product(rows - WIDE)
        write(far_ref, 0)

    @pl.when(jnp.logical_not(is_even()))
    def _():
        write(near_ref, 0)
        near_product(REACH)
        write(far_ref, rows - REACH)


def moments_kernel(f_ref, w_ref, narrow_ref, near_ref, out_ref, v1_out_ref, v0_ref, v1_ref, edge_ref):
    rows, cols = f_ref.shape
    width = cols + LANES
    first_row, last_row, _, _ = at_edges()
    even = is_even()
    own, pad = pl.ds(0, cols), pl.ds(cols, LANES)

    above, below = near_ref[pl.ds(2 * REACH - 8, 8), :], near_ref[pl.ds(REACH, 8), :]
    nothing = jnp.zeros((6, cols), jnp.float32)
    nearest, second, far_weight = (narrow_ref[pl.ds(k, 1), :] for k in range(3))
    far_above = jnp.concatenate([nothing, second, nearest], axis=0)
    far_below = jnp.concatenate([nearest, second, nothing], axis=0)
    top = jnp.where(even, far_above, near_ref[pl.ds(REACH - 8, 8), :] * above)
    bottom = jnp.where(even, near_ref[pl.ds(0, 8), :] * below, far_below)
    top_weight = jnp.where(even, far_weight, above[7:])
    bottom_weight = jnp.where(even, below[:1], far_weight)

    for ref in (v0_ref, v1_ref):
        ref[:, pad] = jnp.zeros((rows + 2 * NEAR, LANES), jnp.float32)
    for start in (0, NEAR + rows):
        v1_ref[pl.ds(start, 8), own] = jnp.zeros((8, cols), jnp.float32)
    v0_ref[pl.ds(0, 8), own] = top
    v0_ref[pl.ds(NEAR + rows, 8), own] = bottom
    for start in range(0, rows, 8):
        at = pl.ds(start, 8)
        v0_ref[pl.ds(NEAR + start, 8), own] = f_ref[at, :] * w_ref[at, :]

    def image(ref, weight, start, count):
        here = ref[pl.ds(start, count), :]
        beside = ref[pl.ds(start - 1, count), own] + ref[pl.ds(start + 1, count), own] + beside_columns(here)[:, :cols]
        here = here[:, :cols]
        return here, weight * here + smooth_weight * (4.0 * here - beside)

    for start in range(0, rows, 8):
        _, out = image(v0_ref, w_ref[pl.ds(start, 8), :], NEAR + start, 8)
        v1_ref[pl.ds(NEAR + start, 8), own] = out
        v1_out_ref[pl.ds(start, 8), :] = out

    def edge_row(weight, at):
        _, out = image(v0_ref, weight, at, 1)
        v1_ref[pl.ds(at, 1), own] = out

    pl.when(jnp.logical_not(first_row))(lambda: edge_row(top_weight, NEAR - 1))
    pl.when(jnp.logical_not(last_row))(lambda: edge_row(bottom_weight, NEAR + rows))

    lane = lax.broadcasted_iota(jnp.int32, (8, LANES), 1)
    sums = [jnp.zeros((8, cols), jnp.float32) for _ in range(4)]
    for start in range(0, rows, 8):
        weight = w_ref[pl.ds(start, 8), :]
        v0 = v0_ref[pl.ds(NEAR + start, 8), own]
        v1, v2 = image(v1_ref, weight, NEAR + start, 8)
        sums = [total + term for total, term in zip(sums, (v0 * v0, v0 * v1, v1 * v1, v1 * v2))]
        edges = jnp.zeros((8, LANES), jnp.float32)
        for k, field in enumerate((v0, v1, v2, weight)):
            edges = jnp.where(lane == k, pltpu.roll(field[:, cols - LANES :], k + 1, 1), edges)
            edges = jnp.where(lane == 4 + k, pltpu.roll(field[:, :LANES], 4 + k, 1), edges)
        edge_ref[pl.ds(start, 8), :] = edges

    result = jnp.zeros((1, LANES), jnp.float32)
    for i, total in enumerate(sums):
        narrow = sum(total[:, k : k + LANES] for k in range(0, cols, LANES))
        total = jnp.sum(jnp.sum(narrow, axis=0, keepdims=True), axis=1, keepdims=True)
        result = jnp.where(lane[:1] == i, total, result)
    vectors = edge_ref[...].T
    message = [result] + [vectors[k : k + 1, :] for k in range(VECTORS)]
    copies = jnp.concatenate(message * 8, axis=0)
    for start in range(0, out_ref.shape[0], copies.shape[0]):
        out_ref[pl.ds(start, copies.shape[0]), :] = copies


def coupled(parts_ref, nrows, ncols):
    count = nrows * ncols
    lam = smooth_weight

    def part(k):
        return parts_ref[:, :, pl.ds(k * LANES, LANES)].reshape(count, LANES)

    device = lax.broadcasted_iota(jnp.int32, (count, LANES), 0)
    lane = lax.broadcasted_iota(jnp.int32, (count, LANES), 1)
    joined = device % ncols < ncols - 1
    a0, a1, ua, wa = (jnp.where(joined, part(1 + k), 0.0) for k in range(4))
    b0, b1, ub, wb = (jnp.where(joined, pltpu.roll(part(5 + k), count - 1, 0), 0.0) for k in range(4))

    def next_row(field):
        inside = pltpu.roll(field, LANES - 1, 1)
        beyond = jnp.where(device < count - ncols, pltpu.roll(inside, count - ncols, 0), 0.0)
        return jnp.where(lane == LANES - 1, beyond, inside)

    def total(field):
        return jnp.sum(jnp.sum(field, axis=0, keepdims=True), axis=1, keepdims=True)

    scalars = jnp.sum(part(0), axis=0, keepdims=True)
    m0, m1, m2, m3 = (total(jnp.where(lane[:1] == i, scalars, 0.0)) for i in range(4))
    m1 = m1 - 2.0 * lam * total(a0 * b0)
    m2 = m2 + total(lam * lam * (a0 * a0 + b0 * b0) - 2.0 * lam * (a1 * b0 + b1 * a0))
    m3 = m3 + total(
        lam * lam * ((wa + 4.0 * lam) * b0 * b0 + (wb + 4.0 * lam) * a0 * a0)
        - 2.0 * lam * (b0 * ua + a0 * ub + (a1 - lam * b0) * (b1 - lam * a0))
        - 2.0 * lam * lam * lam * (a0 * next_row(a0) + b0 * next_row(b0))
    )
    return m0, m1, m2, m3


def neighbours(parts_ref, nrows, ncols):
    row, col = lax.axis_index("rows"), lax.axis_index("cols")
    even = is_even()
    towards = jnp.where(even, 1, -1)
    lane = lax.broadcasted_iota(jnp.int32, (LANES, LANES), 1)
    vectors = []
    for vector, step_col in ((1, -1), (5, 1)):
        for step_row in (0, towards, -towards):
            r, c = row + step_row, col + step_col
            there = (r >= 0) & (r < nrows) & (c >= 0) & (c < ncols)
            index = jnp.where(there, r * ncols + c, 0)
            found = parts_ref[index, :, pl.ds(vector * LANES, LANES)]
            vectors.append(jnp.where(there, found, 0.0))
    vectors.append(jnp.zeros((LANES - len(vectors), LANES), jnp.float32))
    columns = jnp.concatenate(vectors, axis=0).T
    sides = []
    for begin, target in ((0, 0), (3, LANES - 1)):
        own, near, far = (
            jnp.where(lane == target, pltpu.roll(columns, (target - begin - k) % LANES, 1), 0.0) for k in range(3)
        )
        near = jnp.where(even, near[:REACH], near[LANES - REACH :])
        far = jnp.where(even, far[LANES - REACH :], far[:REACH])
        sides.append(jnp.concatenate([own, near, far], axis=0))
    return sides


def fields_kernel(f_ref, w_ref, narrow_ref, near_ref, far_ref, near_v1_ref, far_v1_ref, v0_ref):
    rows, cols = f_ref.shape
    own, pad = pl.ds(0, cols), pl.ds(cols, LANES)
    even = is_even()
    top = f_ref[pl.ds(0, 1), :] * w_ref[pl.ds(0, 1), :]
    bottom = f_ref[pl.ds(rows - 1, 1), :] * w_ref[pl.ds(rows - 1, 1), :]
    beyond_near = jnp.where(even, near_ref[pl.ds(2 * REACH, 1), :], near_ref[pl.ds(2 * REACH + 7, 1), :])
    beyond_far = narrow_ref[pl.ds(3, 1), :]
    v0_ref[:, pad] = jnp.zeros((REACH + 2 * NEAR, LANES), jnp.float32)
    guards = (
        (near_ref, near_v1_ref, jnp.where(even, bottom, beyond_near), jnp.where(even, beyond_near, top)),
        (far_ref, far_v1_ref, jnp.where(even, beyond_far, bottom), jnp.where(even, top, beyond_far)),
    )
    for halo_ref, v1_ref, above, below in guards:
        v0_ref[pl.ds(NEAR - 1, 1), own] = above
        v0_ref[pl.ds(NEAR + REACH, 1), own] = below
        for start in range(0, REACH, 8):
            v0_ref[pl.ds(NEAR + start, 8), own] = halo_ref[pl.ds(start, 8), :] * halo_ref[pl.ds(REACH + start, 8), :]
        for start in range(0, REACH, 8):
            at = NEAR + start
            here = v0_ref[pl.ds(at, 8), :]
            beside = v0_ref[pl.ds(at - 1, 8), own] + v0_ref[pl.ds(at + 1, 8), own] + beside_columns(here)[:, :cols]
            here = here[:, :cols]
            v1_ref[pl.ds(start, 8), :] = halo_ref[pl.ds(REACH + start, 8), :] * here + smooth_weight * (4.0 * here - beside)


def regions(f_ref, w_ref, v1_ref, near_ref, near_v1_ref, far_ref, far_v1_ref, step):
    for start in range(0, f_ref.shape[0], step):
        yield start, (f_ref, start), (w_ref, start), (v1_ref, start)
    for base, halo_ref, field_ref in ((f_ref.shape[0], near_ref, near_v1_ref), (f_ref.shape[0] + REACH, far_ref, far_v1_ref)):
        for start in range(0, REACH, step):
            yield base + start, (halo_ref, start), (halo_ref, REACH + start), (field_ref, start)


def dot(left, right):
    return jnp.dot(left, right, preferred_element_type=jnp.float32)


def row_pass(rowtaps_ref, high, low, rows):
    first_row, last_row, _, _ = at_edges()
    kind = jnp.where(is_even(), first_row.astype(jnp.int32), 2 + last_row.astype(jnp.int32))
    table = rowtaps_ref[kind]
    both = dot(table, high)
    return both[:rows] + (both[rows:] + dot(table[:rows], low))


def edges_kernel(
    nrows, ncols, parts_ref, f_ref, w_ref, v1_ref, near_ref, near_v1_ref, far_ref, far_v1_ref, rowtaps_ref,
    coefficients_ref, left_ref, right_ref, first_ref, last_ref, high_ref, low_ref,
):
    rows, cols = f_ref.shape
    c0, c1 = coefficients(*coupled(parts_ref, nrows, ncols))
    coefficients_ref[pl.ds(0, 8), :] = jnp.broadcast_to(c0, (8, LANES))
    coefficients_ref[pl.ds(8, 8), :] = jnp.broadcast_to(c1, (8, LANES))
    sides = neighbours(parts_ref, nrows, ncols)
    left_ref[...], right_ref[...] = sides

    step = 16
    fields = (f_ref, w_ref, v1_ref, near_ref, near_v1_ref, far_ref, far_v1_ref)
    for side, begin in enumerate((0, cols - LANES)):
        at_cols = pl.ds(begin, LANES)
        for start, *sources in regions(*fields, step):
            flux, weight, v1 = (ref[pl.ds(row, step), at_cols] for ref, row in sources)
            v1 = v1 - smooth_weight * sides[side][start : start + step]
            scatter = flux - (c0 * (flux * weight) + c1 * v1)
            high, low = split_values(scatter * scatter)
            high_ref[pl.ds(start, step), pl.ds(side * LANES, LANES)] = high
            low_ref[pl.ds(start, step), pl.ds(side * LANES, LANES)] = low
    passed = row_pass(rowtaps_ref, high_ref[...], low_ref[...], rows)
    upper, lower = slice(0, rows // 2), slice(rows // 2, rows)
    first, last = passed[:, :LANES], passed[:, LANES:]
    on_left = lax.broadcasted_iota(jnp.int32, (rows // 2, LANES), 1) < REACH
    first_ref[...] = jnp.where(on_left, first[upper], pltpu.roll(first[lower], REACH, 1))
    last_ref[...] = jnp.where(on_left, pltpu.roll(last[upper], REACH, 1), last[lower])


def main_kernel(
    coefficients_ref, left_ref, right_ref, f_ref, w_ref, v1_ref, near_ref, near_v1_ref, far_ref, far_v1_ref, rowtaps_ref, coltaps_ref,
    background_ref, rms_ref, sides_ref, high_ref, low_ref,
):
    rows, cols = f_ref.shape
    c0, c1 = coefficients_ref[pl.ds(0, 1), pl.ds(0, 1)], coefficients_ref[pl.ds(8, 1), pl.ds(0, 1)]
    step = 16
    fields = (f_ref, w_ref, v1_ref, near_ref, near_v1_ref, far_ref, far_v1_ref)
    for start, *sources in regions(*fields, step):
        flux, weight, v1 = (ref[pl.ds(row, step), :] for ref, row in sources)
        at = pl.ds(start, step)
        v1 = jnp.concatenate(
            [
                v1[:, :LANES] - smooth_weight * left_ref[at, :],
                v1[:, LANES : cols - LANES],
                v1[:, cols - LANES :] - smooth_weight * right_ref[at, :],
            ],
            axis=1,
        )
        background = c0 * (flux * weight) + c1 * v1
        if start < rows:
            background_ref[at, :] = background
        scatter = flux - background
        high_ref[at, :], low_ref[at, :] = split_values(scatter * scatter)
    passed = row_pass(rowtaps_ref, high_ref[...], low_ref[...], rows)
    sides_ref[:, pl.ds(0, 2 * LANES)] = passed[:, : 2 * LANES]
    sides_ref[:, pl.ds(2 * LANES, 2 * LANES)] = passed[:, cols - 2 * LANES :]
    high, low = split_values(pltpu.roll(passed, REACH, 1))
    for j in range(1, cols // LANES - 1):
        at = slice(j * LANES, j * LANES + 2 * LANES)
        rms_ref[:, pl.ds(j * LANES, LANES)] = column_pass(coltaps_ref[0], high[:, at], low[:, at])


def column_pass(table, high, low):
    both = dot(high, table)
    smoothed = both[:, :LANES] + (both[:, LANES:] + dot(low, table[:, :LANES]))
    return jnp.sqrt(smoothed + 1e-06)


def final_kernel(rms_in_ref, sides_ref, left_ref, right_ref, coltaps_ref, rms_ref, blocks_ref, sems):
    rows, cols = rms_ref.shape
    del rms_in_ref
    _, _, first_col, last_col = at_edges()
    left, right = left_ref[...], right_ref[...]
    left = jnp.concatenate([pltpu.roll(left, REACH, 1), left], axis=0)
    right = jnp.concatenate([right, pltpu.roll(right, REACH, 1)], axis=0)
    sides = sides_ref[...]
    windows = (
        pltpu.roll(jnp.concatenate([left, sides[:, : 2 * LANES]], axis=1), 3 * LANES - REACH, 1)[:, : 2 * LANES],
        pltpu.roll(jnp.concatenate([sides[:, 2 * LANES :], right], axis=1), 3 * LANES - REACH, 1)[:, : 2 * LANES],
    )
    copies = []
    for side, which in enumerate((first_col.astype(jnp.int32), 2 * last_col.astype(jnp.int32))):
        high, low = split_values(windows[side])
        blocks_ref[side] = column_pass(coltaps_ref[which], high, low)
        target = rms_ref.at[:, pl.ds(side * (cols - LANES), LANES)]
        copies.append(pltpu.make_async_copy(blocks_ref.at[side], target, sems.at[side]))
        copies[-1].start()
    for copy in copies:
        copy.wait()


def shift(block, axis, step):
    count = lax.axis_size(axis)
    pairs = [(i, i + step) for i in range(count) if 0 <= i + step < count]
    return lax.ppermute(block, axis, pairs)


def swap(block, axis, first):
    count = lax.axis_size(axis)
    pairs = [(i, i + 1) for i in range(first, count - 1, 2)]
    return lax.ppermute(block, axis, pairs + [(j, i) for i, j in pairs])


def call(kernel, name, outs, scratch=(), limit=16, in_place=False, kept=()):
    vmem = pl.BlockSpec(memory_space=pltpu.VMEM)
    there = pl.BlockSpec(memory_space=pl.ANY)

    def run(*args):
        return pl.pallas_call(
            kernel,
            out_shape=tuple(
                pltpu.VMEM(shape, jnp.float32) if i in kept else jax.ShapeDtypeStruct(shape, jnp.float32)
                for i, shape in enumerate(outs)
            ),
            in_specs=[there if in_place and i == 0 else vmem for i in range(len(args))],
            out_specs=(there if in_place else vmem,) * len(outs),
            scratch_shapes=list(scratch),
            input_output_aliases={0: 0} if in_place else {},
            compiler_params=pltpu.CompilerParams(vmem_limit_bytes=limit << 20),
            name=name,
        )(*args)

    return run


def shards(coadd_flux, inverse_variance, source_mask):
    rows, cols = coadd_flux.shape
    nrows, ncols = lax.axis_size("rows"), lax.axis_size("cols")
    message = (VECTORS + 1) * LANES

    def scratch(*shape, dtype=jnp.float32):
        return pltpu.VMEM(shape, dtype)

    taken = []
    for above, below in ((0, rows - 1), (1, rows - 2), (REACH, rows - 1 - REACH)):
        start = (jnp.where(is_even(), above, below), 0)
        flux, variance, mask = (
            lax.dynamic_slice(x, start, (1, cols)) for x in (coadd_flux, inverse_variance, source_mask)
        )
        taken.append((flux, weights(variance, mask)))
    products = [flux * weight for flux, weight in taken]
    narrow = swap(jnp.concatenate([products[0], products[1], taken[0][1], products[2]]), "rows", 1)

    own = (coadd_flux, weights(inverse_variance, source_mask))
    to_near, to_far = call(wide_kernel, "wide", ((2 * REACH + 8, cols), (2 * REACH, cols)), kept=(0, 1))(*own)
    to_near, to_far, narrow = lax.optimization_barrier((to_near, to_far, narrow))
    near = swap(to_near, "rows", 0)
    far = swap(to_far, "rows", 1)

    field = scratch(rows + 2 * NEAR, cols + LANES)
    devices = nrows * ncols
    parts, own_v1 = call(
        moments_kernel,
        "moments",
        ((devices * (VECTORS + 1), LANES), (rows, cols)),
        (field, field, scratch(rows, LANES)),
        kept=(1,),
    )(*own, narrow, near)
    parts = lax.all_to_all(parts.reshape(devices, 1, message), ("rows", "cols"), 0, 0, tiled=True)
    parts = pltpu.with_memory_space_constraint(parts, pltpu.VMEM)
    near_v1, far_v1 = call(
        fields_kernel,
        "fields",
        ((REACH, cols), (REACH, cols)),
        (scratch(REACH + 2 * NEAR, cols + LANES),),
        kept=(0, 1),
    )(*own, narrow, near, far)

    row_taps, col_taps = jnp.asarray(row_tables(rows)), jnp.asarray(col_tables())
    fields = (*own, own_v1, near, near_v1, far, far_v1)
    reached, packed = rows + 2 * REACH, (rows // 2, LANES)
    numbers, left, right, first, last = call(
        functools.partial(edges_kernel, nrows, ncols),
        "edges",
        ((16, LANES), (reached, LANES), (reached, LANES), packed, packed),
        (scratch(reached, 2 * LANES, dtype=jnp.bfloat16),) * 2,
        kept=range(5),
    )(parts, *fields, row_taps)
    from_left = shift(last, "cols", 1)
    from_right = shift(first, "cols", -1)
    background, rms, sides = call(
        main_kernel,
        "main",
        ((rows, cols), (rows, cols), (rows, 4 * LANES)),
        (scratch(reached, cols, dtype=jnp.bfloat16),) * 2,
        kept=(2,),
    )(numbers, left, right, *fields, row_taps, col_taps)
    (rms,) = call(
        final_kernel, "final", ((rows, cols),), (scratch(2, rows, LANES), pltpu.SemaphoreType.DMA((2,))), in_place=True
    )(rms, sides, from_left, from_right, col_taps)
    return background, rms


def solution(mesh):
    return jax.shard_map(
        shards,
        mesh=mesh,
        in_specs=(P("rows", "cols"), P("rows", "cols"), P("rows", "cols")),
        out_specs=(P("rows", "cols"), P("rows", "cols")),
        check_vma=False,
    )
```

```python
import functools

import jax
import jax.numpy as jnp
import ml_dtypes
import numpy as np
from jax import lax
from jax.experimental import pallas as pl
from jax.experimental.pallas import tpu as pltpu
from jax.sharding import PartitionSpec as P

RADIUS = 32
REACH = 2 * RADIUS
LANES = 128
WIDE = REACH + 8
NEAR = 8
VECTORS = 8

smooth_weight = 2.0
blur_sigma = 10.0


def squared_taps(length, first, last):
    offsets = np.arange(2 * RADIUS + 1) - RADIUS
    taps = np.exp(-offsets * offsets / (2.0 * blur_sigma * blur_sigma))
    taps = taps / taps.sum()

    def band(count):
        table = np.zeros((count, count + 2 * RADIUS))
        for k in range(2 * RADIUS + 1):
            table[np.arange(count), np.arange(count) + k] = taps[k]
        return table

    inner = band(length + 2 * RADIUS)
    if first:
        inner[:RADIUS] = 0.0
    if last:
        inner[-RADIUS:] = 0.0
    return band(length) @ inner


def split(table):
    high = table.astype(np.float32).astype(ml_dtypes.bfloat16)
    low = (table - high.astype(np.float64)).astype(np.float32).astype(ml_dtypes.bfloat16)
    return high, low


def row_tables(length):
    tables = []
    for first, last, odd in ((False, False, False), (True, False, False), (False, False, True), (False, True, True)):
        table = squared_taps(length, first, last)
        above, own, below = table[:, :REACH], table[:, REACH : REACH + length], table[:, REACH + length :]
        near, far = (above, below) if odd else (below, above)
        if first or last:
            far = np.zeros_like(far)
        tables.append(np.concatenate(split(np.concatenate([own, near, far], axis=1)), axis=0))
    return np.stack(tables)


def col_tables():
    tables = []
    for first, last in ((False, False), (True, False), (False, True)):
        tables.append(np.concatenate(split(squared_taps(LANES, first, last).T), axis=1))
    return np.stack(tables)


def split_values(values):
    high = values.astype(jnp.bfloat16)
    return high, (values - high.astype(jnp.float32)).astype(jnp.bfloat16)


def at_edges():
    row, col = lax.axis_index("rows"), lax.axis_index("cols")
    return (
        row == 0,
        row == lax.axis_size("rows") - 1,
        col == 0,
        col == lax.axis_size("cols") - 1,
    )


def is_even():
    return lax.axis_index("rows") % 2 == 0


def beside_columns(field):
    width = field.shape[1]
    return pltpu.roll(field, 1, 1) + pltpu.roll(field, width - 1, 1)


def weights(inverse_variance, source_mask):
    return inverse_variance * (1.0 - source_mask.astype(jnp.float32))


def coefficients(m0, m1, m2, m3):
    alpha0 = m0 / m1
    norm1 = jnp.maximum(m0 - 2.0 * alpha0 * m1 + alpha0 * alpha0 * m2, 0.0)
    grown = 1.0 + norm1 / m0
    image1 = grown * grown * m1 - 2.0 * grown * alpha0 * m2 + alpha0 * alpha0 * m3
    alpha1 = jnp.where(image1 > 0.0, norm1 / image1, 0.0)
    return alpha0 + alpha1 * grown, -alpha1 * alpha0


def wide_kernel(f_ref, w_ref, near_ref, far_ref):
    rows = f_ref.shape[0]

    def write(out_ref, begin):
        out_ref[pl.ds(0, REACH), :] = f_ref[pl.ds(begin, REACH), :]
        out_ref[pl.ds(REACH, REACH), :] = w_ref[pl.ds(begin, REACH), :]

    def near_product(begin):
        near_ref[pl.ds(2 * REACH, 8), :] = f_ref[pl.ds(begin, 8), :] * w_ref[pl.ds(begin, 8), :]

    @pl.when(is_even())
    def _():
        write(near_ref, rows - REACH)
        near_product(rows - WIDE)
        write(far_ref, 0)

    @pl.when(jnp.logical_not(is_even()))
    def _():
        write(near_ref, 0)
        near_product(REACH)
        write(far_ref, rows - REACH)


def moments_kernel(f_ref, w_ref, narrow_ref, near_ref, out_ref, v1_out_ref, v0_ref, v1_ref, edge_ref):
    rows, cols = f_ref.shape
    width = cols + LANES
    first_row, last_row, _, _ = at_edges()
    even = is_even()
    own, pad = pl.ds(0, cols), pl.ds(cols, LANES)

    above, below = near_ref[pl.ds(2 * REACH - 8, 8), :], near_ref[pl.ds(REACH, 8), :]
    nothing = jnp.zeros((6, cols), jnp.float32)
    nearest, second, far_weight = (narrow_ref[pl.ds(k, 1), :] for k in range(3))
    far_above = jnp.concatenate([nothing, second, nearest], axis=0)
    far_below = jnp.concatenate([nearest, second, nothing], axis=0)
    top = jnp.where(even, far_above, near_ref[pl.ds(REACH - 8, 8), :] * above)
    bottom = jnp.where(even, near_ref[pl.ds(0, 8), :] * below, far_below)
    top_weight = jnp.where(even, far_weight, above[7:])
    bottom_weight = jnp.where(even, below[:1], far_weight)

    for ref in (v0_ref, v1_ref):
        ref[:, pad] = jnp.zeros((rows + 2 * NEAR, LANES), jnp.float32)
    for start in (0, NEAR + rows):
        v1_ref[pl.ds(start, 8), own] = jnp.zeros((8, cols), jnp.float32)
    v0_ref[pl.ds(0, 8), own] = top
    v0_ref[pl.ds(NEAR + rows, 8), own] = bottom
    for start in range(0, rows, 8):
        at = pl.ds(start, 8)
        v0_ref[pl.ds(NEAR + start, 8), own] = f_ref[at, :] * w_ref[at, :]

    def image(ref, weight, start, count):
        here = ref[pl.ds(start, count), :]
        beside = ref[pl.ds(start - 1, count), own] + ref[pl.ds(start + 1, count), own] + beside_columns(here)[:, :cols]
        here = here[:, :cols]
        return here, weight * here + smooth_weight * (4.0 * here - beside)

    for start in range(0, rows, 8):
        _, out = image(v0_ref, w_ref[pl.ds(start, 8), :], NEAR + start, 8)
        v1_ref[pl.ds(NEAR + start, 8), own] = out
        v1_out_ref[pl.ds(start, 8), :] = out

    def edge_row(weight, at):
        _, out = image(v0_ref, weight, at, 1)
        v1_ref[pl.ds(at, 1), own] = out

    pl.when(jnp.logical_not(first_row))(lambda: edge_row(top_weight, NEAR - 1))
    pl.when(jnp.logical_not(last_row))(lambda: edge_row(bottom_weight, NEAR + rows))

    lane = lax.broadcasted_iota(jnp.int32, (8, LANES), 1)
    sums = [jnp.zeros((8, cols), jnp.float32) for _ in range(4)]
    for start in range(0, rows, 8):
        weight = w_ref[pl.ds(start, 8), :]
        v0 = v0_ref[pl.ds(NEAR + start, 8), own]
        v1, v2 = image(v1_ref, weight, NEAR + start, 8)
        sums = [total + term for total, term in zip(sums, (v0 * v0, v0 * v1, v1 * v1, v1 * v2))]
        edges = jnp.zeros((8, LANES), jnp.float32)
        for k, field in enumerate((v0, v1, v2, weight)):
            edges = jnp.where(lane == k, pltpu.roll(field[:, cols - LANES :], k + 1, 1), edges)
            edges = jnp.where(lane == 4 + k, pltpu.roll(field[:, :LANES], 4 + k, 1), edges)
        edge_ref[pl.ds(start, 8), :] = edges

    result = jnp.zeros((1, LANES), jnp.float32)
    for i, total in enumerate(sums):
        narrow = sum(total[:, k : k + LANES] for k in range(0, cols, LANES))
        total = jnp.sum(jnp.sum(narrow, axis=0, keepdims=True), axis=1, keepdims=True)
        result = jnp.where(lane[:1] == i, total, result)
    vectors = edge_ref[...].T
    message = [result] + [vectors[k : k + 1, :] for k in range(VECTORS)]
    copies = jnp.concatenate(message * 8, axis=0)
    for start in range(0, out_ref.shape[0], copies.shape[0]):
        out_ref[pl.ds(start, copies.shape[0]), :] = copies


def coupled(parts_ref, nrows, ncols):
    count = nrows * ncols
    lam = smooth_weight

    def part(k):
        return parts_ref[:, :, pl.ds(k * LANES, LANES)].reshape(count, LANES)

    device = lax.broadcasted_iota(jnp.int32, (count, LANES), 0)
    lane = lax.broadcasted_iota(jnp.int32, (count, LANES), 1)
    joined = device % ncols < ncols - 1
    a0, a1, ua, wa = (jnp.where(joined, part(1 + k), 0.0) for k in range(4))
    b0, b1, ub, wb = (jnp.where(joined, pltpu.roll(part(5 + k), count - 1, 0), 0.0) for k in range(4))

    def next_row(field):
        inside = pltpu.roll(field, LANES - 1, 1)
        beyond = jnp.where(device < count - ncols, pltpu.roll(inside, count - ncols, 0), 0.0)
        return jnp.where(lane == LANES - 1, beyond, inside)

    def total(field):
        return jnp.sum(jnp.sum(field, axis=0, keepdims=True), axis=1, keepdims=True)

    scalars = jnp.sum(part(0), axis=0, keepdims=True)
    m0, m1, m2, m3 = (total(jnp.where(lane[:1] == i, scalars, 0.0)) for i in range(4))
    m1 = m1 - 2.0 * lam * total(a0 * b0)
    m2 = m2 + total(lam * lam * (a0 * a0 + b0 * b0) - 2.0 * lam * (a1 * b0 + b1 * a0))
    m3 = m3 + total(
        lam * lam * ((wa + 4.0 * lam) * b0 * b0 + (wb + 4.0 * lam) * a0 * a0)
        - 2.0 * lam * (b0 * ua + a0 * ub + (a1 - lam * b0) * (b1 - lam * a0))
        - 2.0 * lam * lam * lam * (a0 * next_row(a0) + b0 * next_row(b0))
    )
    return m0, m1, m2, m3


def neighbours(parts_ref, nrows, ncols):
    row, col = lax.axis_index("rows"), lax.axis_index("cols")
    even = is_even()
    towards = jnp.where(even, 1, -1)
    lane = lax.broadcasted_iota(jnp.int32, (LANES, LANES), 1)
    vectors = []
    for vector, step_col in ((1, -1), (5, 1)):
        for step_row in (0, towards, -towards):
            r, c = row + step_row, col + step_col
            there = (r >= 0) & (r < nrows) & (c >= 0) & (c < ncols)
            index = jnp.where(there, r * ncols + c, 0)
            found = parts_ref[index, :, pl.ds(vector * LANES, LANES)]
            vectors.append(jnp.where(there, found, 0.0))
    vectors.append(jnp.zeros((LANES - len(vectors), LANES), jnp.float32))
    columns = jnp.concatenate(vectors, axis=0).T
    sides = []
    for begin, target in ((0, 0), (3, LANES - 1)):
        own, near, far = (
            jnp.where(lane == target, pltpu.roll(columns, (target - begin - k) % LANES, 1), 0.0) for k in range(3)
        )
        near = jnp.where(even, near[:REACH], near[LANES - REACH :])
        far = jnp.where(even, far[LANES - REACH :], far[:REACH])
        sides.append(jnp.concatenate([own, near, far], axis=0))
    return sides


def halo_fields(f_ref, w_ref, narrow_ref, near_ref, far_ref, near_v1_ref, far_v1_ref, v0_ref):
    rows, cols = f_ref.shape
    own, pad = pl.ds(0, cols), pl.ds(cols, LANES)
    even = is_even()
    top = f_ref[pl.ds(0, 1), :] * w_ref[pl.ds(0, 1), :]
    bottom = f_ref[pl.ds(rows - 1, 1), :] * w_ref[pl.ds(rows - 1, 1), :]
    beyond_near = jnp.where(even, near_ref[pl.ds(2 * REACH, 1), :], near_ref[pl.ds(2 * REACH + 7, 1), :])
    beyond_far = narrow_ref[pl.ds(3, 1), :]
    v0_ref[:, pad] = jnp.zeros((REACH + 2 * NEAR, LANES), jnp.float32)
    guards = (
        (near_ref, near_v1_ref, jnp.where(even, bottom, beyond_near), jnp.where(even, beyond_near, top)),
        (far_ref, far_v1_ref, jnp.where(even, beyond_far, bottom), jnp.where(even, top, beyond_far)),
    )
    for halo_ref, v1_ref, above, below in guards:
        v0_ref[pl.ds(NEAR - 1, 1), own] = above
        v0_ref[pl.ds(NEAR + REACH, 1), own] = below
        for start in range(0, REACH, 8):
            v0_ref[pl.ds(NEAR + start, 8), own] = halo_ref[pl.ds(start, 8), :] * halo_ref[pl.ds(REACH + start, 8), :]
        for start in range(0, REACH, 8):
            at = NEAR + start
            here = v0_ref[pl.ds(at, 8), :]
            beside = v0_ref[pl.ds(at - 1, 8), own] + v0_ref[pl.ds(at + 1, 8), own] + beside_columns(here)[:, :cols]
            here = here[:, :cols]
            v1_ref[pl.ds(start, 8), :] = halo_ref[pl.ds(REACH + start, 8), :] * here + smooth_weight * (4.0 * here - beside)


def regions(f_ref, w_ref, v1_ref, near_ref, near_v1_ref, far_ref, far_v1_ref, step):
    for start in range(0, f_ref.shape[0], step):
        yield start, (f_ref, start), (w_ref, start), (v1_ref, start)
    for base, halo_ref, field_ref in ((f_ref.shape[0], near_ref, near_v1_ref), (f_ref.shape[0] + REACH, far_ref, far_v1_ref)):
        for start in range(0, REACH, step):
            yield base + start, (halo_ref, start), (halo_ref, REACH + start), (field_ref, start)


def dot(left, right):
    return jnp.dot(left, right, preferred_element_type=jnp.float32)


def row_pass(rowtaps_ref, high, low, rows):
    table = rowtaps_ref[...]
    both = dot(table, high)
    return both[:rows] + (both[rows:] + dot(table[:rows], low))


def edges_kernel(
    nrows, ncols, parts_ref, f_ref, w_ref, v1_ref, narrow_ref, near_ref, far_ref, rowtaps_ref,
    near_v1_ref, far_v1_ref, coefficients_ref, left_ref, right_ref, first_ref, last_ref, v0_ref, high_ref, low_ref,
):
    rows, cols = f_ref.shape
    halo_fields(f_ref, w_ref, narrow_ref, near_ref, far_ref, near_v1_ref, far_v1_ref, v0_ref)
    c0, c1 = coefficients(*coupled(parts_ref, nrows, ncols))
    coefficients_ref[pl.ds(0, 8), :] = jnp.broadcast_to(c0, (8, LANES))
    coefficients_ref[pl.ds(8, 8), :] = jnp.broadcast_to(c1, (8, LANES))
    sides = neighbours(parts_ref, nrows, ncols)
    left_ref[...], right_ref[...] = sides

    step = 16
    fields = (f_ref, w_ref, v1_ref, near_ref, near_v1_ref, far_ref, far_v1_ref)
    for side, begin in enumerate((0, cols - LANES)):
        at_cols = pl.ds(begin, LANES)
        for start, *sources in regions(*fields, step):
            flux, weight, v1 = (ref[pl.ds(row, step), at_cols] for ref, row in sources)
            v1 = v1 - smooth_weight * sides[side][start : start + step]
            scatter = flux - (c0 * (flux * weight) + c1 * v1)
            high, low = split_values(scatter * scatter)
            high_ref[pl.ds(start, step), pl.ds(side * LANES, LANES)] = high
            low_ref[pl.ds(start, step), pl.ds(side * LANES, LANES)] = low
    passed = row_pass(rowtaps_ref, high_ref[...], low_ref[...], rows)
    upper, lower = slice(0, rows // 2), slice(rows // 2, rows)
    first, last = passed[:, :LANES], passed[:, LANES:]
    on_left = lax.broadcasted_iota(jnp.int32, (rows // 2, LANES), 1) < REACH
    first_ref[...] = jnp.where(on_left, first[upper], pltpu.roll(first[lower], REACH, 1))
    last_ref[...] = jnp.where(on_left, pltpu.roll(last[upper], REACH, 1), last[lower])


def main_kernel(
    coefficients_ref, left_ref, right_ref, f_ref, w_ref, v1_ref, near_ref, near_v1_ref, far_ref, far_v1_ref, rowtaps_ref, coltaps_ref,
    background_ref, rms_ref, sides_ref, high_ref, low_ref,
):
    rows, cols = f_ref.shape
    c0, c1 = coefficients_ref[pl.ds(0, 1), pl.ds(0, 1)], coefficients_ref[pl.ds(8, 1), pl.ds(0, 1)]
    step = 16
    fields = (f_ref, w_ref, v1_ref, near_ref, near_v1_ref, far_ref, far_v1_ref)
    for start, *sources in regions(*fields, step):
        flux, weight, v1 = (ref[pl.ds(row, step), :] for ref, row in sources)
        at = pl.ds(start, step)
        v1 = jnp.concatenate(
            [
                v1[:, :LANES] - smooth_weight * left_ref[at, :],
                v1[:, LANES : cols - LANES],
                v1[:, cols - LANES :] - smooth_weight * right_ref[at, :],
            ],
            axis=1,
        )
        background = c0 * (flux * weight) + c1 * v1
        if start < rows:
            background_ref[at, :] = background
        scatter = flux - background
        high_ref[at, :], low_ref[at, :] = split_values(scatter * scatter)
    passed = row_pass(rowtaps_ref, high_ref[...], low_ref[...], rows)
    sides_ref[:, pl.ds(0, 2 * LANES)] = passed[:, : 2 * LANES]
    sides_ref[:, pl.ds(2 * LANES, 2 * LANES)] = passed[:, cols - 2 * LANES :]
    high, low = split_values(pltpu.roll(passed, REACH, 1))
    for j in range(1, cols // LANES - 1):
        at = slice(j * LANES, j * LANES + 2 * LANES)
        rms_ref[:, pl.ds(j * LANES, LANES)] = column_pass(coltaps_ref[0], high[:, at], low[:, at])


def column_pass(table, high, low):
    both = dot(high, table)
    smoothed = both[:, :LANES] + (both[:, LANES:] + dot(low, table[:, :LANES]))
    return jnp.sqrt(smoothed + 1e-06)


def final_kernel(rms_in_ref, sides_ref, left_ref, right_ref, coltaps_ref, rms_ref, blocks_ref, sems):
    rows, cols = rms_ref.shape
    del rms_in_ref
    _, _, first_col, last_col = at_edges()
    left, right = left_ref[...], right_ref[...]
    left = jnp.concatenate([pltpu.roll(left, REACH, 1), left], axis=0)
    right = jnp.concatenate([right, pltpu.roll(right, REACH, 1)], axis=0)
    sides = sides_ref[...]
    windows = (
        pltpu.roll(jnp.concatenate([left, sides[:, : 2 * LANES]], axis=1), 3 * LANES - REACH, 1)[:, : 2 * LANES],
        pltpu.roll(jnp.concatenate([sides[:, 2 * LANES :], right], axis=1), 3 * LANES - REACH, 1)[:, : 2 * LANES],
    )
    copies = []
    for side, which in enumerate((first_col.astype(jnp.int32), 2 * last_col.astype(jnp.int32))):
        high, low = split_values(windows[side])
        blocks_ref[side] = column_pass(coltaps_ref[which], high, low)
        target = rms_ref.at[:, pl.ds(side * (cols - LANES), LANES)]
        copies.append(pltpu.make_async_copy(blocks_ref.at[side], target, sems.at[side]))
        copies[-1].start()
    for copy in copies:
        copy.wait()


def shift(block, axis, step):
    count = lax.axis_size(axis)
    pairs = [(i, i + step) for i in range(count) if 0 <= i + step < count]
    return lax.ppermute(block, axis, pairs)


def swap(block, axis, first):
    count = lax.axis_size(axis)
    pairs = [(i, i + 1) for i in range(first, count - 1, 2)]
    return lax.ppermute(block, axis, pairs + [(j, i) for i, j in pairs])


def call(kernel, name, outs, scratch=(), limit=16, in_place=False):
    vmem = pl.BlockSpec(memory_space=pltpu.VMEM)
    there = pl.BlockSpec(memory_space=pl.ANY)

    def run(*args):
        return pl.pallas_call(
            kernel,
            out_shape=tuple(jax.ShapeDtypeStruct(shape, jnp.float32) for shape in outs),
            in_specs=[there if in_place and i == 0 else vmem for i in range(len(args))],
            out_specs=(there if in_place else vmem,) * len(outs),
            scratch_shapes=list(scratch),
            input_output_aliases={0: 0} if in_place else {},
            compiler_params=pltpu.CompilerParams(vmem_limit_bytes=limit << 20),
            name=name,
        )(*args)

    return run


def shards(coadd_flux, inverse_variance, source_mask):
    rows, cols = coadd_flux.shape
    nrows, ncols = lax.axis_size("rows"), lax.axis_size("cols")
    message = (VECTORS + 1) * LANES

    def scratch(*shape, dtype=jnp.float32):
        return pltpu.VMEM(shape, dtype)

    taken = []
    for above, below in ((0, rows - 1), (1, rows - 2), (REACH, rows - 1 - REACH)):
        start = (jnp.where(is_even(), above, below), 0)
        flux, variance, mask = (
            lax.dynamic_slice(x, start, (1, cols)) for x in (coadd_flux, inverse_variance, source_mask)
        )
        taken.append((flux, weights(variance, mask)))
    products = [flux * weight for flux, weight in taken]
    narrow = swap(jnp.concatenate([products[0], products[1], taken[0][1], products[2]]), "rows", 1)

    own = (coadd_flux, weights(inverse_variance, source_mask))
    to_near, to_far = call(wide_kernel, "wide", ((2 * REACH + 8, cols), (2 * REACH, cols)))(*own)
    to_near, to_far, narrow = lax.optimization_barrier((to_near, to_far, narrow))
    near = swap(to_near, "rows", 0)
    far = swap(to_far, "rows", 1)

    field = scratch(rows + 2 * NEAR, cols + LANES)
    devices = nrows * ncols
    parts, own_v1 = call(
        moments_kernel,
        "moments",
        ((devices * (VECTORS + 1), LANES), (rows, cols)),
        (field, field, scratch(rows, LANES)),
    )(*own, narrow, near)
    parts = lax.all_to_all(parts.reshape(devices, 1, message), ("rows", "cols"), 0, 0, tiled=True)
    first_row, last_row, _, _ = at_edges()
    kind = jnp.where(is_even(), first_row.astype(jnp.int32), 2 + last_row.astype(jnp.int32))
    row_taps = lax.dynamic_index_in_dim(jnp.asarray(row_tables(rows)), kind, keepdims=False)
    col_taps = jnp.asarray(col_tables())
    reached, packed = rows + 2 * REACH, (rows // 2, LANES)
    near_v1, far_v1, numbers, left, right, first, last = call(
        functools.partial(edges_kernel, nrows, ncols),
        "edges",
        ((REACH, cols), (REACH, cols), (16, LANES), (reached, LANES), (reached, LANES), packed, packed),
        (scratch(REACH + 2 * NEAR, cols + LANES),) + (scratch(reached, 2 * LANES, dtype=jnp.bfloat16),) * 2,
    )(parts, *own, own_v1, narrow, near, far, row_taps)
    fields = (*own, own_v1, near, near_v1, far, far_v1)
    from_left = shift(last, "cols", 1)
    from_right = shift(first, "cols", -1)
    background, rms, sides = call(
        main_kernel,
        "main",
        ((rows, cols), (rows, cols), (rows, 4 * LANES)),
        (scratch(reached, cols, dtype=jnp.bfloat16),) * 2,
    )(numbers, left, right, *fields, row_taps, col_taps)
    (rms,) = call(
        final_kernel, "final", ((rows, cols),), (scratch(2, rows, LANES), pltpu.SemaphoreType.DMA((2,))), in_place=True
    )(rms, sides, from_left, from_right, col_taps)
    return background, rms


def solution(mesh):
    return jax.shard_map(
        shards,
        mesh=mesh,
        in_specs=(P("rows", "cols"), P("rows", "cols"), P("rows", "cols")),
        out_specs=(P("rows", "cols"), P("rows", "cols")),
        check_vma=False,
    )
```

```python
import functools

import jax
import jax.numpy as jnp
import ml_dtypes
import numpy as np
from jax import lax
from jax.experimental import pallas as pl
from jax.experimental.pallas import tpu as pltpu
from jax.sharding import PartitionSpec as P

RADIUS = 32
REACH = 2 * RADIUS
LANES = 128
WIDE = REACH + 8
NEAR = 8
VECTORS = 8

smooth_weight = 2.0
blur_sigma = 10.0


def squared_taps(length, first, last):
    offsets = np.arange(2 * RADIUS + 1) - RADIUS
    taps = np.exp(-offsets * offsets / (2.0 * blur_sigma * blur_sigma))
    taps = taps / taps.sum()

    def band(count):
        table = np.zeros((count, count + 2 * RADIUS))
        for k in range(2 * RADIUS + 1):
            table[np.arange(count), np.arange(count) + k] = taps[k]
        return table

    inner = band(length + 2 * RADIUS)
    if first:
        inner[:RADIUS] = 0.0
    if last:
        inner[-RADIUS:] = 0.0
    return band(length) @ inner


def split(table):
    high = table.astype(np.float32).astype(ml_dtypes.bfloat16)
    low = (table - high.astype(np.float64)).astype(np.float32).astype(ml_dtypes.bfloat16)
    return high, low


def row_tables(length):
    tables = []
    for first, last, odd in ((False, False, False), (True, False, False), (False, False, True), (False, True, True)):
        table = squared_taps(length, first, last)
        above, own, below = table[:, :REACH], table[:, REACH : REACH + length], table[:, REACH + length :]
        near, far = (above, below) if odd else (below, above)
        if first or last:
            far = np.zeros_like(far)
        tables.append(np.concatenate(split(np.concatenate([own, near, far], axis=1)), axis=0))
    return np.stack(tables)


def col_tables():
    tables = []
    for first, last in ((False, False), (True, False), (False, True)):
        tables.append(np.concatenate(split(squared_taps(LANES, first, last).T), axis=1))
    return np.stack(tables)


def split_values(values):
    high = values.astype(jnp.bfloat16)
    return high, (values - high.astype(jnp.float32)).astype(jnp.bfloat16)


def at_edges():
    row, col = lax.axis_index("rows"), lax.axis_index("cols")
    return (
        row == 0,
        row == lax.axis_size("rows") - 1,
        col == 0,
        col == lax.axis_size("cols") - 1,
    )


def is_even(axis="rows"):
    return lax.axis_index(axis) % 2 == 0


def beside_columns(field):
    width = field.shape[1]
    return pltpu.roll(field, 1, 1) + pltpu.roll(field, width - 1, 1)


def weights(inverse_variance, source_mask):
    return inverse_variance * (1.0 - source_mask.astype(jnp.float32))


def coefficients(m0, m1, m2, m3):
    alpha0 = m0 / m1
    norm1 = jnp.maximum(m0 - 2.0 * alpha0 * m1 + alpha0 * alpha0 * m2, 0.0)
    grown = 1.0 + norm1 / m0
    image1 = grown * grown * m1 - 2.0 * grown * alpha0 * m2 + alpha0 * alpha0 * m3
    alpha1 = jnp.where(image1 > 0.0, norm1 / image1, 0.0)
    return alpha0 + alpha1 * grown, -alpha1 * alpha0


def image(ref, weight, start):
    cols = weight.shape[1]
    own = pl.ds(0, cols)
    here = ref[pl.ds(start, 8), :]
    beside = ref[pl.ds(start - 1, 8), own] + ref[pl.ds(start + 1, 8), own] + beside_columns(here)[:, :cols]
    here = here[:, :cols]
    return here, weight * here + smooth_weight * (4.0 * here - beside)


def prepare_kernel(f_ref, w_ref, near_ref, far_ref, v1_ref, v0_ref):
    rows = f_ref.shape[0]

    def write(out_ref, begin):
        out_ref[pl.ds(0, REACH), :] = f_ref[pl.ds(begin, REACH), :]
        out_ref[pl.ds(REACH, REACH), :] = w_ref[pl.ds(begin, REACH), :]

    def near_product(begin):
        near_ref[pl.ds(2 * REACH, 8), :] = f_ref[pl.ds(begin, 8), :] * w_ref[pl.ds(begin, 8), :]

    @pl.when(is_even())
    def _():
        write(near_ref, rows - REACH)
        near_product(rows - WIDE)
        write(far_ref, 0)

    @pl.when(jnp.logical_not(is_even()))
    def _():
        write(near_ref, 0)
        near_product(REACH)
        write(far_ref, rows - REACH)

    cols = f_ref.shape[1]
    own = pl.ds(0, cols)
    v0_ref[:, pl.ds(cols, LANES)] = jnp.zeros((rows + 2 * NEAR, LANES), jnp.float32)
    for start in (0, NEAR + rows):
        v0_ref[pl.ds(start, NEAR), own] = jnp.zeros((NEAR, cols), jnp.float32)
    for start in range(0, rows, 8):
        at = pl.ds(start, 8)
        v0_ref[pl.ds(NEAR + start, 8), own] = f_ref[at, :] * w_ref[at, :]
    for start in range(0, rows, 8):
        _, v1_ref[pl.ds(start, 8), :] = image(v0_ref, w_ref[pl.ds(start, 8), :], NEAR + start)


def moments_kernel(f_ref, w_ref, base_ref, narrow_ref, near_ref, out_ref, v1_out_ref, v1_ref, edge_ref):
    rows, cols = f_ref.shape
    first_row, last_row, _, _ = at_edges()
    even = is_even()
    own, pad = pl.ds(0, cols), pl.ds(cols, LANES)

    def near_rows(nearest, second):
        return (
            near_ref[pl.ds(nearest, 1), :] * near_ref[pl.ds(REACH + nearest, 1), :],
            near_ref[pl.ds(second, 1), :] * near_ref[pl.ds(REACH + second, 1), :],
            near_ref[pl.ds(REACH + nearest, 1), :],
        )

    far_rows = tuple(narrow_ref[pl.ds(k, 1), :] for k in range(3))
    above = [jnp.where(even, far, near) for far, near in zip(far_rows, near_rows(REACH - 1, REACH - 2))]
    below = [jnp.where(even, near, far) for far, near in zip(far_rows, near_rows(0, 1))]

    v1_ref[:, pad] = jnp.zeros((rows + 2 * NEAR, LANES), jnp.float32)
    for start in (0, NEAR + rows):
        v1_ref[pl.ds(start, NEAR), own] = jnp.zeros((NEAR, cols), jnp.float32)
    row = lax.broadcasted_iota(jnp.int32, (8, cols), 0)
    for start in range(0, rows, 8):
        v1 = base_ref[pl.ds(start, 8), :]
        if start == 0:
            v1 = v1 - jnp.where(row == 0, smooth_weight * above[0], 0.0)
        if start == rows - 8:
            v1 = v1 - jnp.where(row == 7, smooth_weight * below[0], 0.0)
        v1_ref[pl.ds(NEAR + start, 8), own] = v1
        v1_out_ref[pl.ds(start, 8), :] = v1

    def edge_row(halo, inner, at):
        nearest, second, weight = halo
        inner = f_ref[pl.ds(inner, 1), :] * w_ref[pl.ds(inner, 1), :]
        padded = jnp.concatenate([nearest, jnp.zeros((1, LANES), jnp.float32)], axis=1)
        beside = second + inner + beside_columns(padded)[:, :cols]
        v1_ref[pl.ds(at, 1), own] = weight * nearest + smooth_weight * (4.0 * nearest - beside)

    pl.when(jnp.logical_not(first_row))(lambda: edge_row(above, 0, NEAR - 1))
    pl.when(jnp.logical_not(last_row))(lambda: edge_row(below, rows - 1, NEAR + rows))

    lane = lax.broadcasted_iota(jnp.int32, (8, LANES), 1)
    sums = [jnp.zeros((8, cols), jnp.float32) for _ in range(4)]
    for start in range(0, rows, 8):
        weight = w_ref[pl.ds(start, 8), :]
        v0 = f_ref[pl.ds(start, 8), :] * weight
        v1, v2 = image(v1_ref, weight, NEAR + start)
        sums = [total + term for total, term in zip(sums, (v0 * v0, v0 * v1, v1 * v1, v1 * v2))]
        edges = jnp.zeros((8, LANES), jnp.float32)
        for k, field in enumerate((v0, v1, v2, weight)):
            edges = jnp.where(lane == k, pltpu.roll(field[:, cols - LANES :], k + 1, 1), edges)
            edges = jnp.where(lane == 4 + k, pltpu.roll(field[:, :LANES], 4 + k, 1), edges)
        edge_ref[pl.ds(start, 8), :] = edges

    result = jnp.zeros((1, LANES), jnp.float32)
    for i, total in enumerate(sums):
        narrow = sum(total[:, k : k + LANES] for k in range(0, cols, LANES))
        total = jnp.sum(jnp.sum(narrow, axis=0, keepdims=True), axis=1, keepdims=True)
        result = jnp.where(lane[:1] == i, total, result)
    vectors = edge_ref[...].T
    message = [result] + [vectors[k : k + 1, :] for k in range(VECTORS)]
    copies = jnp.concatenate(message * 8, axis=0)
    for start in range(0, out_ref.shape[0], copies.shape[0]):
        out_ref[pl.ds(start, copies.shape[0]), :] = copies


def coupled(parts_ref, nrows, ncols):
    count = nrows * ncols
    lam = smooth_weight

    def part(k):
        return parts_ref[:, :, pl.ds(k * LANES, LANES)].reshape(count, LANES)

    device = lax.broadcasted_iota(jnp.int32, (count, LANES), 0)
    lane = lax.broadcasted_iota(jnp.int32, (count, LANES), 1)
    joined = device % ncols < ncols - 1
    a0, a1, ua, wa = (jnp.where(joined, part(1 + k), 0.0) for k in range(4))
    b0, b1, ub, wb = (jnp.where(joined, pltpu.roll(part(5 + k), count - 1, 0), 0.0) for k in range(4))

    def next_row(field):
        inside = pltpu.roll(field, LANES - 1, 1)
        beyond = jnp.where(device < count - ncols, pltpu.roll(inside, count - ncols, 0), 0.0)
        return jnp.where(lane == LANES - 1, beyond, inside)

    def total(field):
        return jnp.sum(jnp.sum(field, axis=0, keepdims=True), axis=1, keepdims=True)

    scalars = jnp.sum(part(0), axis=0, keepdims=True)
    m0, m1, m2, m3 = (total(jnp.where(lane[:1] == i, scalars, 0.0)) for i in range(4))
    m1 = m1 - 2.0 * lam * total(a0 * b0)
    m2 = m2 + total(lam * lam * (a0 * a0 + b0 * b0) - 2.0 * lam * (a1 * b0 + b1 * a0))
    m3 = m3 + total(
        lam * lam * ((wa + 4.0 * lam) * b0 * b0 + (wb + 4.0 * lam) * a0 * a0)
        - 2.0 * lam * (b0 * ua + a0 * ub + (a1 - lam * b0) * (b1 - lam * a0))
        - 2.0 * lam * lam * lam * (a0 * next_row(a0) + b0 * next_row(b0))
    )
    return m0, m1, m2, m3


def neighbours(parts_ref, nrows, ncols):
    row, col = lax.axis_index("rows"), lax.axis_index("cols")
    even = is_even()
    towards = jnp.where(even, 1, -1)
    lane = lax.broadcasted_iota(jnp.int32, (LANES, LANES), 1)
    vectors = []
    for vector, step_col in ((1, -1), (5, 1)):
        for step_row in (0, towards, -towards):
            r, c = row + step_row, col + step_col
            there = (r >= 0) & (r < nrows) & (c >= 0) & (c < ncols)
            index = jnp.where(there, r * ncols + c, 0)
            found = parts_ref[index, :, pl.ds(vector * LANES, LANES)]
            vectors.append(jnp.where(there, found, 0.0))
    vectors.append(jnp.zeros((LANES - len(vectors), LANES), jnp.float32))
    columns = jnp.concatenate(vectors, axis=0).T
    sides = []
    for begin, target in ((0, 0), (3, LANES - 1)):
        own, near, far = (
            jnp.where(lane == target, pltpu.roll(columns, (target - begin - k) % LANES, 1), 0.0) for k in range(3)
        )
        near = jnp.where(even, near[:REACH], near[LANES - REACH :])
        far = jnp.where(even, far[LANES - REACH :], far[:REACH])
        sides.append(jnp.concatenate([own, near, far], axis=0))
    return sides


def guard_rows(f_ref, w_ref, narrow_ref, near_ref, at_cols):
    rows = f_ref.shape[0]
    even = is_even()
    top = f_ref[pl.ds(0, 1), at_cols] * w_ref[pl.ds(0, 1), at_cols]
    bottom = f_ref[pl.ds(rows - 1, 1), at_cols] * w_ref[pl.ds(rows - 1, 1), at_cols]
    near = jnp.where(even, near_ref[pl.ds(2 * REACH, 1), at_cols], near_ref[pl.ds(2 * REACH + 7, 1), at_cols])
    far = narrow_ref[pl.ds(3, 1), at_cols]
    return (
        (jnp.where(even, bottom, near), jnp.where(even, near, top)),
        (jnp.where(even, far, bottom), jnp.where(even, top, far)),
    )


def halo_fields(f_ref, w_ref, narrow_ref, near_ref, far_ref, near_v1_ref, far_v1_ref, v0_ref):
    rows, cols = f_ref.shape
    own, pad = pl.ds(0, cols), pl.ds(cols, LANES)
    v0_ref[:, pad] = jnp.zeros((REACH + 2 * NEAR, LANES), jnp.float32)
    guards = guard_rows(f_ref, w_ref, narrow_ref, near_ref, own)
    for halo_ref, v1_ref, (above, below) in zip((near_ref, far_ref), (near_v1_ref, far_v1_ref), guards):
        v0_ref[pl.ds(NEAR - 1, 1), own] = above
        v0_ref[pl.ds(NEAR + REACH, 1), own] = below
        for start in range(0, REACH, 8):
            v0_ref[pl.ds(NEAR + start, 8), own] = halo_ref[pl.ds(start, 8), :] * halo_ref[pl.ds(REACH + start, 8), :]
        for start in range(0, REACH, 8):
            _, v1_ref[pl.ds(start, 8), :] = image(v0_ref, halo_ref[pl.ds(REACH + start, 8), :], NEAR + start)


def edge_fields(side, f_ref, w_ref, narrow_ref, near_ref, far_ref, near_v1_ref, far_v1_ref, v0_ref):
    cols = f_ref.shape[1]
    at_cols, there = pl.ds(side * (cols - LANES), LANES), pl.ds(side * LANES, LANES)
    outermost = lax.broadcasted_iota(jnp.int32, (8, LANES), 1) == side * (LANES - 1)
    guards = guard_rows(f_ref, w_ref, narrow_ref, near_ref, at_cols)
    for halo_ref, v1_ref, (above, below) in zip((near_ref, far_ref), (near_v1_ref, far_v1_ref), guards):
        v0_ref[pl.ds(NEAR - 1, 1), :] = above
        v0_ref[pl.ds(NEAR + REACH, 1), :] = below
        for start in range(0, REACH, 8):
            at, weight_at = pl.ds(start, 8), pl.ds(REACH + start, 8)
            v0_ref[pl.ds(NEAR + start, 8), :] = halo_ref[at, at_cols] * halo_ref[weight_at, at_cols]
        for start in range(0, REACH, 8):
            here = v0_ref[pl.ds(NEAR + start, 8), :]
            inner = pltpu.roll(here, 1 if side else LANES - 1, 1)
            outer = jnp.where(outermost, 0.0, pltpu.roll(here, LANES - 1 if side else 1, 1))
            beside = v0_ref[pl.ds(NEAR + start - 1, 8), :] + v0_ref[pl.ds(NEAR + start + 1, 8), :] + inner + outer
            weight = halo_ref[pl.ds(REACH + start, 8), at_cols]
            v1_ref[pl.ds(start, 8), there] = weight * here + smooth_weight * (4.0 * here - beside)


def regions(f_ref, w_ref, v1_ref, near_ref, near_v1_ref, far_ref, far_v1_ref, step):
    for start in range(0, f_ref.shape[0], step):
        yield start, (f_ref, start), (w_ref, start), (v1_ref, start)
    for base, halo_ref, field_ref in ((f_ref.shape[0], near_ref, near_v1_ref), (f_ref.shape[0] + REACH, far_ref, far_v1_ref)):
        for start in range(0, REACH, step):
            yield base + start, (halo_ref, start), (halo_ref, REACH + start), (field_ref, start)


def dot(left, right):
    return jnp.dot(left, right, preferred_element_type=jnp.float32)


def row_pass(rowtaps_ref, high, low, rows):
    table = rowtaps_ref[...]
    both = dot(table, high)
    return both[:rows] + (both[rows:] + dot(table[:rows], low))


def edges_kernel(
    nrows, ncols, parts_ref, f_ref, w_ref, v1_ref, narrow_ref, near_ref, far_ref, rowtaps_ref,
    coefficients_ref, left_ref, right_ref, one_ref, other_ref, near_v1_ref, far_v1_ref, v0_ref, high_ref, low_ref,
):
    rows, cols = f_ref.shape
    for side in range(2):
        edge_fields(side, f_ref, w_ref, narrow_ref, near_ref, far_ref, near_v1_ref, far_v1_ref, v0_ref)
    c0, c1 = coefficients(*coupled(parts_ref, nrows, ncols))
    coefficients_ref[pl.ds(0, 8), :] = jnp.broadcast_to(c0, (8, LANES))
    coefficients_ref[pl.ds(8, 8), :] = jnp.broadcast_to(c1, (8, LANES))
    sides = neighbours(parts_ref, nrows, ncols)
    left_ref[...], right_ref[...] = sides

    step = 16
    fields = (f_ref, w_ref, v1_ref, near_ref, near_v1_ref, far_ref, far_v1_ref)
    for side, begin in enumerate((0, cols - LANES)):
        at_cols = pl.ds(begin, LANES)
        for start, (flux_ref, flux_row), (weight_ref, weight_row), (field_ref, field_row) in regions(*fields, step):
            flux, weight = flux_ref[pl.ds(flux_row, step), at_cols], weight_ref[pl.ds(weight_row, step), at_cols]
            v1_cols = at_cols if start < rows else pl.ds(side * LANES, LANES)
            v1 = field_ref[pl.ds(field_row, step), v1_cols]
            v1 = v1 - smooth_weight * sides[side][start : start + step]
            scatter = flux - (c0 * (flux * weight) + c1 * v1)
            high, low = split_values(scatter * scatter)
            high_ref[pl.ds(start, step), pl.ds(side * LANES, LANES)] = high
            low_ref[pl.ds(start, step), pl.ds(side * LANES, LANES)] = low
    passed = row_pass(rowtaps_ref, high_ref[...], low_ref[...], rows)
    upper, lower = slice(0, rows // 2), slice(rows // 2, rows)
    first, last = passed[:, :LANES], passed[:, LANES:]
    on_left = lax.broadcasted_iota(jnp.int32, (rows // 2, LANES), 1) < REACH
    first = jnp.where(on_left, first[upper], pltpu.roll(first[lower], REACH, 1))
    last = jnp.where(on_left, pltpu.roll(last[upper], REACH, 1), last[lower])
    even = is_even("cols")
    one_ref[...] = jnp.where(even, last, first)
    other_ref[...] = jnp.where(even, first, last)


def main_kernel(
    coefficients_ref, left_ref, right_ref, f_ref, w_ref, v1_ref, narrow_ref, near_ref, far_ref, rowtaps_ref, coltaps_ref,
    background_ref, rms_ref, sides_ref, near_v1_ref, far_v1_ref, v0_ref, high_ref, low_ref,
):
    rows, cols = f_ref.shape
    halo_fields(f_ref, w_ref, narrow_ref, near_ref, far_ref, near_v1_ref, far_v1_ref, v0_ref)
    c0, c1 = coefficients_ref[pl.ds(0, 1), pl.ds(0, 1)], coefficients_ref[pl.ds(8, 1), pl.ds(0, 1)]
    step = 16
    fields = (f_ref, w_ref, v1_ref, near_ref, near_v1_ref, far_ref, far_v1_ref)
    for start, *sources in regions(*fields, step):
        flux, weight, v1 = (ref[pl.ds(row, step), :] for ref, row in sources)
        at = pl.ds(start, step)
        v1 = jnp.concatenate(
            [
                v1[:, :LANES] - smooth_weight * left_ref[at, :],
                v1[:, LANES : cols - LANES],
                v1[:, cols - LANES :] - smooth_weight * right_ref[at, :],
            ],
            axis=1,
        )
        background = c0 * (flux * weight) + c1 * v1
        if start < rows:
            background_ref[at, :] = background
        scatter = flux - background
        high_ref[at, :], low_ref[at, :] = split_values(scatter * scatter)
    passed = row_pass(rowtaps_ref, high_ref[...], low_ref[...], rows)
    sides_ref[:, pl.ds(0, 2 * LANES)] = passed[:, : 2 * LANES]
    sides_ref[:, pl.ds(2 * LANES, 2 * LANES)] = passed[:, cols - 2 * LANES :]
    high, low = split_values(pltpu.roll(passed, REACH, 1))
    for j in range(1, cols // LANES - 1):
        at = slice(j * LANES, j * LANES + 2 * LANES)
        rms_ref[:, pl.ds(j * LANES, LANES)] = column_pass(coltaps_ref[0], high[:, at], low[:, at])


def column_pass(table, high, low):
    both = dot(high, table)
    smoothed = both[:, :LANES] + (both[:, LANES:] + dot(low, table[:, :LANES]))
    return jnp.sqrt(smoothed + 1e-06)


def final_kernel(rms_in_ref, sides_ref, one_ref, other_ref, coltaps_ref, rms_ref, blocks_ref, sems):
    rows, cols = rms_ref.shape
    del rms_in_ref
    _, _, first_col, last_col = at_edges()
    even = is_even("cols")
    left = jnp.where(even, other_ref[...], one_ref[...])
    right = jnp.where(even, one_ref[...], other_ref[...])
    left = jnp.concatenate([pltpu.roll(left, REACH, 1), left], axis=0)
    right = jnp.concatenate([right, pltpu.roll(right, REACH, 1)], axis=0)
    sides = sides_ref[...]
    windows = (
        pltpu.roll(jnp.concatenate([left, sides[:, : 2 * LANES]], axis=1), 3 * LANES - REACH, 1)[:, : 2 * LANES],
        pltpu.roll(jnp.concatenate([sides[:, 2 * LANES :], right], axis=1), 3 * LANES - REACH, 1)[:, : 2 * LANES],
    )
    copies = []
    for side, which in enumerate((first_col.astype(jnp.int32), 2 * last_col.astype(jnp.int32))):
        high, low = split_values(windows[side])
        blocks_ref[side] = column_pass(coltaps_ref[which], high, low)
        target = rms_ref.at[:, pl.ds(side * (cols - LANES), LANES)]
        copies.append(pltpu.make_async_copy(blocks_ref.at[side], target, sems.at[side]))
        copies[-1].start()
    for copy in copies:
        copy.wait()


def swap(block, axis, first):
    count = lax.axis_size(axis)
    pairs = [(i, i + 1) for i in range(first, count - 1, 2)]
    return lax.ppermute(block, axis, pairs + [(j, i) for i, j in pairs])


def call(kernel, name, outs, scratch=(), limit=16, in_place=False):
    vmem = pl.BlockSpec(memory_space=pltpu.VMEM)
    there = pl.BlockSpec(memory_space=pl.ANY)

    def run(*args):
        return pl.pallas_call(
            kernel,
            out_shape=tuple(jax.ShapeDtypeStruct(shape, jnp.float32) for shape in outs),
            in_specs=[there if in_place and i == 0 else vmem for i in range(len(args))],
            out_specs=(there if in_place else vmem,) * len(outs),
            scratch_shapes=list(scratch),
            input_output_aliases={0: 0} if in_place else {},
            compiler_params=pltpu.CompilerParams(vmem_limit_bytes=limit << 20),
            name=name,
        )(*args)

    return run


def shards(coadd_flux, inverse_variance, source_mask):
    rows, cols = coadd_flux.shape
    nrows, ncols = lax.axis_size("rows"), lax.axis_size("cols")
    message = (VECTORS + 1) * LANES

    def scratch(*shape, dtype=jnp.float32):
        return pltpu.VMEM(shape, dtype)

    taken = []
    for above, below in ((0, rows - 1), (1, rows - 2), (REACH, rows - 1 - REACH)):
        start = (jnp.where(is_even(), above, below), 0)
        flux, variance, mask = (
            lax.dynamic_slice(x, start, (1, cols)) for x in (coadd_flux, inverse_variance, source_mask)
        )
        taken.append((flux, weights(variance, mask)))
    products = [flux * weight for flux, weight in taken]
    narrow = swap(jnp.concatenate([products[0], products[1], taken[0][1], products[2]]), "rows", 1)

    own = (coadd_flux, weights(inverse_variance, source_mask))
    field = scratch(rows + 2 * NEAR, cols + LANES)
    to_near, to_far, base = call(
        prepare_kernel, "prepare", ((2 * REACH + 8, cols), (2 * REACH, cols), (rows, cols)), (field,)
    )(*own)
    to_near, to_far, narrow = lax.optimization_barrier((to_near, to_far, narrow))
    near = swap(to_near, "rows", 0)
    far = swap(to_far, "rows", 1)

    devices = nrows * ncols
    parts, own_v1 = call(
        moments_kernel,
        "moments",
        ((devices * (VECTORS + 1), LANES), (rows, cols)),
        (field, scratch(rows, LANES)),
    )(*own, base, narrow, near)
    parts = lax.all_to_all(parts.reshape(devices, 1, message), ("rows", "cols"), 0, 0, tiled=True)
    first_row, last_row, _, _ = at_edges()
    kind = jnp.where(is_even(), first_row.astype(jnp.int32), 2 + last_row.astype(jnp.int32))
    row_taps = lax.dynamic_index_in_dim(jnp.asarray(row_tables(rows)), kind, keepdims=False)
    col_taps = jnp.asarray(col_tables())
    reached, packed = rows + 2 * REACH, (rows // 2, LANES)
    fields = (*own, own_v1, narrow, near, far)
    halves = (scratch(REACH, 2 * LANES),) * 2
    numbers, left, right, to_one, to_other = call(
        functools.partial(edges_kernel, nrows, ncols),
        "edges",
        ((16, LANES), (reached, LANES), (reached, LANES), packed, packed),
        halves + (scratch(REACH + 2 * NEAR, LANES),) + (scratch(reached, 2 * LANES, dtype=jnp.bfloat16),) * 2,
    )(parts, *fields, row_taps)
    one = swap(to_one, "cols", 0)
    other = swap(to_other, "cols", 1)
    halves = (scratch(REACH, cols),) * 2
    background, rms, sides = call(
        main_kernel,
        "main",
        ((rows, cols), (rows, cols), (rows, 4 * LANES)),
        halves + (scratch(REACH + 2 * NEAR, cols + LANES),) + (scratch(reached, cols, dtype=jnp.bfloat16),) * 2,
    )(numbers, left, right, *fields, row_taps, col_taps)
    (rms,) = call(
        final_kernel, "final", ((rows, cols),), (scratch(2, rows, LANES), pltpu.SemaphoreType.DMA((2,))), in_place=True
    )(rms, sides, one, other, col_taps)
    return background, rms


def solution(mesh):
    return jax.shard_map(
        shards,
        mesh=mesh,
        in_specs=(P("rows", "cols"), P("rows", "cols"), P("rows", "cols")),
        out_specs=(P("rows", "cols"), P("rows", "cols")),
        check_vma=False,
    )
```

```python
import functools

import jax
import jax.numpy as jnp
import ml_dtypes
import numpy as np
from jax import lax
from jax.experimental import pallas as pl
from jax.experimental.pallas import tpu as pltpu
from jax.sharding import PartitionSpec as P

RADIUS = 32
REACH = 2 * RADIUS
LANES = 128
WIDE = REACH + 8
NEAR = 8
VECTORS = 8

smooth_weight = 2.0
blur_sigma = 10.0


def squared_taps(length, first, last):
    offsets = np.arange(2 * RADIUS + 1) - RADIUS
    taps = np.exp(-offsets * offsets / (2.0 * blur_sigma * blur_sigma))
    taps = taps / taps.sum()

    def band(count):
        table = np.zeros((count, count + 2 * RADIUS))
        for k in range(2 * RADIUS + 1):
            table[np.arange(count), np.arange(count) + k] = taps[k]
        return table

    inner = band(length + 2 * RADIUS)
    if first:
        inner[:RADIUS] = 0.0
    if last:
        inner[-RADIUS:] = 0.0
    return band(length) @ inner


def split(table):
    high = table.astype(np.float32).astype(ml_dtypes.bfloat16)
    low = (table - high.astype(np.float64)).astype(np.float32).astype(ml_dtypes.bfloat16)
    return high, low


def row_tables(length):
    tables = []
    for first, last, odd in ((False, False, False), (True, False, False), (False, False, True), (False, True, True)):
        table = squared_taps(length, first, last)
        above, own, below = table[:, :REACH], table[:, REACH : REACH + length], table[:, REACH + length :]
        near, far = (above, below) if odd else (below, above)
        if first or last:
            far = np.zeros_like(far)
        tables.append(np.concatenate(split(np.concatenate([own, near, far], axis=1)), axis=0))
    return np.stack(tables)


def col_tables():
    tables = []
    for first, last in ((False, False), (True, False), (False, True)):
        tables.append(np.concatenate(split(squared_taps(LANES, first, last).T), axis=1))
    return np.stack(tables)


def split_values(values):
    high = values.astype(jnp.bfloat16)
    return high, (values - high.astype(jnp.float32)).astype(jnp.bfloat16)


def at_edges():
    row, col = lax.axis_index("rows"), lax.axis_index("cols")
    return (
        row == 0,
        row == lax.axis_size("rows") - 1,
        col == 0,
        col == lax.axis_size("cols") - 1,
    )


def is_even(axis="rows"):
    return lax.axis_index(axis) % 2 == 0


def beside_columns(field):
    width = field.shape[1]
    return pltpu.roll(field, 1, 1) + pltpu.roll(field, width - 1, 1)


def weights(inverse_variance, source_mask):
    return inverse_variance * (1.0 - source_mask.astype(jnp.float32))


def coefficients(m0, m1, m2, m3):
    alpha0 = m0 / m1
    norm1 = jnp.maximum(m0 - 2.0 * alpha0 * m1 + alpha0 * alpha0 * m2, 0.0)
    grown = 1.0 + norm1 / m0
    image1 = grown * grown * m1 - 2.0 * grown * alpha0 * m2 + alpha0 * alpha0 * m3
    alpha1 = jnp.where(image1 > 0.0, norm1 / image1, 0.0)
    return alpha0 + alpha1 * grown, -alpha1 * alpha0


def image(ref, weight, start):
    cols = weight.shape[1]
    own = pl.ds(0, cols)
    here = ref[pl.ds(start, 8), :]
    beside = ref[pl.ds(start - 1, 8), own] + ref[pl.ds(start + 1, 8), own] + beside_columns(here)[:, :cols]
    here = here[:, :cols]
    return here, weight * here + smooth_weight * (4.0 * here - beside)


def prepare_kernel(f_ref, w_ref, near_ref, far_ref, v1_ref, v0_ref):
    rows = f_ref.shape[0]

    def write(out_ref, begin):
        out_ref[pl.ds(0, REACH), :] = f_ref[pl.ds(begin, REACH), :]
        out_ref[pl.ds(REACH, REACH), :] = w_ref[pl.ds(begin, REACH), :]

    def near_product(begin):
        near_ref[pl.ds(2 * REACH, 8), :] = f_ref[pl.ds(begin, 8), :] * w_ref[pl.ds(begin, 8), :]

    @pl.when(is_even())
    def _():
        write(near_ref, rows - REACH)
        near_product(rows - WIDE)
        write(far_ref, 0)

    @pl.when(jnp.logical_not(is_even()))
    def _():
        write(near_ref, 0)
        near_product(REACH)
        write(far_ref, rows - REACH)

    cols = f_ref.shape[1]
    own = pl.ds(0, cols)
    v0_ref[:, pl.ds(cols, LANES)] = jnp.zeros((rows + 2 * NEAR, LANES), jnp.float32)
    for start in (0, NEAR + rows):
        v0_ref[pl.ds(start, NEAR), own] = jnp.zeros((NEAR, cols), jnp.float32)
    for start in range(0, rows, 8):
        at = pl.ds(start, 8)
        v0_ref[pl.ds(NEAR + start, 8), own] = f_ref[at, :] * w_ref[at, :]
    for start in range(0, rows, 8):
        _, v1_ref[pl.ds(start, 8), :] = image(v0_ref, w_ref[pl.ds(start, 8), :], NEAR + start)


def moments_kernel(f_ref, w_ref, base_ref, narrow_ref, near_ref, out_ref, v1_out_ref, v1_ref, edge_ref):
    rows, cols = f_ref.shape
    first_row, last_row, _, _ = at_edges()
    even = is_even()
    own, pad = pl.ds(0, cols), pl.ds(cols, LANES)

    def near_rows(nearest, second):
        return (
            near_ref[pl.ds(nearest, 1), :] * near_ref[pl.ds(REACH + nearest, 1), :],
            near_ref[pl.ds(second, 1), :] * near_ref[pl.ds(REACH + second, 1), :],
            near_ref[pl.ds(REACH + nearest, 1), :],
        )

    far_rows = tuple(narrow_ref[pl.ds(k, 1), :] for k in range(3))
    above = [jnp.where(even, far, near) for far, near in zip(far_rows, near_rows(REACH - 1, REACH - 2))]
    below = [jnp.where(even, near, far) for far, near in zip(far_rows, near_rows(0, 1))]

    v1_ref[:, pad] = jnp.zeros((rows + 2 * NEAR, LANES), jnp.float32)
    for start in (0, NEAR + rows):
        v1_ref[pl.ds(start, NEAR), own] = jnp.zeros((NEAR, cols), jnp.float32)
    row = lax.broadcasted_iota(jnp.int32, (8, cols), 0)
    for start in range(0, rows, 8):
        v1 = base_ref[pl.ds(start, 8), :]
        if start == 0:
            v1 = v1 - jnp.where(row == 0, smooth_weight * above[0], 0.0)
        if start == rows - 8:
            v1 = v1 - jnp.where(row == 7, smooth_weight * below[0], 0.0)
        v1_ref[pl.ds(NEAR + start, 8), own] = v1
        v1_out_ref[pl.ds(start, 8), :] = v1

    def edge_row(halo, inner, at):
        nearest, second, weight = halo
        inner = f_ref[pl.ds(inner, 1), :] * w_ref[pl.ds(inner, 1), :]
        padded = jnp.concatenate([nearest, jnp.zeros((1, LANES), jnp.float32)], axis=1)
        beside = second + inner + beside_columns(padded)[:, :cols]
        v1_ref[pl.ds(at, 1), own] = weight * nearest + smooth_weight * (4.0 * nearest - beside)

    pl.when(jnp.logical_not(first_row))(lambda: edge_row(above, 0, NEAR - 1))
    pl.when(jnp.logical_not(last_row))(lambda: edge_row(below, rows - 1, NEAR + rows))

    lane = lax.broadcasted_iota(jnp.int32, (8, LANES), 1)
    sums = [jnp.zeros((8, cols), jnp.float32) for _ in range(4)]
    for start in range(0, rows, 8):
        weight = w_ref[pl.ds(start, 8), :]
        v0 = f_ref[pl.ds(start, 8), :] * weight
        v1, v2 = image(v1_ref, weight, NEAR + start)
        sums = [total + term for total, term in zip(sums, (v0 * v0, v0 * v1, v1 * v1, v1 * v2))]
        edges = jnp.zeros((8, LANES), jnp.float32)
        for k, field in enumerate((v0, v1, v2, weight)):
            edges = jnp.where(lane == k, pltpu.roll(field[:, cols - LANES :], k + 1, 1), edges)
            edges = jnp.where(lane == 4 + k, pltpu.roll(field[:, :LANES], 4 + k, 1), edges)
        edge_ref[pl.ds(start, 8), :] = edges

    result = jnp.zeros((1, LANES), jnp.float32)
    for i, total in enumerate(sums):
        narrow = sum(total[:, k : k + LANES] for k in range(0, cols, LANES))
        total = jnp.sum(jnp.sum(narrow, axis=0, keepdims=True), axis=1, keepdims=True)
        result = jnp.where(lane[:1] == i, total, result)
    vectors = edge_ref[...].T
    message = [result] + [vectors[k : k + 1, :] for k in range(VECTORS)]
    copies = jnp.concatenate(message * 8, axis=0)
    for start in range(0, out_ref.shape[0], copies.shape[0]):
        out_ref[pl.ds(start, copies.shape[0]), :] = copies


def coupled(parts_ref, nrows, ncols):
    count = nrows * ncols
    lam = smooth_weight

    def part(k):
        return parts_ref[:, :, pl.ds(k * LANES, LANES)].reshape(count, LANES)

    device = lax.broadcasted_iota(jnp.int32, (count, LANES), 0)
    lane = lax.broadcasted_iota(jnp.int32, (count, LANES), 1)
    joined = device % ncols < ncols - 1
    a0, a1, ua, wa = (jnp.where(joined, part(1 + k), 0.0) for k in range(4))
    b0, b1, ub, wb = (jnp.where(joined, pltpu.roll(part(5 + k), count - 1, 0), 0.0) for k in range(4))

    def next_row(field):
        inside = pltpu.roll(field, LANES - 1, 1)
        beyond = jnp.where(device < count - ncols, pltpu.roll(inside, count - ncols, 0), 0.0)
        return jnp.where(lane == LANES - 1, beyond, inside)

    def total(field):
        return jnp.sum(jnp.sum(field, axis=0, keepdims=True), axis=1, keepdims=True)

    scalars = jnp.sum(part(0), axis=0, keepdims=True)
    m0, m1, m2, m3 = (total(jnp.where(lane[:1] == i, scalars, 0.0)) for i in range(4))
    m1 = m1 - 2.0 * lam * total(a0 * b0)
    m2 = m2 + total(lam * lam * (a0 * a0 + b0 * b0) - 2.0 * lam * (a1 * b0 + b1 * a0))
    m3 = m3 + total(
        lam * lam * ((wa + 4.0 * lam) * b0 * b0 + (wb + 4.0 * lam) * a0 * a0)
        - 2.0 * lam * (b0 * ua + a0 * ub + (a1 - lam * b0) * (b1 - lam * a0))
        - 2.0 * lam * lam * lam * (a0 * next_row(a0) + b0 * next_row(b0))
    )
    return m0, m1, m2, m3


def neighbours(parts_ref, nrows, ncols):
    row, col = lax.axis_index("rows"), lax.axis_index("cols")
    even = is_even()
    towards = jnp.where(even, 1, -1)
    lane = lax.broadcasted_iota(jnp.int32, (LANES, LANES), 1)
    vectors = []
    for vector, step_col in ((1, -1), (5, 1)):
        for step_row in (0, towards, -towards):
            r, c = row + step_row, col + step_col
            there = (r >= 0) & (r < nrows) & (c >= 0) & (c < ncols)
            index = jnp.where(there, r * ncols + c, 0)
            found = parts_ref[index, :, pl.ds(vector * LANES, LANES)]
            vectors.append(jnp.where(there, found, 0.0))
    vectors.append(jnp.zeros((LANES - len(vectors), LANES), jnp.float32))
    columns = jnp.concatenate(vectors, axis=0).T
    sides = []
    for begin, target in ((0, 0), (3, LANES - 1)):
        own, near, far = (
            jnp.where(lane == target, pltpu.roll(columns, (target - begin - k) % LANES, 1), 0.0) for k in range(3)
        )
        near = jnp.where(even, near[:REACH], near[LANES - REACH :])
        far = jnp.where(even, far[LANES - REACH :], far[:REACH])
        sides.append(jnp.concatenate([own, near, far], axis=0))
    return sides


def guard_rows(f_ref, w_ref, narrow_ref, near_ref, at_cols):
    rows = f_ref.shape[0]
    even = is_even()
    top = f_ref[pl.ds(0, 1), at_cols] * w_ref[pl.ds(0, 1), at_cols]
    bottom = f_ref[pl.ds(rows - 1, 1), at_cols] * w_ref[pl.ds(rows - 1, 1), at_cols]
    near = jnp.where(even, near_ref[pl.ds(2 * REACH, 1), at_cols], near_ref[pl.ds(2 * REACH + 7, 1), at_cols])
    far = narrow_ref[pl.ds(3, 1), at_cols]
    return (
        (jnp.where(even, bottom, near), jnp.where(even, near, top)),
        (jnp.where(even, far, bottom), jnp.where(even, top, far)),
    )


def halo_fields(f_ref, w_ref, narrow_ref, near_ref, far_ref, near_v1_ref, far_v1_ref, v0_ref):
    rows, cols = f_ref.shape
    own, pad = pl.ds(0, cols), pl.ds(cols, LANES)
    v0_ref[:, pad] = jnp.zeros((REACH + 2 * NEAR, LANES), jnp.float32)
    guards = guard_rows(f_ref, w_ref, narrow_ref, near_ref, own)
    for halo_ref, v1_ref, (above, below) in zip((near_ref, far_ref), (near_v1_ref, far_v1_ref), guards):
        v0_ref[pl.ds(NEAR - 1, 1), own] = above
        v0_ref[pl.ds(NEAR + REACH, 1), own] = below
        for start in range(0, REACH, 8):
            v0_ref[pl.ds(NEAR + start, 8), own] = halo_ref[pl.ds(start, 8), :] * halo_ref[pl.ds(REACH + start, 8), :]
        for start in range(0, REACH, 8):
            _, v1_ref[pl.ds(start, 8), :] = image(v0_ref, halo_ref[pl.ds(REACH + start, 8), :], NEAR + start)


def edge_fields(side, f_ref, w_ref, narrow_ref, near_ref, far_ref, near_v1_ref, far_v1_ref, v0_ref):
    cols = f_ref.shape[1]
    at_cols, there = pl.ds(side * (cols - LANES), LANES), pl.ds(side * LANES, LANES)
    outermost = lax.broadcasted_iota(jnp.int32, (8, LANES), 1) == side * (LANES - 1)
    guards = guard_rows(f_ref, w_ref, narrow_ref, near_ref, at_cols)
    for halo_ref, v1_ref, (above, below) in zip((near_ref, far_ref), (near_v1_ref, far_v1_ref), guards):
        v0_ref[pl.ds(NEAR - 1, 1), :] = above
        v0_ref[pl.ds(NEAR + REACH, 1), :] = below
        for start in range(0, REACH, 8):
            at, weight_at = pl.ds(start, 8), pl.ds(REACH + start, 8)
            v0_ref[pl.ds(NEAR + start, 8), :] = halo_ref[at, at_cols] * halo_ref[weight_at, at_cols]
        for start in range(0, REACH, 8):
            here = v0_ref[pl.ds(NEAR + start, 8), :]
            inner = pltpu.roll(here, 1 if side else LANES - 1, 1)
            outer = jnp.where(outermost, 0.0, pltpu.roll(here, LANES - 1 if side else 1, 1))
            beside = v0_ref[pl.ds(NEAR + start - 1, 8), :] + v0_ref[pl.ds(NEAR + start + 1, 8), :] + inner + outer
            weight = halo_ref[pl.ds(REACH + start, 8), at_cols]
            v1_ref[pl.ds(start, 8), there] = weight * here + smooth_weight * (4.0 * here - beside)


def regions(f_ref, w_ref, v1_ref, near_ref, near_v1_ref, far_ref, far_v1_ref, step):
    for start in range(0, f_ref.shape[0], step):
        yield start, (f_ref, start), (w_ref, start), (v1_ref, start)
    for base, halo_ref, field_ref in ((f_ref.shape[0], near_ref, near_v1_ref), (f_ref.shape[0] + REACH, far_ref, far_v1_ref)):
        for start in range(0, REACH, step):
            yield base + start, (halo_ref, start), (halo_ref, REACH + start), (field_ref, start)


def dot(left, right):
    return jnp.dot(left, right, preferred_element_type=jnp.float32)


def row_pass(rowtaps_ref, high, low, rows):
    table = rowtaps_ref[...]
    both = dot(table, high)
    return both[:rows] + (both[rows:] + dot(table[:rows], low))


def edges_kernel(
    nrows, ncols, parts_ref, f_ref, w_ref, v1_ref, narrow_ref, near_ref, far_ref, rowtaps_ref,
    coefficients_ref, left_ref, right_ref, other_ref, one_ref, near_v1_ref, far_v1_ref, v0_ref, high_ref, low_ref,
):
    rows, cols = f_ref.shape
    for side in range(2):
        edge_fields(side, f_ref, w_ref, narrow_ref, near_ref, far_ref, near_v1_ref, far_v1_ref, v0_ref)
    c0, c1 = coefficients(*coupled(parts_ref, nrows, ncols))
    coefficients_ref[pl.ds(0, 8), :] = jnp.broadcast_to(c0, (8, LANES))
    coefficients_ref[pl.ds(8, 8), :] = jnp.broadcast_to(c1, (8, LANES))
    sides = neighbours(parts_ref, nrows, ncols)
    left_ref[...], right_ref[...] = sides

    step = 16
    fields = (f_ref, w_ref, v1_ref, near_ref, near_v1_ref, far_ref, far_v1_ref)
    for side, begin in enumerate((0, cols - LANES)):
        at_cols = pl.ds(begin, LANES)
        for start, (flux_ref, flux_row), (weight_ref, weight_row), (field_ref, field_row) in regions(*fields, step):
            flux, weight = flux_ref[pl.ds(flux_row, step), at_cols], weight_ref[pl.ds(weight_row, step), at_cols]
            v1_cols = at_cols if start < rows else pl.ds(side * LANES, LANES)
            v1 = field_ref[pl.ds(field_row, step), v1_cols]
            v1 = v1 - smooth_weight * sides[side][start : start + step]
            scatter = flux - (c0 * (flux * weight) + c1 * v1)
            high, low = split_values(scatter * scatter)
            high_ref[pl.ds(start, step), pl.ds(side * LANES, LANES)] = high
            low_ref[pl.ds(start, step), pl.ds(side * LANES, LANES)] = low
    passed = row_pass(rowtaps_ref, high_ref[...], low_ref[...], rows)
    upper, lower = slice(0, rows // 2), slice(rows // 2, rows)
    first, last = passed[:, :LANES], passed[:, LANES:]
    on_left = lax.broadcasted_iota(jnp.int32, (rows // 2, LANES), 1) < REACH
    first = jnp.where(on_left, first[upper], pltpu.roll(first[lower], REACH, 1))
    last = jnp.where(on_left, pltpu.roll(last[upper], REACH, 1), last[lower])
    even = is_even("cols")
    one_ref[...] = jnp.where(even, last, first)
    other_ref[...] = jnp.where(even, first, last)


def main_kernel(
    coefficients_ref, left_ref, right_ref, f_ref, w_ref, v1_ref, narrow_ref, near_ref, far_ref, rowtaps_ref, coltaps_ref,
    background_ref, rms_ref, sides_ref, near_v1_ref, far_v1_ref, v0_ref, high_ref, low_ref,
):
    rows, cols = f_ref.shape
    halo_fields(f_ref, w_ref, narrow_ref, near_ref, far_ref, near_v1_ref, far_v1_ref, v0_ref)
    c0, c1 = coefficients_ref[pl.ds(0, 1), pl.ds(0, 1)], coefficients_ref[pl.ds(8, 1), pl.ds(0, 1)]
    step = 16
    fields = (f_ref, w_ref, v1_ref, near_ref, near_v1_ref, far_ref, far_v1_ref)
    for start, *sources in regions(*fields, step):
        flux, weight, v1 = (ref[pl.ds(row, step), :] for ref, row in sources)
        at = pl.ds(start, step)
        v1 = jnp.concatenate(
            [
                v1[:, :LANES] - smooth_weight * left_ref[at, :],
                v1[:, LANES : cols - LANES],
                v1[:, cols - LANES :] - smooth_weight * right_ref[at, :],
            ],
            axis=1,
        )
        background = c0 * (flux * weight) + c1 * v1
        if start < rows:
            background_ref[at, :] = background
        scatter = flux - background
        high_ref[at, :], low_ref[at, :] = split_values(scatter * scatter)
    passed = row_pass(rowtaps_ref, high_ref[...], low_ref[...], rows)
    sides_ref[:, pl.ds(0, 2 * LANES)] = passed[:, : 2 * LANES]
    sides_ref[:, pl.ds(2 * LANES, 2 * LANES)] = passed[:, cols - 2 * LANES :]
    high, low = split_values(pltpu.roll(passed, REACH, 1))
    for j in range(1, cols // LANES - 1):
        at = slice(j * LANES, j * LANES + 2 * LANES)
        rms_ref[:, pl.ds(j * LANES, LANES)] = column_pass(coltaps_ref[0], high[:, at], low[:, at])


def column_pass(table, high, low):
    both = dot(high, table)
    smoothed = both[:, :LANES] + (both[:, LANES:] + dot(low, table[:, :LANES]))
    return jnp.sqrt(smoothed + 1e-06)


def final_kernel(rms_in_ref, sides_ref, other_ref, one_ref, coltaps_ref, rms_ref, blocks_ref, sems):
    rows, cols = rms_ref.shape
    del rms_in_ref
    _, _, first_col, last_col = at_edges()
    even = is_even("cols")
    left = jnp.where(even, other_ref[...], one_ref[...])
    right = jnp.where(even, one_ref[...], other_ref[...])
    left = jnp.concatenate([pltpu.roll(left, REACH, 1), left], axis=0)
    right = jnp.concatenate([right, pltpu.roll(right, REACH, 1)], axis=0)
    sides = sides_ref[...]
    windows = (
        pltpu.roll(jnp.concatenate([left, sides[:, : 2 * LANES]], axis=1), 3 * LANES - REACH, 1)[:, : 2 * LANES],
        pltpu.roll(jnp.concatenate([sides[:, 2 * LANES :], right], axis=1), 3 * LANES - REACH, 1)[:, : 2 * LANES],
    )
    copies = []
    for side, which in enumerate((first_col.astype(jnp.int32), 2 * last_col.astype(jnp.int32))):
        high, low = split_values(windows[side])
        blocks_ref[side] = column_pass(coltaps_ref[which], high, low)
        target = rms_ref.at[:, pl.ds(side * (cols - LANES), LANES)]
        copies.append(pltpu.make_async_copy(blocks_ref.at[side], target, sems.at[side]))
        copies[-1].start()
    for copy in copies:
        copy.wait()


def swap(block, axis, first):
    count = lax.axis_size(axis)
    pairs = [(i, i + 1) for i in range(first, count - 1, 2)]
    return lax.ppermute(block, axis, pairs + [(j, i) for i, j in pairs])


def call(kernel, name, outs, scratch=(), limit=16, in_place=False):
    vmem = pl.BlockSpec(memory_space=pltpu.VMEM)
    there = pl.BlockSpec(memory_space=pl.ANY)

    def run(*args):
        return pl.pallas_call(
            kernel,
            out_shape=tuple(jax.ShapeDtypeStruct(shape, jnp.float32) for shape in outs),
            in_specs=[there if in_place and i == 0 else vmem for i in range(len(args))],
            out_specs=(there if in_place else vmem,) * len(outs),
            scratch_shapes=list(scratch),
            input_output_aliases={0: 0} if in_place else {},
            compiler_params=pltpu.CompilerParams(vmem_limit_bytes=limit << 20),
            name=name,
        )(*args)

    return run


def shards(coadd_flux, inverse_variance, source_mask):
    rows, cols = coadd_flux.shape
    nrows, ncols = lax.axis_size("rows"), lax.axis_size("cols")
    message = (VECTORS + 1) * LANES

    def scratch(*shape, dtype=jnp.float32):
        return pltpu.VMEM(shape, dtype)

    taken = []
    for above, below in ((0, rows - 1), (1, rows - 2), (REACH, rows - 1 - REACH)):
        start = (jnp.where(is_even(), above, below), 0)
        flux, variance, mask = (
            lax.dynamic_slice(x, start, (1, cols)) for x in (coadd_flux, inverse_variance, source_mask)
        )
        taken.append((flux, weights(variance, mask)))
    products = [flux * weight for flux, weight in taken]
    narrow = swap(jnp.concatenate([products[0], products[1], taken[0][1], products[2]]), "rows", 1)

    own = (coadd_flux, weights(inverse_variance, source_mask))
    field = scratch(rows + 2 * NEAR, cols + LANES)
    to_near, to_far, base = call(
        prepare_kernel, "prepare", ((2 * REACH + 8, cols), (2 * REACH, cols), (rows, cols)), (field,)
    )(*own)
    to_near, to_far, narrow = lax.optimization_barrier((to_near, to_far, narrow))
    near = swap(to_near, "rows", 0)
    far = swap(to_far, "rows", 1)

    devices = nrows * ncols
    parts, own_v1 = call(
        moments_kernel,
        "moments",
        ((devices * (VECTORS + 1), LANES), (rows, cols)),
        (field, scratch(rows, LANES)),
    )(*own, base, narrow, near)
    parts = lax.all_to_all(parts.reshape(devices, 1, message), ("rows", "cols"), 0, 0, tiled=True)
    first_row, last_row, _, _ = at_edges()
    kind = jnp.where(is_even(), first_row.astype(jnp.int32), 2 + last_row.astype(jnp.int32))
    row_taps = lax.dynamic_index_in_dim(jnp.asarray(row_tables(rows)), kind, keepdims=False)
    col_taps = jnp.asarray(col_tables())
    reached, packed = rows + 2 * REACH, (rows // 2, LANES)
    fields = (*own, own_v1, narrow, near, far)
    halves = (scratch(REACH, 2 * LANES),) * 2
    numbers, left, right, to_other, to_one = call(
        functools.partial(edges_kernel, nrows, ncols),
        "edges",
        ((16, LANES), (reached, LANES), (reached, LANES), packed, packed),
        halves + (scratch(REACH + 2 * NEAR, LANES),) + (scratch(reached, 2 * LANES, dtype=jnp.bfloat16),) * 2,
    )(parts, *fields, row_taps)
    other = swap(to_other, "cols", 1)
    one = swap(to_one, "cols", 0)
    halves = (scratch(REACH, cols),) * 2
    background, rms, sides = call(
        main_kernel,
        "main",
        ((rows, cols), (rows, cols), (rows, 4 * LANES)),
        halves + (scratch(REACH + 2 * NEAR, cols + LANES),) + (scratch(reached, cols, dtype=jnp.bfloat16),) * 2,
    )(numbers, left, right, *fields, row_taps, col_taps)
    (rms,) = call(
        final_kernel, "final", ((rows, cols),), (scratch(2, rows, LANES), pltpu.SemaphoreType.DMA((2,))), in_place=True
    )(rms, sides, other, one, col_taps)
    return background, rms


def solution(mesh):
    return jax.shard_map(
        shards,
        mesh=mesh,
        in_specs=(P("rows", "cols"), P("rows", "cols"), P("rows", "cols")),
        out_specs=(P("rows", "cols"), P("rows", "cols")),
        check_vma=False,
    )
```

```python
import functools

import jax
import jax.numpy as jnp
import ml_dtypes
import numpy as np
from jax import lax
from jax.experimental import pallas as pl
from jax.experimental.pallas import tpu as pltpu
from jax.sharding import PartitionSpec as P

RADIUS = 32
REACH = 2 * RADIUS
LANES = 128
WIDE = REACH + 8
NEAR = 8
VECTORS = 8

smooth_weight = 2.0
blur_sigma = 10.0


def squared_taps(length, first, last):
    offsets = np.arange(2 * RADIUS + 1) - RADIUS
    taps = np.exp(-offsets * offsets / (2.0 * blur_sigma * blur_sigma))
    taps = taps / taps.sum()

    def band(count):
        table = np.zeros((count, count + 2 * RADIUS))
        for k in range(2 * RADIUS + 1):
            table[np.arange(count), np.arange(count) + k] = taps[k]
        return table

    inner = band(length + 2 * RADIUS)
    if first:
        inner[:RADIUS] = 0.0
    if last:
        inner[-RADIUS:] = 0.0
    return band(length) @ inner


def split(table):
    high = table.astype(np.float32).astype(ml_dtypes.bfloat16)
    low = (table - high.astype(np.float64)).astype(np.float32).astype(ml_dtypes.bfloat16)
    return high, low


def row_tables(length):
    tables = []
    for first, last, odd in ((False, False, False), (True, False, False), (False, False, True), (False, True, True)):
        table = squared_taps(length, first, last)
        above, own, below = table[:, :REACH], table[:, REACH : REACH + length], table[:, REACH + length :]
        near, far = (above, below) if odd else (below, above)
        if first or last:
            far = np.zeros_like(far)
        tables.append(np.concatenate(split(np.concatenate([own, near, far], axis=1)), axis=0))
    return np.stack(tables)


def col_tables():
    tables = []
    for first, last in ((False, False), (True, False), (False, True)):
        table = squared_taps(LANES, first, last)
        if first:
            table[:, :REACH] = 0.0
        if last:
            table[:, REACH + LANES :] = 0.0
        tables.append(np.concatenate(split(table.T), axis=1))
    return np.stack(tables)


def split_values(values):
    high = values.astype(jnp.bfloat16)
    return high, (values - high.astype(jnp.float32)).astype(jnp.bfloat16)


def at_edges():
    row, col = lax.axis_index("rows"), lax.axis_index("cols")
    return (
        row == 0,
        row == lax.axis_size("rows") - 1,
        col == 0,
        col == lax.axis_size("cols") - 1,
    )


def is_even(axis="rows"):
    return lax.axis_index(axis) % 2 == 0


def beside_columns(field):
    width = field.shape[1]
    return pltpu.roll(field, 1, 1) + pltpu.roll(field, width - 1, 1)


def weights(inverse_variance, source_mask):
    return inverse_variance * (1.0 - source_mask.astype(jnp.float32))


def coefficients(m0, m1, m2, m3):
    alpha0 = m0 / m1
    norm1 = jnp.maximum(m0 - 2.0 * alpha0 * m1 + alpha0 * alpha0 * m2, 0.0)
    grown = 1.0 + norm1 / m0
    image1 = grown * grown * m1 - 2.0 * grown * alpha0 * m2 + alpha0 * alpha0 * m3
    alpha1 = jnp.where(image1 > 0.0, norm1 / image1, 0.0)
    return alpha0 + alpha1 * grown, -alpha1 * alpha0


def image(ref, weight, start):
    cols = weight.shape[1]
    own = pl.ds(0, cols)
    here = ref[pl.ds(start, 8), :]
    beside = ref[pl.ds(start - 1, 8), own] + ref[pl.ds(start + 1, 8), own] + beside_columns(here)[:, :cols]
    here = here[:, :cols]
    return here, weight * here + smooth_weight * (4.0 * here - beside)


def prepare_kernel(f_ref, w_ref, near_ref, far_ref, v1_ref, v0_ref):
    rows = f_ref.shape[0]

    def write(out_ref, begin):
        out_ref[pl.ds(0, REACH), :] = f_ref[pl.ds(begin, REACH), :]
        out_ref[pl.ds(REACH, REACH), :] = w_ref[pl.ds(begin, REACH), :]

    def near_product(begin):
        near_ref[pl.ds(2 * REACH, 8), :] = f_ref[pl.ds(begin, 8), :] * w_ref[pl.ds(begin, 8), :]

    @pl.when(is_even())
    def _():
        write(near_ref, rows - REACH)
        near_product(rows - WIDE)
        write(far_ref, 0)

    @pl.when(jnp.logical_not(is_even()))
    def _():
        write(near_ref, 0)
        near_product(REACH)
        write(far_ref, rows - REACH)

    cols = f_ref.shape[1]
    own = pl.ds(0, cols)
    v0_ref[:, pl.ds(cols, LANES)] = jnp.zeros((rows + 2 * NEAR, LANES), jnp.float32)
    for start in (0, NEAR + rows):
        v0_ref[pl.ds(start, NEAR), own] = jnp.zeros((NEAR, cols), jnp.float32)
    for start in range(0, rows, 8):
        at = pl.ds(start, 8)
        v0_ref[pl.ds(NEAR + start, 8), own] = f_ref[at, :] * w_ref[at, :]
    for start in range(0, rows, 8):
        _, v1_ref[pl.ds(start, 8), :] = image(v0_ref, w_ref[pl.ds(start, 8), :], NEAR + start)


def moments_kernel(f_ref, w_ref, base_ref, narrow_ref, near_ref, out_ref, v1_out_ref, v1_ref, edge_ref):
    rows, cols = f_ref.shape
    first_row, last_row, _, _ = at_edges()
    even = is_even()
    own, pad = pl.ds(0, cols), pl.ds(cols, LANES)

    def near_rows(nearest, second):
        return (
            near_ref[pl.ds(nearest, 1), :] * near_ref[pl.ds(REACH + nearest, 1), :],
            near_ref[pl.ds(second, 1), :] * near_ref[pl.ds(REACH + second, 1), :],
            near_ref[pl.ds(REACH + nearest, 1), :],
        )

    outermost = first_row | last_row
    far_rows = tuple(jnp.where(outermost, 0.0, narrow_ref[pl.ds(k, 1), :]) for k in range(3))
    above = [jnp.where(even, far, near) for far, near in zip(far_rows, near_rows(REACH - 1, REACH - 2))]
    below = [jnp.where(even, near, far) for far, near in zip(far_rows, near_rows(0, 1))]

    v1_ref[:, pad] = jnp.zeros((rows + 2 * NEAR, LANES), jnp.float32)
    for start in (0, NEAR + rows):
        v1_ref[pl.ds(start, NEAR), own] = jnp.zeros((NEAR, cols), jnp.float32)
    row = lax.broadcasted_iota(jnp.int32, (8, cols), 0)
    for start in range(0, rows, 8):
        v1 = base_ref[pl.ds(start, 8), :]
        if start == 0:
            v1 = v1 - jnp.where(row == 0, smooth_weight * above[0], 0.0)
        if start == rows - 8:
            v1 = v1 - jnp.where(row == 7, smooth_weight * below[0], 0.0)
        v1_ref[pl.ds(NEAR + start, 8), own] = v1
        v1_out_ref[pl.ds(start, 8), :] = v1

    def edge_row(halo, inner, at):
        nearest, second, weight = halo
        inner = f_ref[pl.ds(inner, 1), :] * w_ref[pl.ds(inner, 1), :]
        padded = jnp.concatenate([nearest, jnp.zeros((1, LANES), jnp.float32)], axis=1)
        beside = second + inner + beside_columns(padded)[:, :cols]
        v1_ref[pl.ds(at, 1), own] = weight * nearest + smooth_weight * (4.0 * nearest - beside)

    pl.when(jnp.logical_not(first_row))(lambda: edge_row(above, 0, NEAR - 1))
    pl.when(jnp.logical_not(last_row))(lambda: edge_row(below, rows - 1, NEAR + rows))

    lane = lax.broadcasted_iota(jnp.int32, (8, LANES), 1)
    sums = [jnp.zeros((8, cols), jnp.float32) for _ in range(4)]
    for start in range(0, rows, 8):
        weight = w_ref[pl.ds(start, 8), :]
        v0 = f_ref[pl.ds(start, 8), :] * weight
        v1, v2 = image(v1_ref, weight, NEAR + start)
        sums = [total + term for total, term in zip(sums, (v0 * v0, v0 * v1, v1 * v1, v1 * v2))]
        edges = jnp.zeros((8, LANES), jnp.float32)
        for k, field in enumerate((v0, v1, v2, weight)):
            edges = jnp.where(lane == k, pltpu.roll(field[:, cols - LANES :], k + 1, 1), edges)
            edges = jnp.where(lane == 4 + k, pltpu.roll(field[:, :LANES], 4 + k, 1), edges)
        edge_ref[pl.ds(start, 8), :] = edges

    result = jnp.zeros((1, LANES), jnp.float32)
    for i, total in enumerate(sums):
        narrow = sum(total[:, k : k + LANES] for k in range(0, cols, LANES))
        total = jnp.sum(jnp.sum(narrow, axis=0, keepdims=True), axis=1, keepdims=True)
        result = jnp.where(lane[:1] == i, total, result)
    vectors = edge_ref[...].T
    message = [result] + [vectors[k : k + 1, :] for k in range(VECTORS)]
    copies = jnp.concatenate(message * 8, axis=0)
    for start in range(0, out_ref.shape[0], copies.shape[0]):
        out_ref[pl.ds(start, copies.shape[0]), :] = copies


def coupled(parts_ref, nrows, ncols):
    count = nrows * ncols
    lam = smooth_weight

    def part(k):
        return parts_ref[:, :, pl.ds(k * LANES, LANES)].reshape(count, LANES)

    device = lax.broadcasted_iota(jnp.int32, (count, LANES), 0)
    lane = lax.broadcasted_iota(jnp.int32, (count, LANES), 1)
    joined = device % ncols < ncols - 1
    a0, a1, ua, wa = (jnp.where(joined, part(1 + k), 0.0) for k in range(4))
    b0, b1, ub, wb = (jnp.where(joined, pltpu.roll(part(5 + k), count - 1, 0), 0.0) for k in range(4))

    def next_row(field):
        inside = pltpu.roll(field, LANES - 1, 1)
        beyond = jnp.where(device < count - ncols, pltpu.roll(inside, count - ncols, 0), 0.0)
        return jnp.where(lane == LANES - 1, beyond, inside)

    def total(field):
        return jnp.sum(jnp.sum(field, axis=0, keepdims=True), axis=1, keepdims=True)

    scalars = jnp.sum(part(0), axis=0, keepdims=True)
    m0, m1, m2, m3 = (total(jnp.where(lane[:1] == i, scalars, 0.0)) for i in range(4))
    m1 = m1 - 2.0 * lam * total(a0 * b0)
    m2 = m2 + total(lam * lam * (a0 * a0 + b0 * b0) - 2.0 * lam * (a1 * b0 + b1 * a0))
    m3 = m3 + total(
        lam * lam * ((wa + 4.0 * lam) * b0 * b0 + (wb + 4.0 * lam) * a0 * a0)
        - 2.0 * lam * (b0 * ua + a0 * ub + (a1 - lam * b0) * (b1 - lam * a0))
        - 2.0 * lam * lam * lam * (a0 * next_row(a0) + b0 * next_row(b0))
    )
    return m0, m1, m2, m3


def neighbours(parts_ref, nrows, ncols):
    row, col = lax.axis_index("rows"), lax.axis_index("cols")
    even = is_even()
    towards = jnp.where(even, 1, -1)
    lane = lax.broadcasted_iota(jnp.int32, (LANES, LANES), 1)
    vectors = []
    for vector, step_col in ((1, -1), (5, 1)):
        for step_row in (0, towards, -towards):
            r, c = row + step_row, col + step_col
            there = (r >= 0) & (r < nrows) & (c >= 0) & (c < ncols)
            index = jnp.where(there, r * ncols + c, 0)
            found = parts_ref[index, :, pl.ds(vector * LANES, LANES)]
            vectors.append(jnp.where(there, found, 0.0))
    vectors.append(jnp.zeros((LANES - len(vectors), LANES), jnp.float32))
    columns = jnp.concatenate(vectors, axis=0).T
    sides = []
    for begin, target in ((0, 0), (3, LANES - 1)):
        own, near, far = (
            jnp.where(lane == target, pltpu.roll(columns, (target - begin - k) % LANES, 1), 0.0) for k in range(3)
        )
        near = jnp.where(even, near[:REACH], near[LANES - REACH :])
        far = jnp.where(even, far[LANES - REACH :], far[:REACH])
        sides.append(jnp.concatenate([own, near, far], axis=0))
    return sides


def guard_rows(f_ref, w_ref, narrow_ref, near_ref, at_cols):
    rows = f_ref.shape[0]
    even = is_even()
    top = f_ref[pl.ds(0, 1), at_cols] * w_ref[pl.ds(0, 1), at_cols]
    bottom = f_ref[pl.ds(rows - 1, 1), at_cols] * w_ref[pl.ds(rows - 1, 1), at_cols]
    near = jnp.where(even, near_ref[pl.ds(2 * REACH, 1), at_cols], near_ref[pl.ds(2 * REACH + 7, 1), at_cols])
    far = narrow_ref[pl.ds(3, 1), at_cols]
    return (
        (jnp.where(even, bottom, near), jnp.where(even, near, top)),
        (jnp.where(even, far, bottom), jnp.where(even, top, far)),
    )


def halo_fields(f_ref, w_ref, narrow_ref, near_ref, far_ref, near_v1_ref, far_v1_ref, v0_ref):
    rows, cols = f_ref.shape
    own, pad = pl.ds(0, cols), pl.ds(cols, LANES)
    v0_ref[:, pad] = jnp.zeros((REACH + 2 * NEAR, LANES), jnp.float32)
    guards = guard_rows(f_ref, w_ref, narrow_ref, near_ref, own)
    for halo_ref, v1_ref, (above, below) in zip((near_ref, far_ref), (near_v1_ref, far_v1_ref), guards):
        v0_ref[pl.ds(NEAR - 1, 1), own] = above
        v0_ref[pl.ds(NEAR + REACH, 1), own] = below
        for start in range(0, REACH, 8):
            v0_ref[pl.ds(NEAR + start, 8), own] = halo_ref[pl.ds(start, 8), :] * halo_ref[pl.ds(REACH + start, 8), :]
        for start in range(0, REACH, 8):
            _, v1_ref[pl.ds(start, 8), :] = image(v0_ref, halo_ref[pl.ds(REACH + start, 8), :], NEAR + start)


def edge_fields(side, f_ref, w_ref, narrow_ref, near_ref, far_ref, near_v1_ref, far_v1_ref, v0_ref):
    cols = f_ref.shape[1]
    at_cols, there = pl.ds(side * (cols - LANES), LANES), pl.ds(side * LANES, LANES)
    outermost = lax.broadcasted_iota(jnp.int32, (8, LANES), 1) == side * (LANES - 1)
    guards = guard_rows(f_ref, w_ref, narrow_ref, near_ref, at_cols)
    for halo_ref, v1_ref, (above, below) in zip((near_ref, far_ref), (near_v1_ref, far_v1_ref), guards):
        v0_ref[pl.ds(NEAR - 1, 1), :] = above
        v0_ref[pl.ds(NEAR + REACH, 1), :] = below
        for start in range(0, REACH, 8):
            at, weight_at = pl.ds(start, 8), pl.ds(REACH + start, 8)
            v0_ref[pl.ds(NEAR + start, 8), :] = halo_ref[at, at_cols] * halo_ref[weight_at, at_cols]
        for start in range(0, REACH, 8):
            here = v0_ref[pl.ds(NEAR + start, 8), :]
            inner = pltpu.roll(here, 1 if side else LANES - 1, 1)
            outer = jnp.where(outermost, 0.0, pltpu.roll(here, LANES - 1 if side else 1, 1))
            beside = v0_ref[pl.ds(NEAR + start - 1, 8), :] + v0_ref[pl.ds(NEAR + start + 1, 8), :] + inner + outer
            weight = halo_ref[pl.ds(REACH + start, 8), at_cols]
            v1_ref[pl.ds(start, 8), there] = weight * here + smooth_weight * (4.0 * here - beside)


def regions(f_ref, w_ref, v1_ref, near_ref, near_v1_ref, far_ref, far_v1_ref, step):
    for start in range(0, f_ref.shape[0], step):
        yield start, (f_ref, start), (w_ref, start), (v1_ref, start)
    for base, halo_ref, field_ref in ((f_ref.shape[0], near_ref, near_v1_ref), (f_ref.shape[0] + REACH, far_ref, far_v1_ref)):
        for start in range(0, REACH, step):
            yield base + start, (halo_ref, start), (halo_ref, REACH + start), (field_ref, start)


def dot(left, right):
    return jnp.dot(left, right, preferred_element_type=jnp.float32)


def row_pass(rowtaps_ref, high, low, rows):
    table = rowtaps_ref[...]
    both = dot(table, high)
    return both[:rows] + (both[rows:] + dot(table[:rows], low))


def edges_kernel(
    nrows, ncols, parts_ref, f_ref, w_ref, v1_ref, narrow_ref, near_ref, far_ref, rowtaps_ref,
    coefficients_ref, left_ref, right_ref, one_ref, other_ref, near_v1_ref, far_v1_ref, v0_ref, high_ref, low_ref,
):
    rows, cols = f_ref.shape
    for side in range(2):
        edge_fields(side, f_ref, w_ref, narrow_ref, near_ref, far_ref, near_v1_ref, far_v1_ref, v0_ref)
    c0, c1 = coefficients(*coupled(parts_ref, nrows, ncols))
    coefficients_ref[pl.ds(0, 8), :] = jnp.broadcast_to(c0, (8, LANES))
    coefficients_ref[pl.ds(8, 8), :] = jnp.broadcast_to(c1, (8, LANES))
    sides = neighbours(parts_ref, nrows, ncols)
    left_ref[...], right_ref[...] = sides

    step = 16
    fields = (f_ref, w_ref, v1_ref, near_ref, near_v1_ref, far_ref, far_v1_ref)
    for side, begin in enumerate((0, cols - LANES)):
        at_cols = pl.ds(begin, LANES)
        for start, (flux_ref, flux_row), (weight_ref, weight_row), (field_ref, field_row) in regions(*fields, step):
            flux, weight = flux_ref[pl.ds(flux_row, step), at_cols], weight_ref[pl.ds(weight_row, step), at_cols]
            v1_cols = at_cols if start < rows else pl.ds(side * LANES, LANES)
            v1 = field_ref[pl.ds(field_row, step), v1_cols]
            v1 = v1 - smooth_weight * sides[side][start : start + step]
            scatter = flux - (c0 * (flux * weight) + c1 * v1)
            high, low = split_values(scatter * scatter)
            high_ref[pl.ds(start, step), pl.ds(side * LANES, LANES)] = high
            low_ref[pl.ds(start, step), pl.ds(side * LANES, LANES)] = low
    passed = row_pass(rowtaps_ref, high_ref[...], low_ref[...], rows)
    upper, lower = slice(0, rows // 2), slice(rows // 2, rows)
    first, last = passed[:, :LANES], passed[:, LANES:]
    on_left = lax.broadcasted_iota(jnp.int32, (rows // 2, LANES), 1) < REACH
    first = jnp.where(on_left, first[upper], pltpu.roll(first[lower], REACH, 1))
    last = jnp.where(on_left, pltpu.roll(last[upper], REACH, 1), last[lower])
    even = is_even("cols")
    one_ref[...] = jnp.where(even, last, first)
    other_ref[...] = jnp.where(even, first, last)


def main_kernel(
    coefficients_ref, left_ref, right_ref, f_ref, w_ref, v1_ref, narrow_ref, near_ref, far_ref, rowtaps_ref, coltaps_ref,
    background_ref, rms_ref, sides_ref, near_v1_ref, far_v1_ref, v0_ref, high_ref, low_ref,
):
    rows, cols = f_ref.shape
    halo_fields(f_ref, w_ref, narrow_ref, near_ref, far_ref, near_v1_ref, far_v1_ref, v0_ref)
    c0, c1 = coefficients_ref[pl.ds(0, 1), pl.ds(0, 1)], coefficients_ref[pl.ds(8, 1), pl.ds(0, 1)]
    step = 16
    fields = (f_ref, w_ref, v1_ref, near_ref, near_v1_ref, far_ref, far_v1_ref)
    for start, *sources in regions(*fields, step):
        flux, weight, v1 = (ref[pl.ds(row, step), :] for ref, row in sources)
        at = pl.ds(start, step)
        v1 = jnp.concatenate(
            [
                v1[:, :LANES] - smooth_weight * left_ref[at, :],
                v1[:, LANES : cols - LANES],
                v1[:, cols - LANES :] - smooth_weight * right_ref[at, :],
            ],
            axis=1,
        )
        background = c0 * (flux * weight) + c1 * v1
        if start < rows:
            background_ref[at, :] = background
        scatter = flux - background
        high_ref[at, :], low_ref[at, :] = split_values(scatter * scatter)
    passed = row_pass(rowtaps_ref, high_ref[...], low_ref[...], rows)
    sides_ref[:, pl.ds(0, 2 * LANES)] = passed[:, : 2 * LANES]
    sides_ref[:, pl.ds(2 * LANES, 2 * LANES)] = passed[:, cols - 2 * LANES :]
    high, low = split_values(pltpu.roll(passed, REACH, 1))
    for j in range(1, cols // LANES - 1):
        at = slice(j * LANES, j * LANES + 2 * LANES)
        rms_ref[:, pl.ds(j * LANES, LANES)] = column_pass(coltaps_ref[0], high[:, at], low[:, at])


def column_pass(table, high, low):
    both = dot(high, table)
    smoothed = both[:, :LANES] + (both[:, LANES:] + dot(low, table[:, :LANES]))
    return jnp.sqrt(smoothed + 1e-06)


def final_kernel(rms_in_ref, sides_ref, one_ref, other_ref, coltaps_ref, rms_ref, blocks_ref, sems):
    rows, cols = rms_ref.shape
    del rms_in_ref
    _, _, first_col, last_col = at_edges()
    even = is_even("cols")
    left = jnp.where(even, other_ref[...], one_ref[...])
    right = jnp.where(even, one_ref[...], other_ref[...])
    left = jnp.concatenate([pltpu.roll(left, REACH, 1), left], axis=0)
    right = jnp.concatenate([right, pltpu.roll(right, REACH, 1)], axis=0)
    sides = sides_ref[...]
    windows = (
        pltpu.roll(jnp.concatenate([left, sides[:, : 2 * LANES]], axis=1), 3 * LANES - REACH, 1)[:, : 2 * LANES],
        pltpu.roll(jnp.concatenate([sides[:, 2 * LANES :], right], axis=1), 3 * LANES - REACH, 1)[:, : 2 * LANES],
    )
    copies = []
    for side, which in enumerate((first_col.astype(jnp.int32), 2 * last_col.astype(jnp.int32))):
        high, low = split_values(windows[side])
        blocks_ref[side] = column_pass(coltaps_ref[which], high, low)
        target = rms_ref.at[:, pl.ds(side * (cols - LANES), LANES)]
        copies.append(pltpu.make_async_copy(blocks_ref.at[side], target, sems.at[side]))
        copies[-1].start()
    for copy in copies:
        copy.wait()


def swap(block, axis, first):
    count = lax.axis_size(axis)
    partner = list(range(count))
    for i in range(first, count - 1, 2):
        partner[i], partner[i + 1] = i + 1, i
    return lax.ppermute(block, axis, list(enumerate(partner)))


def call(kernel, name, outs, scratch=(), limit=16, in_place=False):
    vmem = pl.BlockSpec(memory_space=pltpu.VMEM)
    there = pl.BlockSpec(memory_space=pl.ANY)

    def run(*args):
        return pl.pallas_call(
            kernel,
            out_shape=tuple(jax.ShapeDtypeStruct(shape, jnp.float32) for shape in outs),
            in_specs=[there if in_place and i == 0 else vmem for i in range(len(args))],
            out_specs=(there if in_place else vmem,) * len(outs),
            scratch_shapes=list(scratch),
            input_output_aliases={0: 0} if in_place else {},
            compiler_params=pltpu.CompilerParams(vmem_limit_bytes=limit << 20),
            name=name,
        )(*args)

    return run


def shards(coadd_flux, inverse_variance, source_mask):
    rows, cols = coadd_flux.shape
    nrows, ncols = lax.axis_size("rows"), lax.axis_size("cols")
    message = (VECTORS + 1) * LANES

    def scratch(*shape, dtype=jnp.float32):
        return pltpu.VMEM(shape, dtype)

    taken = []
    for above, below in ((0, rows - 1), (1, rows - 2), (REACH, rows - 1 - REACH)):
        start = (jnp.where(is_even(), above, below), 0)
        flux, variance, mask = (
            lax.dynamic_slice(x, start, (1, cols)) for x in (coadd_flux, inverse_variance, source_mask)
        )
        taken.append((flux, weights(variance, mask)))
    products = [flux * weight for flux, weight in taken]
    narrow = swap(jnp.concatenate([products[0], products[1], taken[0][1], products[2]]), "rows", 1)

    own = (coadd_flux, weights(inverse_variance, source_mask))
    field = scratch(rows + 2 * NEAR, cols + LANES)
    to_near, to_far, base = call(
        prepare_kernel, "prepare", ((2 * REACH + 8, cols), (2 * REACH, cols), (rows, cols)), (field,)
    )(*own)
    to_near, to_far, narrow = lax.optimization_barrier((to_near, to_far, narrow))
    near = swap(to_near, "rows", 0)
    far = swap(to_far, "rows", 1)

    devices = nrows * ncols
    parts, own_v1 = call(
        moments_kernel,
        "moments",
        ((devices * (VECTORS + 1), LANES), (rows, cols)),
        (field, scratch(rows, LANES)),
    )(*own, base, narrow, near)
    parts = lax.all_to_all(parts.reshape(devices, 1, message), ("rows", "cols"), 0, 0, tiled=True)
    first_row, last_row, _, _ = at_edges()
    kind = jnp.where(is_even(), first_row.astype(jnp.int32), 2 + last_row.astype(jnp.int32))
    row_taps = lax.dynamic_index_in_dim(jnp.asarray(row_tables(rows)), kind, keepdims=False)
    col_taps = jnp.asarray(col_tables())
    reached, packed = rows + 2 * REACH, (rows // 2, LANES)
    fields = (*own, own_v1, narrow, near, far)
    halves = (scratch(REACH, 2 * LANES),) * 2
    numbers, left, right, to_one, to_other = call(
        functools.partial(edges_kernel, nrows, ncols),
        "edges",
        ((16, LANES), (reached, LANES), (reached, LANES), packed, packed),
        halves + (scratch(REACH + 2 * NEAR, LANES),) + (scratch(reached, 2 * LANES, dtype=jnp.bfloat16),) * 2,
    )(parts, *fields, row_taps)
    one = swap(to_one, "cols", 0)
    other = swap(to_other, "cols", 1)
    halves = (scratch(REACH, cols),) * 2
    background, rms, sides = call(
        main_kernel,
        "main",
        ((rows, cols), (rows, cols), (rows, 4 * LANES)),
        halves + (scratch(REACH + 2 * NEAR, cols + LANES),) + (scratch(reached, cols, dtype=jnp.bfloat16),) * 2,
    )(numbers, left, right, *fields, row_taps, col_taps)
    (rms,) = call(
        final_kernel, "final", ((rows, cols),), (scratch(2, rows, LANES), pltpu.SemaphoreType.DMA((2,))), in_place=True
    )(rms, sides, one, other, col_taps)
    return background, rms


def solution(mesh):
    return jax.shard_map(
        shards,
        mesh=mesh,
        in_specs=(P("rows", "cols"), P("rows", "cols"), P("rows", "cols")),
        out_specs=(P("rows", "cols"), P("rows", "cols")),
        check_vma=False,
    )
```

```python
import functools

import jax
import jax.numpy as jnp
import ml_dtypes
import numpy as np
from jax import lax
from jax.experimental import pallas as pl
from jax.experimental.pallas import tpu as pltpu
from jax.sharding import PartitionSpec as P

RADIUS = 32
REACH = 2 * RADIUS
LANES = 128
WIDE = REACH + 8
NEAR = 8
VECTORS = 8

smooth_weight = 2.0
blur_sigma = 10.0


def squared_taps(length, first, last):
    offsets = np.arange(2 * RADIUS + 1) - RADIUS
    taps = np.exp(-offsets * offsets / (2.0 * blur_sigma * blur_sigma))
    taps = taps / taps.sum()

    def band(count):
        table = np.zeros((count, count + 2 * RADIUS))
        for k in range(2 * RADIUS + 1):
            table[np.arange(count), np.arange(count) + k] = taps[k]
        return table

    inner = band(length + 2 * RADIUS)
    if first:
        inner[:RADIUS] = 0.0
    if last:
        inner[-RADIUS:] = 0.0
    return band(length) @ inner


def split(table):
    high = table.astype(np.float32).astype(ml_dtypes.bfloat16)
    low = (table - high.astype(np.float64)).astype(np.float32).astype(ml_dtypes.bfloat16)
    return high, low


def row_tables(length):
    tables = []
    for first, last, odd in ((False, False, False), (True, False, False), (False, False, True), (False, True, True)):
        table = squared_taps(length, first, last)
        above, own, below = table[:, :REACH], table[:, REACH : REACH + length], table[:, REACH + length :]
        near, far = (above, below) if odd else (below, above)
        if first or last:
            far = np.zeros_like(far)
        tables.append(np.concatenate(split(np.concatenate([own, near, far], axis=1)), axis=0))
    return np.stack(tables)


def col_tables():
    tables = []
    for first, last in ((False, False), (True, False), (False, True)):
        table = squared_taps(LANES, first, last)
        if first:
            table[:, :REACH] = 0.0
        if last:
            table[:, REACH + LANES :] = 0.0
        tables.append(np.concatenate(split(table.T), axis=1))
    return np.stack(tables)


def split_values(values):
    high = values.astype(jnp.bfloat16)
    return high, (values - high.astype(jnp.float32)).astype(jnp.bfloat16)


def at_edges():
    row, col = lax.axis_index("rows"), lax.axis_index("cols")
    return (
        row == 0,
        row == lax.axis_size("rows") - 1,
        col == 0,
        col == lax.axis_size("cols") - 1,
    )


def is_even(axis="rows"):
    return lax.axis_index(axis) % 2 == 0


def beside_columns(field):
    width = field.shape[1]
    return pltpu.roll(field, 1, 1) + pltpu.roll(field, width - 1, 1)


def weights(inverse_variance, source_mask):
    return inverse_variance * (1.0 - source_mask.astype(jnp.float32))


def coefficients(m0, m1, m2, m3):
    alpha0 = m0 / m1
    norm1 = jnp.maximum(m0 - 2.0 * alpha0 * m1 + alpha0 * alpha0 * m2, 0.0)
    grown = 1.0 + norm1 / m0
    image1 = grown * grown * m1 - 2.0 * grown * alpha0 * m2 + alpha0 * alpha0 * m3
    alpha1 = jnp.where(image1 > 0.0, norm1 / image1, 0.0)
    return alpha0 + alpha1 * grown, -alpha1 * alpha0


def image(ref, weight, start):
    cols = weight.shape[1]
    own = pl.ds(0, cols)
    here = ref[pl.ds(start, 8), :]
    beside = ref[pl.ds(start - 1, 8), own] + ref[pl.ds(start + 1, 8), own] + beside_columns(here)[:, :cols]
    here = here[:, :cols]
    return here, weight * here + smooth_weight * (4.0 * here - beside)


def prepare_kernel(f_ref, w_ref, near_ref, far_ref, v1_ref, v0_ref):
    rows = f_ref.shape[0]

    def write(out_ref, begin):
        out_ref[pl.ds(0, REACH), :] = f_ref[pl.ds(begin, REACH), :]
        out_ref[pl.ds(REACH, REACH), :] = w_ref[pl.ds(begin, REACH), :]

    def near_product(begin):
        near_ref[pl.ds(2 * REACH, 8), :] = f_ref[pl.ds(begin, 8), :] * w_ref[pl.ds(begin, 8), :]

    @pl.when(is_even())
    def _():
        write(near_ref, rows - REACH)
        near_product(rows - WIDE)
        write(far_ref, 0)

    @pl.when(jnp.logical_not(is_even()))
    def _():
        write(near_ref, 0)
        near_product(REACH)
        write(far_ref, rows - REACH)

    cols = f_ref.shape[1]
    own = pl.ds(0, cols)
    v0_ref[:, pl.ds(cols, LANES)] = jnp.zeros((rows + 2 * NEAR, LANES), jnp.float32)
    for start in (0, NEAR + rows):
        v0_ref[pl.ds(start, NEAR), own] = jnp.zeros((NEAR, cols), jnp.float32)
    for start in range(0, rows, 8):
        at = pl.ds(start, 8)
        v0_ref[pl.ds(NEAR + start, 8), own] = f_ref[at, :] * w_ref[at, :]
    for start in range(0, rows, 8):
        _, v1_ref[pl.ds(start, 8), :] = image(v0_ref, w_ref[pl.ds(start, 8), :], NEAR + start)


def moments_kernel(f_ref, w_ref, base_ref, narrow_ref, near_ref, out_ref, v1_out_ref, v1_ref, edge_ref):
    rows, cols = f_ref.shape
    first_row, last_row, _, _ = at_edges()
    even = is_even()
    own, pad = pl.ds(0, cols), pl.ds(cols, LANES)

    def near_rows(nearest, second):
        return (
            near_ref[pl.ds(nearest, 1), :] * near_ref[pl.ds(REACH + nearest, 1), :],
            near_ref[pl.ds(second, 1), :] * near_ref[pl.ds(REACH + second, 1), :],
            near_ref[pl.ds(REACH + nearest, 1), :],
        )

    outermost = first_row | last_row
    far_rows = tuple(jnp.where(outermost, 0.0, narrow_ref[pl.ds(k, 1), :]) for k in range(3))
    above = [jnp.where(even, far, near) for far, near in zip(far_rows, near_rows(REACH - 1, REACH - 2))]
    below = [jnp.where(even, near, far) for far, near in zip(far_rows, near_rows(0, 1))]

    v1_ref[:, pad] = jnp.zeros((rows + 2 * NEAR, LANES), jnp.float32)
    for start in (0, NEAR + rows):
        v1_ref[pl.ds(start, NEAR), own] = jnp.zeros((NEAR, cols), jnp.float32)
    row = lax.broadcasted_iota(jnp.int32, (8, cols), 0)
    for start in range(0, rows, 8):
        v1 = base_ref[pl.ds(start, 8), :]
        if start == 0:
            v1 = v1 - jnp.where(row == 0, smooth_weight * above[0], 0.0)
        if start == rows - 8:
            v1 = v1 - jnp.where(row == 7, smooth_weight * below[0], 0.0)
        v1_ref[pl.ds(NEAR + start, 8), own] = v1
        v1_out_ref[pl.ds(start, 8), :] = v1

    def edge_row(halo, inner, at):
        nearest, second, weight = halo
        inner = f_ref[pl.ds(inner, 1), :] * w_ref[pl.ds(inner, 1), :]
        padded = jnp.concatenate([nearest, jnp.zeros((1, LANES), jnp.float32)], axis=1)
        beside = second + inner + beside_columns(padded)[:, :cols]
        v1_ref[pl.ds(at, 1), own] = weight * nearest + smooth_weight * (4.0 * nearest - beside)

    pl.when(jnp.logical_not(first_row))(lambda: edge_row(above, 0, NEAR - 1))
    pl.when(jnp.logical_not(last_row))(lambda: edge_row(below, rows - 1, NEAR + rows))

    lane = lax.broadcasted_iota(jnp.int32, (8, LANES), 1)
    sums = [jnp.zeros((8, cols), jnp.float32) for _ in range(4)]
    for start in range(0, rows, 8):
        weight = w_ref[pl.ds(start, 8), :]
        v0 = f_ref[pl.ds(start, 8), :] * weight
        v1, v2 = image(v1_ref, weight, NEAR + start)
        sums = [total + term for total, term in zip(sums, (v0 * v0, v0 * v1, v1 * v1, v1 * v2))]
        edges = jnp.zeros((8, LANES), jnp.float32)
        for k, field in enumerate((v0, v1, v2, weight)):
            edges = jnp.where(lane == k, pltpu.roll(field[:, cols - LANES :], k + 1, 1), edges)
            edges = jnp.where(lane == 4 + k, pltpu.roll(field[:, :LANES], 4 + k, 1), edges)
        edge_ref[pl.ds(start, 8), :] = edges

    result = jnp.zeros((1, LANES), jnp.float32)
    for i, total in enumerate(sums):
        narrow = sum(total[:, k : k + LANES] for k in range(0, cols, LANES))
        total = jnp.sum(jnp.sum(narrow, axis=0, keepdims=True), axis=1, keepdims=True)
        result = jnp.where(lane[:1] == i, total, result)
    vectors = edge_ref[...].T
    message = [result] + [vectors[k : k + 1, :] for k in range(VECTORS)]
    copies = jnp.concatenate(message * 8, axis=0)
    for start in range(0, out_ref.shape[0], copies.shape[0]):
        out_ref[pl.ds(start, copies.shape[0]), :] = copies


def coupled(parts_ref, nrows, ncols):
    count = nrows * ncols
    lam = smooth_weight

    def part(k):
        return parts_ref[:, :, pl.ds(k * LANES, LANES)].reshape(count, LANES)

    device = lax.broadcasted_iota(jnp.int32, (count, LANES), 0)
    lane = lax.broadcasted_iota(jnp.int32, (count, LANES), 1)
    joined = device % ncols < ncols - 1
    a0, a1, ua, wa = (jnp.where(joined, part(1 + k), 0.0) for k in range(4))
    b0, b1, ub, wb = (jnp.where(joined, pltpu.roll(part(5 + k), count - 1, 0), 0.0) for k in range(4))

    def next_row(field):
        inside = pltpu.roll(field, LANES - 1, 1)
        beyond = jnp.where(device < count - ncols, pltpu.roll(inside, count - ncols, 0), 0.0)
        return jnp.where(lane == LANES - 1, beyond, inside)

    def total(field):
        return jnp.sum(jnp.sum(field, axis=0, keepdims=True), axis=1, keepdims=True)

    scalars = jnp.sum(part(0), axis=0, keepdims=True)
    m0, m1, m2, m3 = (total(jnp.where(lane[:1] == i, scalars, 0.0)) for i in range(4))
    m1 = m1 - 2.0 * lam * total(a0 * b0)
    m2 = m2 + total(lam * lam * (a0 * a0 + b0 * b0) - 2.0 * lam * (a1 * b0 + b1 * a0))
    m3 = m3 + total(
        lam * lam * ((wa + 4.0 * lam) * b0 * b0 + (wb + 4.0 * lam) * a0 * a0)
        - 2.0 * lam * (b0 * ua + a0 * ub + (a1 - lam * b0) * (b1 - lam * a0))
        - 2.0 * lam * lam * lam * (a0 * next_row(a0) + b0 * next_row(b0))
    )
    return m0, m1, m2, m3


def neighbours(parts_ref, nrows, ncols):
    row, col = lax.axis_index("rows"), lax.axis_index("cols")
    even = is_even()
    towards = jnp.where(even, 1, -1)
    lane = lax.broadcasted_iota(jnp.int32, (LANES, LANES), 1)
    vectors = []
    for vector, step_col in ((1, -1), (5, 1)):
        for step_row in (0, towards, -towards):
            r, c = row + step_row, col + step_col
            there = (r >= 0) & (r < nrows) & (c >= 0) & (c < ncols)
            index = jnp.where(there, r * ncols + c, 0)
            found = parts_ref[index, :, pl.ds(vector * LANES, LANES)]
            vectors.append(jnp.where(there, found, 0.0))
    vectors.append(jnp.zeros((LANES - len(vectors), LANES), jnp.float32))
    columns = jnp.concatenate(vectors, axis=0).T
    sides = []
    for begin, target in ((0, 0), (3, LANES - 1)):
        own, near, far = (
            jnp.where(lane == target, pltpu.roll(columns, (target - begin - k) % LANES, 1), 0.0) for k in range(3)
        )
        near = jnp.where(even, near[:REACH], near[LANES - REACH :])
        far = jnp.where(even, far[LANES - REACH :], far[:REACH])
        sides.append(jnp.concatenate([own, near, far], axis=0))
    return sides


def guard_rows(f_ref, w_ref, narrow_ref, near_ref, at_cols):
    rows = f_ref.shape[0]
    even = is_even()
    top = f_ref[pl.ds(0, 1), at_cols] * w_ref[pl.ds(0, 1), at_cols]
    bottom = f_ref[pl.ds(rows - 1, 1), at_cols] * w_ref[pl.ds(rows - 1, 1), at_cols]
    near = jnp.where(even, near_ref[pl.ds(2 * REACH, 1), at_cols], near_ref[pl.ds(2 * REACH + 7, 1), at_cols])
    far = narrow_ref[pl.ds(3, 1), at_cols]
    return (
        (jnp.where(even, bottom, near), jnp.where(even, near, top)),
        (jnp.where(even, far, bottom), jnp.where(even, top, far)),
    )


def halo_fields(f_ref, w_ref, narrow_ref, near_ref, far_ref, near_v1_ref, far_v1_ref, v0_ref):
    rows, cols = f_ref.shape
    own, pad = pl.ds(0, cols), pl.ds(cols, LANES)
    v0_ref[:, pad] = jnp.zeros((REACH + 2 * NEAR, LANES), jnp.float32)
    guards = guard_rows(f_ref, w_ref, narrow_ref, near_ref, own)
    for halo_ref, v1_ref, (above, below) in zip((near_ref, far_ref), (near_v1_ref, far_v1_ref), guards):
        v0_ref[pl.ds(NEAR - 1, 1), own] = above
        v0_ref[pl.ds(NEAR + REACH, 1), own] = below
        for start in range(0, REACH, 8):
            v0_ref[pl.ds(NEAR + start, 8), own] = halo_ref[pl.ds(start, 8), :] * halo_ref[pl.ds(REACH + start, 8), :]
        for start in range(0, REACH, 8):
            _, v1_ref[pl.ds(start, 8), :] = image(v0_ref, halo_ref[pl.ds(REACH + start, 8), :], NEAR + start)


def edge_fields(side, f_ref, w_ref, narrow_ref, near_ref, far_ref, near_v1_ref, far_v1_ref, v0_ref):
    cols = f_ref.shape[1]
    at_cols, there = pl.ds(side * (cols - LANES), LANES), pl.ds(side * LANES, LANES)
    outermost = lax.broadcasted_iota(jnp.int32, (8, LANES), 1) == side * (LANES - 1)
    guards = guard_rows(f_ref, w_ref, narrow_ref, near_ref, at_cols)
    for halo_ref, v1_ref, (above, below) in zip((near_ref, far_ref), (near_v1_ref, far_v1_ref), guards):
        v0_ref[pl.ds(NEAR - 1, 1), :] = above
        v0_ref[pl.ds(NEAR + REACH, 1), :] = below
        for start in range(0, REACH, 8):
            at, weight_at = pl.ds(start, 8), pl.ds(REACH + start, 8)
            v0_ref[pl.ds(NEAR + start, 8), :] = halo_ref[at, at_cols] * halo_ref[weight_at, at_cols]
        for start in range(0, REACH, 8):
            here = v0_ref[pl.ds(NEAR + start, 8), :]
            inner = pltpu.roll(here, 1 if side else LANES - 1, 1)
            outer = jnp.where(outermost, 0.0, pltpu.roll(here, LANES - 1 if side else 1, 1))
            beside = v0_ref[pl.ds(NEAR + start - 1, 8), :] + v0_ref[pl.ds(NEAR + start + 1, 8), :] + inner + outer
            weight = halo_ref[pl.ds(REACH + start, 8), at_cols]
            v1_ref[pl.ds(start, 8), there] = weight * here + smooth_weight * (4.0 * here - beside)


def regions(f_ref, w_ref, v1_ref, near_ref, near_v1_ref, far_ref, far_v1_ref, step):
    for start in range(0, f_ref.shape[0], step):
        yield start, (f_ref, start), (w_ref, start), (v1_ref, start)
    for base, halo_ref, field_ref in ((f_ref.shape[0], near_ref, near_v1_ref), (f_ref.shape[0] + REACH, far_ref, far_v1_ref)):
        for start in range(0, REACH, step):
            yield base + start, (halo_ref, start), (halo_ref, REACH + start), (field_ref, start)


def dot(left, right):
    return jnp.dot(left, right, preferred_element_type=jnp.float32)


def row_pass(rowtaps_ref, high, low, rows):
    table = rowtaps_ref[...]
    both = dot(table, high)
    return both[:rows] + (both[rows:] + dot(table[:rows], low))


def edges_kernel(
    nrows, ncols, parts_ref, f_ref, w_ref, v1_ref, narrow_ref, near_ref, far_ref, rowtaps_ref,
    coefficients_ref, left_ref, right_ref, one_ref, other_ref, near_v1_ref, far_v1_ref, v0_ref, high_ref, low_ref,
):
    rows, cols = f_ref.shape
    for side in range(2):
        edge_fields(side, f_ref, w_ref, narrow_ref, near_ref, far_ref, near_v1_ref, far_v1_ref, v0_ref)
    c0, c1 = coefficients(*coupled(parts_ref, nrows, ncols))
    coefficients_ref[pl.ds(0, 8), :] = jnp.broadcast_to(c0, (8, LANES))
    coefficients_ref[pl.ds(8, 8), :] = jnp.broadcast_to(c1, (8, LANES))
    sides = neighbours(parts_ref, nrows, ncols)
    left_ref[...], right_ref[...] = sides

    step = 16
    fields = (f_ref, w_ref, v1_ref, near_ref, near_v1_ref, far_ref, far_v1_ref)
    for side, begin in enumerate((0, cols - LANES)):
        at_cols = pl.ds(begin, LANES)
        for start, (flux_ref, flux_row), (weight_ref, weight_row), (field_ref, field_row) in regions(*fields, step):
            flux, weight = flux_ref[pl.ds(flux_row, step), at_cols], weight_ref[pl.ds(weight_row, step), at_cols]
            v1_cols = at_cols if start < rows else pl.ds(side * LANES, LANES)
            v1 = field_ref[pl.ds(field_row, step), v1_cols]
            v1 = v1 - smooth_weight * sides[side][start : start + step]
            scatter = flux - (c0 * (flux * weight) + c1 * v1)
            high, low = split_values(scatter * scatter)
            high_ref[pl.ds(start, step), pl.ds(side * LANES, LANES)] = high
            low_ref[pl.ds(start, step), pl.ds(side * LANES, LANES)] = low
    passed = row_pass(rowtaps_ref, high_ref[...], low_ref[...], rows)
    upper, lower = slice(0, rows // 2), slice(rows // 2, rows)
    first, last = passed[:, :LANES], passed[:, LANES:]
    on_left = lax.broadcasted_iota(jnp.int32, (rows // 2, LANES), 1) < REACH
    first = jnp.where(on_left, first[upper], pltpu.roll(first[lower], REACH, 1))
    last = jnp.where(on_left, pltpu.roll(last[upper], REACH, 1), last[lower])
    even = is_even("cols")
    one_ref[...] = jnp.where(even, last, first)
    other_ref[...] = jnp.where(even, first, last)


def main_kernel(
    coefficients_ref, left_ref, right_ref, f_ref, w_ref, v1_ref, narrow_ref, near_ref, far_ref, rowtaps_ref, coltaps_ref,
    background_ref, rms_ref, sides_ref, near_v1_ref, far_v1_ref, v0_ref, high_ref, low_ref,
):
    rows, cols = f_ref.shape
    halo_fields(f_ref, w_ref, narrow_ref, near_ref, far_ref, near_v1_ref, far_v1_ref, v0_ref)
    c0, c1 = coefficients_ref[pl.ds(0, 1), pl.ds(0, 1)], coefficients_ref[pl.ds(8, 1), pl.ds(0, 1)]
    step = 16
    fields = (f_ref, w_ref, v1_ref, near_ref, near_v1_ref, far_ref, far_v1_ref)
    for start, *sources in regions(*fields, step):
        flux, weight, v1 = (ref[pl.ds(row, step), :] for ref, row in sources)
        at = pl.ds(start, step)
        v1 = jnp.concatenate(
            [
                v1[:, :LANES] - smooth_weight * left_ref[at, :],
                v1[:, LANES : cols - LANES],
                v1[:, cols - LANES :] - smooth_weight * right_ref[at, :],
            ],
            axis=1,
        )
        background = c0 * (flux * weight) + c1 * v1
        if start < rows:
            background_ref[at, :] = background
        scatter = flux - background
        high_ref[at, :], low_ref[at, :] = split_values(scatter * scatter)
    passed = row_pass(rowtaps_ref, high_ref[...], low_ref[...], rows)
    sides_ref[:, pl.ds(0, 2 * LANES)] = passed[:, : 2 * LANES]
    sides_ref[:, pl.ds(2 * LANES, 2 * LANES)] = passed[:, cols - 2 * LANES :]
    high, low = split_values(pltpu.roll(passed, REACH, 1))
    for j in range(1, cols // LANES - 1):
        at = slice(j * LANES, j * LANES + 2 * LANES)
        rms_ref[:, pl.ds(j * LANES, LANES)] = column_pass(coltaps_ref[0], high[:, at], low[:, at])


def column_pass(table, high, low):
    both = dot(high, table)
    smoothed = both[:, :LANES] + (both[:, LANES:] + dot(low, table[:, :LANES]))
    return jnp.sqrt(smoothed + 1e-06)


def final_kernel(rms_in_ref, sides_ref, one_ref, other_ref, coltaps_ref, rms_ref, blocks_ref, sems):
    rows, cols = rms_ref.shape
    del rms_in_ref
    _, _, first_col, last_col = at_edges()
    even = is_even("cols")
    left = jnp.where(even, other_ref[...], one_ref[...])
    right = jnp.where(even, one_ref[...], other_ref[...])
    left = jnp.concatenate([pltpu.roll(left, REACH, 1), left], axis=0)
    right = jnp.concatenate([right, pltpu.roll(right, REACH, 1)], axis=0)
    sides = sides_ref[...]
    windows = (
        pltpu.roll(jnp.concatenate([left, sides[:, : 2 * LANES]], axis=1), 3 * LANES - REACH, 1)[:, : 2 * LANES],
        pltpu.roll(jnp.concatenate([sides[:, 2 * LANES :], right], axis=1), 3 * LANES - REACH, 1)[:, : 2 * LANES],
    )
    copies = []
    for side, which in enumerate((first_col.astype(jnp.int32), 2 * last_col.astype(jnp.int32))):
        high, low = split_values(windows[side])
        blocks_ref[side] = column_pass(coltaps_ref[which], high, low)
        target = rms_ref.at[:, pl.ds(side * (cols - LANES), LANES)]
        copies.append(pltpu.make_async_copy(blocks_ref.at[side], target, sems.at[side]))
        copies[-1].start()
    for copy in copies:
        copy.wait()


def swap(block, axis, first):
    count = lax.axis_size(axis)
    pairs = [(i, (i + 1) % count) for i in range(first, count, 2)]
    return lax.ppermute(block, axis, pairs + [(j, i) for i, j in pairs])


def call(kernel, name, outs, scratch=(), limit=16, in_place=False):
    vmem = pl.BlockSpec(memory_space=pltpu.VMEM)
    there = pl.BlockSpec(memory_space=pl.ANY)

    def run(*args):
        return pl.pallas_call(
            kernel,
            out_shape=tuple(jax.ShapeDtypeStruct(shape, jnp.float32) for shape in outs),
            in_specs=[there if in_place and i == 0 else vmem for i in range(len(args))],
            out_specs=(there if in_place else vmem,) * len(outs),
            scratch_shapes=list(scratch),
            input_output_aliases={0: 0} if in_place else {},
            compiler_params=pltpu.CompilerParams(vmem_limit_bytes=limit << 20),
            name=name,
        )(*args)

    return run


def shards(coadd_flux, inverse_variance, source_mask):
    rows, cols = coadd_flux.shape
    nrows, ncols = lax.axis_size("rows"), lax.axis_size("cols")
    message = (VECTORS + 1) * LANES

    def scratch(*shape, dtype=jnp.float32):
        return pltpu.VMEM(shape, dtype)

    taken = []
    for above, below in ((0, rows - 1), (1, rows - 2), (REACH, rows - 1 - REACH)):
        start = (jnp.where(is_even(), above, below), 0)
        flux, variance, mask = (
            lax.dynamic_slice(x, start, (1, cols)) for x in (coadd_flux, inverse_variance, source_mask)
        )
        taken.append((flux, weights(variance, mask)))
    products = [flux * weight for flux, weight in taken]
    narrow = swap(jnp.concatenate([products[0], products[1], taken[0][1], products[2]]), "rows", 1)

    own = (coadd_flux, weights(inverse_variance, source_mask))
    field = scratch(rows + 2 * NEAR, cols + LANES)
    to_near, to_far, base = call(
        prepare_kernel, "prepare", ((2 * REACH + 8, cols), (2 * REACH, cols), (rows, cols)), (field,)
    )(*own)
    to_near, to_far, narrow = lax.optimization_barrier((to_near, to_far, narrow))
    near = swap(to_near, "rows", 0)
    far = swap(to_far, "rows", 1)

    devices = nrows * ncols
    parts, own_v1 = call(
        moments_kernel,
        "moments",
        ((devices * (VECTORS + 1), LANES), (rows, cols)),
        (field, scratch(rows, LANES)),
    )(*own, base, narrow, near)
    parts = lax.all_to_all(parts.reshape(devices, 1, message), ("rows", "cols"), 0, 0, tiled=True)
    first_row, last_row, _, _ = at_edges()
    kind = jnp.where(is_even(), first_row.astype(jnp.int32), 2 + last_row.astype(jnp.int32))
    row_taps = lax.dynamic_index_in_dim(jnp.asarray(row_tables(rows)), kind, keepdims=False)
    col_taps = jnp.asarray(col_tables())
    reached, packed = rows + 2 * REACH, (rows // 2, LANES)
    fields = (*own, own_v1, narrow, near, far)
    halves = (scratch(REACH, 2 * LANES),) * 2
    numbers, left, right, to_one, to_other = call(
        functools.partial(edges_kernel, nrows, ncols),
        "edges",
        ((16, LANES), (reached, LANES), (reached, LANES), packed, packed),
        halves + (scratch(REACH + 2 * NEAR, LANES),) + (scratch(reached, 2 * LANES, dtype=jnp.bfloat16),) * 2,
    )(parts, *fields, row_taps)
    one = swap(to_one, "cols", 0)
    other = swap(to_other, "cols", 1)
    halves = (scratch(REACH, cols),) * 2
    background, rms, sides = call(
        main_kernel,
        "main",
        ((rows, cols), (rows, cols), (rows, 4 * LANES)),
        halves + (scratch(REACH + 2 * NEAR, cols + LANES),) + (scratch(reached, cols, dtype=jnp.bfloat16),) * 2,
    )(numbers, left, right, *fields, row_taps, col_taps)
    (rms,) = call(
        final_kernel, "final", ((rows, cols),), (scratch(2, rows, LANES), pltpu.SemaphoreType.DMA((2,))), in_place=True
    )(rms, sides, one, other, col_taps)
    return background, rms


def solution(mesh):
    return jax.shard_map(
        shards,
        mesh=mesh,
        in_specs=(P("rows", "cols"), P("rows", "cols"), P("rows", "cols")),
        out_specs=(P("rows", "cols"), P("rows", "cols")),
        check_vma=False,
    )
```

```python
import functools

import jax
import jax.numpy as jnp
import ml_dtypes
import numpy as np
from jax import lax
from jax.experimental import pallas as pl
from jax.experimental.pallas import tpu as pltpu
from jax.sharding import PartitionSpec as P

RADIUS = 32
REACH = 2 * RADIUS
LANES = 128
WIDE = REACH + 8
NEAR = 8
VECTORS = 8

smooth_weight = 2.0
blur_sigma = 10.0


def squared_taps(length, first, last):
    offsets = np.arange(2 * RADIUS + 1) - RADIUS
    taps = np.exp(-offsets * offsets / (2.0 * blur_sigma * blur_sigma))
    taps = taps / taps.sum()

    def band(count):
        table = np.zeros((count, count + 2 * RADIUS))
        for k in range(2 * RADIUS + 1):
            table[np.arange(count), np.arange(count) + k] = taps[k]
        return table

    inner = band(length + 2 * RADIUS)
    if first:
        inner[:RADIUS] = 0.0
    if last:
        inner[-RADIUS:] = 0.0
    return band(length) @ inner


def split(table):
    high = table.astype(np.float32).astype(ml_dtypes.bfloat16)
    low = (table - high.astype(np.float64)).astype(np.float32).astype(ml_dtypes.bfloat16)
    return high, low


def row_tables(length):
    tables = []
    for first, last, odd in ((False, False, False), (True, False, False), (False, False, True), (False, True, True)):
        table = squared_taps(length, first, last)
        above, own, below = table[:, :REACH], table[:, REACH : REACH + length], table[:, REACH + length :]
        near, far = (above, below) if odd else (below, above)
        if first or last:
            far = np.zeros_like(far)
        tables.append(np.concatenate(split(np.concatenate([own, near, far], axis=1)), axis=0))
    return np.stack(tables)


def col_tables():
    tables = []
    for first, last in ((False, False), (True, False), (False, True)):
        table = squared_taps(LANES, first, last)
        if first:
            table[:, :REACH] = 0.0
        if last:
            table[:, REACH + LANES :] = 0.0
        tables.append(np.concatenate(split(table.T), axis=1))
    return np.stack(tables)


def split_values(values):
    high = values.astype(jnp.bfloat16)
    return high, (values - high.astype(jnp.float32)).astype(jnp.bfloat16)


def at_edges():
    row, col = lax.axis_index("rows"), lax.axis_index("cols")
    return (
        row == 0,
        row == lax.axis_size("rows") - 1,
        col == 0,
        col == lax.axis_size("cols") - 1,
    )


def is_even(axis="rows"):
    return lax.axis_index(axis) % 2 == 0


def beside_columns(field):
    width = field.shape[1]
    return pltpu.roll(field, 1, 1) + pltpu.roll(field, width - 1, 1)


def weights(inverse_variance, source_mask):
    return inverse_variance * (1.0 - source_mask.astype(jnp.float32))


def coefficients(m0, m1, m2, m3):
    alpha0 = m0 / m1
    norm1 = jnp.maximum(m0 - 2.0 * alpha0 * m1 + alpha0 * alpha0 * m2, 0.0)
    grown = 1.0 + norm1 / m0
    image1 = grown * grown * m1 - 2.0 * grown * alpha0 * m2 + alpha0 * alpha0 * m3
    alpha1 = jnp.where(image1 > 0.0, norm1 / image1, 0.0)
    return alpha0 + alpha1 * grown, -alpha1 * alpha0


def image(ref, weight, start):
    cols = weight.shape[1]
    own = pl.ds(0, cols)
    here = ref[pl.ds(start, 8), :]
    beside = ref[pl.ds(start - 1, 8), own] + ref[pl.ds(start + 1, 8), own] + beside_columns(here)[:, :cols]
    here = here[:, :cols]
    return here, weight * here + smooth_weight * (4.0 * here - beside)


def prepare_kernel(f_ref, w_ref, near_ref, far_ref, v1_ref, v0_ref):
    rows = f_ref.shape[0]

    def write(out_ref, begin):
        out_ref[pl.ds(0, REACH), :] = f_ref[pl.ds(begin, REACH), :]
        out_ref[pl.ds(REACH, REACH), :] = w_ref[pl.ds(begin, REACH), :]

    def near_product(begin):
        near_ref[pl.ds(2 * REACH, 8), :] = f_ref[pl.ds(begin, 8), :] * w_ref[pl.ds(begin, 8), :]

    @pl.when(is_even())
    def _():
        write(near_ref, rows - REACH)
        near_product(rows - WIDE)
        write(far_ref, 0)

    @pl.when(jnp.logical_not(is_even()))
    def _():
        write(near_ref, 0)
        near_product(REACH)
        write(far_ref, rows - REACH)

    cols = f_ref.shape[1]
    own = pl.ds(0, cols)
    v0_ref[:, pl.ds(cols, LANES)] = jnp.zeros((rows + 2 * NEAR, LANES), jnp.float32)
    for start in (0, NEAR + rows):
        v0_ref[pl.ds(start, NEAR), own] = jnp.zeros((NEAR, cols), jnp.float32)
    for start in range(0, rows, 8):
        at = pl.ds(start, 8)
        v0_ref[pl.ds(NEAR + start, 8), own] = f_ref[at, :] * w_ref[at, :]
    for start in range(0, rows, 8):
        _, v1_ref[pl.ds(start, 8), :] = image(v0_ref, w_ref[pl.ds(start, 8), :], NEAR + start)


def moments_kernel(f_ref, w_ref, base_ref, narrow_ref, near_ref, out_ref, v1_out_ref, v1_ref, edge_ref):
    rows, cols = f_ref.shape
    first_row, last_row, _, _ = at_edges()
    even = is_even()
    own, pad = pl.ds(0, cols), pl.ds(cols, LANES)

    def near_rows(nearest, second):
        return (
            near_ref[pl.ds(nearest, 1), :] * near_ref[pl.ds(REACH + nearest, 1), :],
            near_ref[pl.ds(second, 1), :] * near_ref[pl.ds(REACH + second, 1), :],
            near_ref[pl.ds(REACH + nearest, 1), :],
        )

    outermost = first_row | last_row
    far_rows = tuple(jnp.where(outermost, 0.0, narrow_ref[pl.ds(k, 1), :]) for k in range(3))
    above = [jnp.where(even, far, near) for far, near in zip(far_rows, near_rows(REACH - 1, REACH - 2))]
    below = [jnp.where(even, near, far) for far, near in zip(far_rows, near_rows(0, 1))]

    v1_ref[:, pad] = jnp.zeros((rows + 2 * NEAR, LANES), jnp.float32)
    for start in (0, NEAR + rows):
        v1_ref[pl.ds(start, NEAR), own] = jnp.zeros((NEAR, cols), jnp.float32)
    row = lax.broadcasted_iota(jnp.int32, (8, cols), 0)
    for start in range(0, rows, 8):
        v1 = base_ref[pl.ds(start, 8), :]
        if start == 0:
            v1 = v1 - jnp.where(row == 0, smooth_weight * above[0], 0.0)
        if start == rows - 8:
            v1 = v1 - jnp.where(row == 7, smooth_weight * below[0], 0.0)
        v1_ref[pl.ds(NEAR + start, 8), own] = v1
        v1_out_ref[pl.ds(start, 8), :] = v1

    def edge_row(halo, inner, at):
        nearest, second, weight = halo
        inner = f_ref[pl.ds(inner, 1), :] * w_ref[pl.ds(inner, 1), :]
        padded = jnp.concatenate([nearest, jnp.zeros((1, LANES), jnp.float32)], axis=1)
        beside = second + inner + beside_columns(padded)[:, :cols]
        v1_ref[pl.ds(at, 1), own] = weight * nearest + smooth_weight * (4.0 * nearest - beside)

    pl.when(jnp.logical_not(first_row))(lambda: edge_row(above, 0, NEAR - 1))
    pl.when(jnp.logical_not(last_row))(lambda: edge_row(below, rows - 1, NEAR + rows))

    lane = lax.broadcasted_iota(jnp.int32, (8, LANES), 1)
    sums = [jnp.zeros((8, cols), jnp.float32) for _ in range(4)]
    for start in range(0, rows, 8):
        weight = w_ref[pl.ds(start, 8), :]
        v0 = f_ref[pl.ds(start, 8), :] * weight
        v1, v2 = image(v1_ref, weight, NEAR + start)
        sums = [total + term for total, term in zip(sums, (v0 * v0, v0 * v1, v1 * v1, v1 * v2))]
        edges = jnp.zeros((8, LANES), jnp.float32)
        for k, field in enumerate((v0, v1, v2, weight)):
            edges = jnp.where(lane == k, pltpu.roll(field[:, cols - LANES :], k + 1, 1), edges)
            edges = jnp.where(lane == 4 + k, pltpu.roll(field[:, :LANES], 4 + k, 1), edges)
        edge_ref[pl.ds(start, 8), :] = edges

    result = jnp.zeros((1, LANES), jnp.float32)
    for i, total in enumerate(sums):
        narrow = sum(total[:, k : k + LANES] for k in range(0, cols, LANES))
        total = jnp.sum(jnp.sum(narrow, axis=0, keepdims=True), axis=1, keepdims=True)
        result = jnp.where(lane[:1] == i, total, result)
    vectors = edge_ref[...].T
    message = [result] + [vectors[k : k + 1, :] for k in range(VECTORS)]
    copies = jnp.concatenate(message * 8, axis=0)
    for start in range(0, out_ref.shape[0], copies.shape[0]):
        out_ref[pl.ds(start, copies.shape[0]), :] = copies


def coupled(parts_ref, nrows, ncols):
    count = nrows * ncols
    lam = smooth_weight

    def part(k):
        return parts_ref[:, :, pl.ds(k * LANES, LANES)].reshape(count, LANES)

    device = lax.broadcasted_iota(jnp.int32, (count, LANES), 0)
    lane = lax.broadcasted_iota(jnp.int32, (count, LANES), 1)
    joined = device % ncols < ncols - 1
    a0, a1, ua, wa = (jnp.where(joined, part(1 + k), 0.0) for k in range(4))
    b0, b1, ub, wb = (jnp.where(joined, pltpu.roll(part(5 + k), count - 1, 0), 0.0) for k in range(4))

    def next_row(field):
        inside = pltpu.roll(field, LANES - 1, 1)
        beyond = jnp.where(device < count - ncols, pltpu.roll(inside, count - ncols, 0), 0.0)
        return jnp.where(lane == LANES - 1, beyond, inside)

    def total(field):
        return jnp.sum(jnp.sum(field, axis=0, keepdims=True), axis=1, keepdims=True)

    scalars = jnp.sum(part(0), axis=0, keepdims=True)
    m0, m1, m2, m3 = (total(jnp.where(lane[:1] == i, scalars, 0.0)) for i in range(4))
    m1 = m1 - 2.0 * lam * total(a0 * b0)
    m2 = m2 + total(lam * lam * (a0 * a0 + b0 * b0) - 2.0 * lam * (a1 * b0 + b1 * a0))
    m3 = m3 + total(
        lam * lam * ((wa + 4.0 * lam) * b0 * b0 + (wb + 4.0 * lam) * a0 * a0)
        - 2.0 * lam * (b0 * ua + a0 * ub + (a1 - lam * b0) * (b1 - lam * a0))
        - 2.0 * lam * lam * lam * (a0 * next_row(a0) + b0 * next_row(b0))
    )
    return m0, m1, m2, m3


def neighbours(parts_ref, nrows, ncols):
    row, col = lax.axis_index("rows"), lax.axis_index("cols")
    even = is_even()
    towards = jnp.where(even, 1, -1)
    lane = lax.broadcasted_iota(jnp.int32, (LANES, LANES), 1)
    vectors = []
    for vector, step_col in ((1, -1), (5, 1)):
        for step_row in (0, towards, -towards):
            r, c = row + step_row, col + step_col
            there = (r >= 0) & (r < nrows) & (c >= 0) & (c < ncols)
            index = jnp.where(there, r * ncols + c, 0)
            found = parts_ref[index, :, pl.ds(vector * LANES, LANES)]
            vectors.append(jnp.where(there, found, 0.0))
    vectors.append(jnp.zeros((LANES - len(vectors), LANES), jnp.float32))
    columns = jnp.concatenate(vectors, axis=0).T
    sides = []
    for begin, target in ((0, 0), (3, LANES - 1)):
        own, near, far = (
            jnp.where(lane == target, pltpu.roll(columns, (target - begin - k) % LANES, 1), 0.0) for k in range(3)
        )
        near = jnp.where(even, near[:REACH], near[LANES - REACH :])
        far = jnp.where(even, far[LANES - REACH :], far[:REACH])
        sides.append(jnp.concatenate([own, near, far], axis=0))
    return sides


def guard_rows(f_ref, w_ref, narrow_ref, near_ref, at_cols):
    rows = f_ref.shape[0]
    even = is_even()
    top = f_ref[pl.ds(0, 1), at_cols] * w_ref[pl.ds(0, 1), at_cols]
    bottom = f_ref[pl.ds(rows - 1, 1), at_cols] * w_ref[pl.ds(rows - 1, 1), at_cols]
    near = jnp.where(even, near_ref[pl.ds(2 * REACH, 1), at_cols], near_ref[pl.ds(2 * REACH + 7, 1), at_cols])
    far = narrow_ref[pl.ds(3, 1), at_cols]
    return (
        (jnp.where(even, bottom, near), jnp.where(even, near, top)),
        (jnp.where(even, far, bottom), jnp.where(even, top, far)),
    )


def halo_fields(f_ref, w_ref, narrow_ref, near_ref, far_ref, near_v1_ref, far_v1_ref, v0_ref):
    rows, cols = f_ref.shape
    own, pad = pl.ds(0, cols), pl.ds(cols, LANES)
    v0_ref[:, pad] = jnp.zeros((REACH + 2 * NEAR, LANES), jnp.float32)
    guards = guard_rows(f_ref, w_ref, narrow_ref, near_ref, own)
    for halo_ref, v1_ref, (above, below) in zip((near_ref, far_ref), (near_v1_ref, far_v1_ref), guards):
        v0_ref[pl.ds(NEAR - 1, 1), own] = above
        v0_ref[pl.ds(NEAR + REACH, 1), own] = below
        for start in range(0, REACH, 8):
            v0_ref[pl.ds(NEAR + start, 8), own] = halo_ref[pl.ds(start, 8), :] * halo_ref[pl.ds(REACH + start, 8), :]
        for start in range(0, REACH, 8):
            _, v1_ref[pl.ds(start, 8), :] = image(v0_ref, halo_ref[pl.ds(REACH + start, 8), :], NEAR + start)


def edge_fields(side, f_ref, w_ref, narrow_ref, near_ref, far_ref, near_v1_ref, far_v1_ref, v0_ref):
    cols = f_ref.shape[1]
    at_cols, there = pl.ds(side * (cols - LANES), LANES), pl.ds(side * LANES, LANES)
    outermost = lax.broadcasted_iota(jnp.int32, (8, LANES), 1) == side * (LANES - 1)
    guards = guard_rows(f_ref, w_ref, narrow_ref, near_ref, at_cols)
    for halo_ref, v1_ref, (above, below) in zip((near_ref, far_ref), (near_v1_ref, far_v1_ref), guards):
        v0_ref[pl.ds(NEAR - 1, 1), :] = above
        v0_ref[pl.ds(NEAR + REACH, 1), :] = below
        for start in range(0, REACH, 8):
            at, weight_at = pl.ds(start, 8), pl.ds(REACH + start, 8)
            v0_ref[pl.ds(NEAR + start, 8), :] = halo_ref[at, at_cols] * halo_ref[weight_at, at_cols]
        for start in range(0, REACH, 8):
            here = v0_ref[pl.ds(NEAR + start, 8), :]
            inner = pltpu.roll(here, 1 if side else LANES - 1, 1)
            outer = jnp.where(outermost, 0.0, pltpu.roll(here, LANES - 1 if side else 1, 1))
            beside = v0_ref[pl.ds(NEAR + start - 1, 8), :] + v0_ref[pl.ds(NEAR + start + 1, 8), :] + inner + outer
            weight = halo_ref[pl.ds(REACH + start, 8), at_cols]
            v1_ref[pl.ds(start, 8), there] = weight * here + smooth_weight * (4.0 * here - beside)


def regions(f_ref, w_ref, v1_ref, near_ref, near_v1_ref, far_ref, far_v1_ref, step):
    for start in range(0, f_ref.shape[0], step):
        yield start, (f_ref, start), (w_ref, start), (v1_ref, start)
    for base, halo_ref, field_ref in ((f_ref.shape[0], near_ref, near_v1_ref), (f_ref.shape[0] + REACH, far_ref, far_v1_ref)):
        for start in range(0, REACH, step):
            yield base + start, (halo_ref, start), (halo_ref, REACH + start), (field_ref, start)


def dot(left, right):
    return jnp.dot(left, right, preferred_element_type=jnp.float32)


def row_pass(rowtaps_ref, high, low, rows):
    table = rowtaps_ref[...]
    both = dot(table, high)
    return both[:rows] + (both[rows:] + dot(table[:rows], low))


def edges_kernel(
    nrows, ncols, parts_ref, f_ref, w_ref, v1_ref, narrow_ref, near_ref, far_ref, rowtaps_ref,
    coefficients_ref, left_ref, right_ref, one_ref, other_ref, near_v1_ref, far_v1_ref, v0_ref, high_ref, low_ref,
):
    rows, cols = f_ref.shape
    for side in range(2):
        edge_fields(side, f_ref, w_ref, narrow_ref, near_ref, far_ref, near_v1_ref, far_v1_ref, v0_ref)
    c0, c1 = coefficients(*coupled(parts_ref, nrows, ncols))
    coefficients_ref[pl.ds(0, 8), :] = jnp.broadcast_to(c0, (8, LANES))
    coefficients_ref[pl.ds(8, 8), :] = jnp.broadcast_to(c1, (8, LANES))
    sides = neighbours(parts_ref, nrows, ncols)
    left_ref[...], right_ref[...] = sides

    step = 16
    fields = (f_ref, w_ref, v1_ref, near_ref, near_v1_ref, far_ref, far_v1_ref)
    for side, begin in enumerate((0, cols - LANES)):
        at_cols = pl.ds(begin, LANES)
        for start, (flux_ref, flux_row), (weight_ref, weight_row), (field_ref, field_row) in regions(*fields, step):
            flux, weight = flux_ref[pl.ds(flux_row, step), at_cols], weight_ref[pl.ds(weight_row, step), at_cols]
            v1_cols = at_cols if start < rows else pl.ds(side * LANES, LANES)
            v1 = field_ref[pl.ds(field_row, step), v1_cols]
            v1 = v1 - smooth_weight * sides[side][start : start + step]
            scatter = flux - (c0 * (flux * weight) + c1 * v1)
            high, low = split_values(scatter * scatter)
            high_ref[pl.ds(start, step), pl.ds(side * LANES, LANES)] = high
            low_ref[pl.ds(start, step), pl.ds(side * LANES, LANES)] = low
    passed = row_pass(rowtaps_ref, high_ref[...], low_ref[...], rows)
    upper, lower = slice(0, rows // 2), slice(rows // 2, rows)
    first, last = passed[:, :LANES], passed[:, LANES:]
    on_left = lax.broadcasted_iota(jnp.int32, (rows // 2, LANES), 1) < REACH
    first = jnp.where(on_left, first[upper], pltpu.roll(first[lower], REACH, 1))
    last = jnp.where(on_left, pltpu.roll(last[upper], REACH, 1), last[lower])
    even = is_even("cols")
    one_ref[...] = jnp.where(even, last, first)
    other_ref[...] = jnp.where(even, first, last)


def main_kernel(
    coefficients_ref, left_ref, right_ref, f_ref, w_ref, v1_ref, narrow_ref, near_ref, far_ref, rowtaps_ref, coltaps_ref,
    background_ref, rms_ref, sides_ref, near_v1_ref, far_v1_ref, v0_ref, high_ref, low_ref,
):
    rows, cols = f_ref.shape
    halo_fields(f_ref, w_ref, narrow_ref, near_ref, far_ref, near_v1_ref, far_v1_ref, v0_ref)
    c0, c1 = coefficients_ref[pl.ds(0, 1), pl.ds(0, 1)], coefficients_ref[pl.ds(8, 1), pl.ds(0, 1)]
    step = 16
    fields = (f_ref, w_ref, v1_ref, near_ref, near_v1_ref, far_ref, far_v1_ref)
    for start, *sources in regions(*fields, step):
        flux, weight, v1 = (ref[pl.ds(row, step), :] for ref, row in sources)
        at = pl.ds(start, step)
        v1 = jnp.concatenate(
            [
                v1[:, :LANES] - smooth_weight * left_ref[at, :],
                v1[:, LANES : cols - LANES],
                v1[:, cols - LANES :] - smooth_weight * right_ref[at, :],
            ],
            axis=1,
        )
        background = c0 * (flux * weight) + c1 * v1
        if start < rows:
            background_ref[at, :] = background
        scatter = flux - background
        high_ref[at, :], low_ref[at, :] = split_values(scatter * scatter)
    passed = row_pass(rowtaps_ref, high_ref[...], low_ref[...], rows)
    sides_ref[:, pl.ds(0, 2 * LANES)] = passed[:, : 2 * LANES]
    sides_ref[:, pl.ds(2 * LANES, 2 * LANES)] = passed[:, cols - 2 * LANES :]
    high, low = split_values(pltpu.roll(passed, REACH, 1))
    for j in range(1, cols // LANES - 1):
        at = slice(j * LANES, j * LANES + 2 * LANES)
        rms_ref[:, pl.ds(j * LANES, LANES)] = column_pass(coltaps_ref[0], high[:, at], low[:, at])


def column_pass(table, high, low):
    both = dot(high, table)
    smoothed = both[:, :LANES] + (both[:, LANES:] + dot(low, table[:, :LANES]))
    return jnp.sqrt(smoothed + 1e-06)


def final_kernel(rms_in_ref, sides_ref, one_ref, other_ref, coltaps_ref, rms_ref, blocks_ref, sems):
    rows, cols = rms_ref.shape
    del rms_in_ref
    _, _, first_col, last_col = at_edges()
    even = is_even("cols")
    left = jnp.where(even, other_ref[...], one_ref[...])
    right = jnp.where(even, one_ref[...], other_ref[...])
    left = jnp.concatenate([pltpu.roll(left, REACH, 1), left], axis=0)
    right = jnp.concatenate([right, pltpu.roll(right, REACH, 1)], axis=0)
    sides = sides_ref[...]
    windows = (
        pltpu.roll(jnp.concatenate([left, sides[:, : 2 * LANES]], axis=1), 3 * LANES - REACH, 1)[:, : 2 * LANES],
        pltpu.roll(jnp.concatenate([sides[:, 2 * LANES :], right], axis=1), 3 * LANES - REACH, 1)[:, : 2 * LANES],
    )
    copies = []
    for side, which in enumerate((first_col.astype(jnp.int32), 2 * last_col.astype(jnp.int32))):
        high, low = split_values(windows[side])
        blocks_ref[side] = column_pass(coltaps_ref[which], high, low)
        target = rms_ref.at[:, pl.ds(side * (cols - LANES), LANES)]
        copies.append(pltpu.make_async_copy(blocks_ref.at[side], target, sems.at[side]))
        copies[-1].start()
    for copy in copies:
        copy.wait()


def swap(block, axis, first):
    nrows, ncols = lax.axis_size("rows"), lax.axis_size("cols")
    count = lax.axis_size(axis)
    pairs = []
    for r in range(nrows):
        for c in range(ncols):
            along = r if axis == "rows" else c
            other = along + 1 if (along - first) % 2 == 0 else along - 1
            if 0 <= other < count:
                partner = (other, c) if axis == "rows" else (r, other)
            else:
                partner = (r, c ^ 1) if axis == "rows" else (r ^ 1, c)
            pairs.append((r * ncols + c, partner[0] * ncols + partner[1]))
    return lax.ppermute(block, ("rows", "cols"), pairs)


def call(kernel, name, outs, scratch=(), limit=16, in_place=False):
    vmem = pl.BlockSpec(memory_space=pltpu.VMEM)
    there = pl.BlockSpec(memory_space=pl.ANY)

    def run(*args):
        return pl.pallas_call(
            kernel,
            out_shape=tuple(jax.ShapeDtypeStruct(shape, jnp.float32) for shape in outs),
            in_specs=[there if in_place and i == 0 else vmem for i in range(len(args))],
            out_specs=(there if in_place else vmem,) * len(outs),
            scratch_shapes=list(scratch),
            input_output_aliases={0: 0} if in_place else {},
            compiler_params=pltpu.CompilerParams(vmem_limit_bytes=limit << 20),
            name=name,
        )(*args)

    return run


def shards(coadd_flux, inverse_variance, source_mask):
    rows, cols = coadd_flux.shape
    nrows, ncols = lax.axis_size("rows"), lax.axis_size("cols")
    message = (VECTORS + 1) * LANES

    def scratch(*shape, dtype=jnp.float32):
        return pltpu.VMEM(shape, dtype)

    taken = []
    for above, below in ((0, rows - 1), (1, rows - 2), (REACH, rows - 1 - REACH)):
        start = (jnp.where(is_even(), above, below), 0)
        flux, variance, mask = (
            lax.dynamic_slice(x, start, (1, cols)) for x in (coadd_flux, inverse_variance, source_mask)
        )
        taken.append((flux, weights(variance, mask)))
    products = [flux * weight for flux, weight in taken]
    narrow = swap(jnp.concatenate([products[0], products[1], taken[0][1], products[2]]), "rows", 1)

    own = (coadd_flux, weights(inverse_variance, source_mask))
    field = scratch(rows + 2 * NEAR, cols + LANES)
    to_near, to_far, base = call(
        prepare_kernel, "prepare", ((2 * REACH + 8, cols), (2 * REACH, cols), (rows, cols)), (field,)
    )(*own)
    to_near, to_far, narrow = lax.optimization_barrier((to_near, to_far, narrow))
    near = swap(to_near, "rows", 0)
    far = swap(to_far, "rows", 1)

    devices = nrows * ncols
    parts, own_v1 = call(
        moments_kernel,
        "moments",
        ((devices * (VECTORS + 1), LANES), (rows, cols)),
        (field, scratch(rows, LANES)),
    )(*own, base, narrow, near)
    parts = lax.all_to_all(parts.reshape(devices, 1, message), ("rows", "cols"), 0, 0, tiled=True)
    first_row, last_row, _, _ = at_edges()
    kind = jnp.where(is_even(), first_row.astype(jnp.int32), 2 + last_row.astype(jnp.int32))
    row_taps = lax.dynamic_index_in_dim(jnp.asarray(row_tables(rows)), kind, keepdims=False)
    col_taps = jnp.asarray(col_tables())
    reached, packed = rows + 2 * REACH, (rows // 2, LANES)
    fields = (*own, own_v1, narrow, near, far)
    halves = (scratch(REACH, 2 * LANES),) * 2
    numbers, left, right, to_one, to_other = call(
        functools.partial(edges_kernel, nrows, ncols),
        "edges",
        ((16, LANES), (reached, LANES), (reached, LANES), packed, packed),
        halves + (scratch(REACH + 2 * NEAR, LANES),) + (scratch(reached, 2 * LANES, dtype=jnp.bfloat16),) * 2,
    )(parts, *fields, row_taps)
    one = swap(to_one, "cols", 0)
    other = swap(to_other, "cols", 1)
    halves = (scratch(REACH, cols),) * 2
    background, rms, sides = call(
        main_kernel,
        "main",
        ((rows, cols), (rows, cols), (rows, 4 * LANES)),
        halves + (scratch(REACH + 2 * NEAR, cols + LANES),) + (scratch(reached, cols, dtype=jnp.bfloat16),) * 2,
    )(numbers, left, right, *fields, row_taps, col_taps)
    (rms,) = call(
        final_kernel, "final", ((rows, cols),), (scratch(2, rows, LANES), pltpu.SemaphoreType.DMA((2,))), in_place=True
    )(rms, sides, one, other, col_taps)
    return background, rms


def solution(mesh):
    return jax.shard_map(
        shards,
        mesh=mesh,
        in_specs=(P("rows", "cols"), P("rows", "cols"), P("rows", "cols")),
        out_specs=(P("rows", "cols"), P("rows", "cols")),
        check_vma=False,
    )
```

```python
import functools

import jax
import jax.numpy as jnp
import ml_dtypes
import numpy as np
from jax import lax
from jax.experimental import pallas as pl
from jax.experimental.pallas import tpu as pltpu
from jax.sharding import PartitionSpec as P

RADIUS = 32
REACH = 2 * RADIUS
LANES = 128
WIDE = REACH + 8
NEAR = 8
VECTORS = 8

smooth_weight = 2.0
blur_sigma = 10.0


def squared_taps(length, first, last):
    offsets = np.arange(2 * RADIUS + 1) - RADIUS
    taps = np.exp(-offsets * offsets / (2.0 * blur_sigma * blur_sigma))
    taps = taps / taps.sum()

    def band(count):
        table = np.zeros((count, count + 2 * RADIUS))
        for k in range(2 * RADIUS + 1):
            table[np.arange(count), np.arange(count) + k] = taps[k]
        return table

    inner = band(length + 2 * RADIUS)
    if first:
        inner[:RADIUS] = 0.0
    if last:
        inner[-RADIUS:] = 0.0
    return band(length) @ inner


def split(table):
    high = table.astype(np.float32).astype(ml_dtypes.bfloat16)
    low = (table - high.astype(np.float64)).astype(np.float32).astype(ml_dtypes.bfloat16)
    return high, low


def row_tables(length):
    tables = []
    for first, last, odd in ((False, False, False), (True, False, False), (False, False, True), (False, True, True)):
        table = squared_taps(length, first, last)
        above, own, below = table[:, :REACH], table[:, REACH : REACH + length], table[:, REACH + length :]
        near, far = (above, below) if odd else (below, above)
        if first or last:
            far = np.zeros_like(far)
        tables.append(np.concatenate(split(np.concatenate([own, near, far], axis=1)), axis=0))
    return np.stack(tables)


def col_tables():
    tables = []
    for first, last in ((False, False), (True, False), (False, True)):
        table = squared_taps(LANES, first, last)
        if first:
            table[:, :REACH] = 0.0
        if last:
            table[:, REACH + LANES :] = 0.0
        tables.append(np.concatenate(split(table.T), axis=1))
    return np.stack(tables)


def side_tables():
    table = squared_taps(LANES, False, False).T
    tables = []
    for part in (table[:REACH], table[REACH + LANES :]):
        nothing = np.zeros_like(part)
        tables.append(np.concatenate(split(np.block([[part, nothing], [nothing, part]])), axis=1))
    return np.stack(tables)


def split_values(values):
    high = values.astype(jnp.bfloat16)
    return high, (values - high.astype(jnp.float32)).astype(jnp.bfloat16)


def at_edges():
    row, col = lax.axis_index("rows"), lax.axis_index("cols")
    return (
        row == 0,
        row == lax.axis_size("rows") - 1,
        col == 0,
        col == lax.axis_size("cols") - 1,
    )


def is_even(axis="rows"):
    return lax.axis_index(axis) % 2 == 0


def beside_columns(field):
    width = field.shape[1]
    return pltpu.roll(field, 1, 1) + pltpu.roll(field, width - 1, 1)


def weights(inverse_variance, source_mask):
    return inverse_variance * (1.0 - source_mask.astype(jnp.float32))


def coefficients(m0, m1, m2, m3):
    alpha0 = m0 / m1
    norm1 = jnp.maximum(m0 - 2.0 * alpha0 * m1 + alpha0 * alpha0 * m2, 0.0)
    grown = 1.0 + norm1 / m0
    image1 = grown * grown * m1 - 2.0 * grown * alpha0 * m2 + alpha0 * alpha0 * m3
    alpha1 = jnp.where(image1 > 0.0, norm1 / image1, 0.0)
    return alpha0 + alpha1 * grown, -alpha1 * alpha0


def image(ref, weight, start):
    cols = weight.shape[1]
    own = pl.ds(0, cols)
    here = ref[pl.ds(start, 8), :]
    beside = ref[pl.ds(start - 1, 8), own] + ref[pl.ds(start + 1, 8), own] + beside_columns(here)[:, :cols]
    here = here[:, :cols]
    return here, weight * here + smooth_weight * (4.0 * here - beside)


def columns_to_lanes(fields, edges, lane):
    for k, field in fields:
        edges = jnp.where(lane == k, pltpu.roll(field[:, field.shape[1] - LANES :], k + 1, 1), edges)
        edges = jnp.where(lane == 4 + k, pltpu.roll(field[:, :LANES], 4 + k, 1), edges)
    return edges


def prepare_kernel(f_ref, w_ref, near_ref, far_ref, v1_ref, sums_ref, edge_ref, v0_ref):
    rows = f_ref.shape[0]

    def write(out_ref, begin):
        out_ref[pl.ds(0, REACH), :] = f_ref[pl.ds(begin, REACH), :]
        out_ref[pl.ds(REACH, REACH), :] = w_ref[pl.ds(begin, REACH), :]

    def near_product(begin):
        near_ref[pl.ds(2 * REACH, 8), :] = f_ref[pl.ds(begin, 8), :] * w_ref[pl.ds(begin, 8), :]

    @pl.when(is_even())
    def _():
        write(near_ref, rows - REACH)
        near_product(rows - WIDE)
        write(far_ref, 0)

    @pl.when(jnp.logical_not(is_even()))
    def _():
        write(near_ref, 0)
        near_product(REACH)
        write(far_ref, rows - REACH)

    cols = f_ref.shape[1]
    own = pl.ds(0, cols)
    v0_ref[:, pl.ds(cols, LANES)] = jnp.zeros((rows + 2 * NEAR, LANES), jnp.float32)
    for start in (0, NEAR + rows):
        v0_ref[pl.ds(start, NEAR), own] = jnp.zeros((NEAR, cols), jnp.float32)
    for start in range(0, rows, 8):
        at = pl.ds(start, 8)
        v0_ref[pl.ds(NEAR + start, 8), own] = f_ref[at, :] * w_ref[at, :]
    lane = lax.broadcasted_iota(jnp.int32, (8, LANES), 1)
    sums = [jnp.zeros((8, cols), jnp.float32) for _ in range(3)]
    for start in range(0, rows, 8):
        at = pl.ds(start, 8)
        weight = w_ref[at, :]
        v0, v1 = image(v0_ref, weight, NEAR + start)
        v1_ref[at, :] = v1
        sums = [total + term for total, term in zip(sums, (v0 * v0, v0 * v1, v1 * v1))]
        edge_ref[at, :] = columns_to_lanes(((0, v0), (3, weight)), jnp.zeros((8, LANES), jnp.float32), lane)
    for i, total in enumerate(sums):
        sums_ref[pl.ds(8 * i, 8), :] = sum(total[:, k : k + LANES] for k in range(0, cols, LANES))


def moments_kernel(f_ref, w_ref, base_ref, sums_ref, edge_in_ref, narrow_ref, near_ref, out_ref, v1_out_ref, v1_ref, edge_ref):
    rows, cols = f_ref.shape
    first_row, last_row, _, _ = at_edges()
    even = is_even()
    own, pad = pl.ds(0, cols), pl.ds(cols, LANES)

    def near_rows(nearest, second):
        return (
            near_ref[pl.ds(nearest, 1), :] * near_ref[pl.ds(REACH + nearest, 1), :],
            near_ref[pl.ds(second, 1), :] * near_ref[pl.ds(REACH + second, 1), :],
            near_ref[pl.ds(REACH + nearest, 1), :],
        )

    outermost = first_row | last_row
    far_rows = tuple(jnp.where(outermost, 0.0, narrow_ref[pl.ds(k, 1), :]) for k in range(3))
    above = [jnp.where(even, far, near) for far, near in zip(far_rows, near_rows(REACH - 1, REACH - 2))]
    below = [jnp.where(even, near, far) for far, near in zip(far_rows, near_rows(0, 1))]

    v1_ref[:, pad] = jnp.zeros((rows + 2 * NEAR, LANES), jnp.float32)
    for start in (0, NEAR + rows):
        v1_ref[pl.ds(start, NEAR), own] = jnp.zeros((NEAR, cols), jnp.float32)
    row = lax.broadcasted_iota(jnp.int32, (8, cols), 0)
    for start in range(0, rows, 8):
        v1 = base_ref[pl.ds(start, 8), :]
        if start == 0:
            v1 = v1 - jnp.where(row == 0, smooth_weight * above[0], 0.0)
        if start == rows - 8:
            v1 = v1 - jnp.where(row == 7, smooth_weight * below[0], 0.0)
        v1_ref[pl.ds(NEAR + start, 8), own] = v1
        v1_out_ref[pl.ds(start, 8), :] = v1

    def edge_row(halo, inner, at):
        nearest, second, weight = halo
        inner = f_ref[pl.ds(inner, 1), :] * w_ref[pl.ds(inner, 1), :]
        padded = jnp.concatenate([nearest, jnp.zeros((1, LANES), jnp.float32)], axis=1)
        beside = second + inner + beside_columns(padded)[:, :cols]
        v1_ref[pl.ds(at, 1), own] = weight * nearest + smooth_weight * (4.0 * nearest - beside)

    pl.when(jnp.logical_not(first_row))(lambda: edge_row(above, 0, NEAR - 1))
    pl.when(jnp.logical_not(last_row))(lambda: edge_row(below, rows - 1, NEAR + rows))

    lane = lax.broadcasted_iota(jnp.int32, (8, LANES), 1)
    last_sum = jnp.zeros((8, cols), jnp.float32)
    for start in range(0, rows, 8):
        at = pl.ds(start, 8)
        v1, v2 = image(v1_ref, w_ref[at, :], NEAR + start)
        last_sum = last_sum + v1 * v2
        edge_ref[at, :] = columns_to_lanes(((1, v1), (2, v2)), edge_in_ref[at, :], lane)

    def narrowed(total):
        return sum(total[:, k : k + LANES] for k in range(0, cols, LANES))

    first_sum = [jnp.zeros((1, cols), jnp.float32) for _ in range(2)]
    for halo, inner in ((above, 0), (below, rows - 1)):
        at = pl.ds(inner, 1)
        added = -smooth_weight * halo[0]
        first_sum[0] = first_sum[0] + f_ref[at, :] * w_ref[at, :] * added
        first_sum[1] = first_sum[1] + (2.0 * base_ref[at, :] + added) * added
    totals = [jnp.sum(sums_ref[pl.ds(8 * i, 8), :], axis=0, keepdims=True) for i in range(3)]
    totals = [totals[0], totals[1] + narrowed(first_sum[0]), totals[2] + narrowed(first_sum[1])]
    totals.append(jnp.sum(narrowed(last_sum), axis=0, keepdims=True))
    result = jnp.zeros((1, LANES), jnp.float32)
    for i, total in enumerate(totals):
        result = jnp.where(lane[:1] == i, jnp.sum(total, axis=1, keepdims=True), result)
    vectors = edge_ref[...].T
    message = [result] + [vectors[k : k + 1, :] for k in range(VECTORS)]
    copies = jnp.concatenate(message * 8, axis=0)
    for start in range(0, out_ref.shape[0], copies.shape[0]):
        out_ref[pl.ds(start, copies.shape[0]), :] = copies


def coupled(parts_ref, nrows, ncols):
    count = nrows * ncols
    lam = smooth_weight

    def part(k):
        return parts_ref[:, :, pl.ds(k * LANES, LANES)].reshape(count, LANES)

    device = lax.broadcasted_iota(jnp.int32, (count, LANES), 0)
    lane = lax.broadcasted_iota(jnp.int32, (count, LANES), 1)
    joined = device % ncols < ncols - 1
    a0, a1, ua, wa = (jnp.where(joined, part(1 + k), 0.0) for k in range(4))
    b0, b1, ub, wb = (jnp.where(joined, pltpu.roll(part(5 + k), count - 1, 0), 0.0) for k in range(4))

    def next_row(field):
        inside = pltpu.roll(field, LANES - 1, 1)
        beyond = jnp.where(device < count - ncols, pltpu.roll(inside, count - ncols, 0), 0.0)
        return jnp.where(lane == LANES - 1, beyond, inside)

    def total(field):
        return jnp.sum(jnp.sum(field, axis=0, keepdims=True), axis=1, keepdims=True)

    scalars = jnp.sum(part(0), axis=0, keepdims=True)
    m0, m1, m2, m3 = (total(jnp.where(lane[:1] == i, scalars, 0.0)) for i in range(4))
    m1 = m1 - 2.0 * lam * total(a0 * b0)
    m2 = m2 + total(lam * lam * (a0 * a0 + b0 * b0) - 2.0 * lam * (a1 * b0 + b1 * a0))
    m3 = m3 + total(
        lam * lam * ((wa + 4.0 * lam) * b0 * b0 + (wb + 4.0 * lam) * a0 * a0)
        - 2.0 * lam * (b0 * ua + a0 * ub + (a1 - lam * b0) * (b1 - lam * a0))
        - 2.0 * lam * lam * lam * (a0 * next_row(a0) + b0 * next_row(b0))
    )
    return m0, m1, m2, m3


def neighbours(parts_ref, nrows, ncols):
    row, col = lax.axis_index("rows"), lax.axis_index("cols")
    even = is_even()
    towards = jnp.where(even, 1, -1)
    lane = lax.broadcasted_iota(jnp.int32, (LANES, LANES), 1)
    vectors = []
    for vector, step_col in ((1, -1), (5, 1)):
        for step_row in (0, towards, -towards):
            r, c = row + step_row, col + step_col
            there = (r >= 0) & (r < nrows) & (c >= 0) & (c < ncols)
            index = jnp.where(there, r * ncols + c, 0)
            found = parts_ref[index, :, pl.ds(vector * LANES, LANES)]
            vectors.append(jnp.where(there, found, 0.0))
    vectors.append(jnp.zeros((LANES - len(vectors), LANES), jnp.float32))
    columns = jnp.concatenate(vectors, axis=0).T
    sides = []
    for begin, target in ((0, 0), (3, LANES - 1)):
        own, near, far = (
            jnp.where(lane == target, pltpu.roll(columns, (target - begin - k) % LANES, 1), 0.0) for k in range(3)
        )
        near = jnp.where(even, near[:REACH], near[LANES - REACH :])
        far = jnp.where(even, far[LANES - REACH :], far[:REACH])
        sides.append(jnp.concatenate([own, near, far], axis=0))
    return sides


def guard_rows(f_ref, w_ref, narrow_ref, near_ref, at_cols):
    rows = f_ref.shape[0]
    even = is_even()
    top = f_ref[pl.ds(0, 1), at_cols] * w_ref[pl.ds(0, 1), at_cols]
    bottom = f_ref[pl.ds(rows - 1, 1), at_cols] * w_ref[pl.ds(rows - 1, 1), at_cols]
    near = jnp.where(even, near_ref[pl.ds(2 * REACH, 1), at_cols], near_ref[pl.ds(2 * REACH + 7, 1), at_cols])
    far = narrow_ref[pl.ds(3, 1), at_cols]
    return (
        (jnp.where(even, bottom, near), jnp.where(even, near, top)),
        (jnp.where(even, far, bottom), jnp.where(even, top, far)),
    )


def halo_fields(f_ref, w_ref, narrow_ref, near_ref, far_ref, near_v1_ref, far_v1_ref, v0_ref):
    rows, cols = f_ref.shape
    own, pad = pl.ds(0, cols), pl.ds(cols, LANES)
    v0_ref[:, pad] = jnp.zeros((REACH + 2 * NEAR, LANES), jnp.float32)
    guards = guard_rows(f_ref, w_ref, narrow_ref, near_ref, own)
    for halo_ref, v1_ref, (above, below) in zip((near_ref, far_ref), (near_v1_ref, far_v1_ref), guards):
        v0_ref[pl.ds(NEAR - 1, 1), own] = above
        v0_ref[pl.ds(NEAR + REACH, 1), own] = below
        for start in range(0, REACH, 8):
            v0_ref[pl.ds(NEAR + start, 8), own] = halo_ref[pl.ds(start, 8), :] * halo_ref[pl.ds(REACH + start, 8), :]
        for start in range(0, REACH, 8):
            _, v1_ref[pl.ds(start, 8), :] = image(v0_ref, halo_ref[pl.ds(REACH + start, 8), :], NEAR + start)


def edge_fields(side, f_ref, w_ref, narrow_ref, near_ref, far_ref, near_v1_ref, far_v1_ref, v0_ref):
    cols = f_ref.shape[1]
    at_cols, there = pl.ds(side * (cols - LANES), LANES), pl.ds(side * LANES, LANES)
    outermost = lax.broadcasted_iota(jnp.int32, (8, LANES), 1) == side * (LANES - 1)
    guards = guard_rows(f_ref, w_ref, narrow_ref, near_ref, at_cols)
    for halo_ref, v1_ref, (above, below) in zip((near_ref, far_ref), (near_v1_ref, far_v1_ref), guards):
        v0_ref[pl.ds(NEAR - 1, 1), :] = above
        v0_ref[pl.ds(NEAR + REACH, 1), :] = below
        for start in range(0, REACH, 8):
            at, weight_at = pl.ds(start, 8), pl.ds(REACH + start, 8)
            v0_ref[pl.ds(NEAR + start, 8), :] = halo_ref[at, at_cols] * halo_ref[weight_at, at_cols]
        for start in range(0, REACH, 8):
            here = v0_ref[pl.ds(NEAR + start, 8), :]
            inner = pltpu.roll(here, 1 if side else LANES - 1, 1)
            outer = jnp.where(outermost, 0.0, pltpu.roll(here, LANES - 1 if side else 1, 1))
            beside = v0_ref[pl.ds(NEAR + start - 1, 8), :] + v0_ref[pl.ds(NEAR + start + 1, 8), :] + inner + outer
            weight = halo_ref[pl.ds(REACH + start, 8), at_cols]
            v1_ref[pl.ds(start, 8), there] = weight * here + smooth_weight * (4.0 * here - beside)


def regions(f_ref, w_ref, v1_ref, near_ref, near_v1_ref, far_ref, far_v1_ref, step):
    for start in range(0, f_ref.shape[0], step):
        yield start, (f_ref, start), (w_ref, start), (v1_ref, start)
    for base, halo_ref, field_ref in ((f_ref.shape[0], near_ref, near_v1_ref), (f_ref.shape[0] + REACH, far_ref, far_v1_ref)):
        for start in range(0, REACH, step):
            yield base + start, (halo_ref, start), (halo_ref, REACH + start), (field_ref, start)


def dot(left, right):
    return jnp.dot(left, right, preferred_element_type=jnp.float32)


def row_pass(rowtaps_ref, high, low, rows):
    table = rowtaps_ref[...]
    both = dot(table, high)
    return both[:rows] + (both[rows:] + dot(table[:rows], low))


def edges_kernel(
    nrows, ncols, parts_ref, f_ref, w_ref, v1_ref, narrow_ref, near_ref, far_ref, rowtaps_ref,
    coefficients_ref, left_ref, right_ref, one_ref, other_ref, near_v1_ref, far_v1_ref, v0_ref, high_ref, low_ref,
):
    rows, cols = f_ref.shape
    for side in range(2):
        edge_fields(side, f_ref, w_ref, narrow_ref, near_ref, far_ref, near_v1_ref, far_v1_ref, v0_ref)
    c0, c1 = coefficients(*coupled(parts_ref, nrows, ncols))
    coefficients_ref[pl.ds(0, 8), :] = jnp.broadcast_to(c0, (8, LANES))
    coefficients_ref[pl.ds(8, 8), :] = jnp.broadcast_to(c1, (8, LANES))
    sides = neighbours(parts_ref, nrows, ncols)
    left_ref[...], right_ref[...] = sides

    step = 16
    fields = (f_ref, w_ref, v1_ref, near_ref, near_v1_ref, far_ref, far_v1_ref)
    for side, begin in enumerate((0, cols - LANES)):
        at_cols = pl.ds(begin, LANES)
        for start, (flux_ref, flux_row), (weight_ref, weight_row), (field_ref, field_row) in regions(*fields, step):
            flux, weight = flux_ref[pl.ds(flux_row, step), at_cols], weight_ref[pl.ds(weight_row, step), at_cols]
            v1_cols = at_cols if start < rows else pl.ds(side * LANES, LANES)
            v1 = field_ref[pl.ds(field_row, step), v1_cols]
            v1 = v1 - smooth_weight * sides[side][start : start + step]
            scatter = flux - (c0 * (flux * weight) + c1 * v1)
            high, low = split_values(scatter * scatter)
            high_ref[pl.ds(start, step), pl.ds(side * LANES, LANES)] = high
            low_ref[pl.ds(start, step), pl.ds(side * LANES, LANES)] = low
    passed = row_pass(rowtaps_ref, high_ref[...], low_ref[...], rows)
    upper, lower = slice(0, rows // 2), slice(rows // 2, rows)
    first, last = passed[:, :LANES], passed[:, LANES:]
    on_left = lax.broadcasted_iota(jnp.int32, (rows // 2, LANES), 1) < REACH
    first = jnp.where(on_left, first[upper], pltpu.roll(first[lower], REACH, 1))
    last = jnp.where(on_left, pltpu.roll(last[upper], REACH, 1), last[lower])
    even = is_even("cols")
    one_ref[...] = jnp.where(even, last, first)
    other_ref[...] = jnp.where(even, first, last)


def main_kernel(
    coefficients_ref, left_ref, right_ref, f_ref, w_ref, v1_ref, narrow_ref, near_ref, far_ref, rowtaps_ref, coltaps_ref,
    background_ref, rms_ref, sides_ref, near_v1_ref, far_v1_ref, v0_ref, high_ref, low_ref,
):
    rows, cols = f_ref.shape
    halo_fields(f_ref, w_ref, narrow_ref, near_ref, far_ref, near_v1_ref, far_v1_ref, v0_ref)
    c0, c1 = coefficients_ref[pl.ds(0, 1), pl.ds(0, 1)], coefficients_ref[pl.ds(8, 1), pl.ds(0, 1)]
    step = 16
    fields = (f_ref, w_ref, v1_ref, near_ref, near_v1_ref, far_ref, far_v1_ref)
    for start, *sources in regions(*fields, step):
        flux, weight, v1 = (ref[pl.ds(row, step), :] for ref, row in sources)
        at = pl.ds(start, step)
        v1 = jnp.concatenate(
            [
                v1[:, :LANES] - smooth_weight * left_ref[at, :],
                v1[:, LANES : cols - LANES],
                v1[:, cols - LANES :] - smooth_weight * right_ref[at, :],
            ],
            axis=1,
        )
        background = c0 * (flux * weight) + c1 * v1
        if start < rows:
            background_ref[at, :] = background
        scatter = flux - background
        high_ref[at, :], low_ref[at, :] = split_values(scatter * scatter)
    passed = row_pass(rowtaps_ref, high_ref[...], low_ref[...], rows)
    _, _, first_col, last_col = at_edges()
    nothing = jnp.zeros((rows, LANES), jnp.float32)
    passed = jnp.concatenate([nothing, passed, nothing], axis=1)
    high, low = split_values(pltpu.roll(passed, passed.shape[1] - (LANES - REACH), 1))
    blocks = cols // LANES
    kinds = {0: first_col.astype(jnp.int32), blocks - 1: 2 * last_col.astype(jnp.int32)}
    for j in range(blocks):
        at = slice(j * LANES, j * LANES + 2 * LANES)
        smoothed = product_of_pairs(high[:, at], low[:, at], coltaps_ref[kinds.get(j, 0)])
        if j in kinds:
            sides_ref[:, pl.ds(LANES * (j > 0), LANES)] = smoothed
        else:
            rms_ref[:, pl.ds(j * LANES, LANES)] = jnp.sqrt(smoothed + 1e-06)


def product_of_pairs(high, low, table):
    count = table.shape[1] // 2
    both = dot(high, table)
    return both[:, :count] + (both[:, count:] + dot(low, table[:, :count]))


def final_kernel(rms_in_ref, sides_ref, one_ref, other_ref, sidetaps_ref, rms_ref, blocks_ref, sems):
    rows, cols = rms_ref.shape
    del rms_in_ref
    _, _, first_col, last_col = at_edges()
    even = is_even("cols")
    left = jnp.where(even, other_ref[...], one_ref[...])
    right = jnp.where(even, one_ref[...], other_ref[...])
    copies = []
    for side, (halo, outside) in enumerate(((left, first_col), (right, last_col))):
        high, low = split_values(halo)
        added = product_of_pairs(high, low, sidetaps_ref[side])
        added = jnp.where(outside, 0.0, jnp.concatenate([added[:, :LANES], added[:, LANES:]], axis=0))
        blocks_ref[side] = jnp.sqrt(sides_ref[:, pl.ds(side * LANES, LANES)] + added + 1e-06)
        target = rms_ref.at[:, pl.ds(side * (cols - LANES), LANES)]
        copies.append(pltpu.make_async_copy(blocks_ref.at[side], target, sems.at[side]))
        copies[-1].start()
    for copy in copies:
        copy.wait()


def swap(block, axis, first):
    nrows, ncols = lax.axis_size("rows"), lax.axis_size("cols")
    count = lax.axis_size(axis)
    pairs = []
    for r in range(nrows):
        for c in range(ncols):
            along = r if axis == "rows" else c
            other = along + 1 if (along - first) % 2 == 0 else along - 1
            if 0 <= other < count:
                partner = (other, c) if axis == "rows" else (r, other)
            else:
                partner = (r, c ^ 1) if axis == "rows" else (r ^ 1, c)
            pairs.append((r * ncols + c, partner[0] * ncols + partner[1]))
    return lax.ppermute(block, ("rows", "cols"), pairs)


def call(kernel, name, outs, scratch=(), limit=16, in_place=False):
    vmem = pl.BlockSpec(memory_space=pltpu.VMEM)
    there = pl.BlockSpec(memory_space=pl.ANY)

    def run(*args):
        return pl.pallas_call(
            kernel,
            out_shape=tuple(jax.ShapeDtypeStruct(shape, jnp.float32) for shape in outs),
            in_specs=[there if in_place and i == 0 else vmem for i in range(len(args))],
            out_specs=(there if in_place else vmem,) * len(outs),
            scratch_shapes=list(scratch),
            input_output_aliases={0: 0} if in_place else {},
            compiler_params=pltpu.CompilerParams(vmem_limit_bytes=limit << 20),
            name=name,
        )(*args)

    return run


def shards(coadd_flux, inverse_variance, source_mask):
    rows, cols = coadd_flux.shape
    nrows, ncols = lax.axis_size("rows"), lax.axis_size("cols")
    message = (VECTORS + 1) * LANES

    def scratch(*shape, dtype=jnp.float32):
        return pltpu.VMEM(shape, dtype)

    taken = []
    for above, below in ((0, rows - 1), (1, rows - 2), (REACH, rows - 1 - REACH)):
        start = (jnp.where(is_even(), above, below), 0)
        flux, variance, mask = (
            lax.dynamic_slice(x, start, (1, cols)) for x in (coadd_flux, inverse_variance, source_mask)
        )
        taken.append((flux, weights(variance, mask)))
    products = [flux * weight for flux, weight in taken]
    narrow = swap(jnp.concatenate([products[0], products[1], taken[0][1], products[2]]), "rows", 1)

    own = (coadd_flux, weights(inverse_variance, source_mask))
    field = scratch(rows + 2 * NEAR, cols + LANES)
    to_near, to_far, *base = call(
        prepare_kernel,
        "prepare",
        ((2 * REACH + 8, cols), (2 * REACH, cols), (rows, cols), (3 * 8, LANES), (rows, LANES)),
        (field,),
    )(*own)
    to_near, to_far, narrow = lax.optimization_barrier((to_near, to_far, narrow))
    near = swap(to_near, "rows", 0)
    far = swap(to_far, "rows", 1)

    devices = nrows * ncols
    parts, own_v1 = call(
        moments_kernel,
        "moments",
        ((devices * (VECTORS + 1), LANES), (rows, cols)),
        (field, scratch(rows, LANES)),
    )(*own, *base, narrow, near)
    parts = lax.all_to_all(parts.reshape(devices, 1, message), ("rows", "cols"), 0, 0, tiled=True)
    first_row, last_row, _, _ = at_edges()
    kind = jnp.where(is_even(), first_row.astype(jnp.int32), 2 + last_row.astype(jnp.int32))
    row_taps = lax.dynamic_index_in_dim(jnp.asarray(row_tables(rows)), kind, keepdims=False)
    col_taps = jnp.asarray(col_tables())
    reached, packed = rows + 2 * REACH, (rows // 2, LANES)
    fields = (*own, own_v1, narrow, near, far)
    halves = (scratch(REACH, 2 * LANES),) * 2
    numbers, left, right, to_one, to_other = call(
        functools.partial(edges_kernel, nrows, ncols),
        "edges",
        ((16, LANES), (reached, LANES), (reached, LANES), packed, packed),
        halves + (scratch(REACH + 2 * NEAR, LANES),) + (scratch(reached, 2 * LANES, dtype=jnp.bfloat16),) * 2,
    )(parts, *fields, row_taps)
    one = swap(to_one, "cols", 0)
    other = swap(to_other, "cols", 1)
    halves = (scratch(REACH, cols),) * 2
    background, rms, sides = call(
        main_kernel,
        "main",
        ((rows, cols), (rows, cols), (rows, 2 * LANES)),
        halves + (scratch(REACH + 2 * NEAR, cols + LANES),) + (scratch(reached, cols, dtype=jnp.bfloat16),) * 2,
    )(numbers, left, right, *fields, row_taps, col_taps)
    (rms,) = call(
        final_kernel, "final", ((rows, cols),), (scratch(2, rows, LANES), pltpu.SemaphoreType.DMA((2,))), in_place=True
    )(rms, sides, one, other, jnp.asarray(side_tables()))
    return background, rms


def solution(mesh):
    return jax.shard_map(
        shards,
        mesh=mesh,
        in_specs=(P("rows", "cols"), P("rows", "cols"), P("rows", "cols")),
        out_specs=(P("rows", "cols"), P("rows", "cols")),
        check_vma=False,
    )
```

```python
import functools

import jax
import jax.numpy as jnp
import ml_dtypes
import numpy as np
from jax import lax
from jax.experimental import pallas as pl
from jax.experimental.pallas import tpu as pltpu
from jax.sharding import PartitionSpec as P

RADIUS = 32
REACH = 2 * RADIUS
LANES = 128
WIDE = REACH + 8
NEAR = 8
VECTORS = 8

smooth_weight = 2.0
blur_sigma = 10.0


def squared_taps(length, first, last):
    offsets = np.arange(2 * RADIUS + 1) - RADIUS
    taps = np.exp(-offsets * offsets / (2.0 * blur_sigma * blur_sigma))
    taps = taps / taps.sum()

    def band(count):
        table = np.zeros((count, count + 2 * RADIUS))
        for k in range(2 * RADIUS + 1):
            table[np.arange(count), np.arange(count) + k] = taps[k]
        return table

    inner = band(length + 2 * RADIUS)
    if first:
        inner[:RADIUS] = 0.0
    if last:
        inner[-RADIUS:] = 0.0
    return band(length) @ inner


def split(table):
    high = table.astype(np.float32).astype(ml_dtypes.bfloat16)
    low = (table - high.astype(np.float64)).astype(np.float32).astype(ml_dtypes.bfloat16)
    return high, low


def row_tables(length):
    tables = []
    for first, last, odd in ((False, False, False), (True, False, False), (False, False, True), (False, True, True)):
        table = squared_taps(length, first, last)
        above, own, below = table[:, :REACH], table[:, REACH : REACH + length], table[:, REACH + length :]
        near, far = (above, below) if odd else (below, above)
        if first or last:
            far = np.zeros_like(far)
        tables.append(np.concatenate(split(np.concatenate([own, near, far], axis=1)), axis=0))
    return np.stack(tables)


def col_tables():
    tables = []
    for first, last in ((False, False), (True, False), (False, True)):
        table = squared_taps(LANES, first, last)
        if first:
            table[:, :REACH] = 0.0
        if last:
            table[:, REACH + LANES :] = 0.0
        tables.append(np.concatenate(split(table.T), axis=1))
    return np.stack(tables)


def side_tables():
    table = squared_taps(LANES, False, False).T
    tables = []
    for part in (table[:REACH], table[REACH + LANES :]):
        nothing = np.zeros_like(part)
        tables.append(np.concatenate(split(np.block([[part, nothing], [nothing, part]])), axis=1))
    return np.stack(tables)


def split_values(values):
    high = values.astype(jnp.bfloat16)
    return high, (values - high.astype(jnp.float32)).astype(jnp.bfloat16)


def at_edges():
    row, col = lax.axis_index("rows"), lax.axis_index("cols")
    return (
        row == 0,
        row == lax.axis_size("rows") - 1,
        col == 0,
        col == lax.axis_size("cols") - 1,
    )


def is_even(axis="rows"):
    return lax.axis_index(axis) % 2 == 0


def beside_columns(field):
    width = field.shape[1]
    return pltpu.roll(field, 1, 1) + pltpu.roll(field, width - 1, 1)


def weights(inverse_variance, source_mask):
    return inverse_variance * (1.0 - source_mask.astype(jnp.float32))


def coefficients(m0, m1, m2, m3):
    alpha0 = m0 / m1
    norm1 = jnp.maximum(m0 - 2.0 * alpha0 * m1 + alpha0 * alpha0 * m2, 0.0)
    grown = 1.0 + norm1 / m0
    image1 = grown * grown * m1 - 2.0 * grown * alpha0 * m2 + alpha0 * alpha0 * m3
    alpha1 = jnp.where(image1 > 0.0, norm1 / image1, 0.0)
    return alpha0 + alpha1 * grown, -alpha1 * alpha0


def image(ref, weight, start):
    cols = weight.shape[1]
    own = pl.ds(0, cols)
    here = ref[pl.ds(start, 8), :]
    beside = ref[pl.ds(start - 1, 8), own] + ref[pl.ds(start + 1, 8), own] + beside_columns(here)[:, :cols]
    here = here[:, :cols]
    return here, weight * here + smooth_weight * (4.0 * here - beside)


def columns_to_lanes(fields, edges, lane):
    for k, field in fields:
        edges = jnp.where(lane == k, pltpu.roll(field[:, field.shape[1] - LANES :], k + 1, 1), edges)
        edges = jnp.where(lane == 4 + k, pltpu.roll(field[:, :LANES], 4 + k, 1), edges)
    return edges


def prepare_kernel(f_ref, w_ref, near_ref, far_ref, v1_ref, sums_ref, edge_ref, v0_ref):
    rows = f_ref.shape[0]

    def write(out_ref, begin):
        out_ref[pl.ds(0, REACH), :] = f_ref[pl.ds(begin, REACH), :]
        out_ref[pl.ds(REACH, REACH), :] = w_ref[pl.ds(begin, REACH), :]

    def near_product(begin):
        near_ref[pl.ds(2 * REACH, 8), :] = f_ref[pl.ds(begin, 8), :] * w_ref[pl.ds(begin, 8), :]

    @pl.when(is_even())
    def _():
        write(near_ref, rows - REACH)
        near_product(rows - WIDE)
        write(far_ref, 0)

    @pl.when(jnp.logical_not(is_even()))
    def _():
        write(near_ref, 0)
        near_product(REACH)
        write(far_ref, rows - REACH)

    cols = f_ref.shape[1]
    own = pl.ds(0, cols)
    v0_ref[:, pl.ds(cols, LANES)] = jnp.zeros((rows + 2 * NEAR, LANES), jnp.float32)
    for start in (0, NEAR + rows):
        v0_ref[pl.ds(start, NEAR), own] = jnp.zeros((NEAR, cols), jnp.float32)
    for start in range(0, rows, 8):
        at = pl.ds(start, 8)
        v0_ref[pl.ds(NEAR + start, 8), own] = f_ref[at, :] * w_ref[at, :]
    lane = lax.broadcasted_iota(jnp.int32, (8, LANES), 1)
    sums = [jnp.zeros((8, cols), jnp.float32) for _ in range(3)]
    for start in range(0, rows, 8):
        at = pl.ds(start, 8)
        weight = w_ref[at, :]
        v0, v1 = image(v0_ref, weight, NEAR + start)
        v1_ref[at, :] = v1
        sums = [total + term for total, term in zip(sums, (v0 * v0, v0 * v1, v1 * v1))]
        edge_ref[at, :] = columns_to_lanes(((0, v0), (3, weight)), jnp.zeros((8, LANES), jnp.float32), lane)
    for i, total in enumerate(sums):
        sums_ref[pl.ds(8 * i, 8), :] = sum(total[:, k : k + LANES] for k in range(0, cols, LANES))


def moments_kernel(f_ref, w_ref, base_ref, sums_ref, edge_in_ref, narrow_ref, near_ref, out_ref, v1_ref, edge_ref):
    rows, cols = f_ref.shape
    first_row, last_row, _, _ = at_edges()
    even = is_even()
    own, pad = pl.ds(0, cols), pl.ds(cols, LANES)

    def near_rows(nearest, second):
        return (
            near_ref[pl.ds(nearest, 1), :] * near_ref[pl.ds(REACH + nearest, 1), :],
            near_ref[pl.ds(second, 1), :] * near_ref[pl.ds(REACH + second, 1), :],
            near_ref[pl.ds(REACH + nearest, 1), :],
        )

    outermost = first_row | last_row
    far_rows = tuple(jnp.where(outermost, 0.0, narrow_ref[pl.ds(k, 1), :]) for k in range(3))
    above = [jnp.where(even, far, near) for far, near in zip(far_rows, near_rows(REACH - 1, REACH - 2))]
    below = [jnp.where(even, near, far) for far, near in zip(far_rows, near_rows(0, 1))]

    v1_ref[:, pad] = jnp.zeros((rows + 2 * NEAR, LANES), jnp.float32)
    for start in (0, NEAR + rows):
        v1_ref[pl.ds(start, NEAR), own] = jnp.zeros((NEAR, cols), jnp.float32)
    row = lax.broadcasted_iota(jnp.int32, (8, cols), 0)
    for start in range(0, rows, 8):
        v1 = base_ref[pl.ds(start, 8), :]
        if start == 0:
            v1 = v1 - jnp.where(row == 0, smooth_weight * above[0], 0.0)
        if start == rows - 8:
            v1 = v1 - jnp.where(row == 7, smooth_weight * below[0], 0.0)
        v1_ref[pl.ds(NEAR + start, 8), own] = v1

    def edge_row(halo, inner, at):
        nearest, second, weight = halo
        inner = f_ref[pl.ds(inner, 1), :] * w_ref[pl.ds(inner, 1), :]
        padded = jnp.concatenate([nearest, jnp.zeros((1, LANES), jnp.float32)], axis=1)
        beside = second + inner + beside_columns(padded)[:, :cols]
        v1_ref[pl.ds(at, 1), own] = weight * nearest + smooth_weight * (4.0 * nearest - beside)

    pl.when(jnp.logical_not(first_row))(lambda: edge_row(above, 0, NEAR - 1))
    pl.when(jnp.logical_not(last_row))(lambda: edge_row(below, rows - 1, NEAR + rows))

    lane = lax.broadcasted_iota(jnp.int32, (8, LANES), 1)
    last_sum = jnp.zeros((8, cols), jnp.float32)
    for start in range(0, rows, 8):
        at = pl.ds(start, 8)
        v1, v2 = image(v1_ref, w_ref[at, :], NEAR + start)
        last_sum = last_sum + v1 * v2
        edge_ref[at, :] = columns_to_lanes(((1, v1), (2, v2)), edge_in_ref[at, :], lane)

    def narrowed(total):
        return sum(total[:, k : k + LANES] for k in range(0, cols, LANES))

    first_sum = [jnp.zeros((1, cols), jnp.float32) for _ in range(2)]
    for halo, inner in ((above, 0), (below, rows - 1)):
        at = pl.ds(inner, 1)
        added = -smooth_weight * halo[0]
        first_sum[0] = first_sum[0] + f_ref[at, :] * w_ref[at, :] * added
        first_sum[1] = first_sum[1] + (2.0 * base_ref[at, :] + added) * added
    totals = [jnp.sum(sums_ref[pl.ds(8 * i, 8), :], axis=0, keepdims=True) for i in range(3)]
    totals = [totals[0], totals[1] + narrowed(first_sum[0]), totals[2] + narrowed(first_sum[1])]
    totals.append(jnp.sum(narrowed(last_sum), axis=0, keepdims=True))
    result = jnp.zeros((1, LANES), jnp.float32)
    for i, total in enumerate(totals):
        result = jnp.where(lane[:1] == i, jnp.sum(total, axis=1, keepdims=True), result)
    vectors = edge_ref[...].T
    message = [result] + [vectors[k : k + 1, :] for k in range(VECTORS)]
    copies = jnp.concatenate(message * 8, axis=0)
    for start in range(0, out_ref.shape[0], copies.shape[0]):
        out_ref[pl.ds(start, copies.shape[0]), :] = copies


def coupled(parts_ref, nrows, ncols):
    count = nrows * ncols
    lam = smooth_weight

    def part(k):
        return parts_ref[:, :, pl.ds(k * LANES, LANES)].reshape(count, LANES)

    device = lax.broadcasted_iota(jnp.int32, (count, LANES), 0)
    lane = lax.broadcasted_iota(jnp.int32, (count, LANES), 1)
    joined = device % ncols < ncols - 1
    a0, a1, ua, wa = (jnp.where(joined, part(1 + k), 0.0) for k in range(4))
    b0, b1, ub, wb = (jnp.where(joined, pltpu.roll(part(5 + k), count - 1, 0), 0.0) for k in range(4))

    def next_row(field):
        inside = pltpu.roll(field, LANES - 1, 1)
        beyond = jnp.where(device < count - ncols, pltpu.roll(inside, count - ncols, 0), 0.0)
        return jnp.where(lane == LANES - 1, beyond, inside)

    def total(field):
        return jnp.sum(jnp.sum(field, axis=0, keepdims=True), axis=1, keepdims=True)

    scalars = jnp.sum(part(0), axis=0, keepdims=True)
    m0, m1, m2, m3 = (total(jnp.where(lane[:1] == i, scalars, 0.0)) for i in range(4))
    m1 = m1 - 2.0 * lam * total(a0 * b0)
    m2 = m2 + total(lam * lam * (a0 * a0 + b0 * b0) - 2.0 * lam * (a1 * b0 + b1 * a0))
    m3 = m3 + total(
        lam * lam * ((wa + 4.0 * lam) * b0 * b0 + (wb + 4.0 * lam) * a0 * a0)
        - 2.0 * lam * (b0 * ua + a0 * ub + (a1 - lam * b0) * (b1 - lam * a0))
        - 2.0 * lam * lam * lam * (a0 * next_row(a0) + b0 * next_row(b0))
    )
    return m0, m1, m2, m3


def neighbours(parts_ref, nrows, ncols):
    row, col = lax.axis_index("rows"), lax.axis_index("cols")
    even = is_even()
    towards = jnp.where(even, 1, -1)
    lane = lax.broadcasted_iota(jnp.int32, (LANES, LANES), 1)
    vectors = []
    for vector, step_col in ((1, -1), (5, 1)):
        for step_row in (0, towards, -towards):
            r, c = row + step_row, col + step_col
            there = (r >= 0) & (r < nrows) & (c >= 0) & (c < ncols)
            index = jnp.where(there, r * ncols + c, 0)
            found = parts_ref[index, :, pl.ds(vector * LANES, LANES)]
            vectors.append(jnp.where(there, found, 0.0))
    vectors.append(jnp.zeros((LANES - len(vectors), LANES), jnp.float32))
    columns = jnp.concatenate(vectors, axis=0).T
    sides = []
    for begin, target in ((0, 0), (3, LANES - 1)):
        own, near, far = (
            jnp.where(lane == target, pltpu.roll(columns, (target - begin - k) % LANES, 1), 0.0) for k in range(3)
        )
        near = jnp.where(even, near[:REACH], near[LANES - REACH :])
        far = jnp.where(even, far[LANES - REACH :], far[:REACH])
        sides.append(jnp.concatenate([own, near, far], axis=0))
    return sides


def guard_rows(f_ref, w_ref, narrow_ref, near_ref, at_cols):
    rows = f_ref.shape[0]
    first_row, last_row, _, _ = at_edges()
    even = is_even()
    top = f_ref[pl.ds(0, 1), at_cols] * w_ref[pl.ds(0, 1), at_cols]
    bottom = f_ref[pl.ds(rows - 1, 1), at_cols] * w_ref[pl.ds(rows - 1, 1), at_cols]
    near_last = near_ref[pl.ds(REACH - 1, 1), at_cols] * near_ref[pl.ds(2 * REACH - 1, 1), at_cols]
    near_first = near_ref[pl.ds(0, 1), at_cols] * near_ref[pl.ds(REACH, 1), at_cols]
    far_nearest = jnp.where(first_row | last_row, 0.0, narrow_ref[pl.ds(0, 1), at_cols])
    near = jnp.where(even, near_ref[pl.ds(2 * REACH, 1), at_cols], near_ref[pl.ds(2 * REACH + 7, 1), at_cols])
    far = narrow_ref[pl.ds(3, 1), at_cols]
    return (
        (jnp.where(even, far_nearest, near_last), jnp.where(even, near_first, far_nearest)),
        (jnp.where(even, bottom, near), jnp.where(even, near, top)),
        (jnp.where(even, far, bottom), jnp.where(even, top, far)),
    )


def sources(f_ref, w_ref, near_ref, far_ref, v1_refs):
    rows = f_ref.shape[0]
    return (
        (rows, f_ref, w_ref, 0, v1_refs[0]),
        (REACH, near_ref, near_ref, REACH, v1_refs[1]),
        (REACH, far_ref, far_ref, REACH, v1_refs[2]),
    )


def all_fields(f_ref, w_ref, narrow_ref, near_ref, far_ref, v1_refs, v0_ref):
    rows, cols = f_ref.shape
    own, pad = pl.ds(0, cols), pl.ds(cols, LANES)
    v0_ref[:, pad] = jnp.zeros((rows + 2 * NEAR, LANES), jnp.float32)
    guards = guard_rows(f_ref, w_ref, narrow_ref, near_ref, own)
    for (count, flux_ref, weight_ref, weight_row, v1_ref), (above, below) in zip(
        sources(f_ref, w_ref, near_ref, far_ref, v1_refs), guards
    ):
        v0_ref[pl.ds(NEAR - 1, 1), own] = above
        v0_ref[pl.ds(NEAR + count, 1), own] = below
        for start in range(0, count, 8):
            v0_ref[pl.ds(NEAR + start, 8), own] = flux_ref[pl.ds(start, 8), :] * weight_ref[pl.ds(weight_row + start, 8), :]
        for start in range(0, count, 8):
            _, v1_ref[pl.ds(start, 8), :] = image(v0_ref, weight_ref[pl.ds(weight_row + start, 8), :], NEAR + start)


def edge_fields(side, f_ref, w_ref, narrow_ref, near_ref, far_ref, v1_refs, v0_ref):
    cols = f_ref.shape[1]
    at_cols, there = pl.ds(side * (cols - LANES), LANES), pl.ds(side * LANES, LANES)
    outermost = lax.broadcasted_iota(jnp.int32, (8, LANES), 1) == side * (LANES - 1)
    guards = guard_rows(f_ref, w_ref, narrow_ref, near_ref, at_cols)
    for (count, flux_ref, weight_ref, weight_row, v1_ref), (above, below) in zip(
        sources(f_ref, w_ref, near_ref, far_ref, v1_refs), guards
    ):
        v0_ref[pl.ds(NEAR - 1, 1), :] = above
        v0_ref[pl.ds(NEAR + count, 1), :] = below
        for start in range(0, count, 8):
            weight = weight_ref[pl.ds(weight_row + start, 8), at_cols]
            v0_ref[pl.ds(NEAR + start, 8), :] = flux_ref[pl.ds(start, 8), at_cols] * weight
        for start in range(0, count, 8):
            here = v0_ref[pl.ds(NEAR + start, 8), :]
            inner = pltpu.roll(here, 1 if side else LANES - 1, 1)
            outer = jnp.where(outermost, 0.0, pltpu.roll(here, LANES - 1 if side else 1, 1))
            beside = v0_ref[pl.ds(NEAR + start - 1, 8), :] + v0_ref[pl.ds(NEAR + start + 1, 8), :] + inner + outer
            weight = weight_ref[pl.ds(weight_row + start, 8), at_cols]
            v1_ref[pl.ds(start, 8), there] = weight * here + smooth_weight * (4.0 * here - beside)


def regions(f_ref, w_ref, near_ref, far_ref, v1_refs, step):
    base = 0
    for count, flux_ref, weight_ref, weight_row, v1_ref in sources(f_ref, w_ref, near_ref, far_ref, v1_refs):
        for start in range(0, count, step):
            yield base + start, (flux_ref, start), (weight_ref, weight_row + start), (v1_ref, start)
        base += count


def dot(left, right):
    return jnp.dot(left, right, preferred_element_type=jnp.float32)


def row_pass(rowtaps_ref, high, low, rows):
    table = rowtaps_ref[...]
    both = dot(table, high)
    return both[:rows] + (both[rows:] + dot(table[:rows], low))


def edges_kernel(
    nrows, ncols, parts_ref, f_ref, w_ref, narrow_ref, near_ref, far_ref, rowtaps_ref,
    coefficients_ref, left_ref, right_ref, one_ref, other_ref, own_v1_ref, near_v1_ref, far_v1_ref, v0_ref, high_ref, low_ref,
):
    rows, cols = f_ref.shape
    v1_refs = (own_v1_ref, near_v1_ref, far_v1_ref)
    for side in range(2):
        edge_fields(side, f_ref, w_ref, narrow_ref, near_ref, far_ref, v1_refs, v0_ref)
    c0, c1 = coefficients(*coupled(parts_ref, nrows, ncols))
    coefficients_ref[pl.ds(0, 8), :] = jnp.broadcast_to(c0, (8, LANES))
    coefficients_ref[pl.ds(8, 8), :] = jnp.broadcast_to(c1, (8, LANES))
    sides = neighbours(parts_ref, nrows, ncols)
    left_ref[...], right_ref[...] = sides

    step = 16
    fields = (f_ref, w_ref, near_ref, far_ref, v1_refs)
    for side, begin in enumerate((0, cols - LANES)):
        at_cols = pl.ds(begin, LANES)
        for start, (flux_ref, flux_row), (weight_ref, weight_row), (field_ref, field_row) in regions(*fields, step):
            flux, weight = flux_ref[pl.ds(flux_row, step), at_cols], weight_ref[pl.ds(weight_row, step), at_cols]
            v1 = field_ref[pl.ds(field_row, step), pl.ds(side * LANES, LANES)]
            v1 = v1 - smooth_weight * sides[side][start : start + step]
            scatter = flux - (c0 * (flux * weight) + c1 * v1)
            high, low = split_values(scatter * scatter)
            high_ref[pl.ds(start, step), pl.ds(side * LANES, LANES)] = high
            low_ref[pl.ds(start, step), pl.ds(side * LANES, LANES)] = low
    passed = row_pass(rowtaps_ref, high_ref[...], low_ref[...], rows)
    upper, lower = slice(0, rows // 2), slice(rows // 2, rows)
    first, last = passed[:, :LANES], passed[:, LANES:]
    on_left = lax.broadcasted_iota(jnp.int32, (rows // 2, LANES), 1) < REACH
    first = jnp.where(on_left, first[upper], pltpu.roll(first[lower], REACH, 1))
    last = jnp.where(on_left, pltpu.roll(last[upper], REACH, 1), last[lower])
    even = is_even("cols")
    one_ref[...] = jnp.where(even, last, first)
    other_ref[...] = jnp.where(even, first, last)


def main_kernel(
    coefficients_ref, left_ref, right_ref, f_ref, w_ref, narrow_ref, near_ref, far_ref, rowtaps_ref, coltaps_ref,
    background_ref, rms_ref, sides_ref, own_v1_ref, near_v1_ref, far_v1_ref, v0_ref, high_ref, low_ref,
):
    rows, cols = f_ref.shape
    v1_refs = (own_v1_ref, near_v1_ref, far_v1_ref)
    all_fields(f_ref, w_ref, narrow_ref, near_ref, far_ref, v1_refs, v0_ref)
    c0, c1 = coefficients_ref[pl.ds(0, 1), pl.ds(0, 1)], coefficients_ref[pl.ds(8, 1), pl.ds(0, 1)]
    step = 16
    fields = (f_ref, w_ref, near_ref, far_ref, v1_refs)
    for start, *here in regions(*fields, step):
        flux, weight, v1 = (ref[pl.ds(row, step), :] for ref, row in here)
        at = pl.ds(start, step)
        v1 = jnp.concatenate(
            [
                v1[:, :LANES] - smooth_weight * left_ref[at, :],
                v1[:, LANES : cols - LANES],
                v1[:, cols - LANES :] - smooth_weight * right_ref[at, :],
            ],
            axis=1,
        )
        background = c0 * (flux * weight) + c1 * v1
        if start < rows:
            background_ref[at, :] = background
        scatter = flux - background
        high_ref[at, :], low_ref[at, :] = split_values(scatter * scatter)
    passed = row_pass(rowtaps_ref, high_ref[...], low_ref[...], rows)
    _, _, first_col, last_col = at_edges()
    nothing = jnp.zeros((rows, LANES), jnp.float32)
    passed = jnp.concatenate([nothing, passed, nothing], axis=1)
    high, low = split_values(pltpu.roll(passed, passed.shape[1] - (LANES - REACH), 1))
    blocks = cols // LANES
    kinds = {0: first_col.astype(jnp.int32), blocks - 1: 2 * last_col.astype(jnp.int32)}
    for j in range(blocks):
        at = slice(j * LANES, j * LANES + 2 * LANES)
        smoothed = product_of_pairs(high[:, at], low[:, at], coltaps_ref[kinds.get(j, 0)])
        if j in kinds:
            sides_ref[:, pl.ds(LANES * (j > 0), LANES)] = smoothed
        else:
            rms_ref[:, pl.ds(j * LANES, LANES)] = jnp.sqrt(smoothed + 1e-06)


def product_of_pairs(high, low, table):
    count = table.shape[1] // 2
    both = dot(high, table)
    return both[:, :count] + (both[:, count:] + dot(low, table[:, :count]))


def final_kernel(rms_in_ref, sides_ref, one_ref, other_ref, sidetaps_ref, rms_ref, blocks_ref, sems):
    rows, cols = rms_ref.shape
    del rms_in_ref
    _, _, first_col, last_col = at_edges()
    even = is_even("cols")
    left = jnp.where(even, other_ref[...], one_ref[...])
    right = jnp.where(even, one_ref[...], other_ref[...])
    copies = []
    for side, (halo, outside) in enumerate(((left, first_col), (right, last_col))):
        high, low = split_values(halo)
        added = product_of_pairs(high, low, sidetaps_ref[side])
        added = jnp.where(outside, 0.0, jnp.concatenate([added[:, :LANES], added[:, LANES:]], axis=0))
        blocks_ref[side] = jnp.sqrt(sides_ref[:, pl.ds(side * LANES, LANES)] + added + 1e-06)
        target = rms_ref.at[:, pl.ds(side * (cols - LANES), LANES)]
        copies.append(pltpu.make_async_copy(blocks_ref.at[side], target, sems.at[side]))
        copies[-1].start()
    for copy in copies:
        copy.wait()


def swap(block, axis, first):
    nrows, ncols = lax.axis_size("rows"), lax.axis_size("cols")
    count = lax.axis_size(axis)
    pairs = []
    for r in range(nrows):
        for c in range(ncols):
            along = r if axis == "rows" else c
            other = along + 1 if (along - first) % 2 == 0 else along - 1
            if 0 <= other < count:
                partner = (other, c) if axis == "rows" else (r, other)
            else:
                partner = (r, c ^ 1) if axis == "rows" else (r ^ 1, c)
            pairs.append((r * ncols + c, partner[0] * ncols + partner[1]))
    return lax.ppermute(block, ("rows", "cols"), pairs)


def call(kernel, name, outs, scratch=(), limit=16, in_place=False):
    vmem = pl.BlockSpec(memory_space=pltpu.VMEM)
    there = pl.BlockSpec(memory_space=pl.ANY)

    def run(*args):
        return pl.pallas_call(
            kernel,
            out_shape=tuple(jax.ShapeDtypeStruct(shape, jnp.float32) for shape in outs),
            in_specs=[there if in_place and i == 0 else vmem for i in range(len(args))],
            out_specs=(there if in_place else vmem,) * len(outs),
            scratch_shapes=list(scratch),
            input_output_aliases={0: 0} if in_place else {},
            compiler_params=pltpu.CompilerParams(vmem_limit_bytes=limit << 20),
            name=name,
        )(*args)

    return run


def shards(coadd_flux, inverse_variance, source_mask):
    rows, cols = coadd_flux.shape
    nrows, ncols = lax.axis_size("rows"), lax.axis_size("cols")
    message = (VECTORS + 1) * LANES

    def scratch(*shape, dtype=jnp.float32):
        return pltpu.VMEM(shape, dtype)

    taken = []
    for above, below in ((0, rows - 1), (1, rows - 2), (REACH, rows - 1 - REACH)):
        start = (jnp.where(is_even(), above, below), 0)
        flux, variance, mask = (
            lax.dynamic_slice(x, start, (1, cols)) for x in (coadd_flux, inverse_variance, source_mask)
        )
        taken.append((flux, weights(variance, mask)))
    products = [flux * weight for flux, weight in taken]
    narrow = swap(jnp.concatenate([products[0], products[1], taken[0][1], products[2]]), "rows", 1)

    own = (coadd_flux, weights(inverse_variance, source_mask))
    field = scratch(rows + 2 * NEAR, cols + LANES)
    to_near, to_far, *base = call(
        prepare_kernel,
        "prepare",
        ((2 * REACH + 8, cols), (2 * REACH, cols), (rows, cols), (3 * 8, LANES), (rows, LANES)),
        (field,),
    )(*own)
    to_near, to_far, narrow = lax.optimization_barrier((to_near, to_far, narrow))
    near = swap(to_near, "rows", 0)
    far = swap(to_far, "rows", 1)

    devices = nrows * ncols
    (parts,) = call(
        moments_kernel,
        "moments",
        ((devices * (VECTORS + 1), LANES),),
        (field, scratch(rows, LANES)),
    )(*own, *base, narrow, near)
    parts = lax.all_to_all(parts.reshape(devices, 1, message), ("rows", "cols"), 0, 0, tiled=True)
    first_row, last_row, _, _ = at_edges()
    kind = jnp.where(is_even(), first_row.astype(jnp.int32), 2 + last_row.astype(jnp.int32))
    row_taps = lax.dynamic_index_in_dim(jnp.asarray(row_tables(rows)), kind, keepdims=False)
    col_taps = jnp.asarray(col_tables())
    reached, packed = rows + 2 * REACH, (rows // 2, LANES)
    fields = (*own, narrow, near, far)
    v1_parts = [scratch(count, 2 * LANES) for count in (rows, REACH, REACH)]
    numbers, left, right, to_one, to_other = call(
        functools.partial(edges_kernel, nrows, ncols),
        "edges",
        ((16, LANES), (reached, LANES), (reached, LANES), packed, packed),
        [*v1_parts, scratch(rows + 2 * NEAR, LANES)] + [scratch(reached, 2 * LANES, dtype=jnp.bfloat16)] * 2,
    )(parts, *fields, row_taps)
    one = swap(to_one, "cols", 0)
    other = swap(to_other, "cols", 1)
    v1_parts = [scratch(count, cols) for count in (rows, REACH, REACH)]
    background, rms, sides = call(
        main_kernel,
        "main",
        ((rows, cols), (rows, cols), (rows, 2 * LANES)),
        [*v1_parts, field] + [scratch(reached, cols, dtype=jnp.bfloat16)] * 2,
    )(numbers, left, right, *fields, row_taps, col_taps)
    (rms,) = call(
        final_kernel, "final", ((rows, cols),), (scratch(2, rows, LANES), pltpu.SemaphoreType.DMA((2,))), in_place=True
    )(rms, sides, one, other, jnp.asarray(side_tables()))
    return background, rms


def solution(mesh):
    return jax.shard_map(
        shards,
        mesh=mesh,
        in_specs=(P("rows", "cols"), P("rows", "cols"), P("rows", "cols")),
        out_specs=(P("rows", "cols"), P("rows", "cols")),
        check_vma=False,
    )
```

```python
import functools

import jax
import jax.numpy as jnp
import ml_dtypes
import numpy as np
from jax import lax
from jax.experimental import pallas as pl
from jax.experimental.pallas import tpu as pltpu
from jax.sharding import PartitionSpec as P

RADIUS = 32
REACH = 2 * RADIUS
LANES = 128
WIDE = REACH + 8
NEAR = 8
VECTORS = 8

smooth_weight = 2.0
blur_sigma = 10.0


def squared_taps(length, first, last):
    offsets = np.arange(2 * RADIUS + 1) - RADIUS
    taps = np.exp(-offsets * offsets / (2.0 * blur_sigma * blur_sigma))
    taps = taps / taps.sum()

    def band(count):
        table = np.zeros((count, count + 2 * RADIUS))
        for k in range(2 * RADIUS + 1):
            table[np.arange(count), np.arange(count) + k] = taps[k]
        return table

    inner = band(length + 2 * RADIUS)
    if first:
        inner[:RADIUS] = 0.0
    if last:
        inner[-RADIUS:] = 0.0
    return band(length) @ inner


def split(table):
    high = table.astype(np.float32).astype(ml_dtypes.bfloat16)
    low = (table - high.astype(np.float64)).astype(np.float32).astype(ml_dtypes.bfloat16)
    return high, low


def row_tables(length):
    tables = []
    for first, last, odd in ((False, False, False), (True, False, False), (False, False, True), (False, True, True)):
        table = squared_taps(length, first, last)
        above, own, below = table[:, :REACH], table[:, REACH : REACH + length], table[:, REACH + length :]
        near, far = (above, below) if odd else (below, above)
        if first or last:
            far = np.zeros_like(far)
        tables.append(np.concatenate(split(np.concatenate([own, near, far], axis=1)), axis=0))
    return np.stack(tables)


def col_tables():
    tables = []
    for first, last in ((False, False), (True, False), (False, True)):
        table = squared_taps(LANES, first, last)
        if first:
            table[:, :REACH] = 0.0
        if last:
            table[:, REACH + LANES :] = 0.0
        tables.append(np.concatenate(split(table.T), axis=1))
    return np.stack(tables)


def side_tables():
    table = squared_taps(LANES, False, False).T
    tables = []
    for part in (table[:REACH], table[REACH + LANES :]):
        nothing = np.zeros_like(part)
        tables.append(np.concatenate(split(np.block([[part, nothing], [nothing, part]])), axis=1))
    return np.stack(tables)


def split_values(values):
    high = values.astype(jnp.bfloat16)
    return high, (values - high.astype(jnp.float32)).astype(jnp.bfloat16)


def at_edges():
    row, col = lax.axis_index("rows"), lax.axis_index("cols")
    return (
        row == 0,
        row == lax.axis_size("rows") - 1,
        col == 0,
        col == lax.axis_size("cols") - 1,
    )


def is_even(axis="rows"):
    return lax.axis_index(axis) % 2 == 0


def beside_columns(field):
    width = field.shape[1]
    return pltpu.roll(field, 1, 1) + pltpu.roll(field, width - 1, 1)


def weights(inverse_variance, source_mask):
    return inverse_variance * (1.0 - source_mask.astype(jnp.float32))


def coefficients(m0, m1, m2, m3):
    alpha0 = m0 / m1
    norm1 = jnp.maximum(m0 - 2.0 * alpha0 * m1 + alpha0 * alpha0 * m2, 0.0)
    grown = 1.0 + norm1 / m0
    image1 = grown * grown * m1 - 2.0 * grown * alpha0 * m2 + alpha0 * alpha0 * m3
    alpha1 = jnp.where(image1 > 0.0, norm1 / image1, 0.0)
    return alpha0 + alpha1 * grown, -alpha1 * alpha0


def image(ref, weight, start):
    cols = weight.shape[1]
    own = pl.ds(0, cols)
    here = ref[pl.ds(start, 8), :]
    beside = ref[pl.ds(start - 1, 8), own] + ref[pl.ds(start + 1, 8), own] + beside_columns(here)[:, :cols]
    here = here[:, :cols]
    return here, weight * here + smooth_weight * (4.0 * here - beside)


def columns_to_lanes(fields, edges, lane):
    for k, field in fields:
        edges = jnp.where(lane == k, pltpu.roll(field[:, field.shape[1] - LANES :], k + 1, 1), edges)
        edges = jnp.where(lane == 4 + k, pltpu.roll(field[:, :LANES], 4 + k, 1), edges)
    return edges


def prepare_kernel(f_ref, w_ref, near_ref, far_ref, v1_ref, sums_ref, edge_ref, v0_ref):
    rows = f_ref.shape[0]

    def write(out_ref, begin):
        out_ref[pl.ds(0, REACH), :] = f_ref[pl.ds(begin, REACH), :]
        out_ref[pl.ds(REACH, REACH), :] = w_ref[pl.ds(begin, REACH), :]

    def near_product(begin):
        near_ref[pl.ds(2 * REACH, 8), :] = f_ref[pl.ds(begin, 8), :] * w_ref[pl.ds(begin, 8), :]

    @pl.when(is_even())
    def _():
        write(near_ref, rows - REACH)
        near_product(rows - WIDE)
        write(far_ref, 0)

    @pl.when(jnp.logical_not(is_even()))
    def _():
        write(near_ref, 0)
        near_product(REACH)
        write(far_ref, rows - REACH)

    cols = f_ref.shape[1]
    own = pl.ds(0, cols)
    v0_ref[:, pl.ds(cols, LANES)] = jnp.zeros((rows + 2 * NEAR, LANES), jnp.float32)
    for start in (0, NEAR + rows):
        v0_ref[pl.ds(start, NEAR), own] = jnp.zeros((NEAR, cols), jnp.float32)
    for start in range(0, rows, 8):
        at = pl.ds(start, 8)
        v0_ref[pl.ds(NEAR + start, 8), own] = f_ref[at, :] * w_ref[at, :]
    lane = lax.broadcasted_iota(jnp.int32, (8, LANES), 1)
    sums = [jnp.zeros((8, cols), jnp.float32) for _ in range(3)]
    for start in range(0, rows, 8):
        at = pl.ds(start, 8)
        weight = w_ref[at, :]
        v0, v1 = image(v0_ref, weight, NEAR + start)
        v1_ref[at, :] = v1
        sums = [total + term for total, term in zip(sums, (v0 * v0, v0 * v1, v1 * v1))]
        edge_ref[at, :] = columns_to_lanes(((0, v0), (3, weight)), jnp.zeros((8, LANES), jnp.float32), lane)
    for i, total in enumerate(sums):
        sums_ref[pl.ds(8 * i, 8), :] = sum(total[:, k : k + LANES] for k in range(0, cols, LANES))


def moments_kernel(f_ref, w_ref, base_ref, sums_ref, edge_in_ref, narrow_ref, near_ref, out_ref, v1_ref, edge_ref, copies_ref, sems):
    rows, cols = f_ref.shape
    first_row, last_row, _, _ = at_edges()
    even = is_even()
    own, pad = pl.ds(0, cols), pl.ds(cols, LANES)

    def near_rows(nearest, second):
        return (
            near_ref[pl.ds(nearest, 1), :] * near_ref[pl.ds(REACH + nearest, 1), :],
            near_ref[pl.ds(second, 1), :] * near_ref[pl.ds(REACH + second, 1), :],
            near_ref[pl.ds(REACH + nearest, 1), :],
        )

    outermost = first_row | last_row
    far_rows = tuple(jnp.where(outermost, 0.0, narrow_ref[pl.ds(k, 1), :]) for k in range(3))
    above = [jnp.where(even, far, near) for far, near in zip(far_rows, near_rows(REACH - 1, REACH - 2))]
    below = [jnp.where(even, near, far) for far, near in zip(far_rows, near_rows(0, 1))]

    v1_ref[:, pad] = jnp.zeros((rows + 2 * NEAR, LANES), jnp.float32)
    for start in (0, NEAR + rows):
        v1_ref[pl.ds(start, NEAR), own] = jnp.zeros((NEAR, cols), jnp.float32)
    row = lax.broadcasted_iota(jnp.int32, (8, cols), 0)
    for start in range(0, rows, 8):
        v1 = base_ref[pl.ds(start, 8), :]
        if start == 0:
            v1 = v1 - jnp.where(row == 0, smooth_weight * above[0], 0.0)
        if start == rows - 8:
            v1 = v1 - jnp.where(row == 7, smooth_weight * below[0], 0.0)
        v1_ref[pl.ds(NEAR + start, 8), own] = v1

    def edge_row(halo, inner, at):
        nearest, second, weight = halo
        inner = f_ref[pl.ds(inner, 1), :] * w_ref[pl.ds(inner, 1), :]
        padded = jnp.concatenate([nearest, jnp.zeros((1, LANES), jnp.float32)], axis=1)
        beside = second + inner + beside_columns(padded)[:, :cols]
        v1_ref[pl.ds(at, 1), own] = weight * nearest + smooth_weight * (4.0 * nearest - beside)

    pl.when(jnp.logical_not(first_row))(lambda: edge_row(above, 0, NEAR - 1))
    pl.when(jnp.logical_not(last_row))(lambda: edge_row(below, rows - 1, NEAR + rows))

    lane = lax.broadcasted_iota(jnp.int32, (8, LANES), 1)
    last_sum = jnp.zeros((8, cols), jnp.float32)
    for start in range(0, rows, 8):
        at = pl.ds(start, 8)
        v1, v2 = image(v1_ref, w_ref[at, :], NEAR + start)
        last_sum = last_sum + v1 * v2
        edge_ref[at, :] = columns_to_lanes(((1, v1), (2, v2)), edge_in_ref[at, :], lane)

    def narrowed(total):
        return sum(total[:, k : k + LANES] for k in range(0, cols, LANES))

    first_sum = [jnp.zeros((1, cols), jnp.float32) for _ in range(2)]
    for halo, inner in ((above, 0), (below, rows - 1)):
        at = pl.ds(inner, 1)
        added = -smooth_weight * halo[0]
        first_sum[0] = first_sum[0] + f_ref[at, :] * w_ref[at, :] * added
        first_sum[1] = first_sum[1] + (2.0 * base_ref[at, :] + added) * added
    totals = [jnp.sum(sums_ref[pl.ds(8 * i, 8), :], axis=0, keepdims=True) for i in range(3)]
    totals = [totals[0], totals[1] + narrowed(first_sum[0]), totals[2] + narrowed(first_sum[1])]
    totals.append(jnp.sum(narrowed(last_sum), axis=0, keepdims=True))
    result = jnp.zeros((1, LANES), jnp.float32)
    for i, total in enumerate(totals):
        result = jnp.where(lane[:1] == i, jnp.sum(total, axis=1, keepdims=True), result)
    vectors = edge_ref[...].T
    message = [result] + [vectors[k : k + 1, :] for k in range(VECTORS)]
    copies_ref[...] = jnp.concatenate(message * 8, axis=0)
    count = copies_ref.shape[0]
    sent = []
    for i in range(out_ref.shape[0] // count):
        sent.append(pltpu.make_async_copy(copies_ref, out_ref.at[pl.ds(i * count, count), :], sems.at[i]))
        sent[-1].start()
    for copy in sent:
        copy.wait()


def coupled(parts_ref, nrows, ncols):
    count = nrows * ncols
    lam = smooth_weight

    def part(k):
        return parts_ref[:, :, pl.ds(k * LANES, LANES)].reshape(count, LANES)

    device = lax.broadcasted_iota(jnp.int32, (count, LANES), 0)
    lane = lax.broadcasted_iota(jnp.int32, (count, LANES), 1)
    joined = device % ncols < ncols - 1
    a0, a1, ua, wa = (jnp.where(joined, part(1 + k), 0.0) for k in range(4))
    b0, b1, ub, wb = (jnp.where(joined, pltpu.roll(part(5 + k), count - 1, 0), 0.0) for k in range(4))

    def next_row(field):
        inside = pltpu.roll(field, LANES - 1, 1)
        beyond = jnp.where(device < count - ncols, pltpu.roll(inside, count - ncols, 0), 0.0)
        return jnp.where(lane == LANES - 1, beyond, inside)

    def total(field):
        return jnp.sum(jnp.sum(field, axis=0, keepdims=True), axis=1, keepdims=True)

    scalars = jnp.sum(part(0), axis=0, keepdims=True)
    m0, m1, m2, m3 = (total(jnp.where(lane[:1] == i, scalars, 0.0)) for i in range(4))
    m1 = m1 - 2.0 * lam * total(a0 * b0)
    m2 = m2 + total(lam * lam * (a0 * a0 + b0 * b0) - 2.0 * lam * (a1 * b0 + b1 * a0))
    m3 = m3 + total(
        lam * lam * ((wa + 4.0 * lam) * b0 * b0 + (wb + 4.0 * lam) * a0 * a0)
        - 2.0 * lam * (b0 * ua + a0 * ub + (a1 - lam * b0) * (b1 - lam * a0))
        - 2.0 * lam * lam * lam * (a0 * next_row(a0) + b0 * next_row(b0))
    )
    return m0, m1, m2, m3


def neighbours(parts_ref, nrows, ncols):
    row, col = lax.axis_index("rows"), lax.axis_index("cols")
    even = is_even()
    towards = jnp.where(even, 1, -1)
    lane = lax.broadcasted_iota(jnp.int32, (LANES, LANES), 1)
    vectors = []
    for vector, step_col in ((1, -1), (5, 1)):
        for step_row in (0, towards, -towards):
            r, c = row + step_row, col + step_col
            there = (r >= 0) & (r < nrows) & (c >= 0) & (c < ncols)
            index = jnp.where(there, r * ncols + c, 0)
            found = parts_ref[index, :, pl.ds(vector * LANES, LANES)]
            vectors.append(jnp.where(there, found, 0.0))
    vectors.append(jnp.zeros((LANES - len(vectors), LANES), jnp.float32))
    columns = jnp.concatenate(vectors, axis=0).T
    sides = []
    for begin, target in ((0, 0), (3, LANES - 1)):
        own, near, far = (
            jnp.where(lane == target, pltpu.roll(columns, (target - begin - k) % LANES, 1), 0.0) for k in range(3)
        )
        near = jnp.where(even, near[:REACH], near[LANES - REACH :])
        far = jnp.where(even, far[LANES - REACH :], far[:REACH])
        sides.append(jnp.concatenate([own, near, far], axis=0))
    return sides


def guard_rows(f_ref, w_ref, narrow_ref, near_ref, at_cols):
    rows = f_ref.shape[0]
    first_row, last_row, _, _ = at_edges()
    even = is_even()
    top = f_ref[pl.ds(0, 1), at_cols] * w_ref[pl.ds(0, 1), at_cols]
    bottom = f_ref[pl.ds(rows - 1, 1), at_cols] * w_ref[pl.ds(rows - 1, 1), at_cols]
    near_last = near_ref[pl.ds(REACH - 1, 1), at_cols] * near_ref[pl.ds(2 * REACH - 1, 1), at_cols]
    near_first = near_ref[pl.ds(0, 1), at_cols] * near_ref[pl.ds(REACH, 1), at_cols]
    far_nearest = jnp.where(first_row | last_row, 0.0, narrow_ref[pl.ds(0, 1), at_cols])
    near = jnp.where(even, near_ref[pl.ds(2 * REACH, 1), at_cols], near_ref[pl.ds(2 * REACH + 7, 1), at_cols])
    far = narrow_ref[pl.ds(3, 1), at_cols]
    return (
        (jnp.where(even, far_nearest, near_last), jnp.where(even, near_first, far_nearest)),
        (jnp.where(even, bottom, near), jnp.where(even, near, top)),
        (jnp.where(even, far, bottom), jnp.where(even, top, far)),
    )


def sources(f_ref, w_ref, near_ref, far_ref, v1_refs):
    rows = f_ref.shape[0]
    return (
        (rows, f_ref, w_ref, 0, v1_refs[0]),
        (REACH, near_ref, near_ref, REACH, v1_refs[1]),
        (REACH, far_ref, far_ref, REACH, v1_refs[2]),
    )


def all_fields(f_ref, w_ref, narrow_ref, near_ref, far_ref, v1_refs, v0_ref):
    rows, cols = f_ref.shape
    own, pad = pl.ds(0, cols), pl.ds(cols, LANES)
    v0_ref[:, pad] = jnp.zeros((rows + 2 * NEAR, LANES), jnp.float32)
    guards = guard_rows(f_ref, w_ref, narrow_ref, near_ref, own)
    for (count, flux_ref, weight_ref, weight_row, v1_ref), (above, below) in zip(
        sources(f_ref, w_ref, near_ref, far_ref, v1_refs), guards
    ):
        v0_ref[pl.ds(NEAR - 1, 1), own] = above
        v0_ref[pl.ds(NEAR + count, 1), own] = below
        for start in range(0, count, 8):
            v0_ref[pl.ds(NEAR + start, 8), own] = flux_ref[pl.ds(start, 8), :] * weight_ref[pl.ds(weight_row + start, 8), :]
        for start in range(0, count, 8):
            _, v1_ref[pl.ds(start, 8), :] = image(v0_ref, weight_ref[pl.ds(weight_row + start, 8), :], NEAR + start)


def edge_fields(side, f_ref, w_ref, narrow_ref, near_ref, far_ref, v1_refs, v0_ref):
    cols = f_ref.shape[1]
    at_cols, there = pl.ds(side * (cols - LANES), LANES), pl.ds(side * LANES, LANES)
    outermost = lax.broadcasted_iota(jnp.int32, (8, LANES), 1) == side * (LANES - 1)
    guards = guard_rows(f_ref, w_ref, narrow_ref, near_ref, at_cols)
    for (count, flux_ref, weight_ref, weight_row, v1_ref), (above, below) in zip(
        sources(f_ref, w_ref, near_ref, far_ref, v1_refs), guards
    ):
        v0_ref[pl.ds(NEAR - 1, 1), :] = above
        v0_ref[pl.ds(NEAR + count, 1), :] = below
        for start in range(0, count, 8):
            weight = weight_ref[pl.ds(weight_row + start, 8), at_cols]
            v0_ref[pl.ds(NEAR + start, 8), :] = flux_ref[pl.ds(start, 8), at_cols] * weight
        for start in range(0, count, 8):
            here = v0_ref[pl.ds(NEAR + start, 8), :]
            inner = pltpu.roll(here, 1 if side else LANES - 1, 1)
            outer = jnp.where(outermost, 0.0, pltpu.roll(here, LANES - 1 if side else 1, 1))
            beside = v0_ref[pl.ds(NEAR + start - 1, 8), :] + v0_ref[pl.ds(NEAR + start + 1, 8), :] + inner + outer
            weight = weight_ref[pl.ds(weight_row + start, 8), at_cols]
            v1_ref[pl.ds(start, 8), there] = weight * here + smooth_weight * (4.0 * here - beside)


def regions(f_ref, w_ref, near_ref, far_ref, v1_refs, step):
    base = 0
    for count, flux_ref, weight_ref, weight_row, v1_ref in sources(f_ref, w_ref, near_ref, far_ref, v1_refs):
        for start in range(0, count, step):
            yield base + start, (flux_ref, start), (weight_ref, weight_row + start), (v1_ref, start)
        base += count


def dot(left, right):
    return jnp.dot(left, right, preferred_element_type=jnp.float32)


def row_pass(rowtaps_ref, high, low, rows):
    table = rowtaps_ref[...]
    both = dot(table, high)
    return both[:rows] + (both[rows:] + dot(table[:rows], low))


def edges_kernel(
    nrows, ncols, parts_ref, f_ref, w_ref, narrow_ref, near_ref, far_ref, rowtaps_ref,
    coefficients_ref, left_ref, right_ref, one_ref, other_ref, own_v1_ref, near_v1_ref, far_v1_ref, v0_ref, high_ref, low_ref,
):
    rows, cols = f_ref.shape
    v1_refs = (own_v1_ref, near_v1_ref, far_v1_ref)
    for side in range(2):
        edge_fields(side, f_ref, w_ref, narrow_ref, near_ref, far_ref, v1_refs, v0_ref)
    c0, c1 = coefficients(*coupled(parts_ref, nrows, ncols))
    coefficients_ref[pl.ds(0, 8), :] = jnp.broadcast_to(c0, (8, LANES))
    coefficients_ref[pl.ds(8, 8), :] = jnp.broadcast_to(c1, (8, LANES))
    sides = neighbours(parts_ref, nrows, ncols)
    left_ref[...], right_ref[...] = sides

    step = 16
    fields = (f_ref, w_ref, near_ref, far_ref, v1_refs)
    for side, begin in enumerate((0, cols - LANES)):
        at_cols = pl.ds(begin, LANES)
        for start, (flux_ref, flux_row), (weight_ref, weight_row), (field_ref, field_row) in regions(*fields, step):
            flux, weight = flux_ref[pl.ds(flux_row, step), at_cols], weight_ref[pl.ds(weight_row, step), at_cols]
            v1 = field_ref[pl.ds(field_row, step), pl.ds(side * LANES, LANES)]
            v1 = v1 - smooth_weight * sides[side][start : start + step]
            scatter = flux - (c0 * (flux * weight) + c1 * v1)
            high, low = split_values(scatter * scatter)
            high_ref[pl.ds(start, step), pl.ds(side * LANES, LANES)] = high
            low_ref[pl.ds(start, step), pl.ds(side * LANES, LANES)] = low
    passed = row_pass(rowtaps_ref, high_ref[...], low_ref[...], rows)
    upper, lower = slice(0, rows // 2), slice(rows // 2, rows)
    first, last = passed[:, :LANES], passed[:, LANES:]
    on_left = lax.broadcasted_iota(jnp.int32, (rows // 2, LANES), 1) < REACH
    first = jnp.where(on_left, first[upper], pltpu.roll(first[lower], REACH, 1))
    last = jnp.where(on_left, pltpu.roll(last[upper], REACH, 1), last[lower])
    even = is_even("cols")
    one_ref[...] = jnp.where(even, last, first)
    other_ref[...] = jnp.where(even, first, last)


def main_kernel(
    coefficients_ref, left_ref, right_ref, f_ref, w_ref, narrow_ref, near_ref, far_ref, rowtaps_ref, coltaps_ref,
    background_ref, rms_ref, sides_ref, own_v1_ref, near_v1_ref, far_v1_ref, v0_ref, high_ref, low_ref,
):
    rows, cols = f_ref.shape
    v1_refs = (own_v1_ref, near_v1_ref, far_v1_ref)
    all_fields(f_ref, w_ref, narrow_ref, near_ref, far_ref, v1_refs, v0_ref)
    c0, c1 = coefficients_ref[pl.ds(0, 1), pl.ds(0, 1)], coefficients_ref[pl.ds(8, 1), pl.ds(0, 1)]
    step = 16
    fields = (f_ref, w_ref, near_ref, far_ref, v1_refs)
    for start, *here in regions(*fields, step):
        flux, weight, v1 = (ref[pl.ds(row, step), :] for ref, row in here)
        at = pl.ds(start, step)
        v1 = jnp.concatenate(
            [
                v1[:, :LANES] - smooth_weight * left_ref[at, :],
                v1[:, LANES : cols - LANES],
                v1[:, cols - LANES :] - smooth_weight * right_ref[at, :],
            ],
            axis=1,
        )
        background = c0 * (flux * weight) + c1 * v1
        if start < rows:
            background_ref[at, :] = background
        scatter = flux - background
        high_ref[at, :], low_ref[at, :] = split_values(scatter * scatter)
    passed = row_pass(rowtaps_ref, high_ref[...], low_ref[...], rows)
    _, _, first_col, last_col = at_edges()
    nothing = jnp.zeros((rows, LANES), jnp.float32)
    passed = jnp.concatenate([nothing, passed, nothing], axis=1)
    high, low = split_values(pltpu.roll(passed, passed.shape[1] - (LANES - REACH), 1))
    blocks = cols // LANES
    kinds = {0: first_col.astype(jnp.int32), blocks - 1: 2 * last_col.astype(jnp.int32)}
    for j in range(blocks):
        at = slice(j * LANES, j * LANES + 2 * LANES)
        smoothed = product_of_pairs(high[:, at], low[:, at], coltaps_ref[kinds.get(j, 0)])
        if j in kinds:
            sides_ref[:, pl.ds(LANES * (j > 0), LANES)] = smoothed
        else:
            rms_ref[:, pl.ds(j * LANES, LANES)] = jnp.sqrt(smoothed + 1e-06)


def product_of_pairs(high, low, table):
    count = table.shape[1] // 2
    both = dot(high, table)
    return both[:, :count] + (both[:, count:] + dot(low, table[:, :count]))


def final_kernel(rms_in_ref, sides_ref, one_ref, other_ref, sidetaps_ref, rms_ref, blocks_ref, sems):
    rows, cols = rms_ref.shape
    del rms_in_ref
    _, _, first_col, last_col = at_edges()
    even = is_even("cols")
    left = jnp.where(even, other_ref[...], one_ref[...])
    right = jnp.where(even, one_ref[...], other_ref[...])
    copies = []
    for side, (halo, outside) in enumerate(((left, first_col), (right, last_col))):
        high, low = split_values(halo)
        added = product_of_pairs(high, low, sidetaps_ref[side])
        added = jnp.where(outside, 0.0, jnp.concatenate([added[:, :LANES], added[:, LANES:]], axis=0))
        blocks_ref[side] = jnp.sqrt(sides_ref[:, pl.ds(side * LANES, LANES)] + added + 1e-06)
        target = rms_ref.at[:, pl.ds(side * (cols - LANES), LANES)]
        copies.append(pltpu.make_async_copy(blocks_ref.at[side], target, sems.at[side]))
        copies[-1].start()
    for copy in copies:
        copy.wait()


def swap(block, axis, first):
    nrows, ncols = lax.axis_size("rows"), lax.axis_size("cols")
    count = lax.axis_size(axis)
    pairs = []
    for r in range(nrows):
        for c in range(ncols):
            along = r if axis == "rows" else c
            other = along + 1 if (along - first) % 2 == 0 else along - 1
            if 0 <= other < count:
                partner = (other, c) if axis == "rows" else (r, other)
            else:
                partner = (r, c ^ 1) if axis == "rows" else (r ^ 1, c)
            pairs.append((r * ncols + c, partner[0] * ncols + partner[1]))
    return lax.ppermute(block, ("rows", "cols"), pairs)


def call(kernel, name, outs, scratch=(), limit=16, in_place=False, out_there=False):
    vmem = pl.BlockSpec(memory_space=pltpu.VMEM)
    there = pl.BlockSpec(memory_space=pl.ANY)

    def run(*args):
        return pl.pallas_call(
            kernel,
            out_shape=tuple(jax.ShapeDtypeStruct(shape, jnp.float32) for shape in outs),
            in_specs=[there if in_place and i == 0 else vmem for i in range(len(args))],
            out_specs=(there if in_place or out_there else vmem,) * len(outs),
            scratch_shapes=list(scratch),
            input_output_aliases={0: 0} if in_place else {},
            compiler_params=pltpu.CompilerParams(vmem_limit_bytes=limit << 20),
            name=name,
        )(*args)

    return run


def shards(coadd_flux, inverse_variance, source_mask):
    rows, cols = coadd_flux.shape
    nrows, ncols = lax.axis_size("rows"), lax.axis_size("cols")
    message = (VECTORS + 1) * LANES

    def scratch(*shape, dtype=jnp.float32):
        return pltpu.VMEM(shape, dtype)

    taken = []
    for above, below in ((0, rows - 1), (1, rows - 2), (REACH, rows - 1 - REACH)):
        start = (jnp.where(is_even(), above, below), 0)
        flux, variance, mask = (
            lax.dynamic_slice(x, start, (1, cols)) for x in (coadd_flux, inverse_variance, source_mask)
        )
        taken.append((flux, weights(variance, mask)))
    products = [flux * weight for flux, weight in taken]
    narrow = swap(jnp.concatenate([products[0], products[1], taken[0][1], products[2]]), "rows", 1)

    own = (coadd_flux, weights(inverse_variance, source_mask))
    field = scratch(rows + 2 * NEAR, cols + LANES)
    to_near, to_far, *base = call(
        prepare_kernel,
        "prepare",
        ((2 * REACH + 8, cols), (2 * REACH, cols), (rows, cols), (3 * 8, LANES), (rows, LANES)),
        (field,),
    )(*own)
    to_near, to_far, narrow = lax.optimization_barrier((to_near, to_far, narrow))
    near = swap(to_near, "rows", 0)
    far = swap(to_far, "rows", 1)

    devices = nrows * ncols
    rows_sent = 8 * (VECTORS + 1)
    (parts,) = call(
        moments_kernel,
        "moments",
        ((devices * (VECTORS + 1), LANES),),
        (field, scratch(rows, LANES), scratch(rows_sent, LANES), pltpu.SemaphoreType.DMA((devices // 8,))),
        out_there=True,
    )(*own, *base, narrow, near)
    parts = lax.all_to_all(parts.reshape(devices, 1, message), ("rows", "cols"), 0, 0, tiled=True)
    first_row, last_row, _, _ = at_edges()
    kind = jnp.where(is_even(), first_row.astype(jnp.int32), 2 + last_row.astype(jnp.int32))
    row_taps = lax.dynamic_index_in_dim(jnp.asarray(row_tables(rows)), kind, keepdims=False)
    col_taps = jnp.asarray(col_tables())
    reached, packed = rows + 2 * REACH, (rows // 2, LANES)
    fields = (*own, narrow, near, far)
    v1_parts = [scratch(count, 2 * LANES) for count in (rows, REACH, REACH)]
    numbers, left, right, to_one, to_other = call(
        functools.partial(edges_kernel, nrows, ncols),
        "edges",
        ((16, LANES), (reached, LANES), (reached, LANES), packed, packed),
        [*v1_parts, scratch(rows + 2 * NEAR, LANES)] + [scratch(reached, 2 * LANES, dtype=jnp.bfloat16)] * 2,
    )(parts, *fields, row_taps)
    one = swap(to_one, "cols", 0)
    other = swap(to_other, "cols", 1)
    v1_parts = [scratch(count, cols) for count in (rows, REACH, REACH)]
    background, rms, sides = call(
        main_kernel,
        "main",
        ((rows, cols), (rows, cols), (rows, 2 * LANES)),
        [*v1_parts, field] + [scratch(reached, cols, dtype=jnp.bfloat16)] * 2,
    )(numbers, left, right, *fields, row_taps, col_taps)
    (rms,) = call(
        final_kernel, "final", ((rows, cols),), (scratch(2, rows, LANES), pltpu.SemaphoreType.DMA((2,))), in_place=True
    )(rms, sides, one, other, jnp.asarray(side_tables()))
    return background, rms


def solution(mesh):
    return jax.shard_map(
        shards,
        mesh=mesh,
        in_specs=(P("rows", "cols"), P("rows", "cols"), P("rows", "cols")),
        out_specs=(P("rows", "cols"), P("rows", "cols")),
        check_vma=False,
    )
```

```python
import functools

import jax
import jax.numpy as jnp
import ml_dtypes
import numpy as np
from jax import lax
from jax.experimental import pallas as pl
from jax.experimental.pallas import tpu as pltpu
from jax.sharding import PartitionSpec as P

RADIUS = 32
REACH = 2 * RADIUS
LANES = 128
WIDE = REACH + 8
NEAR = 8
VECTORS = 8

smooth_weight = 2.0
blur_sigma = 10.0


def squared_taps(length, first, last):
    offsets = np.arange(2 * RADIUS + 1) - RADIUS
    taps = np.exp(-offsets * offsets / (2.0 * blur_sigma * blur_sigma))
    taps = taps / taps.sum()

    def band(count):
        table = np.zeros((count, count + 2 * RADIUS))
        for k in range(2 * RADIUS + 1):
            table[np.arange(count), np.arange(count) + k] = taps[k]
        return table

    inner = band(length + 2 * RADIUS)
    if first:
        inner[:RADIUS] = 0.0
    if last:
        inner[-RADIUS:] = 0.0
    return band(length) @ inner


def split(table):
    high = table.astype(np.float32).astype(ml_dtypes.bfloat16)
    low = (table - high.astype(np.float64)).astype(np.float32).astype(ml_dtypes.bfloat16)
    return high, low


def row_tables(length):
    tables = []
    for first, last, odd in ((False, False, False), (True, False, False), (False, False, True), (False, True, True)):
        table = squared_taps(length, first, last)
        above, own, below = table[:, :REACH], table[:, REACH : REACH + length], table[:, REACH + length :]
        near, far = (above, below) if odd else (below, above)
        if first or last:
            far = np.zeros_like(far)
        tables.append(np.concatenate(split(np.concatenate([own, near, far], axis=1)), axis=0))
    return np.stack(tables)


def col_tables():
    tables = []
    for first, last in ((False, False), (True, False), (False, True)):
        table = squared_taps(LANES, first, last)
        if first:
            table[:, :REACH] = 0.0
        if last:
            table[:, REACH + LANES :] = 0.0
        tables.append(np.concatenate(split(table.T), axis=1))
    return np.stack(tables)


def side_tables():
    table = squared_taps(LANES, False, False).T
    tables = []
    for part in (table[:REACH], table[REACH + LANES :]):
        nothing = np.zeros_like(part)
        tables.append(np.concatenate(split(np.block([[part, nothing], [nothing, part]])), axis=1))
    return np.stack(tables)


def split_values(values):
    high = values.astype(jnp.bfloat16)
    return high, (values - high.astype(jnp.float32)).astype(jnp.bfloat16)


def at_edges():
    row, col = lax.axis_index("rows"), lax.axis_index("cols")
    return (
        row == 0,
        row == lax.axis_size("rows") - 1,
        col == 0,
        col == lax.axis_size("cols") - 1,
    )


def is_even(axis="rows"):
    return lax.axis_index(axis) % 2 == 0


def beside_columns(field):
    width = field.shape[1]
    return pltpu.roll(field, 1, 1) + pltpu.roll(field, width - 1, 1)


def weights(inverse_variance, source_mask):
    return inverse_variance * (1.0 - source_mask.astype(jnp.float32))


def coefficients(m0, m1, m2, m3):
    alpha0 = m0 / m1
    norm1 = jnp.maximum(m0 - 2.0 * alpha0 * m1 + alpha0 * alpha0 * m2, 0.0)
    grown = 1.0 + norm1 / m0
    image1 = grown * grown * m1 - 2.0 * grown * alpha0 * m2 + alpha0 * alpha0 * m3
    alpha1 = jnp.where(image1 > 0.0, norm1 / image1, 0.0)
    return alpha0 + alpha1 * grown, -alpha1 * alpha0


def image(ref, weight, start):
    cols = weight.shape[1]
    own = pl.ds(0, cols)
    here = ref[pl.ds(start, 8), :]
    beside = ref[pl.ds(start - 1, 8), own] + ref[pl.ds(start + 1, 8), own] + beside_columns(here)[:, :cols]
    here = here[:, :cols]
    return here, weight * here + smooth_weight * (4.0 * here - beside)


def columns_to_lanes(fields, edges, lane):
    for k, field in fields:
        edges = jnp.where(lane == k, pltpu.roll(field[:, field.shape[1] - LANES :], k + 1, 1), edges)
        edges = jnp.where(lane == 4 + k, pltpu.roll(field[:, :LANES], 4 + k, 1), edges)
    return edges


def prepare_kernel(f_ref, w_ref, near_ref, far_ref, v1_ref, sums_ref, edge_ref, v0_ref):
    rows = f_ref.shape[0]

    def write(out_ref, begin):
        out_ref[pl.ds(0, REACH), :] = f_ref[pl.ds(begin, REACH), :]
        out_ref[pl.ds(REACH, REACH), :] = w_ref[pl.ds(begin, REACH), :]

    def near_product(begin):
        near_ref[pl.ds(2 * REACH, 8), :] = f_ref[pl.ds(begin, 8), :] * w_ref[pl.ds(begin, 8), :]

    @pl.when(is_even())
    def _():
        write(near_ref, rows - REACH)
        near_product(rows - WIDE)
        write(far_ref, 0)

    @pl.when(jnp.logical_not(is_even()))
    def _():
        write(near_ref, 0)
        near_product(REACH)
        write(far_ref, rows - REACH)

    cols = f_ref.shape[1]
    own = pl.ds(0, cols)
    v0_ref[:, pl.ds(cols, LANES)] = jnp.zeros((rows + 2 * NEAR, LANES), jnp.float32)
    for start in (0, NEAR + rows):
        v0_ref[pl.ds(start, NEAR), own] = jnp.zeros((NEAR, cols), jnp.float32)
    for start in range(0, rows, 8):
        at = pl.ds(start, 8)
        v0_ref[pl.ds(NEAR + start, 8), own] = f_ref[at, :] * w_ref[at, :]
    lane = lax.broadcasted_iota(jnp.int32, (8, LANES), 1)
    sums = [jnp.zeros((8, cols), jnp.float32) for _ in range(3)]
    for start in range(0, rows, 8):
        at = pl.ds(start, 8)
        weight = w_ref[at, :]
        v0, v1 = image(v0_ref, weight, NEAR + start)
        v1_ref[at, :] = v1
        sums = [total + term for total, term in zip(sums, (v0 * v0, v0 * v1, v1 * v1))]
        edge_ref[at, :] = columns_to_lanes(((0, v0), (3, weight)), jnp.zeros((8, LANES), jnp.float32), lane)
    for i, total in enumerate(sums):
        sums_ref[pl.ds(8 * i, 8), :] = sum(total[:, k : k + LANES] for k in range(0, cols, LANES))


def moments_kernel(f_ref, w_ref, base_ref, sums_ref, edge_in_ref, narrow_ref, near_ref, out_ref, v1_ref, edge_ref):
    rows, cols = f_ref.shape
    first_row, last_row, _, _ = at_edges()
    even = is_even()
    own, pad = pl.ds(0, cols), pl.ds(cols, LANES)

    def near_rows(nearest, second):
        return (
            near_ref[pl.ds(nearest, 1), :] * near_ref[pl.ds(REACH + nearest, 1), :],
            near_ref[pl.ds(second, 1), :] * near_ref[pl.ds(REACH + second, 1), :],
            near_ref[pl.ds(REACH + nearest, 1), :],
        )

    outermost = first_row | last_row
    far_rows = tuple(jnp.where(outermost, 0.0, narrow_ref[pl.ds(k, 1), :]) for k in range(3))
    above = [jnp.where(even, far, near) for far, near in zip(far_rows, near_rows(REACH - 1, REACH - 2))]
    below = [jnp.where(even, near, far) for far, near in zip(far_rows, near_rows(0, 1))]

    v1_ref[:, pad] = jnp.zeros((rows + 2 * NEAR, LANES), jnp.float32)
    for start in (0, NEAR + rows):
        v1_ref[pl.ds(start, NEAR), own] = jnp.zeros((NEAR, cols), jnp.float32)
    row = lax.broadcasted_iota(jnp.int32, (8, cols), 0)
    for start in range(0, rows, 8):
        v1 = base_ref[pl.ds(start, 8), :]
        if start == 0:
            v1 = v1 - jnp.where(row == 0, smooth_weight * above[0], 0.0)
        if start == rows - 8:
            v1 = v1 - jnp.where(row == 7, smooth_weight * below[0], 0.0)
        v1_ref[pl.ds(NEAR + start, 8), own] = v1

    def edge_row(halo, inner, at):
        nearest, second, weight = halo
        inner = f_ref[pl.ds(inner, 1), :] * w_ref[pl.ds(inner, 1), :]
        padded = jnp.concatenate([nearest, jnp.zeros((1, LANES), jnp.float32)], axis=1)
        beside = second + inner + beside_columns(padded)[:, :cols]
        v1_ref[pl.ds(at, 1), own] = weight * nearest + smooth_weight * (4.0 * nearest - beside)

    pl.when(jnp.logical_not(first_row))(lambda: edge_row(above, 0, NEAR - 1))
    pl.when(jnp.logical_not(last_row))(lambda: edge_row(below, rows - 1, NEAR + rows))

    lane = lax.broadcasted_iota(jnp.int32, (8, LANES), 1)
    last_sum = jnp.zeros((8, cols), jnp.float32)
    for start in range(0, rows, 8):
        at = pl.ds(start, 8)
        v1, v2 = image(v1_ref, w_ref[at, :], NEAR + start)
        last_sum = last_sum + v1 * v2
        edge_ref[at, :] = columns_to_lanes(((1, v1), (2, v2)), edge_in_ref[at, :], lane)

    def narrowed(total):
        return sum(total[:, k : k + LANES] for k in range(0, cols, LANES))

    first_sum = [jnp.zeros((1, cols), jnp.float32) for _ in range(2)]
    for halo, inner in ((above, 0), (below, rows - 1)):
        at = pl.ds(inner, 1)
        added = -smooth_weight * halo[0]
        first_sum[0] = first_sum[0] + f_ref[at, :] * w_ref[at, :] * added
        first_sum[1] = first_sum[1] + (2.0 * base_ref[at, :] + added) * added
    totals = [jnp.sum(sums_ref[pl.ds(8 * i, 8), :], axis=0, keepdims=True) for i in range(3)]
    totals = [totals[0], totals[1] + narrowed(first_sum[0]), totals[2] + narrowed(first_sum[1])]
    totals.append(jnp.sum(narrowed(last_sum), axis=0, keepdims=True))
    result = jnp.zeros((1, LANES), jnp.float32)
    for i, total in enumerate(totals):
        result = jnp.where(lane[:1] == i, jnp.sum(total, axis=1, keepdims=True), result)
    vectors = edge_ref[...].T
    message = [result] + [vectors[k : k + 1, :] for k in range(VECTORS)]
    copies = jnp.concatenate(message * 8, axis=0)
    for start in range(0, out_ref.shape[0], copies.shape[0]):
        out_ref[pl.ds(start, copies.shape[0]), :] = copies


def coupled(parts_ref, nrows, ncols):
    count = nrows * ncols
    lam = smooth_weight

    def part(k):
        return parts_ref[:, :, pl.ds(k * LANES, LANES)].reshape(count, LANES)

    device = lax.broadcasted_iota(jnp.int32, (count, LANES), 0)
    lane = lax.broadcasted_iota(jnp.int32, (count, LANES), 1)
    joined = device % ncols < ncols - 1
    a0, a1, ua, wa = (jnp.where(joined, part(1 + k), 0.0) for k in range(4))
    b0, b1, ub, wb = (jnp.where(joined, pltpu.roll(part(5 + k), count - 1, 0), 0.0) for k in range(4))

    def next_row(field):
        inside = pltpu.roll(field, LANES - 1, 1)
        beyond = jnp.where(device < count - ncols, pltpu.roll(inside, count - ncols, 0), 0.0)
        return jnp.where(lane == LANES - 1, beyond, inside)

    def total(field):
        return jnp.sum(jnp.sum(field, axis=0, keepdims=True), axis=1, keepdims=True)

    scalars = jnp.sum(part(0), axis=0, keepdims=True)
    m0, m1, m2, m3 = (total(jnp.where(lane[:1] == i, scalars, 0.0)) for i in range(4))
    m1 = m1 - 2.0 * lam * total(a0 * b0)
    m2 = m2 + total(lam * lam * (a0 * a0 + b0 * b0) - 2.0 * lam * (a1 * b0 + b1 * a0))
    m3 = m3 + total(
        lam * lam * ((wa + 4.0 * lam) * b0 * b0 + (wb + 4.0 * lam) * a0 * a0)
        - 2.0 * lam * (b0 * ua + a0 * ub + (a1 - lam * b0) * (b1 - lam * a0))
        - 2.0 * lam * lam * lam * (a0 * next_row(a0) + b0 * next_row(b0))
    )
    return m0, m1, m2, m3


def neighbours(parts_ref, nrows, ncols):
    row, col = lax.axis_index("rows"), lax.axis_index("cols")
    even = is_even()
    towards = jnp.where(even, 1, -1)
    lane = lax.broadcasted_iota(jnp.int32, (LANES, LANES), 1)
    vectors = []
    for vector, step_col in ((1, -1), (5, 1)):
        for step_row in (0, towards, -towards):
            r, c = row + step_row, col + step_col
            there = (r >= 0) & (r < nrows) & (c >= 0) & (c < ncols)
            index = jnp.where(there, r * ncols + c, 0)
            found = parts_ref[index, :, pl.ds(vector * LANES, LANES)]
            vectors.append(jnp.where(there, found, 0.0))
    vectors.append(jnp.zeros((LANES - len(vectors), LANES), jnp.float32))
    columns = jnp.concatenate(vectors, axis=0).T
    sides = []
    for begin, target in ((0, 0), (3, LANES - 1)):
        own, near, far = (
            jnp.where(lane == target, pltpu.roll(columns, (target - begin - k) % LANES, 1), 0.0) for k in range(3)
        )
        near = jnp.where(even, near[:REACH], near[LANES - REACH :])
        far = jnp.where(even, far[LANES - REACH :], far[:REACH])
        sides.append(jnp.concatenate([own, near, far], axis=0))
    return sides


def guard_rows(f_ref, w_ref, narrow_ref, near_ref, at_cols):
    rows = f_ref.shape[0]
    first_row, last_row, _, _ = at_edges()
    even = is_even()
    top = f_ref[pl.ds(0, 1), at_cols] * w_ref[pl.ds(0, 1), at_cols]
    bottom = f_ref[pl.ds(rows - 1, 1), at_cols] * w_ref[pl.ds(rows - 1, 1), at_cols]
    near_last = near_ref[pl.ds(REACH - 1, 1), at_cols] * near_ref[pl.ds(2 * REACH - 1, 1), at_cols]
    near_first = near_ref[pl.ds(0, 1), at_cols] * near_ref[pl.ds(REACH, 1), at_cols]
    far_nearest = jnp.where(first_row | last_row, 0.0, narrow_ref[pl.ds(0, 1), at_cols])
    near = jnp.where(even, near_ref[pl.ds(2 * REACH, 1), at_cols], near_ref[pl.ds(2 * REACH + 7, 1), at_cols])
    far = narrow_ref[pl.ds(3, 1), at_cols]
    return (
        (jnp.where(even, far_nearest, near_last), jnp.where(even, near_first, far_nearest)),
        (jnp.where(even, bottom, near), jnp.where(even, near, top)),
        (jnp.where(even, far, bottom), jnp.where(even, top, far)),
    )


def sources(f_ref, w_ref, near_ref, far_ref, v1_refs):
    rows = f_ref.shape[0]
    return (
        (rows, f_ref, w_ref, 0, v1_refs[0]),
        (REACH, near_ref, near_ref, REACH, v1_refs[1]),
        (REACH, far_ref, far_ref, REACH, v1_refs[2]),
    )


def all_fields(f_ref, w_ref, narrow_ref, near_ref, far_ref, v1_refs, v0_ref):
    rows, cols = f_ref.shape
    own, pad = pl.ds(0, cols), pl.ds(cols, LANES)
    v0_ref[:, pad] = jnp.zeros((rows + 2 * NEAR, LANES), jnp.float32)
    guards = guard_rows(f_ref, w_ref, narrow_ref, near_ref, own)
    for (count, flux_ref, weight_ref, weight_row, v1_ref), (above, below) in zip(
        sources(f_ref, w_ref, near_ref, far_ref, v1_refs), guards
    ):
        v0_ref[pl.ds(NEAR - 1, 1), own] = above
        v0_ref[pl.ds(NEAR + count, 1), own] = below
        for start in range(0, count, 8):
            v0_ref[pl.ds(NEAR + start, 8), own] = flux_ref[pl.ds(start, 8), :] * weight_ref[pl.ds(weight_row + start, 8), :]
        for start in range(0, count, 8):
            _, v1_ref[pl.ds(start, 8), :] = image(v0_ref, weight_ref[pl.ds(weight_row + start, 8), :], NEAR + start)


def edge_fields(side, f_ref, w_ref, narrow_ref, near_ref, far_ref, v1_refs, v0_ref):
    cols = f_ref.shape[1]
    at_cols, there = pl.ds(side * (cols - LANES), LANES), pl.ds(side * LANES, LANES)
    outermost = lax.broadcasted_iota(jnp.int32, (8, LANES), 1) == side * (LANES - 1)
    guards = guard_rows(f_ref, w_ref, narrow_ref, near_ref, at_cols)
    for (count, flux_ref, weight_ref, weight_row, v1_ref), (above, below) in zip(
        sources(f_ref, w_ref, near_ref, far_ref, v1_refs), guards
    ):
        v0_ref[pl.ds(NEAR - 1, 1), :] = above
        v0_ref[pl.ds(NEAR + count, 1), :] = below
        for start in range(0, count, 8):
            weight = weight_ref[pl.ds(weight_row + start, 8), at_cols]
            v0_ref[pl.ds(NEAR + start, 8), :] = flux_ref[pl.ds(start, 8), at_cols] * weight
        for start in range(0, count, 8):
            here = v0_ref[pl.ds(NEAR + start, 8), :]
            inner = pltpu.roll(here, 1 if side else LANES - 1, 1)
            outer = jnp.where(outermost, 0.0, pltpu.roll(here, LANES - 1 if side else 1, 1))
            beside = v0_ref[pl.ds(NEAR + start - 1, 8), :] + v0_ref[pl.ds(NEAR + start + 1, 8), :] + inner + outer
            weight = weight_ref[pl.ds(weight_row + start, 8), at_cols]
            v1_ref[pl.ds(start, 8), there] = weight * here + smooth_weight * (4.0 * here - beside)


def regions(f_ref, w_ref, near_ref, far_ref, v1_refs, step):
    base = 0
    for count, flux_ref, weight_ref, weight_row, v1_ref in sources(f_ref, w_ref, near_ref, far_ref, v1_refs):
        for start in range(0, count, step):
            yield base + start, (flux_ref, start), (weight_ref, weight_row + start), (v1_ref, start)
        base += count


def dot(left, right):
    return jnp.dot(left, right, preferred_element_type=jnp.float32)


def row_pass(rowtaps_ref, high, low, rows):
    table = rowtaps_ref[...]
    both = dot(table, high)
    return both[:rows] + (both[rows:] + dot(table[:rows], low))


def edges_kernel(
    nrows, ncols, parts_ref, f_ref, w_ref, narrow_ref, near_ref, far_ref, rowtaps_ref,
    coefficients_ref, left_ref, right_ref, one_ref, other_ref, own_v1_ref, near_v1_ref, far_v1_ref, v0_ref, high_ref, low_ref,
):
    rows, cols = f_ref.shape
    v1_refs = (own_v1_ref, near_v1_ref, far_v1_ref)
    for side in range(2):
        edge_fields(side, f_ref, w_ref, narrow_ref, near_ref, far_ref, v1_refs, v0_ref)
    c0, c1 = coefficients(*coupled(parts_ref, nrows, ncols))
    coefficients_ref[pl.ds(0, 8), :] = jnp.broadcast_to(c0, (8, LANES))
    coefficients_ref[pl.ds(8, 8), :] = jnp.broadcast_to(c1, (8, LANES))
    sides = neighbours(parts_ref, nrows, ncols)
    left_ref[...], right_ref[...] = sides

    step = 16
    fields = (f_ref, w_ref, near_ref, far_ref, v1_refs)
    for side, begin in enumerate((0, cols - LANES)):
        at_cols = pl.ds(begin, LANES)
        for start, (flux_ref, flux_row), (weight_ref, weight_row), (field_ref, field_row) in regions(*fields, step):
            flux, weight = flux_ref[pl.ds(flux_row, step), at_cols], weight_ref[pl.ds(weight_row, step), at_cols]
            v1 = field_ref[pl.ds(field_row, step), pl.ds(side * LANES, LANES)]
            v1 = v1 - smooth_weight * sides[side][start : start + step]
            scatter = flux - (c0 * (flux * weight) + c1 * v1)
            high, low = split_values(scatter * scatter)
            high_ref[pl.ds(start, step), pl.ds(side * LANES, LANES)] = high
            low_ref[pl.ds(start, step), pl.ds(side * LANES, LANES)] = low
    passed = row_pass(rowtaps_ref, high_ref[...], low_ref[...], rows)
    upper, lower = slice(0, rows // 2), slice(rows // 2, rows)
    first, last = passed[:, :LANES], passed[:, LANES:]
    on_left = lax.broadcasted_iota(jnp.int32, (rows // 2, LANES), 1) < REACH
    first = jnp.where(on_left, first[upper], pltpu.roll(first[lower], REACH, 1))
    last = jnp.where(on_left, pltpu.roll(last[upper], REACH, 1), last[lower])
    even = is_even("cols")
    one_ref[...] = jnp.where(even, last, first)
    other_ref[...] = jnp.where(even, first, last)


def main_kernel(
    coefficients_ref, left_ref, right_ref, f_ref, w_ref, narrow_ref, near_ref, far_ref, rowtaps_ref, coltaps_ref,
    background_ref, rms_ref, sides_ref, own_v1_ref, near_v1_ref, far_v1_ref, v0_ref, high_ref, low_ref,
):
    rows, cols = f_ref.shape
    v1_refs = (own_v1_ref, near_v1_ref, far_v1_ref)
    all_fields(f_ref, w_ref, narrow_ref, near_ref, far_ref, v1_refs, v0_ref)
    c0, c1 = coefficients_ref[pl.ds(0, 1), pl.ds(0, 1)], coefficients_ref[pl.ds(8, 1), pl.ds(0, 1)]
    step = 16
    fields = (f_ref, w_ref, near_ref, far_ref, v1_refs)
    for start, *here in regions(*fields, step):
        flux, weight, v1 = (ref[pl.ds(row, step), :] for ref, row in here)
        at = pl.ds(start, step)
        v1 = jnp.concatenate(
            [
                v1[:, :LANES] - smooth_weight * left_ref[at, :],
                v1[:, LANES : cols - LANES],
                v1[:, cols - LANES :] - smooth_weight * right_ref[at, :],
            ],
            axis=1,
        )
        background = c0 * (flux * weight) + c1 * v1
        if start < rows:
            background_ref[at, :] = background
        scatter = flux - background
        high_ref[at, :], low_ref[at, :] = split_values(scatter * scatter)
    passed = row_pass(rowtaps_ref, high_ref[...], low_ref[...], rows)
    _, _, first_col, last_col = at_edges()
    nothing = jnp.zeros((rows, LANES), jnp.float32)
    passed = jnp.concatenate([nothing, passed, nothing], axis=1)
    high, low = split_values(pltpu.roll(passed, passed.shape[1] - (LANES - REACH), 1))
    blocks = cols // LANES
    kinds = {0: first_col.astype(jnp.int32), blocks - 1: 2 * last_col.astype(jnp.int32)}
    for j in range(blocks):
        at = slice(j * LANES, j * LANES + 2 * LANES)
        smoothed = product_of_pairs(high[:, at], low[:, at], coltaps_ref[kinds.get(j, 0)])
        if j in kinds:
            sides_ref[:, pl.ds(LANES * (j > 0), LANES)] = smoothed
        else:
            rms_ref[:, pl.ds(j * LANES, LANES)] = jnp.sqrt(smoothed + 1e-06)


def product_of_pairs(high, low, table):
    count = table.shape[1] // 2
    both = dot(high, table)
    return both[:, :count] + (both[:, count:] + dot(low, table[:, :count]))


def final_kernel(rms_in_ref, sides_ref, one_ref, other_ref, sidetaps_ref, rms_ref, blocks_ref, sems):
    rows, cols = rms_ref.shape
    del rms_in_ref
    _, _, first_col, last_col = at_edges()
    even = is_even("cols")
    left = jnp.where(even, other_ref[...], one_ref[...])
    right = jnp.where(even, one_ref[...], other_ref[...])
    copies = []
    for side, (halo, outside) in enumerate(((left, first_col), (right, last_col))):
        high, low = split_values(halo)
        added = product_of_pairs(high, low, sidetaps_ref[side])
        added = jnp.where(outside, 0.0, jnp.concatenate([added[:, :LANES], added[:, LANES:]], axis=0))
        blocks_ref[side] = jnp.sqrt(sides_ref[:, pl.ds(side * LANES, LANES)] + added + 1e-06)
        target = rms_ref.at[:, pl.ds(side * (cols - LANES), LANES)]
        copies.append(pltpu.make_async_copy(blocks_ref.at[side], target, sems.at[side]))
        copies[-1].start()
    for copy in copies:
        copy.wait()


def swap(block, axis, first):
    nrows, ncols = lax.axis_size("rows"), lax.axis_size("cols")
    count = lax.axis_size(axis)
    pairs = []
    for r in range(nrows):
        for c in range(ncols):
            along = r if axis == "rows" else c
            other = along + 1 if (along - first) % 2 == 0 else along - 1
            if 0 <= other < count:
                partner = (other, c) if axis == "rows" else (r, other)
            else:
                partner = (r, c ^ 1) if axis == "rows" else (r ^ 1, c)
            pairs.append((r * ncols + c, partner[0] * ncols + partner[1]))
    return lax.ppermute(block, ("rows", "cols"), pairs)


def call(kernel, name, outs, scratch=(), limit=16, in_place=False):
    vmem = pl.BlockSpec(memory_space=pltpu.VMEM)
    there = pl.BlockSpec(memory_space=pl.ANY)

    def run(*args):
        return pl.pallas_call(
            kernel,
            out_shape=tuple(jax.ShapeDtypeStruct(shape, jnp.float32) for shape in outs),
            in_specs=[there if in_place and i == 0 else vmem for i in range(len(args))],
            out_specs=(there if in_place else vmem,) * len(outs),
            scratch_shapes=list(scratch),
            input_output_aliases={0: 0} if in_place else {},
            compiler_params=pltpu.CompilerParams(vmem_limit_bytes=limit << 20),
            name=name,
        )(*args)

    return run


def shards(coadd_flux, inverse_variance, source_mask):
    rows, cols = coadd_flux.shape
    nrows, ncols = lax.axis_size("rows"), lax.axis_size("cols")
    message = (VECTORS + 1) * LANES

    def scratch(*shape, dtype=jnp.float32):
        return pltpu.VMEM(shape, dtype)

    taken = []
    for above, below in ((0, rows - 1), (1, rows - 2), (REACH, rows - 1 - REACH)):
        flux, variance, mask = (
            jnp.where(is_even(), x[above : above + 1], x[below : below + 1])
            for x in (coadd_flux, inverse_variance, source_mask)
        )
        taken.append((flux, weights(variance, mask)))
    products = [flux * weight for flux, weight in taken]
    narrow = swap(jnp.concatenate([products[0], products[1], taken[0][1], products[2]]), "rows", 1)

    own = (coadd_flux, weights(inverse_variance, source_mask))
    field = scratch(rows + 2 * NEAR, cols + LANES)
    to_near, to_far, *base = call(
        prepare_kernel,
        "prepare",
        ((2 * REACH + 8, cols), (2 * REACH, cols), (rows, cols), (3 * 8, LANES), (rows, LANES)),
        (field,),
    )(*own)
    to_near, to_far, narrow = lax.optimization_barrier((to_near, to_far, narrow))
    near = swap(to_near, "rows", 0)
    far = swap(to_far, "rows", 1)

    devices = nrows * ncols
    (parts,) = call(
        moments_kernel,
        "moments",
        ((devices * (VECTORS + 1), LANES),),
        (field, scratch(rows, LANES)),
    )(*own, *base, narrow, near)
    parts = lax.all_to_all(parts.reshape(devices, 1, message), ("rows", "cols"), 0, 0, tiled=True)
    first_row, last_row, _, _ = at_edges()
    kind = jnp.where(is_even(), first_row.astype(jnp.int32), 2 + last_row.astype(jnp.int32))
    row_taps = lax.dynamic_index_in_dim(jnp.asarray(row_tables(rows)), kind, keepdims=False)
    col_taps = jnp.asarray(col_tables())
    reached, packed = rows + 2 * REACH, (rows // 2, LANES)
    fields = (*own, narrow, near, far)
    v1_parts = [scratch(count, 2 * LANES) for count in (rows, REACH, REACH)]
    numbers, left, right, to_one, to_other = call(
        functools.partial(edges_kernel, nrows, ncols),
        "edges",
        ((16, LANES), (reached, LANES), (reached, LANES), packed, packed),
        [*v1_parts, scratch(rows + 2 * NEAR, LANES)] + [scratch(reached, 2 * LANES, dtype=jnp.bfloat16)] * 2,
    )(parts, *fields, row_taps)
    one = swap(to_one, "cols", 0)
    other = swap(to_other, "cols", 1)
    v1_parts = [scratch(count, cols) for count in (rows, REACH, REACH)]
    background, rms, sides = call(
        main_kernel,
        "main",
        ((rows, cols), (rows, cols), (rows, 2 * LANES)),
        [*v1_parts, field] + [scratch(reached, cols, dtype=jnp.bfloat16)] * 2,
    )(numbers, left, right, *fields, row_taps, col_taps)
    (rms,) = call(
        final_kernel, "final", ((rows, cols),), (scratch(2, rows, LANES), pltpu.SemaphoreType.DMA((2,))), in_place=True
    )(rms, sides, one, other, jnp.asarray(side_tables()))
    return background, rms


def solution(mesh):
    return jax.shard_map(
        shards,
        mesh=mesh,
        in_specs=(P("rows", "cols"), P("rows", "cols"), P("rows", "cols")),
        out_specs=(P("rows", "cols"), P("rows", "cols")),
        check_vma=False,
    )
```
